32 devices in a mesh: sp: 4 (over z), fsdp: 8 (over y, x, core).
Axes of the slice: x: 2, y: 2, z: 4, core: 2. Of those that a mesh axis runs over, the one named last changes fastest.
Arguments:
- tokens: bfloat16 [8, 512, 2048], P('fsdp', 'sp'), may hold values from -6 to 6
- expert_ids: int32 [8, 512, 8], P('fsdp', 'sp'), may hold values from 0 to 15, all different within a row; in each aligned block of 128 rows (0 to 127, 128 to 255, ..., all dimensions but the last counted through in order) at most 80 rows name the same one
- attn_gain: float32 [2048], P('fsdp'), may hold values from 0.25 to 1.75
- query_weight: float32 [2048, 4096], P('fsdp'), may hold values from -0.125 to 0.125
- key_weight: float32 [2048, 512], P('fsdp'), may hold values from -0.125 to 0.125
- value_weight: float32 [2048, 512], P('fsdp'), may hold values from -0.125 to 0.125
- q_gain: float32 [128], P('fsdp'), may hold values from 0.25 to 1.75
- k_gain: float32 [128], P('fsdp'), may hold values from 0.25 to 1.75
- output_weight: float32 [4096, 2048], P('fsdp'), may hold values from -0.375 to 0.375
- ffn_gain: float32 [2048], P('fsdp'), may hold values from 0.25 to 1.75
- router_weight: float32 [2048, 16], P('fsdp'), may hold values from -0.0625 to 0.0625
- w_gate: float32 [16, 2048, 768], P(None, 'fsdp'), may hold values from -0.125 to 0.125
- w_up: float32 [16, 2048, 768], P(None, 'fsdp'), may hold values from -0.125 to 0.125
- w_down: float32 [16, 768, 2048], P(None, 'fsdp'), may hold values from -0.625 to 0.625
- cotangent: bfloat16 [8, 512, 2048], P('fsdp', 'sp'), may hold values from -6 to 6
Outputs:
- mixed: bfloat16 [8, 512, 2048], P('fsdp', 'sp')
- grad_tokens: float32 [8, 512, 2048], P('fsdp', 'sp')
- grad_attn_gain: float32 [2048], P('fsdp')
- grad_w_query: float32 [2048, 4096], P('fsdp')
- grad_w_key: float32 [2048, 512], P('fsdp')
- grad_w_value: float32 [2048, 512], P('fsdp')
- grad_q_gain: float32 [128], P('fsdp')
- grad_k_gain: float32 [128], P('fsdp')
- grad_w_out: float32 [4096, 2048], P('fsdp')
- grad_ffn_gain: float32 [2048], P('fsdp')
- grad_w_router: float32 [2048, 16], P('fsdp')
- grad_w_gate: float32 [16, 2048, 768], P(None, 'fsdp')
- grad_w_up: float32 [16, 2048, 768], P(None, 'fsdp')
- grad_w_down: float32 [16, 768, 2048], P(None, 'fsdp')
The draws below stay inside these ranges and needn't reach their ends.
Inputs may be any that keep to these rules, and one draw needn't show every extreme that they name: `expert_ids`: each token names 8 different experts. In the rows of one device, no expert is named more than 80 times, and in every draw some expert of some device is named exactly 80 times.
All inputs are finite; a program needn't handle non-finite values.
Results may differ from the reference program's by a relative error of at most 0.023.
Values may be sent and summed in bfloat16 or wider, within the bound.
A program may use at most 320 MiB of HBM per device.

```python
import math
from functools import partial
import jax
import jax.numpy as jnp
import numpy as np
from jax import lax

D = 2048
QUERY_HEADS = 32
KEY_VALUE_HEADS = 4
HEAD_SIZE = 128
FF = 768
EXPERTS = 16
TOPK = 8
TOK_DEV = 128
CAP = 80
SEQ_LEN = 512
SEQS = 8
N_SP = 4


def shard_levels(rng, dims, cuts, low, largest):
    def one(axis_at, shards_of):
        steps = jax.random.uniform(jax.random.fold_in(jax.random.fold_in(rng, 6), axis_at), (shards_of,), jnp.float32, low / len(cuts), largest / len(cuts))
        return jnp.repeat(jnp.exp(steps), dims[axis_at] // shards_of).reshape((-1,) + (1,) * (len(dims) - axis_at - 1))

    level = one(*cuts[0])
    for cut in cuts[1:]:
        level = level * one(*cut)
    return level


def deal_out(own_key, own, number, rows, number_of, top, bound, skew):
    ranking = jax.random.permutation(own_key, number_of)
    packed, common = shares(number_of, rows * top, bound, skew, True), shares(number_of, rows * top, bound, skew, False)
    places = jnp.arange(number_of)

    def named(tallies, rotation):
        used = int((tallies > 0).sum())
        fixed = max(1, used // 4)
        shifted = fixed + (places - fixed + rotation * (used - fixed)) % max(1, number_of - fixed)
        return jnp.zeros((number_of,), jnp.int32).at[ranking[jnp.where(places < fixed, places, shifted)]].set(jnp.asarray(tallies, jnp.int32))

    tallies = jnp.where(number % 4 == 0, named(packed, number // 4), named(common, number - number // 4 - 1))
    mixed = jax.random.permutation(jax.random.fold_in(own, 3), number_of)
    giver, receiver = mixed[0:number_of // 2 * 2:2], mixed[1:number_of // 2 * 2:2]
    room = jnp.minimum(tallies[giver] - 1, bound - tallies[receiver]) // 2
    room = jnp.where((giver == ranking[0]) | (receiver == ranking[0]) | (tallies[receiver] == 0), 0, jnp.maximum(room, 0))
    shifted = jax.random.randint(jax.random.fold_in(own, 4), (number_of // 2,), 0, 1 << 20) % (room + 1)
    tallies = tallies.at[giver].add(-shifted).at[receiver].add(shifted)
    members = jnp.searchsorted(jnp.cumsum(tallies), jnp.arange(rows * top), side="right").astype(jnp.int32)
    listing = members.reshape(top, rows).T
    listing = listing[jax.random.permutation(jax.random.fold_in(own, 1), rows)]
    rotation = jax.random.randint(jax.random.fold_in(own, 2), (rows, 1), 0, top)
    return jnp.take_along_axis(listing, (jnp.arange(top)[None, :] + rotation) % top, axis=1)


def shares(count, total, reach, lean, full):
    loads = [(1 << 20) // math.isqrt(standing ** lean) + 1 for standing in range(1, count + 1)]
    largest = reach if full else min(reach, max(-(-total // count), total * loads[0] // sum(loads)))
    least = 1 if total - largest >= count - 1 else 0
    counts, spare = [largest] + [least] * (count - 1), total - largest - least * (count - 1)
    while spare > 0:
        candidates = [i for i in range(1, count) if counts[i] < largest] or [i for i in range(1, count) if counts[i] < reach]
        mass, left = sum([loads[i] for i in candidates]), spare
        for i in candidates:
            more = min(reach - counts[i], max(1, left * loads[i] // mass), spare)
            counts[i] = counts[i] + more
            spare = spare - more
    return np.array(counts)


def normal_values(stream_key, extent, deviation, most, cuts=(), held_as=jnp.bfloat16):
    gain = shard_levels(stream_key, extent, cuts, -0.22, 0.18) if cuts else 1.0
    entries = jax.random.normal(stream_key, extent, jnp.float32) * deviation * gain
    return jnp.minimum(jnp.maximum(entries, -most), most).astype(held_as)


def setup_inputs(seed: int = 0) -> dict:
    splits = jax.random.split(jax.random.key(seed), 16)
    tokens = normal_values(splits[0], (SEQS, SEQ_LEN, D), 1.0, 6.0, ((0, 8), (1, 4)))
    expert_ids_keys = jax.random.split(jax.random.fold_in(splits[1], 1), SEQS * SEQ_LEN // TOK_DEV)
    expert_ids_turns = jax.random.permutation(jax.random.fold_in(splits[1], 3), SEQS * SEQ_LEN // TOK_DEV)
    expert_ids = jax.vmap(lambda own, number: deal_out(jax.random.fold_in(splits[1], 2), own, number, TOK_DEV, EXPERTS, TOPK, CAP, 0))(expert_ids_keys, expert_ids_turns).reshape((SEQS, SEQ_LEN, TOPK))
    attn_gain = jnp.clip(1.0 + 0.15 * jax.random.normal(splits[2], (D,), jnp.float32), 0.25, 1.75)
    query_weight = normal_values(splits[3], (D, QUERY_HEADS * HEAD_SIZE), D ** -0.5, 0.125, ((0, 8),), jnp.float32)
    key_weight = normal_values(splits[4], (D, KEY_VALUE_HEADS * HEAD_SIZE), D ** -0.5, 0.125, ((0, 8),), jnp.float32)
    value_weight = normal_values(splits[5], (D, KEY_VALUE_HEADS * HEAD_SIZE), D ** -0.5, 0.125, ((0, 8),), jnp.float32)
    q_gain = jnp.clip(1.0 + 0.15 * jax.random.normal(splits[6], (HEAD_SIZE,), jnp.float32), 0.25, 1.75)
    k_gain = jnp.clip(1.0 + 0.15 * jax.random.normal(splits[7], (HEAD_SIZE,), jnp.float32), 0.25, 1.75)
    output_weight = normal_values(splits[8], (QUERY_HEADS * HEAD_SIZE, D), (QUERY_HEADS * HEAD_SIZE // 16) ** -0.5, 0.375, ((0, 8),), jnp.float32)
    ffn_gain = jnp.clip(1.0 + 0.15 * jax.random.normal(splits[9], (D,), jnp.float32), 0.25, 1.75)
    router_weight = normal_values(splits[10], (D, EXPERTS), (4 * D) ** -0.5, 0.0625, ((0, 8),), jnp.float32)
    w_gate = normal_values(splits[11], (EXPERTS, D, FF), D ** -0.5, 0.125, ((1, 8),), jnp.float32)
    w_up = normal_values(splits[12], (EXPERTS, D, FF), D ** -0.5, 0.125, ((1, 8),), jnp.float32)
    w_down = normal_values(splits[13], (EXPERTS, FF, D), (FF // 8) ** -0.5, 0.625, ((1, 8),), jnp.float32)
    cotangent = normal_values(splits[14], (SEQS, SEQ_LEN, D), 1.0, 6.0, ((0, 8), (1, 4)))
    return {"tokens": tokens, "expert_ids": expert_ids, "attn_gain": attn_gain, "query_weight": query_weight, "key_weight": key_weight, "value_weight": value_weight, "q_gain": q_gain, "k_gain": k_gain, "output_weight": output_weight, "ffn_gain": ffn_gain, "router_weight": router_weight, "w_gate": w_gate, "w_up": w_up, "w_down": w_down, "cotangent": cotangent}


@jax.custom_vjp
def low_precision(v):
    return lax.optimization_barrier(v.astype(jnp.bfloat16)).astype(jnp.float32)

@jax.custom_vjp
def low_precision_backward(v):
    return v

def low_keep(v):
    return (low_precision(v), None)

def low_pass(kept, grad):
    return (grad,)

def back_keep(v):
    return (v, None)

def back_low(kept, grad):
    return (low_precision(grad),)
low_precision.defvjp(low_keep, low_pass)
low_precision_backward.defvjp(back_keep, back_low)
EPS = 1e-06
THETA = 1000000.0
HIGH_PRECISION = lax.Precision.HIGHEST

def rms_norm(values_in, gain_vec):
    return values_in * lax.rsqrt(lax.optimization_barrier(jnp.mean(values_in * values_in, axis=-1, keepdims=True)) + EPS) * gain_vec

def rotate(values_in, angles):
    half_dim = values_in.shape[-1] // 2
    cosine = jnp.cos(angles)[:, None, :]
    sine_part = jnp.sin(angles)[:, None, :]
    first_half = values_in[..., :half_dim]
    second = values_in[..., half_dim:]
    return jnp.concatenate([first_half * cosine - second * sine_part, second * cosine + first_half * sine_part], axis=-1)

def head_prep(linear, gain_vec, angles):
    return rotate(rms_norm(linear, gain_vec), angles)

def attend(pieces):
    query_grp, key_rows, value_rows = pieces
    sequence_length = key_rows.shape[0]
    score_scale = 1.0 / math.sqrt(key_rows.shape[1])
    scores = low_precision_backward(jnp.einsum('qhd,kd->hqk', query_grp, key_rows, precision=HIGH_PRECISION) * score_scale)
    row_idx = jnp.arange(sequence_length, dtype=jnp.int32)
    causal = row_idx[None, :] <= row_idx[:, None]
    scores = jnp.where(causal[None], scores, -1e+30)
    prob_rows = low_precision(jax.nn.softmax(scores, axis=-1))
    return jnp.einsum('hqk,kd->qhd', prob_rows, value_rows, precision=HIGH_PRECISION)

def layer(routes, x_rows, attn_gain, query_weight, key_weight, value_weight, q_gain, k_gain, output_weight, ffn_gain, router_weight, w_gate, w_up, w_down):
    sequence_count, sequence_length, model_width = x_rows.shape
    repeat = N_SP // KEY_VALUE_HEADS
    group = QUERY_HEADS // N_SP
    input_normed = low_precision(rms_norm(x_rows, low_precision(attn_gain)))
    half_dim = HEAD_SIZE // 2
    inverse_freq = THETA ** (-(jnp.arange(half_dim, dtype=jnp.float32) * 2.0 / HEAD_SIZE))
    positions = jnp.arange(sequence_length, dtype=jnp.int32).astype(jnp.float32)
    angles = positions[:, None] * inverse_freq[None, :]
    query_linear = low_precision_backward(jnp.einsum('vng,gx->vnx', input_normed, low_precision(query_weight), precision=HIGH_PRECISION)).reshape(sequence_count, sequence_length, QUERY_HEADS, HEAD_SIZE)
    queries = low_precision_backward(low_precision(head_prep(query_linear, low_precision(q_gain), angles)))
    key_linear = low_precision_backward(jnp.einsum('vng,gx->vnx', input_normed, low_precision(key_weight), precision=HIGH_PRECISION)).reshape(sequence_count, sequence_length, KEY_VALUE_HEADS, HEAD_SIZE)
    key_rep = low_precision_backward(jnp.repeat(low_precision(head_prep(key_linear, low_precision(k_gain), angles)), repeat, axis=2))
    value_linear = low_precision_backward(jnp.einsum('vng,gx->vnx', input_normed, low_precision(value_weight), precision=HIGH_PRECISION)).reshape(sequence_count, sequence_length, KEY_VALUE_HEADS, HEAD_SIZE)
    value_rep = low_precision_backward(jnp.repeat(low_precision(value_linear), repeat, axis=2))
    query_grp = queries.reshape(sequence_count, sequence_length, N_SP, group, HEAD_SIZE).transpose(0, 2, 1, 3, 4).reshape(sequence_count * N_SP, sequence_length, group, HEAD_SIZE)
    key_grp = key_rep.transpose(0, 2, 1, 3).reshape(sequence_count * N_SP, sequence_length, HEAD_SIZE)
    value_grp = value_rep.transpose(0, 2, 1, 3).reshape(sequence_count * N_SP, sequence_length, HEAD_SIZE)
    attended_rows = lax.map(jax.checkpoint(attend), (query_grp, key_grp, value_grp))
    attended_rows = attended_rows.reshape(sequence_count, N_SP, sequence_length, group, HEAD_SIZE).transpose(0, 2, 1, 3, 4).reshape(sequence_count, sequence_length, QUERY_HEADS * HEAD_SIZE)
    attended_rows = low_precision_backward(low_precision(attended_rows))
    branch_output = low_precision_backward(jnp.einsum('nhx,xz->nhz', attended_rows, low_precision(output_weight), precision=HIGH_PRECISION))
    mid_rows = x_rows + branch_output
    hidden_normed = low_precision(rms_norm(mid_rows, low_precision(ffn_gain)))
    router_logits = jnp.einsum('vng,gx->vnx', hidden_normed, low_precision(router_weight), precision=HIGH_PRECISION)
    chosen = jnp.take_along_axis(router_logits, routes, axis=-1)
    gate_probs = jax.nn.softmax(chosen, axis=-1)
    onehot = (routes[..., None] == jnp.arange(EXPERTS, dtype=jnp.int32)).astype(jnp.float32)
    combine = lax.optimization_barrier(jnp.sum(gate_probs[..., None] * onehot, axis=-2)).reshape(sequence_count * sequence_length, EXPERTS)
    flat_hn = hidden_normed.reshape(sequence_count * sequence_length, model_width)

    def expert_term(total_sum, pieces):
        gate_w, up_w, down_w, weight_col = pieces
        gate_pre = low_precision_backward(jnp.dot(flat_hn, low_precision(gate_w), precision=HIGH_PRECISION))
        up_pre = low_precision_backward(jnp.dot(flat_hn, low_precision(up_w), precision=HIGH_PRECISION))
        hidden = low_precision(jax.nn.silu(gate_pre) * up_pre)
        result = low_precision_backward(jnp.dot(hidden, low_precision(down_w), precision=HIGH_PRECISION))
        return (total_sum + weight_col[:, None] * result, None)
    start_sum = jnp.zeros((sequence_count * sequence_length, model_width), jnp.float32)
    moe_sum, unused = lax.scan(jax.checkpoint(expert_term), start_sum, (w_gate, w_up, w_down, combine.T))
    return mid_rows + moe_sum.reshape(sequence_count, sequence_length, model_width)

def reference(tokens, expert_ids, attn_gain, query_weight, key_weight, value_weight, q_gain, k_gain, output_weight, ffn_gain, router_weight, w_gate, w_up, w_down, cotangent):
    x_rows = tokens.astype(jnp.float32)
    forward = partial(layer, expert_ids)
    mixed, pull = jax.vjp(forward, x_rows, attn_gain, query_weight, key_weight, value_weight, q_gain, k_gain, output_weight, ffn_gain, router_weight, w_gate, w_up, w_down)
    grads = pull(cotangent.astype(jnp.float32))
    return (mixed.astype(jnp.bfloat16), grads[0], grads[1], grads[2], grads[3], grads[4], grads[5], grads[6], grads[7], grads[8], grads[9], grads[10], grads[11], grads[12])
```

```python
import math
from typing import Callable, NamedTuple

import jax
import jax.numpy as jnp
from jax import lax
from jax.experimental import pallas as pl
from jax.experimental.pallas import tpu as pltpu
from jax.sharding import PartitionSpec as P

QUERY_HEADS = 32
KEY_VALUE_HEADS = 4
HEAD_SIZE = 128
CAP = 80
LANES = 128

EPS = 1e-06
THETA = 1000000.0
HIGH_PRECISION = lax.Precision.HIGHEST
BF16 = jnp.bfloat16
FLOAT = jnp.float32
MESH = pl.DeviceIdType.MESH


def rms_norm(values_in, gain_vec):
    return (
        values_in
        * lax.rsqrt(jnp.mean(values_in * values_in, axis=-1, keepdims=True) + EPS)
        * gain_vec
    )


def rotate(values_in, cosine, sine_part):
    half_dim = values_in.shape[-1] // 2
    first_half = values_in[..., :half_dim]
    second = values_in[..., half_dim:]
    return jnp.concatenate(
        [first_half * cosine - second * sine_part, second * cosine + first_half * sine_part],
        axis=-1,
    )


def contract_rows(left_mat, right_mat):
    return lax.dot_general(
        left_mat, right_mat, (((0,), (0,)), ((), ())), preferred_element_type=FLOAT
    )


def contract_cols(left_mat, right_mat):
    return lax.dot_general(
        left_mat, right_mat, (((1,), (1,)), ((), ())), preferred_element_type=FLOAT
    )


def matmul(left_mat, right_mat):
    return jnp.dot(left_mat, right_mat, preferred_element_type=FLOAT)


def flip(index, mask):
    bit = 1
    while bit <= mask:
        if mask & bit:
            index = index + bit * (1 - 2 * lax.rem(lax.div(index, bit), 2))
        bit *= 2
    return index


class Send(NamedTuple):
    src: Callable
    dst: Callable
    dz: int
    df: int
    after: int | None = None


def exchange(name, cid, arrays, out_shapes, sends):
    n_in, n_out = len(arrays), len(out_shapes)
    peers = sorted({(s.dz, s.df) for s in sends} - {(0, 0)})

    def kernel(*refs):
        ins, outs = refs[:n_in], refs[n_in : n_in + n_out]
        send_sems, recv_sems = refs[n_in + n_out :]
        z = lax.axis_index("sp")
        f = lax.axis_index("fsdp")
        barrier = pltpu.get_barrier_semaphore()
        for dz, df in peers:
            pl.semaphore_signal(
                barrier, inc=1, device_id=(flip(z, dz), flip(f, df)), device_id_type=MESH
            )
        pl.semaphore_wait(barrier, len(peers))
        copies = []
        for k, s in enumerate(sends):
            src = s.src(ins, outs, z, f)
            dst = s.dst(ins, outs, z, f)
            if (s.dz, s.df) == (0, 0):
                copies.append(pltpu.make_async_copy(src, dst, recv_sems.at[k]))
            else:
                copies.append(
                    pltpu.make_async_remote_copy(
                        src_ref=src,
                        dst_ref=dst,
                        send_sem=send_sems.at[k],
                        recv_sem=recv_sems.at[k],
                        device_id=(flip(z, s.dz), flip(f, s.df)),
                        device_id_type=MESH,
                    )
                )
        arrived = set()

        def arrive(k):
            if k not in arrived:
                arrived.add(k)
                s = sends[k]
                if (s.dz, s.df) == (0, 0):
                    copies[k].wait()
                else:
                    copies[k].wait_recv()

        for k, s in enumerate(sends):
            if s.after is None:
                copies[k].start()
        for k, s in enumerate(sends):
            if s.after is not None:
                arrive(s.after)
                copies[k].start()
        for k, s in enumerate(sends):
            if (s.dz, s.df) != (0, 0):
                copies[k].wait_send()
            arrive(k)

    result = pl.pallas_call(
        kernel,
        out_shape=[jax.ShapeDtypeStruct(shape, BF16) for shape in out_shapes],
        in_specs=[pl.BlockSpec(memory_space=pl.ANY)] * n_in,
        out_specs=[pl.BlockSpec(memory_space=pl.ANY)] * n_out,
        scratch_shapes=[
            pltpu.SemaphoreType.DMA((len(sends),)),
            pltpu.SemaphoreType.DMA((len(sends),)),
        ],
        compiler_params=pltpu.CompilerParams(collective_id=cid, has_side_effects=True),
        name=name,
    )(*arrays)
    return result


def body(
    tokens,
    expert_ids,
    attn_gain,
    query_weight,
    key_weight,
    value_weight,
    q_gain,
    k_gain,
    output_weight,
    ffn_gain,
    router_weight,
    w_gate,
    w_up,
    w_down,
    cotangent,
):
    nsp = lax.axis_size("sp")
    nf = lax.axis_size("fsdp")
    z = lax.axis_index("sp")
    f = lax.axis_index("fsdp")
    rows = tokens.shape[1]
    width = tokens.shape[2]
    shard = width // nf
    n_heads, kv_heads, head_dim = QUERY_HEADS, KEY_VALUE_HEADS, HEAD_SIZE
    my_heads = n_heads // nf
    rep = nf // kv_heads
    q_cols = my_heads * head_dim
    qkv_cols = q_cols + 2 * head_dim
    score_scale = 1.0 / math.sqrt(head_dim)
    n_experts = w_gate.shape[0]
    hidden_size = w_gate.shape[2]
    hid_shard = w_down.shape[1]
    plane_experts = n_experts // nsp
    parts = nf // plane_experts
    cap = CAP
    seqs = nf
    part = lax.rem(f, parts)
    place = lax.div(f, parts)
    expert = z * plane_experts + place

    small = jnp.concatenate(
        [
            attn_gain.astype(BF16),
            ffn_gain.astype(BF16),
            q_gain.astype(BF16),
            k_gain.astype(BF16),
            router_weight.astype(BF16).reshape(-1),
        ]
    )
    small_rows = 16
    small = jnp.pad(small, (0, small_rows * width - small.shape[0])).reshape(small_rows, width)
    x_pay = jnp.concatenate([tokens[0], small], axis=0)
    pay_rows = rows + small_rows
    by_head = query_weight.astype(BF16).reshape(shard, nf, q_cols)
    key_b = jnp.repeat(key_weight.astype(BF16).reshape(shard, kv_heads, head_dim), rep, axis=1)
    value_b = jnp.repeat(value_weight.astype(BF16).reshape(shard, kv_heads, head_dim), rep, axis=1)
    qkv_pay = jnp.concatenate([by_head, key_b, value_b], axis=2).transpose(1, 0, 2)
    routes = expert_ids[0]
    expert_iota = jnp.arange(n_experts, dtype=jnp.int32)
    routed = jnp.any(routes[:, :, None] == expert_iota[None, None, :], axis=1)
    dy_pay = jnp.concatenate(
        [
            cotangent[0],
            routed.astype(BF16),
            jnp.zeros((rows, LANES - n_experts), BF16),
        ],
        axis=1,
    )
    wide = width + LANES

    def plane_cast(weight):
        return lax.dynamic_slice_in_dim(weight, z * plane_experts, plane_experts, 0).astype(BF16)

    gate_pay, up_pay, down_pay = plane_cast(w_gate), plane_cast(w_up), plane_cast(w_down)

    sends = []
    for m in range(0, nf, 2):
        sends.append(
            Send(
                lambda i, o, z, f, m=m: i[0],
                lambda i, o, z, f: o[0].at[f],
                0,
                m,
            )
        )
    for m in range(nf):
        sends.append(
            Send(
                lambda i, o, z, f, m=m: i[1].at[flip(f, m)],
                lambda i, o, z, f, m=m: o[1].at[f],
                0,
                m,
            )
        )
    for m in range(nsp):
        sends.append(
            Send(lambda i, o, z, f: i[2], lambda i, o, z, f, m=m: o[2].at[m], m, 0)
        )
    for m in range(0, nf, 2):
        if m == 0:
            sends.append(
                Send(lambda i, o, z, f: i[0], lambda i, o, z, f: o[0].at[f], 0, 1)
            )
        else:
            sends.append(
                Send(
                    lambda i, o, z, f, m=m: o[0].at[flip(f, m)],
                    lambda i, o, z, f, m=m: o[0].at[flip(f, m)],
                    0,
                    1,
                    m // 2,
                )
            )
    x_all, w_qkv, dy_z = exchange(
        "gather_inputs",
        0,
        (x_pay, qkv_pay, dy_pay),
        ((nf, pay_rows, width), (nf, shard, qkv_cols), (nsp, rows, wide)),
        sends,
    )

    sends = []
    for which in range(3):
        for s in range(plane_experts):
            first = len(sends)
            sends.append(
                Send(
                    lambda i, o, z, f, s=s, w=which: i[w].at[flip(lax.div(f, parts), s)],
                    lambda i, o, z, f, w=which: o[w].at[f],
                    0,
                    s * parts,
                )
            )
    first_stage = len(sends)
    for which in range(3):
        for s in range(plane_experts):
            for p in range(1, parts):
                index = which * plane_experts + s
                if s == 0:
                    sends.append(
                        Send(
                            lambda i, o, z, f, w=which: i[w].at[lax.div(f, parts)],
                            lambda i, o, z, f, w=which: o[w].at[f],
                            0,
                            p,
                        )
                    )
                else:
                    sends.append(
                        Send(
                            lambda i, o, z, f, s=s, w=which: o[w].at[flip(f, s * parts)],
                            lambda i, o, z, f, s=s, w=which: o[w].at[flip(f, s * parts)],
                            0,
                            p,
                            index,
                        )
                    )
    gate_all, up_all, down_all = exchange(
        "gather_experts",
        1,
        (gate_pay, up_pay, down_pay),
        ((nf, shard, hidden_size), (nf, shard, hidden_size), (nf, hid_shard, width)),
        sends,
    )
    wg_b = gate_all.reshape(width, hidden_size)
    wu_b = up_all.reshape(width, hidden_size)
    wd_b = down_all.reshape(hidden_size, width)

    small_all = x_all[:, rows:, :].reshape(nf, small_rows * width)
    at = 0
    pieces = []
    for size in (shard, shard, head_dim // nf, head_dim // nf, shard * n_experts):
        pieces.append(small_all[:, at : at + size])
        at += size
    g_attn = pieces[0].reshape(width).astype(FLOAT)
    g_ffn = pieces[1].reshape(width).astype(FLOAT)
    g_query = pieces[2].reshape(head_dim).astype(FLOAT)
    g_key = pieces[3].reshape(head_dim).astype(FLOAT)
    wr_b = pieces[4].reshape(width, n_experts)

    xn_b = (
        rms_norm(x_all[:, :rows, :].astype(FLOAT), g_attn).astype(BF16).reshape(seqs * rows, width)
    )
    w_qkv = w_qkv.reshape(width, qkv_cols)
    qkv_lin = matmul(xn_b, w_qkv)
    q_lin = qkv_lin[:, :q_cols].reshape(seqs, rows, my_heads, head_dim)
    k_lin = qkv_lin[:, q_cols : q_cols + head_dim].reshape(seqs, rows, 1, head_dim)
    v_b = qkv_lin[:, q_cols + head_dim :].astype(BF16)
    half_dim = head_dim // 2
    inverse_freq = THETA ** (-(jnp.arange(half_dim, dtype=FLOAT) * 2.0 / head_dim))
    positions = (z * rows + jnp.arange(rows, dtype=jnp.int32)).astype(FLOAT)
    angles = positions[:, None] * inverse_freq[None, :]
    cosine = jnp.cos(angles)[None, :, None, :]
    sine_part = jnp.sin(angles)[None, :, None, :]

    def prep_heads(linear, gain_vec):
        return rotate(rms_norm(linear, gain_vec), cosine, sine_part)

    q_b = prep_heads(q_lin, g_query).astype(BF16)
    k_b = prep_heads(k_lin, g_key).astype(BF16).reshape(seqs * rows, head_dim)

    kv_pay = jnp.concatenate([k_b, v_b], axis=1)
    piece = seqs * rows // rep
    sends = []
    for d in range(nsp):
        sends.append(
            Send(
                lambda i, o, z, f: i[0].at[pl.ds(lax.rem(f, rep) * piece, piece)],
                lambda i, o, z, f, d=d: o[0].at[d, pl.ds(lax.rem(f, rep) * piece, piece)],
                d,
                0,
            )
        )
    for d in range(nsp):
        for p in range(1, rep):
            sends.append(
                Send(
                    lambda i, o, z, f, d=d: o[0].at[d, pl.ds(lax.rem(f, rep) * piece, piece)],
                    lambda i, o, z, f, d=d: o[0].at[d, pl.ds(lax.rem(f, rep) * piece, piece)],
                    0,
                    p,
                    d,
                )
            )
    (kv_z,) = exchange(
        "gather_keys", 2, (kv_pay,), ((nsp, seqs * rows, 2 * head_dim),), sends
    )
    kv_seq = kv_z.reshape(nsp, seqs, rows, 2 * head_dim).transpose(1, 0, 2, 3)
    kv_seq = kv_seq.reshape(seqs, nsp * rows, 2 * head_dim)
    keys = kv_seq[:, :, :head_dim]
    values = kv_seq[:, :, head_dim:]

    q_rows = q_b.transpose(0, 2, 1, 3)
    plane_of = jnp.bitwise_xor(jnp.arange(nsp, dtype=jnp.int32), z)
    key_pos = (plane_of[:, None] * rows + jnp.arange(rows, dtype=jnp.int32)[None, :]).reshape(-1)
    query_pos = z * rows + jnp.arange(rows, dtype=jnp.int32)
    causal = key_pos[None, :] <= query_pos[:, None]
    scores = (
        jnp.einsum("nhqd,nkd->nhqk", q_rows, keys, preferred_element_type=FLOAT) * score_scale
    )
    scores = jnp.where(causal[None, None], scores, -1e30)
    row_top = jnp.max(scores, axis=3, keepdims=True)
    expo = jnp.exp(scores - row_top)
    probs = (expo / jnp.sum(expo, axis=3, keepdims=True)).astype(BF16)
    o_rows = jnp.einsum("nhqk,nkd->nqhd", probs, values, preferred_element_type=FLOAT)
    o_mat = o_rows.astype(BF16).reshape(seqs * rows, q_cols)
    wo_b = output_weight.astype(BF16)

    def pair_then_plane(partial, name, cid):
        split = partial.astype(BF16).reshape(nf // 2, 2, rows, width)
        (other,) = exchange(
            name + "_pair",
            cid,
            (split,),
            ((nf // 2, rows, width),),
            [Send(lambda i, o, z, f: i[0].at[:, 1 - lax.rem(f, 2)], lambda i, o, z, f: o[0], 0, 1)],
        )
        own = lax.dynamic_index_in_dim(split, lax.rem(f, 2), 1, keepdims=False)
        summed = (own.astype(FLOAT) + other.astype(FLOAT)).astype(BF16)
        sends = [
            Send(
                lambda i, o, z, f, j=j: i[0].at[flip(lax.div(f, 2), j)],
                lambda i, o, z, f, j=j: o[0].at[j],
                0,
                2 * j,
            )
            for j in range(nf // 2)
        ]
        (blocks,) = exchange(
            name + "_plane", cid + 1, (summed,), ((nf // 2, rows, width),), sends
        )
        return jnp.sum(blocks.astype(FLOAT), axis=0)

    x_rows = tokens[0].astype(FLOAT)
    mid_rows = x_rows + pair_then_plane(matmul(o_mat, wo_b), "out_sum", 3)
    hn_b = rms_norm(mid_rows, g_ffn).astype(BF16)
    logits = matmul(hn_b, wr_b)
    logits = jnp.where(routed, logits, -1e30)
    expo = jnp.where(routed, jnp.exp(logits - jnp.max(logits, axis=1, keepdims=True)), 0.0)
    gates = expo / jnp.sum(expo, axis=1, keepdims=True)

    def two_parts(exact):
        high = exact.astype(BF16)
        return high, (exact - high.astype(FLOAT)).astype(BF16)

    gate_high, gate_low = two_parts(gates)
    hn_pay = jnp.concatenate(
        [hn_b, gate_high, gate_low, jnp.zeros((rows, LANES - 2 * n_experts), BF16)], axis=1
    )
    (hn_z,) = exchange(
        "hidden_planes",
        5,
        (hn_pay,),
        ((nsp, rows, wide),),
        [
            Send(lambda i, o, z, f: i[0], lambda i, o, z, f, d=d: o[0].at[d], d, 0)
            for d in range(nsp)
        ],
    )

    own_experts = z * plane_experts + jnp.bitwise_xor(
        place, jnp.arange(plane_experts, dtype=jnp.int32)
    )
    own_hot = (expert_iota[:, None] == own_experts[None, :]).astype(FLOAT)
    routed_z = lax.dot_general(
        own_hot,
        dy_z[:, :, width : width + n_experts].astype(FLOAT),
        (((0,), (2,)), ((), ())),
        preferred_element_type=FLOAT,
    ).transpose(1, 0, 2)
    earlier = jnp.triu(jnp.ones((rows, rows), FLOAT), 1)
    rank = jnp.dot(
        routed_z.reshape(nsp * plane_experts, rows), earlier, preferred_element_type=FLOAT
    ).reshape(nsp, plane_experts, rows)
    rank = rank * routed_z + (routed_z - 1.0)
    pick = (
        rank[:, :, None, :] == jnp.arange(cap, dtype=FLOAT)[None, None, :, None]
    ).astype(BF16)
    pick = pick.reshape(nsp, plane_experts * cap, rows)

    def select(source):
        picked = jnp.einsum("drt,dtc->drc", pick, source, preferred_element_type=FLOAT)
        return picked.astype(BF16).reshape(nsp, plane_experts, cap, source.shape[2])

    hn_pick = select(hn_z)
    dy_pick = select(dy_z[:, :, :width])
    sends = []
    for which in range(2):
        for s in range(plane_experts):
            sends.append(
                Send(
                    lambda i, o, z, f, s=s, w=which: i[w].at[:, s],
                    lambda i, o, z, f, s=s, w=which: o[w].at[s],
                    0,
                    s * parts,
                )
            )
    hn_rows, dy_rows = exchange(
        "rows_to_experts",
        6,
        (hn_pick, dy_pick),
        ((plane_experts, nsp, cap, wide), (plane_experts, nsp, cap, width)),
        sends,
    )

    n_rows = plane_experts * nsp * cap
    hn_wide = hn_rows.reshape(n_rows, wide)
    hn_in = hn_wide[:, :width]
    dy_in = dy_rows.reshape(n_rows, width)
    hot = (jnp.arange(n_experts, dtype=jnp.int32) == expert).astype(FLOAT)
    tail = hn_wide[:, width : width + 2 * n_experts].astype(FLOAT)
    row_gate = jnp.sum(
        (tail[:, :n_experts] + tail[:, n_experts:]) * hot[None, :], axis=1, keepdims=True
    )
    gate_pre = matmul(hn_in, wg_b)
    up_pre = matmul(hn_in, wu_b)
    sigma = jax.nn.sigmoid(gate_pre)
    act_f = gate_pre * sigma
    hidden = (act_f * up_pre).astype(BF16)
    result = matmul(hidden, wd_b)
    dy_f = dy_in.astype(FLOAT)
    row_dgate = jnp.sum(result * dy_f, axis=1, keepdims=True)
    weighted = (row_gate * result).astype(BF16)
    d_result = (row_gate * dy_f).astype(BF16)
    d_hidden = contract_cols(d_result, wd_b)
    d_gate_pre = (d_hidden * up_pre * sigma * (1.0 + gate_pre * (1.0 - sigma))).astype(BF16)
    d_up_pre = (d_hidden * act_f).astype(BF16)
    d_in = (contract_cols(d_gate_pre, wg_b) + contract_cols(d_up_pre, wu_b)).astype(BF16)
    dgate_high, dgate_low = two_parts(row_dgate * hot[None, :])
    d_in_wide = jnp.concatenate(
        [d_in, dgate_high, dgate_low, jnp.zeros((n_rows, LANES - 2 * n_experts), BF16)], axis=1
    )

    (d_back,) = exchange(
        "rows_from_experts",
        7,
        (d_in_wide.reshape(plane_experts, nsp, cap, wide),),
        ((nsp, plane_experts, cap, wide),),
        [
            Send(
                lambda i, o, z, f, s=s: i[0].at[s],
                lambda i, o, z, f, s=s: o[0].at[:, s],
                0,
                s * parts,
            )
            for s in range(plane_experts)
        ],
    )

    def combine(returned):
        flat = returned.reshape(nsp, plane_experts * cap, returned.shape[3])
        return jnp.einsum("drt,drc->dtc", pick, flat, preferred_element_type=FLOAT).astype(BF16)

    (d_home,) = exchange(
        "hidden_grads_home",
        8,
        (combine(d_back),),
        ((nsp, rows, wide),),
        [
            Send(lambda i, o, z, f, d=d: i[0].at[d], lambda i, o, z, f, d=d: o[0].at[d], d, 0)
            for d in range(nsp)
        ],
    )
    d_home = jnp.sum(d_home.astype(FLOAT), axis=0)
    tail = d_home[:, width:]
    d_gates = tail[:, :n_experts] + tail[:, n_experts : 2 * n_experts]
    d_logits = gates * (d_gates - jnp.sum(gates * d_gates, axis=1, keepdims=True))
    d_router = jnp.dot(hn_b.astype(FLOAT).T, d_logits, precision=HIGH_PRECISION)
    d_hn = d_home[:, :width] + jnp.dot(d_logits, wr_b.astype(FLOAT).T, precision=HIGH_PRECISION)
    grad_out = cotangent[0].astype(FLOAT)
    unused, ffn_pull = jax.vjp(rms_norm, mid_rows, g_ffn)
    d_mid_norm, d_ffn_gain = ffn_pull(d_hn)
    d_mid = grad_out + d_mid_norm

    back = weighted.reshape(plane_experts, nsp, cap, width)
    back = [
        lax.ppermute(back[s], "fsdp", [(i, i ^ (s * parts)) for i in range(nf)])
        if s
        else back[0]
        for s in range(plane_experts)
    ]
    out_blocks = combine(jnp.stack(back, axis=1))
    moe_sum = out_blocks[0].astype(FLOAT)
    for d in range(1, nsp):
        moe_sum = moe_sum + lax.ppermute(
            out_blocks[d], "sp", [(i, i ^ d) for i in range(nsp)]
        ).astype(FLOAT)
    mixed = (mid_rows + moe_sum).astype(BF16)[None]

    def to_shards(full):
        tail_shape = full.shape[1:]
        full = full.astype(BF16).reshape((plane_experts, parts) + tail_shape)

        def of_part(p):
            return lax.dynamic_index_in_dim(full, flip(part, p), 1, keepdims=False)

        total = of_part(0).astype(FLOAT)
        for p in range(1, parts):
            total = total + lax.ppermute(
                of_part(p), "fsdp", [(i, i ^ p) for i in range(nf)]
            ).astype(FLOAT)
        total = total.astype(BF16)
        got = []
        for s in range(plane_experts):
            block = lax.dynamic_index_in_dim(total, flip(place, s), 0, keepdims=False)
            if s:
                block = lax.ppermute(
                    block, "fsdp", [(i, i ^ (s * parts)) for i in range(nf)]
                )
            got.append(block)
        return jnp.stack(got)

    def all_planes(block):
        block = jnp.take(
            block, jnp.bitwise_xor(jnp.arange(plane_experts, dtype=jnp.int32), place), axis=0
        )
        right, left = [block], [block]
        for step in range(1, nsp):
            right.append(
                lax.ppermute(right[-1], "sp", [(i, i + 1) for i in range(step - 1, nsp - 1)])
            )
            left.append(
                lax.ppermute(left[-1], "sp", [(i + 1, i) for i in range(0, nsp - step)])
            )
        full = jnp.zeros((n_experts,) + block.shape[1:], FLOAT)
        for d in range(nsp):
            value = block.astype(FLOAT)
            if d:
                value = right[d].astype(FLOAT) + left[nsp - d].astype(FLOAT)
            full = lax.dynamic_update_slice_in_dim(
                full, value, lax.rem(z - d + nsp, nsp) * plane_experts, 0
            )
        return full

    d_down = contract_rows(hidden, d_result).reshape(nf, hid_shard, width)
    d_gate_w = contract_rows(hn_in, d_gate_pre).reshape(nf, shard, hidden_size)
    d_up_w = contract_rows(hn_in, d_up_pre).reshape(nf, shard, hidden_size)
    grad_down = all_planes(to_shards(d_down))
    grad_gate = all_planes(to_shards(d_gate_w))
    grad_up = all_planes(to_shards(d_up_w))

    d_attn_b = d_mid.astype(BF16)
    sends = [
        Send(lambda i, o, z, f: i[0], lambda i, o, z, f: o[0].at[f], 0, m)
        for m in range(0, nf, 2)
    ]
    for m in range(0, nf, 2):
        if m == 0:
            sends.append(Send(lambda i, o, z, f: i[0], lambda i, o, z, f: o[0].at[f], 0, 1))
        else:
            sends.append(
                Send(
                    lambda i, o, z, f, m=m: o[0].at[flip(f, m)],
                    lambda i, o, z, f, m=m: o[0].at[flip(f, m)],
                    0,
                    1,
                    m // 2,
                )
            )
    (da_all,) = exchange("gather_grads", 9, (d_attn_b,), ((nf, rows, width),), sends)
    da_all = da_all.reshape(seqs * rows, width)
    d_wo = contract_rows(o_mat, da_all)
    d_o = contract_cols(da_all, wo_b).astype(BF16).reshape(seqs, rows, my_heads, head_dim)
    d_o = d_o.transpose(0, 2, 1, 3)
    d_val = jnp.einsum("nhqk,nhqd->nkd", probs, d_o, preferred_element_type=FLOAT)
    d_probs = jnp.einsum("nhqd,nkd->nhqk", d_o, values, preferred_element_type=FLOAT)
    probs_f = probs.astype(FLOAT)
    d_scores = (
        probs_f * (d_probs - jnp.sum(probs_f * d_probs, axis=3, keepdims=True))
    ).astype(BF16)
    dq = (
        jnp.einsum("nhqk,nkd->nqhd", d_scores, keys, preferred_element_type=FLOAT) * score_scale
    ).astype(BF16)
    d_key = (
        jnp.einsum("nhqk,nhqd->nkd", d_scores, q_rows, preferred_element_type=FLOAT) * score_scale
    )
    d_kv = jnp.concatenate([d_key, d_val], axis=2).astype(BF16)
    d_kv = d_kv.reshape(seqs, nsp, rows, 2 * head_dim).transpose(1, 0, 2, 3)
    d_kv = d_kv.reshape(nsp, seqs * rows, 2 * head_dim)
    (d_kv,) = exchange(
        "key_grads_planes",
        10,
        (d_kv,),
        ((nsp, seqs * rows, 2 * head_dim),),
        [
            Send(lambda i, o, z, f, d=d: i[0].at[d], lambda i, o, z, f, d=d: o[0].at[d], d, 0)
            for d in range(nsp)
        ],
    )
    d_kv = jnp.sum(d_kv.astype(FLOAT), axis=0).astype(BF16)
    (d_kv,) = exchange(
        "key_grads_group",
        11,
        (d_kv,),
        ((rep, seqs * rows, 2 * head_dim),),
        [
            Send(lambda i, o, z, f: i[0], lambda i, o, z, f, p=p: o[0].at[p], 0, p)
            for p in range(rep)
        ],
    )
    d_kv = jnp.sum(d_kv.astype(FLOAT), axis=0)
    unused, q_pull = jax.vjp(prep_heads, q_lin, g_query)
    d_q_lin, d_q_gain = q_pull(dq.astype(FLOAT))
    unused, k_pull = jax.vjp(prep_heads, k_lin, g_key)
    d_k_lin, d_k_gain = k_pull(d_kv[:, :head_dim].reshape(seqs, rows, 1, head_dim))
    dq_b = d_q_lin.astype(BF16).reshape(seqs * rows, q_cols)
    dk_b = d_k_lin.astype(BF16).reshape(seqs * rows, head_dim)
    dv_b = d_kv[:, head_dim:].astype(BF16)
    d_qkv = jnp.concatenate([dq_b, dk_b, dv_b], axis=1)
    share = 1.0 / rep
    d_qkv_shared = jnp.concatenate([dq_b, dk_b * BF16(share), dv_b * BF16(share)], axis=1)
    d_w_qkv = contract_rows(xn_b, d_qkv).astype(BF16).reshape(nf, shard, qkv_cols)
    (d_w_shard,) = exchange(
        "head_grads_to_shards",
        12,
        (d_w_qkv,),
        ((nf, shard, qkv_cols),),
        [
            Send(
                lambda i, o, z, f, m=m: i[0].at[flip(f, m)],
                lambda i, o, z, f, m=m: o[0].at[f],
                0,
                m,
            )
            for m in range(nf)
        ],
    )
    d_wq = d_w_shard[:, :, :q_cols].transpose(1, 0, 2).reshape(shard, n_heads * head_dim)
    d_wkv = d_w_shard[::rep, :, q_cols:].reshape(kv_heads, shard, 2, head_dim)
    d_wkv = d_wkv.transpose(2, 1, 0, 3).reshape(2 * shard, kv_heads * head_dim)
    d_xn = pair_then_plane(contract_cols(d_qkv_shared, w_qkv), "input_sum", 13)
    unused, attn_pull = jax.vjp(rms_norm, x_rows, g_attn)
    d_x_norm, d_attn_gain = attn_pull(d_xn)
    grad_tokens = (d_mid + d_x_norm)[None]

    sum_out = lax.psum(d_wo.astype(BF16), "sp").astype(FLOAT)
    sum_q, sum_kv = lax.psum((d_wq, d_wkv), "sp")
    sum_q = sum_q.astype(FLOAT)
    sum_kv = sum_kv.astype(FLOAT)
    gain_sums = lax.psum(
        jnp.concatenate(
            [
                d_attn_gain,
                d_ffn_gain,
                d_q_gain,
                d_k_gain * share,
                d_router.reshape(-1),
            ]
        ),
        ("sp", "fsdp"),
    )
    at = 0
    pieces = []
    for size in (width, width, head_dim, head_dim, width * n_experts):
        whole = gain_sums[at : at + size]
        pieces.append(lax.dynamic_slice_in_dim(whole, f * (size // nf), size // nf, 0))
        at += size
    return (
        mixed,
        grad_tokens,
        pieces[0],
        sum_q,
        sum_kv[:shard],
        sum_kv[shard:],
        pieces[2],
        pieces[3],
        sum_out,
        pieces[1],
        pieces[4].reshape(shard, n_experts),
        grad_gate,
        grad_up,
        grad_down,
    )


def solution(mesh):
    by_token = P("fsdp", "sp", None)
    by_row = P("fsdp", None)
    by_inner = P(None, "fsdp", None)
    in_specs = (
        by_token,
        by_token,
        P("fsdp"),
        by_row,
        by_row,
        by_row,
        P("fsdp"),
        P("fsdp"),
        by_row,
        P("fsdp"),
        by_row,
        by_inner,
        by_inner,
        by_inner,
        by_token,
    )
    out_specs = (
        by_token,
        by_token,
        P("fsdp"),
        by_row,
        by_row,
        by_row,
        P("fsdp"),
        P("fsdp"),
        by_row,
        P("fsdp"),
        by_row,
        by_inner,
        by_inner,
        by_inner,
    )
    return jax.shard_map(body, mesh=mesh, in_specs=in_specs, out_specs=out_specs, check_vma=False)
```

```python
import math
from typing import Callable, NamedTuple

import jax
import jax.numpy as jnp
from jax import lax
from jax.experimental import pallas as pl
from jax.experimental.pallas import tpu as pltpu
from jax.sharding import PartitionSpec as P

QUERY_HEADS = 32
KEY_VALUE_HEADS = 4
HEAD_SIZE = 128
CAP = 80
LANES = 128

EPS = 1e-06
THETA = 1000000.0
HIGH_PRECISION = lax.Precision.HIGHEST
BF16 = jnp.bfloat16
FLOAT = jnp.float32
MESH = pl.DeviceIdType.MESH


def rms_norm(values_in, gain_vec):
    return (
        values_in
        * lax.rsqrt(jnp.mean(values_in * values_in, axis=-1, keepdims=True) + EPS)
        * gain_vec
    )


def rotate(values_in, cosine, sine_part):
    half_dim = values_in.shape[-1] // 2
    first_half = values_in[..., :half_dim]
    second = values_in[..., half_dim:]
    return jnp.concatenate(
        [first_half * cosine - second * sine_part, second * cosine + first_half * sine_part],
        axis=-1,
    )


def contract_rows(left_mat, right_mat):
    return lax.dot_general(
        left_mat, right_mat, (((0,), (0,)), ((), ())), preferred_element_type=FLOAT
    )


def contract_cols(left_mat, right_mat):
    return lax.dot_general(
        left_mat, right_mat, (((1,), (1,)), ((), ())), preferred_element_type=FLOAT
    )


def matmul(left_mat, right_mat):
    return jnp.dot(left_mat, right_mat, preferred_element_type=FLOAT)


def flip(index, mask):
    bit = 1
    while bit <= mask:
        if mask & bit:
            index = index + bit * (1 - 2 * lax.rem(lax.div(index, bit), 2))
        bit *= 2
    return index


class Send(NamedTuple):
    src: Callable
    dst: Callable
    dz: int
    df: int
    after: int | None = None


def exchange(name, cid, arrays, out_shapes, sends, micros):
    n_in, n_out = len(arrays), len(out_shapes)
    peers = sorted({(s.dz, s.df) for s in sends} - {(0, 0)})

    def kernel(*refs):
        ins, outs = refs[:n_in], refs[n_in : n_in + n_out]
        send_sems, recv_sems = refs[n_in + n_out :]
        z = lax.axis_index("sp")
        f = lax.axis_index("fsdp")
        barrier = pltpu.get_barrier_semaphore()
        for dz, df in peers:
            pl.semaphore_signal(
                barrier, inc=1, device_id=(flip(z, dz), flip(f, df)), device_id_type=MESH
            )
        pl.semaphore_wait(barrier, len(peers))
        copies = []
        for k, s in enumerate(sends):
            src = s.src(ins, outs, z, f)
            dst = s.dst(ins, outs, z, f)
            if (s.dz, s.df) == (0, 0):
                copies.append(pltpu.make_async_copy(src, dst, recv_sems.at[k]))
            else:
                copies.append(
                    pltpu.make_async_remote_copy(
                        src_ref=src,
                        dst_ref=dst,
                        send_sem=send_sems.at[k],
                        recv_sem=recv_sems.at[k],
                        device_id=(flip(z, s.dz), flip(f, s.df)),
                        device_id_type=MESH,
                    )
                )
        arrived = set()

        def arrive(k):
            if k not in arrived:
                arrived.add(k)
                s = sends[k]
                if (s.dz, s.df) == (0, 0):
                    copies[k].wait()
                else:
                    copies[k].wait_recv()

        for k, s in enumerate(sends):
            if s.after is None:
                copies[k].start()
        for k, s in enumerate(sends):
            if s.after is not None:
                arrive(s.after)
                copies[k].start()
        for k, s in enumerate(sends):
            if (s.dz, s.df) != (0, 0):
                copies[k].wait_send()
            arrive(k)

    result = pl.pallas_call(
        kernel,
        out_shape=[jax.ShapeDtypeStruct(shape, BF16) for shape in out_shapes],
        in_specs=[pl.BlockSpec(memory_space=pl.ANY)] * n_in,
        out_specs=[pl.BlockSpec(memory_space=pl.ANY)] * n_out,
        scratch_shapes=[
            pltpu.SemaphoreType.DMA((len(sends),)),
            pltpu.SemaphoreType.DMA((len(sends),)),
        ],
        compiler_params=pltpu.CompilerParams(collective_id=cid, has_side_effects=True),
        cost_estimate=pl.CostEstimate(
            flops=0, bytes_accessed=int(micros * 3.0e6), transcendentals=0
        ),
        name=name,
    )(*arrays)
    return result


def body(
    tokens,
    expert_ids,
    attn_gain,
    query_weight,
    key_weight,
    value_weight,
    q_gain,
    k_gain,
    output_weight,
    ffn_gain,
    router_weight,
    w_gate,
    w_up,
    w_down,
    cotangent,
):
    nsp = lax.axis_size("sp")
    nf = lax.axis_size("fsdp")
    z = lax.axis_index("sp")
    f = lax.axis_index("fsdp")
    rows = tokens.shape[1]
    width = tokens.shape[2]
    shard = width // nf
    n_heads, kv_heads, head_dim = QUERY_HEADS, KEY_VALUE_HEADS, HEAD_SIZE
    my_heads = n_heads // nf
    rep = nf // kv_heads
    q_cols = my_heads * head_dim
    qkv_cols = q_cols + 2 * head_dim
    score_scale = 1.0 / math.sqrt(head_dim)
    n_experts = w_gate.shape[0]
    hidden_size = w_gate.shape[2]
    hid_shard = w_down.shape[1]
    plane_experts = n_experts // nsp
    parts = nf // plane_experts
    cap = CAP
    seqs = nf
    part = lax.rem(f, parts)
    place = lax.div(f, parts)
    expert = z * plane_experts + place

    small = jnp.concatenate(
        [
            attn_gain.astype(BF16),
            ffn_gain.astype(BF16),
            q_gain.astype(BF16),
            k_gain.astype(BF16),
            router_weight.astype(BF16).reshape(-1),
        ]
    )
    small_rows = 16
    small = jnp.pad(small, (0, small_rows * width - small.shape[0])).reshape(small_rows, width)
    x_pay = jnp.concatenate([tokens[0], small], axis=0)
    pay_rows = rows + small_rows
    by_head = query_weight.astype(BF16).reshape(shard, nf, q_cols)
    key_b = jnp.repeat(key_weight.astype(BF16).reshape(shard, kv_heads, head_dim), rep, axis=1)
    value_b = jnp.repeat(value_weight.astype(BF16).reshape(shard, kv_heads, head_dim), rep, axis=1)
    qkv_pay = jnp.concatenate([by_head, key_b, value_b], axis=2).transpose(1, 0, 2)
    routes = expert_ids[0]
    expert_iota = jnp.arange(n_experts, dtype=jnp.int32)
    routed = jnp.any(routes[:, :, None] == expert_iota[None, None, :], axis=1)
    dy_pay = jnp.concatenate(
        [
            cotangent[0],
            routed.astype(BF16),
            jnp.zeros((rows, LANES - n_experts), BF16),
        ],
        axis=1,
    )
    wide = width + LANES

    def plane_cast(weight):
        return lax.dynamic_slice_in_dim(weight, z * plane_experts, plane_experts, 0).astype(BF16)

    gate_pay, up_pay, down_pay = plane_cast(w_gate), plane_cast(w_up), plane_cast(w_down)

    sends = []
    for m in range(0, nf, 2):
        sends.append(
            Send(
                lambda i, o, z, f, m=m: i[0],
                lambda i, o, z, f: o[0].at[f],
                0,
                m,
            )
        )
    for m in range(nf):
        sends.append(
            Send(
                lambda i, o, z, f, m=m: i[1].at[flip(f, m)],
                lambda i, o, z, f, m=m: o[1].at[f],
                0,
                m,
            )
        )
    for m in range(nsp):
        sends.append(
            Send(lambda i, o, z, f: i[2], lambda i, o, z, f, m=m: o[2].at[m], m, 0)
        )
    for m in range(0, nf, 2):
        if m == 0:
            sends.append(
                Send(lambda i, o, z, f: i[0], lambda i, o, z, f: o[0].at[f], 0, 1)
            )
        else:
            sends.append(
                Send(
                    lambda i, o, z, f, m=m: o[0].at[flip(f, m)],
                    lambda i, o, z, f, m=m: o[0].at[flip(f, m)],
                    0,
                    1,
                    m // 2,
                )
            )
    x_all, w_qkv, dy_z = exchange(
        "gather_inputs",
        0,
        (x_pay, qkv_pay, dy_pay),
        ((nf, pay_rows, width), (nf, shard, qkv_cols), (nsp, rows, wide)),
        sends,
        65,
    )

    small_all = x_all[:, rows:, :].reshape(nf, small_rows * width)
    at = 0
    pieces = []
    for size in (shard, shard, head_dim // nf, head_dim // nf, shard * n_experts):
        pieces.append(small_all[:, at : at + size])
        at += size
    g_attn = pieces[0].reshape(width).astype(FLOAT)
    g_ffn = pieces[1].reshape(width).astype(FLOAT)
    g_query = pieces[2].reshape(head_dim).astype(FLOAT)
    g_key = pieces[3].reshape(head_dim).astype(FLOAT)
    wr_b = pieces[4].reshape(width, n_experts)

    xn_b = (
        rms_norm(x_all[:, :rows, :].astype(FLOAT), g_attn).astype(BF16).reshape(seqs * rows, width)
    )
    w_qkv = w_qkv.reshape(width, qkv_cols)
    qkv_lin = matmul(xn_b, w_qkv)
    q_lin = qkv_lin[:, :q_cols].reshape(seqs, rows, my_heads, head_dim)
    k_lin = qkv_lin[:, q_cols : q_cols + head_dim].reshape(seqs, rows, 1, head_dim)
    v_b = qkv_lin[:, q_cols + head_dim :].astype(BF16)
    half_dim = head_dim // 2
    inverse_freq = THETA ** (-(jnp.arange(half_dim, dtype=FLOAT) * 2.0 / head_dim))
    positions = (z * rows + jnp.arange(rows, dtype=jnp.int32)).astype(FLOAT)
    angles = positions[:, None] * inverse_freq[None, :]
    cosine = jnp.cos(angles)[None, :, None, :]
    sine_part = jnp.sin(angles)[None, :, None, :]

    def prep_heads(linear, gain_vec):
        return rotate(rms_norm(linear, gain_vec), cosine, sine_part)

    q_b = prep_heads(q_lin, g_query).astype(BF16)
    k_b = prep_heads(k_lin, g_key).astype(BF16).reshape(seqs * rows, head_dim)

    kv_pay = jnp.concatenate([k_b, v_b], axis=1)
    piece = seqs * rows // rep
    sends = []
    for d in range(nsp):
        sends.append(
            Send(
                lambda i, o, z, f: i[0].at[pl.ds(lax.rem(f, rep) * piece, piece)],
                lambda i, o, z, f, d=d: o[0].at[d, pl.ds(lax.rem(f, rep) * piece, piece)],
                d,
                0,
            )
        )
    for d in range(nsp):
        for p in range(1, rep):
            sends.append(
                Send(
                    lambda i, o, z, f, d=d: o[0].at[d, pl.ds(lax.rem(f, rep) * piece, piece)],
                    lambda i, o, z, f, d=d: o[0].at[d, pl.ds(lax.rem(f, rep) * piece, piece)],
                    0,
                    p,
                    d,
                )
            )
    for which in range(3):
        for s in range(plane_experts):
            stage = len(sends)
            sends.append(
                Send(
                    lambda i, o, z, f, s=s, w=which: i[1 + w].at[flip(lax.div(f, parts), s)],
                    lambda i, o, z, f, w=which: o[1 + w].at[f],
                    0,
                    s * parts,
                )
            )
            for p in range(1, parts):
                if s == 0:
                    forward = Send(
                        lambda i, o, z, f, w=which: i[1 + w].at[lax.div(f, parts)],
                        lambda i, o, z, f, w=which: o[1 + w].at[f],
                        0,
                        p,
                    )
                else:
                    forward = Send(
                        lambda i, o, z, f, s=s, w=which: o[1 + w].at[flip(f, s * parts)],
                        lambda i, o, z, f, s=s, w=which: o[1 + w].at[flip(f, s * parts)],
                        0,
                        p,
                        stage,
                    )
                sends.append(forward)
    kv_z, gate_all, up_all, down_all = exchange(
        "keys_and_experts",
        1,
        (kv_pay, gate_pay, up_pay, down_pay),
        (
            (nsp, seqs * rows, 2 * head_dim),
            (nf, shard, hidden_size),
            (nf, shard, hidden_size),
            (nf, hid_shard, width),
        ),
        sends,
        55,
    )
    wg_b = gate_all.reshape(width, hidden_size)
    wu_b = up_all.reshape(width, hidden_size)
    wd_b = down_all.reshape(hidden_size, width)
    kv_seq = kv_z.reshape(nsp, seqs, rows, 2 * head_dim).transpose(1, 0, 2, 3)
    kv_seq = kv_seq.reshape(seqs, nsp * rows, 2 * head_dim)
    keys = kv_seq[:, :, :head_dim]
    values = kv_seq[:, :, head_dim:]

    q_rows = q_b.transpose(0, 2, 1, 3)
    plane_of = jnp.bitwise_xor(jnp.arange(nsp, dtype=jnp.int32), z)
    key_pos = (plane_of[:, None] * rows + jnp.arange(rows, dtype=jnp.int32)[None, :]).reshape(-1)
    query_pos = z * rows + jnp.arange(rows, dtype=jnp.int32)
    causal = key_pos[None, :] <= query_pos[:, None]
    scores = (
        jnp.einsum("nhqd,nkd->nhqk", q_rows, keys, preferred_element_type=FLOAT) * score_scale
    )
    scores = jnp.where(causal[None, None], scores, -1e30)
    row_top = jnp.max(scores, axis=3, keepdims=True)
    expo = jnp.exp(scores - row_top)
    probs = (expo / jnp.sum(expo, axis=3, keepdims=True)).astype(BF16)
    o_rows = jnp.einsum("nhqk,nkd->nqhd", probs, values, preferred_element_type=FLOAT)
    o_mat = o_rows.astype(BF16).reshape(seqs * rows, q_cols)
    wo_b = output_weight.astype(BF16)

    def pair_then_plane(partial, name, cid):
        split = partial.astype(BF16).reshape(nf // 2, 2, rows, width)
        (other,) = exchange(
            name + "_pair",
            cid,
            (split,),
            ((nf // 2, rows, width),),
            [Send(lambda i, o, z, f: i[0].at[:, 1 - lax.rem(f, 2)], lambda i, o, z, f: o[0], 0, 1)],
            8,
        )
        own = lax.dynamic_index_in_dim(split, lax.rem(f, 2), 1, keepdims=False)
        summed = (own.astype(FLOAT) + other.astype(FLOAT)).astype(BF16)
        sends = [
            Send(
                lambda i, o, z, f, j=j: i[0].at[flip(lax.div(f, 2), j)],
                lambda i, o, z, f, j=j: o[0].at[j],
                0,
                2 * j,
            )
            for j in range(nf // 2)
        ]
        (blocks,) = exchange(
            name + "_plane", cid + 1, (summed,), ((nf // 2, rows, width),), sends, 27
        )
        return jnp.sum(blocks.astype(FLOAT), axis=0)

    x_rows = tokens[0].astype(FLOAT)
    mid_rows = x_rows + pair_then_plane(matmul(o_mat, wo_b), "out_sum", 3)
    hn_b = rms_norm(mid_rows, g_ffn).astype(BF16)
    logits = matmul(hn_b, wr_b)
    logits = jnp.where(routed, logits, -1e30)
    expo = jnp.where(routed, jnp.exp(logits - jnp.max(logits, axis=1, keepdims=True)), 0.0)
    gates = expo / jnp.sum(expo, axis=1, keepdims=True)

    def two_parts(exact):
        high = exact.astype(BF16)
        return high, (exact - high.astype(FLOAT)).astype(BF16)

    own_experts = z * plane_experts + jnp.bitwise_xor(
        place, jnp.arange(plane_experts, dtype=jnp.int32)
    )
    own_hot = (expert_iota[:, None] == own_experts[None, :]).astype(FLOAT)
    routed_z = lax.dot_general(
        own_hot,
        dy_z[:, :, width : width + n_experts].astype(FLOAT),
        (((0,), (2,)), ((), ())),
        preferred_element_type=FLOAT,
    ).transpose(1, 0, 2)
    earlier = jnp.triu(jnp.ones((rows, rows), FLOAT), 1)
    rank = jnp.dot(
        routed_z.reshape(nsp * plane_experts, rows), earlier, preferred_element_type=FLOAT
    ).reshape(nsp, plane_experts, rows)
    rank = rank * routed_z + (routed_z - 1.0)
    pick = (
        rank[:, :, None, :] == jnp.arange(cap, dtype=FLOAT)[None, None, :, None]
    ).astype(BF16)
    pick = pick.reshape(nsp, plane_experts * cap, rows)

    def select(source):
        picked = jnp.einsum("drt,dtc->drc", pick, source, preferred_element_type=FLOAT)
        return picked.astype(BF16).reshape(nsp, plane_experts, cap, source.shape[2])

    def to_experts(which):
        return [
            Send(
                lambda i, o, z, f, s=s: i[which].at[:, s],
                lambda i, o, z, f, s=s: o[which].at[s],
                0,
                s * parts,
            )
            for s in range(plane_experts)
        ]

    gate_high, gate_low = two_parts(gates)
    gate_lanes = jnp.concatenate(
        [gate_high, gate_low, jnp.zeros((rows, LANES - 2 * n_experts), BF16)], axis=1
    )
    hn_z, gate_z, dy_rows = exchange(
        "hidden_planes",
        5,
        (hn_b, gate_lanes, select(dy_z[:, :, :width])),
        ((nsp, rows, width), (nsp, rows, LANES), (plane_experts, nsp, cap, width)),
        [
            Send(lambda i, o, z, f, w=w: i[w], lambda i, o, z, f, d=d, w=w: o[w].at[d], d, 0)
            for w in range(2)
            for d in range(nsp)
        ]
        + to_experts(2),
        58,
    )
    hn_rows, gate_rows = exchange(
        "rows_to_experts",
        6,
        (select(hn_z), select(gate_z)),
        ((plane_experts, nsp, cap, width), (plane_experts, nsp, cap, LANES)),
        to_experts(0) + to_experts(1),
        60,
    )

    n_rows = plane_experts * nsp * cap
    hn_in = hn_rows.reshape(n_rows, width)
    dy_in = dy_rows.reshape(n_rows, width)
    hot = (jnp.arange(n_experts, dtype=jnp.int32) == expert).astype(FLOAT)
    tail = gate_rows.reshape(n_rows, LANES)[:, : 2 * n_experts].astype(FLOAT)
    row_gate = jnp.sum(
        (tail[:, :n_experts] + tail[:, n_experts:]) * hot[None, :], axis=1, keepdims=True
    )
    gate_pre = matmul(hn_in, wg_b)
    up_pre = matmul(hn_in, wu_b)
    sigma = jax.nn.sigmoid(gate_pre)
    act_f = gate_pre * sigma
    hidden = (act_f * up_pre).astype(BF16)
    result = matmul(hidden, wd_b)
    dy_f = dy_in.astype(FLOAT)
    row_dgate = jnp.sum(result * dy_f, axis=1, keepdims=True)
    weighted = (row_gate * result).astype(BF16)
    d_result = (row_gate * dy_f).astype(BF16)
    d_hidden = contract_cols(d_result, wd_b)
    d_gate_pre = (d_hidden * up_pre * sigma * (1.0 + gate_pre * (1.0 - sigma))).astype(BF16)
    d_up_pre = (d_hidden * act_f).astype(BF16)
    d_in = (contract_cols(d_gate_pre, wg_b) + contract_cols(d_up_pre, wu_b)).astype(BF16)
    dgate_high, dgate_low = two_parts(row_dgate * hot[None, :])
    dgate_lanes = jnp.concatenate(
        [dgate_high, dgate_low, jnp.zeros((n_rows, LANES - 2 * n_experts), BF16)], axis=1
    )

    def by_shard(full, inner):
        return full.astype(BF16).reshape((plane_experts, parts) + inner)

    d_weights = (
        by_shard(contract_rows(hidden, d_result), (hid_shard, width)),
        by_shard(contract_rows(hn_in, d_gate_pre), (shard, hidden_size)),
        by_shard(contract_rows(hn_in, d_up_pre), (shard, hidden_size)),
    )
    shard_shapes = [w.shape[2:] for w in d_weights]

    sends = []
    for w in range(2):
        for s in range(plane_experts):
            sends.append(
                Send(
                    lambda i, o, z, f, s=s, w=w: i[w].at[s],
                    lambda i, o, z, f, s=s, w=w: o[w].at[:, s],
                    0,
                    s * parts,
                )
            )
    for w in range(3):
        for p in range(1, parts):
            sends.append(
                Send(
                    lambda i, o, z, f, p=p, w=w: i[2 + w].at[:, flip(lax.rem(f, parts), p)],
                    lambda i, o, z, f, p=p, w=w: o[2 + w].at[p - 1],
                    0,
                    p,
                )
            )
    d_back, dgate_back, *d_others = exchange(
        "rows_from_experts",
        7,
        (
            d_in.reshape(plane_experts, nsp, cap, width),
            dgate_lanes.reshape(plane_experts, nsp, cap, LANES),
        )
        + d_weights,
        [(nsp, plane_experts, cap, width), (nsp, plane_experts, cap, LANES)]
        + [(parts - 1, plane_experts) + tuple(shape) for shape in shard_shapes],
        sends,
        70,
    )

    def combine(returned):
        flat = returned.reshape(nsp, plane_experts * cap, returned.shape[3])
        return jnp.einsum("drt,drc->dtc", pick, flat, preferred_element_type=FLOAT).astype(BF16)

    summed = []
    for own, others in zip(d_weights, d_others):
        total = lax.dynamic_index_in_dim(own, part, 1, keepdims=False).astype(FLOAT)
        summed.append((total + jnp.sum(others.astype(FLOAT), axis=0)).astype(BF16))
    sends = [
        Send(lambda i, o, z, f, d=d, w=w: i[w].at[d], lambda i, o, z, f, d=d, w=w: o[w].at[d], d, 0)
        for w in range(2)
        for d in range(nsp)
    ]
    for w in range(2, 5):
        for s in range(plane_experts):
            sends.append(
                Send(
                    lambda i, o, z, f, s=s, w=w: i[w].at[flip(lax.div(f, parts), s)],
                    lambda i, o, z, f, s=s, w=w: o[w].at[lax.div(f, parts)],
                    0,
                    s * parts,
                )
            )
    d_home, dgate_home, *shards = exchange(
        "hidden_grads_home",
        8,
        (combine(d_back), combine(dgate_back), *summed),
        [(nsp, rows, width), (nsp, rows, LANES)]
        + [(plane_experts,) + tuple(shape) for shape in shard_shapes],
        sends,
        58,
    )
    all_down, all_gate, all_up = [
        lax.all_gather(block, "sp", axis=0, tiled=True) for block in shards
    ]
    d_home = jnp.sum(d_home.astype(FLOAT), axis=0)
    tail = jnp.sum(dgate_home.astype(FLOAT), axis=0)
    d_gates = tail[:, :n_experts] + tail[:, n_experts : 2 * n_experts]
    d_logits = gates * (d_gates - jnp.sum(gates * d_gates, axis=1, keepdims=True))
    d_router = jnp.dot(hn_b.astype(FLOAT).T, d_logits, precision=HIGH_PRECISION)
    d_hn = d_home + jnp.dot(d_logits, wr_b.astype(FLOAT).T, precision=HIGH_PRECISION)
    grad_out = cotangent[0].astype(FLOAT)
    unused, ffn_pull = jax.vjp(rms_norm, mid_rows, g_ffn)
    d_mid_norm, d_ffn_gain = ffn_pull(d_hn)
    d_mid = grad_out + d_mid_norm

    d_attn_b = d_mid.astype(BF16)
    sends = [
        Send(lambda i, o, z, f: i[0], lambda i, o, z, f: o[0].at[f], 0, m)
        for m in range(0, nf, 2)
    ]
    for m in range(0, nf, 2):
        if m == 0:
            sends.append(Send(lambda i, o, z, f: i[0], lambda i, o, z, f: o[0].at[f], 0, 1))
        else:
            sends.append(
                Send(
                    lambda i, o, z, f, m=m: o[0].at[flip(f, m)],
                    lambda i, o, z, f, m=m: o[0].at[flip(f, m)],
                    0,
                    1,
                    m // 2,
                )
            )
    (da_all,) = exchange("gather_grads", 9, (d_attn_b,), ((nf, rows, width),), sends, 30)
    da_all = da_all.reshape(seqs * rows, width)
    d_wo = contract_rows(o_mat, da_all)
    d_o = contract_cols(da_all, wo_b).astype(BF16).reshape(seqs, rows, my_heads, head_dim)
    d_o = d_o.transpose(0, 2, 1, 3)
    d_val = jnp.einsum("nhqk,nhqd->nkd", probs, d_o, preferred_element_type=FLOAT)
    d_probs = jnp.einsum("nhqd,nkd->nhqk", d_o, values, preferred_element_type=FLOAT)
    probs_f = probs.astype(FLOAT)
    d_scores = (
        probs_f * (d_probs - jnp.sum(probs_f * d_probs, axis=3, keepdims=True))
    ).astype(BF16)
    dq = (
        jnp.einsum("nhqk,nkd->nqhd", d_scores, keys, preferred_element_type=FLOAT) * score_scale
    ).astype(BF16)
    d_key = (
        jnp.einsum("nhqk,nhqd->nkd", d_scores, q_rows, preferred_element_type=FLOAT) * score_scale
    )
    d_kv = jnp.concatenate([d_key, d_val], axis=2).astype(BF16)
    d_kv = d_kv.reshape(seqs, nsp, rows, 2 * head_dim).transpose(1, 0, 2, 3)
    d_kv = d_kv.reshape(nsp, seqs * rows, 2 * head_dim)
    sends = [
        Send(lambda i, o, z, f, d=d: i[0].at[d], lambda i, o, z, f, d=d: o[0].at[d], d, 0)
        for d in range(nsp)
    ]
    for s in range(plane_experts):
        sends.append(
            Send(
                lambda i, o, z, f, s=s: i[1].at[s],
                lambda i, o, z, f, s=s: o[1].at[:, s],
                0,
                s * parts,
            )
        )
    d_kv, out_back = exchange(
        "key_grads_planes",
        10,
        (d_kv, weighted.reshape(plane_experts, nsp, cap, width)),
        ((nsp, seqs * rows, 2 * head_dim), (nsp, plane_experts, cap, width)),
        sends,
        60,
    )
    out_blocks = combine(out_back)
    moe_sum = out_blocks[0].astype(FLOAT)
    for d in range(1, nsp):
        moe_sum = moe_sum + lax.ppermute(
            out_blocks[d], "sp", [(i, i ^ d) for i in range(nsp)]
        ).astype(FLOAT)
    mixed = (mid_rows + moe_sum).astype(BF16)[None]
    d_kv = jnp.sum(d_kv.astype(FLOAT), axis=0).astype(BF16)
    d_kv, all_down = lax.optimization_barrier((d_kv, all_down))
    (d_kv,) = exchange(
        "key_grads_group",
        11,
        (d_kv,),
        ((rep, seqs * rows, 2 * head_dim),),
        [
            Send(lambda i, o, z, f: i[0], lambda i, o, z, f, p=p: o[0].at[p], 0, p)
            for p in range(rep)
        ],
        8,
    )
    d_kv = jnp.sum(d_kv.astype(FLOAT), axis=0)
    unused, q_pull = jax.vjp(prep_heads, q_lin, g_query)
    d_q_lin, d_q_gain = q_pull(dq.astype(FLOAT))
    unused, k_pull = jax.vjp(prep_heads, k_lin, g_key)
    d_k_lin, d_k_gain = k_pull(d_kv[:, :head_dim].reshape(seqs, rows, 1, head_dim))
    dq_b = d_q_lin.astype(BF16).reshape(seqs * rows, q_cols)
    dk_b = d_k_lin.astype(BF16).reshape(seqs * rows, head_dim)
    dv_b = d_kv[:, head_dim:].astype(BF16)
    d_qkv = jnp.concatenate([dq_b, dk_b, dv_b], axis=1)
    share = 1.0 / rep
    d_qkv_shared = jnp.concatenate([dq_b, dk_b * BF16(share), dv_b * BF16(share)], axis=1)
    d_w_qkv = contract_rows(xn_b, d_qkv).astype(BF16).reshape(nf, shard, qkv_cols)
    d_xn = pair_then_plane(contract_cols(d_qkv_shared, w_qkv), "input_sum", 13)
    unused, attn_pull = jax.vjp(rms_norm, x_rows, g_attn)
    d_x_norm, d_attn_gain = attn_pull(d_xn)
    grad_tokens = (d_mid + d_x_norm)[None]

    smalls = jnp.concatenate(
        [
            d_attn_gain.reshape(nf, shard),
            d_ffn_gain.reshape(nf, shard),
            d_q_gain.reshape(nf, head_dim // nf),
            (d_k_gain * share).reshape(nf, head_dim // nf),
            d_router.reshape(nf, shard * n_experts),
        ],
        axis=1,
    ).astype(BF16)
    small_size = smalls.shape[1]
    small_cols = pl.cdiv(small_size, kv_heads * head_dim) * kv_heads * head_dim // small_rows
    small_cols = pl.cdiv(small_cols, LANES) * LANES
    smalls = jnp.pad(smalls, ((0, 0), (0, small_rows * small_cols - small_size)))
    d_w_shard, small_shard = exchange(
        "head_grads_to_shards",
        12,
        (d_w_qkv, smalls.reshape(nf, small_rows, small_cols)),
        ((nf, shard, qkv_cols), (nf, small_rows, small_cols)),
        [
            Send(
                lambda i, o, z, f, m=m, w=w: i[w].at[flip(f, m)],
                lambda i, o, z, f, m=m, w=w: o[w].at[f],
                0,
                m,
            )
            for w in range(2)
            for m in range(nf)
        ],
        36,
    )
    d_wq = d_w_shard[:, :, :q_cols].transpose(1, 0, 2).reshape(shard, n_heads * head_dim)
    d_wkv = d_w_shard[::rep, :, q_cols:].reshape(kv_heads, shard, 2, head_dim)
    d_wkv = d_wkv.transpose(2, 1, 0, 3).reshape(2 * shard, kv_heads * head_dim)
    small_sum = jnp.sum(small_shard.astype(FLOAT), axis=0).astype(BF16)
    sum_out = lax.psum(d_wo.astype(BF16), "sp").astype(FLOAT)
    kv_cols = kv_heads * head_dim
    d_wkv = jnp.concatenate([d_wkv, small_sum.reshape(-1, kv_cols)], axis=0)
    sum_q, sum_kv = lax.psum((d_wq, d_wkv), "sp")
    sum_q = sum_q.astype(FLOAT)
    sum_kv = sum_kv.astype(FLOAT)
    small_sum = sum_kv[2 * shard :].reshape(-1)
    at = 0
    pieces = []
    for size in (shard, shard, head_dim // nf, head_dim // nf, shard * n_experts):
        pieces.append(small_sum[at : at + size])
        at += size
    return (
        mixed,
        grad_tokens,
        pieces[0],
        sum_q,
        sum_kv[:shard],
        sum_kv[shard : 2 * shard],
        pieces[2],
        pieces[3],
        sum_out,
        pieces[1],
        pieces[4].reshape(shard, n_experts),
        all_gate.astype(FLOAT),
        all_up.astype(FLOAT),
        all_down.astype(FLOAT),
    )


def solution(mesh):
    by_token = P("fsdp", "sp", None)
    by_row = P("fsdp", None)
    by_inner = P(None, "fsdp", None)
    in_specs = (
        by_token,
        by_token,
        P("fsdp"),
        by_row,
        by_row,
        by_row,
        P("fsdp"),
        P("fsdp"),
        by_row,
        P("fsdp"),
        by_row,
        by_inner,
        by_inner,
        by_inner,
        by_token,
    )
    out_specs = (
        by_token,
        by_token,
        P("fsdp"),
        by_row,
        by_row,
        by_row,
        P("fsdp"),
        P("fsdp"),
        by_row,
        P("fsdp"),
        by_row,
        by_inner,
        by_inner,
        by_inner,
    )
    return jax.shard_map(body, mesh=mesh, in_specs=in_specs, out_specs=out_specs, check_vma=False)
```

```python
import math
from typing import Callable, NamedTuple

import jax
import jax.numpy as jnp
from jax import lax
from jax.experimental import pallas as pl
from jax.experimental.pallas import tpu as pltpu
from jax.sharding import PartitionSpec as P

QUERY_HEADS = 32
KEY_VALUE_HEADS = 4
HEAD_SIZE = 128
CAP = 80
LANES = 128

EPS = 1e-06
THETA = 1000000.0
HIGH_PRECISION = lax.Precision.HIGHEST
BF16 = jnp.bfloat16
FLOAT = jnp.float32
MESH = pl.DeviceIdType.MESH


def rms_norm(values_in, gain_vec):
    return (
        values_in
        * lax.rsqrt(jnp.mean(values_in * values_in, axis=-1, keepdims=True) + EPS)
        * gain_vec
    )


def rotate(values_in, cosine, sine_part):
    half_dim = values_in.shape[-1] // 2
    first_half = values_in[..., :half_dim]
    second = values_in[..., half_dim:]
    return jnp.concatenate(
        [first_half * cosine - second * sine_part, second * cosine + first_half * sine_part],
        axis=-1,
    )


def contract_rows(left_mat, right_mat):
    return lax.dot_general(
        left_mat, right_mat, (((0,), (0,)), ((), ())), preferred_element_type=FLOAT
    )


def contract_cols(left_mat, right_mat):
    return lax.dot_general(
        left_mat, right_mat, (((1,), (1,)), ((), ())), preferred_element_type=FLOAT
    )


def matmul(left_mat, right_mat):
    return jnp.dot(left_mat, right_mat, preferred_element_type=FLOAT)


def flip(index, mask):
    bit = 1
    while bit <= mask:
        if mask & bit:
            index = index + bit * (1 - 2 * lax.rem(lax.div(index, bit), 2))
        bit *= 2
    return index


class _ShapeOnly:
    def __init__(self, shape):
        self.shape = tuple(shape)

    @property
    def at(self):
        return self

    def __getitem__(self, index):
        index = index if isinstance(index, tuple) else (index,)
        shape = []
        for size, i in zip(self.shape, index):
            if isinstance(i, slice):
                shape.append(len(range(*i.indices(size))))
            elif hasattr(i, "size") and hasattr(i, "start"):
                shape.append(i.size)
        return _ShapeOnly(tuple(shape) + self.shape[len(index) :])


class Send(NamedTuple):
    src: Callable
    dst: Callable
    dz: int
    df: int
    after: int | None = None


def exchange(name, cid, arrays, out_shapes, sends, micros):
    n_in, n_out = len(arrays), len(out_shapes)
    peers = sorted({(s.dz, s.df) for s in sends} - {(0, 0)})
    stays = [k for k, s in enumerate(sends) if (s.dz, s.df) == (0, 0)]
    stay_shapes = []

    def probe(*refs):
        for k in stays:
            view = sends[k].src(refs, None, jnp.int32(0), jnp.int32(0))
            stay_shapes.append(view.shape)

    probe(*[_ShapeOnly(a.shape) for a in arrays])

    def kernel(*refs):
        ins, outs = refs[:n_in], refs[n_in : n_in + n_out]
        send_sems, recv_sems = refs[n_in + n_out : n_in + n_out + 2]
        bounce = dict(zip(stays, refs[n_in + n_out + 2 :]))
        z = lax.axis_index("sp")
        f = lax.axis_index("fsdp")
        barrier = pltpu.get_barrier_semaphore()
        for dz, df in peers:
            pl.semaphore_signal(
                barrier, inc=1, device_id=(flip(z, dz), flip(f, df)), device_id_type=MESH
            )
        pl.semaphore_wait(barrier, len(peers))
        copies = []
        for k, s in enumerate(sends):
            src = s.src(ins, outs, z, f)
            dst = s.dst(ins, outs, z, f)
            if (s.dz, s.df) == (0, 0):
                copies.append(
                    (
                        pltpu.make_async_copy(src, bounce[k], recv_sems.at[k]),
                        pltpu.make_async_copy(bounce[k], dst, send_sems.at[k]),
                    )
                )
            else:
                copies.append(
                    pltpu.make_async_remote_copy(
                        src_ref=src,
                        dst_ref=dst,
                        send_sem=send_sems.at[k],
                        recv_sem=recv_sems.at[k],
                        device_id=(flip(z, s.dz), flip(f, s.df)),
                        device_id_type=MESH,
                    )
                )
        arrived = set()

        def arrive(k):
            if k not in arrived:
                arrived.add(k)
                s = sends[k]
                if (s.dz, s.df) == (0, 0):
                    copies[k][1].wait()
                else:
                    copies[k].wait_recv()

        for k, s in enumerate(sends):
            if k in stays:
                copies[k][0].start()
            elif s.after is None:
                copies[k].start()
        for k in stays:
            copies[k][0].wait()
            copies[k][1].start()
        for k, s in enumerate(sends):
            if s.after is not None:
                arrive(s.after)
                copies[k].start()
        for k, s in enumerate(sends):
            if (s.dz, s.df) != (0, 0):
                copies[k].wait_send()
            arrive(k)

    result = pl.pallas_call(
        kernel,
        out_shape=[jax.ShapeDtypeStruct(shape, BF16) for shape in out_shapes],
        in_specs=[pl.BlockSpec(memory_space=pl.ANY)] * n_in,
        out_specs=[pl.BlockSpec(memory_space=pl.ANY)] * n_out,
        scratch_shapes=[
            pltpu.SemaphoreType.DMA((len(sends),)),
            pltpu.SemaphoreType.DMA((len(sends),)),
        ]
        + [pltpu.VMEM(shape, BF16) for shape in stay_shapes],
        compiler_params=pltpu.CompilerParams(
            collective_id=cid, has_side_effects=True, vmem_limit_bytes=32 * 1024 * 1024
        ),
        cost_estimate=pl.CostEstimate(
            flops=0, bytes_accessed=int(micros * 3.0e6), transcendentals=0
        ),
        name=name,
    )(*arrays)
    return result


def body(
    tokens,
    expert_ids,
    attn_gain,
    query_weight,
    key_weight,
    value_weight,
    q_gain,
    k_gain,
    output_weight,
    ffn_gain,
    router_weight,
    w_gate,
    w_up,
    w_down,
    cotangent,
):
    nsp = lax.axis_size("sp")
    nf = lax.axis_size("fsdp")
    z = lax.axis_index("sp")
    f = lax.axis_index("fsdp")
    rows = tokens.shape[1]
    width = tokens.shape[2]
    shard = width // nf
    n_heads, kv_heads, head_dim = QUERY_HEADS, KEY_VALUE_HEADS, HEAD_SIZE
    my_heads = n_heads // nf
    rep = nf // kv_heads
    q_cols = my_heads * head_dim
    qkv_cols = q_cols + 2 * head_dim
    score_scale = 1.0 / math.sqrt(head_dim)
    n_experts = w_gate.shape[0]
    hidden_size = w_gate.shape[2]
    hid_shard = w_down.shape[1]
    plane_experts = n_experts // nsp
    parts = nf // plane_experts
    cap = CAP
    seqs = nf
    part = lax.rem(f, parts)
    place = lax.div(f, parts)
    expert = z * plane_experts + place

    def swap_f(block, mask):
        return lax.ppermute(block, "fsdp", [(i, i ^ mask) for i in range(nf)])

    def swap_z(block, mask):
        return lax.ppermute(block, "sp", [(i, i ^ mask) for i in range(nsp)])

    small = jnp.concatenate(
        [
            attn_gain.astype(BF16),
            ffn_gain.astype(BF16),
            q_gain.astype(BF16),
            k_gain.astype(BF16),
            router_weight.astype(BF16).reshape(-1),
        ]
    )
    small_rows = 16
    small = jnp.pad(small, (0, small_rows * width - small.shape[0])).reshape(small_rows, width)
    x_pay = jnp.concatenate([tokens[0], small], axis=0)
    pay_rows = rows + small_rows
    by_head = query_weight.astype(BF16).reshape(shard, nf, q_cols)
    key_b = jnp.repeat(key_weight.astype(BF16).reshape(shard, kv_heads, head_dim), rep, axis=1)
    value_b = jnp.repeat(value_weight.astype(BF16).reshape(shard, kv_heads, head_dim), rep, axis=1)
    qkv_pay = jnp.concatenate([by_head, key_b, value_b], axis=2).transpose(1, 0, 2)
    routes = expert_ids[0]
    expert_iota = jnp.arange(n_experts, dtype=jnp.int32)
    routed = jnp.any(routes[:, :, None] == expert_iota[None, None, :], axis=1)
    dy_pay = jnp.concatenate(
        [
            cotangent[0],
            routed.astype(BF16),
            jnp.zeros((rows, LANES - n_experts), BF16),
        ],
        axis=1,
    )
    wide = width + LANES

    def plane_cast(weight):
        return lax.dynamic_slice_in_dim(weight, z * plane_experts, plane_experts, 0).astype(BF16)

    gate_pay, up_pay, down_pay = plane_cast(w_gate), plane_cast(w_up), plane_cast(w_down)

    sends = []
    for m in range(0, nf, 2):
        sends.append(
            Send(
                lambda i, o, z, f, m=m: i[0],
                lambda i, o, z, f: o[0].at[f],
                0,
                m,
            )
        )
    for m in range(nf):
        sends.append(
            Send(
                lambda i, o, z, f, m=m: i[1].at[flip(f, m)],
                lambda i, o, z, f, m=m: o[1].at[f],
                0,
                m,
            )
        )
    for m in range(nsp):
        sends.append(
            Send(lambda i, o, z, f: i[2], lambda i, o, z, f, m=m: o[2].at[m], m, 0)
        )
    for m in range(0, nf, 2):
        if m == 0:
            sends.append(
                Send(lambda i, o, z, f: i[0], lambda i, o, z, f: o[0].at[f], 0, 1)
            )
        else:
            sends.append(
                Send(
                    lambda i, o, z, f, m=m: o[0].at[flip(f, m)],
                    lambda i, o, z, f, m=m: o[0].at[flip(f, m)],
                    0,
                    1,
                    m // 2,
                )
            )
    x_all, w_qkv, dy_z = exchange(
        "gather_inputs",
        0,
        (x_pay, qkv_pay, dy_pay),
        ((nf, pay_rows, width), (nf, shard, qkv_cols), (nsp, rows, wide)),
        sends,
        65,
    )

    small_all = x_all[:, rows:, :].reshape(nf, small_rows * width)
    at = 0
    pieces = []
    for size in (shard, shard, head_dim // nf, head_dim // nf, shard * n_experts):
        pieces.append(small_all[:, at : at + size])
        at += size
    g_attn = pieces[0].reshape(width).astype(FLOAT)
    g_ffn = pieces[1].reshape(width).astype(FLOAT)
    g_query = pieces[2].reshape(head_dim).astype(FLOAT)
    g_key = pieces[3].reshape(head_dim).astype(FLOAT)
    wr_b = pieces[4].reshape(width, n_experts)

    xn_b = (
        rms_norm(x_all[:, :rows, :].astype(FLOAT), g_attn).astype(BF16).reshape(seqs * rows, width)
    )
    w_qkv = w_qkv.reshape(width, qkv_cols)
    qkv_lin = matmul(xn_b, w_qkv)
    q_lin = qkv_lin[:, :q_cols].reshape(seqs, rows, my_heads, head_dim)
    k_lin = qkv_lin[:, q_cols : q_cols + head_dim].reshape(seqs, rows, 1, head_dim)
    v_b = qkv_lin[:, q_cols + head_dim :].astype(BF16)
    half_dim = head_dim // 2
    inverse_freq = THETA ** (-(jnp.arange(half_dim, dtype=FLOAT) * 2.0 / head_dim))
    positions = (z * rows + jnp.arange(rows, dtype=jnp.int32)).astype(FLOAT)
    angles = positions[:, None] * inverse_freq[None, :]
    cosine = jnp.cos(angles)[None, :, None, :]
    sine_part = jnp.sin(angles)[None, :, None, :]

    def prep_heads(linear, gain_vec):
        return rotate(rms_norm(linear, gain_vec), cosine, sine_part)

    q_b = prep_heads(q_lin, g_query).astype(BF16)
    k_b = prep_heads(k_lin, g_key).astype(BF16).reshape(seqs * rows, head_dim)

    kv_pay = jnp.concatenate([k_b, v_b], axis=1)
    piece = seqs * rows // rep
    sends = []
    for d in range(nsp):
        sends.append(
            Send(
                lambda i, o, z, f: i[0].at[pl.ds(lax.rem(f, rep) * piece, piece)],
                lambda i, o, z, f, d=d: o[0].at[d, pl.ds(lax.rem(f, rep) * piece, piece)],
                d,
                0,
            )
        )
    for d in range(nsp):
        for p in range(1, rep):
            sends.append(
                Send(
                    lambda i, o, z, f, d=d: o[0].at[d, pl.ds(lax.rem(f, rep) * piece, piece)],
                    lambda i, o, z, f, d=d: o[0].at[d, pl.ds(lax.rem(f, rep) * piece, piece)],
                    0,
                    p,
                    d,
                )
            )
    for which in range(3):
        for s in range(plane_experts):
            stage = len(sends)
            sends.append(
                Send(
                    lambda i, o, z, f, s=s, w=which: i[1 + w].at[flip(lax.div(f, parts), s)],
                    lambda i, o, z, f, w=which: o[1 + w].at[f],
                    0,
                    s * parts,
                )
            )
            for p in range(1, parts):
                if s == 0:
                    forward = Send(
                        lambda i, o, z, f, w=which: i[1 + w].at[lax.div(f, parts)],
                        lambda i, o, z, f, w=which: o[1 + w].at[f],
                        0,
                        p,
                    )
                else:
                    forward = Send(
                        lambda i, o, z, f, s=s, w=which: o[1 + w].at[flip(f, s * parts)],
                        lambda i, o, z, f, s=s, w=which: o[1 + w].at[flip(f, s * parts)],
                        0,
                        p,
                        stage,
                    )
                sends.append(forward)
    kv_z, gate_all, up_all, down_all = exchange(
        "keys_and_experts",
        1,
        (kv_pay, gate_pay, up_pay, down_pay),
        (
            (nsp, seqs * rows, 2 * head_dim),
            (nf, shard, hidden_size),
            (nf, shard, hidden_size),
            (nf, hid_shard, width),
        ),
        sends,
        55,
    )
    wg_b = gate_all.reshape(width, hidden_size)
    wu_b = up_all.reshape(width, hidden_size)
    wd_b = down_all.reshape(hidden_size, width)
    kv_seq = kv_z.reshape(nsp, seqs, rows, 2 * head_dim).transpose(1, 0, 2, 3)
    kv_seq = kv_seq.reshape(seqs, nsp * rows, 2 * head_dim)
    keys = kv_seq[:, :, :head_dim]
    values = kv_seq[:, :, head_dim:]

    q_rows = q_b.transpose(0, 2, 1, 3)
    plane_of = jnp.bitwise_xor(jnp.arange(nsp, dtype=jnp.int32), z)
    key_pos = (plane_of[:, None] * rows + jnp.arange(rows, dtype=jnp.int32)[None, :]).reshape(-1)
    query_pos = z * rows + jnp.arange(rows, dtype=jnp.int32)
    causal = key_pos[None, :] <= query_pos[:, None]
    scores = (
        jnp.einsum("nhqd,nkd->nhqk", q_rows, keys, preferred_element_type=FLOAT) * score_scale
    )
    scores = jnp.where(causal[None, None], scores, -1e30)
    row_top = jnp.max(scores, axis=3, keepdims=True)
    expo = jnp.exp(scores - row_top)
    probs = (expo / jnp.sum(expo, axis=3, keepdims=True)).astype(BF16)
    o_rows = jnp.einsum("nhqk,nkd->nqhd", probs, values, preferred_element_type=FLOAT)
    o_mat = o_rows.astype(BF16).reshape(seqs * rows, q_cols)
    wo_b = output_weight.astype(BF16)

    def pair_then_plane(partial, name, cid):
        split = partial.astype(BF16).reshape(nf // 2, 2, rows, width)
        (other,) = exchange(
            name + "_pair",
            cid,
            (split,),
            ((nf // 2, rows, width),),
            [Send(lambda i, o, z, f: i[0].at[:, 1 - lax.rem(f, 2)], lambda i, o, z, f: o[0], 0, 1)],
            8,
        )
        own = lax.dynamic_index_in_dim(split, lax.rem(f, 2), 1, keepdims=False)
        summed = (own.astype(FLOAT) + other.astype(FLOAT)).astype(BF16)
        sends = [
            Send(
                lambda i, o, z, f, j=j: i[0].at[flip(lax.div(f, 2), j)],
                lambda i, o, z, f, j=j: o[0].at[j],
                0,
                2 * j,
            )
            for j in range(nf // 2)
        ]
        (blocks,) = exchange(
            name + "_plane", cid + 1, (summed,), ((nf // 2, rows, width),), sends, 27
        )
        return jnp.sum(blocks.astype(FLOAT), axis=0)

    x_rows = tokens[0].astype(FLOAT)
    mid_rows = x_rows + pair_then_plane(matmul(o_mat, wo_b), "out_sum", 3)
    hn_b = rms_norm(mid_rows, g_ffn).astype(BF16)
    logits = matmul(hn_b, wr_b)
    logits = jnp.where(routed, logits, -1e30)
    expo = jnp.where(routed, jnp.exp(logits - jnp.max(logits, axis=1, keepdims=True)), 0.0)
    gates = expo / jnp.sum(expo, axis=1, keepdims=True)

    def two_parts(exact):
        high = exact.astype(BF16)
        return high, (exact - high.astype(FLOAT)).astype(BF16)

    own_experts = z * plane_experts + jnp.bitwise_xor(
        place, jnp.arange(plane_experts, dtype=jnp.int32)
    )
    own_hot = (expert_iota[:, None] == own_experts[None, :]).astype(FLOAT)
    routed_z = lax.dot_general(
        own_hot,
        dy_z[:, :, width : width + n_experts].astype(FLOAT),
        (((0,), (2,)), ((), ())),
        preferred_element_type=FLOAT,
    ).transpose(1, 0, 2)
    earlier = jnp.triu(jnp.ones((rows, rows), FLOAT), 1)
    rank = jnp.dot(
        routed_z.reshape(nsp * plane_experts, rows), earlier, preferred_element_type=FLOAT
    ).reshape(nsp, plane_experts, rows)
    rank = rank * routed_z + (routed_z - 1.0)
    pick = (
        rank[:, :, None, :] == jnp.arange(cap, dtype=FLOAT)[None, None, :, None]
    ).astype(BF16)
    pick = pick.reshape(nsp, plane_experts * cap, rows)

    def select(source):
        picked = jnp.einsum("drt,dtc->drc", pick, source, preferred_element_type=FLOAT)
        return picked.astype(BF16).reshape(nsp, plane_experts, cap, source.shape[2])

    def to_experts(which):
        return [
            Send(
                lambda i, o, z, f, s=s: i[which].at[:, s],
                lambda i, o, z, f, s=s: o[which].at[s],
                0,
                s * parts,
            )
            for s in range(plane_experts)
        ]

    gate_high, gate_low = two_parts(gates)
    gate_lanes = jnp.concatenate(
        [gate_high, gate_low, jnp.zeros((rows, LANES - 2 * n_experts), BF16)], axis=1
    )
    hn_z, gate_z, dy_rows = exchange(
        "hidden_planes",
        5,
        (hn_b, gate_lanes, select(dy_z[:, :, :width])),
        ((nsp, rows, width), (nsp, rows, LANES), (plane_experts, nsp, cap, width)),
        [
            Send(lambda i, o, z, f, w=w: i[w], lambda i, o, z, f, d=d, w=w: o[w].at[d], d, 0)
            for w in range(2)
            for d in range(nsp)
        ]
        + to_experts(2),
        58,
    )
    hn_rows, gate_rows = exchange(
        "rows_to_experts",
        6,
        (select(hn_z), select(gate_z)),
        ((plane_experts, nsp, cap, width), (plane_experts, nsp, cap, LANES)),
        to_experts(0) + to_experts(1),
        60,
    )

    n_rows = plane_experts * nsp * cap
    hn_in = hn_rows.reshape(n_rows, width)
    dy_in = dy_rows.reshape(n_rows, width)
    hot = (jnp.arange(n_experts, dtype=jnp.int32) == expert).astype(FLOAT)
    tail = gate_rows.reshape(n_rows, LANES)[:, : 2 * n_experts].astype(FLOAT)
    row_gate = jnp.sum(
        (tail[:, :n_experts] + tail[:, n_experts:]) * hot[None, :], axis=1, keepdims=True
    )
    gate_pre = matmul(hn_in, wg_b)
    up_pre = matmul(hn_in, wu_b)
    sigma = jax.nn.sigmoid(gate_pre)
    act_f = gate_pre * sigma
    hidden = (act_f * up_pre).astype(BF16)
    dy_f = dy_in.astype(FLOAT)
    d_result = (row_gate * dy_f).astype(BF16)

    def by_shard(full, inner):
        return full.astype(BF16).reshape((plane_experts, parts) + inner)

    def pair_total(own, others):
        total = lax.dynamic_index_in_dim(own, part, 1, keepdims=False).astype(FLOAT)
        for other in others:
            total = total + other.astype(FLOAT)
        return total.astype(BF16)

    d_down = by_shard(contract_rows(hidden, d_result), (hid_shard, width))
    d_down = pair_total(
        d_down,
        [
            swap_f(lax.dynamic_index_in_dim(d_down, flip(part, p), 1, keepdims=False), p)
            for p in range(1, parts)
        ],
    )
    d_down = jnp.stack(
        [
            swap_f(
                lax.dynamic_index_in_dim(d_down, flip(place, s), 0, keepdims=False), s * parts
            )
            if s
            else lax.dynamic_index_in_dim(d_down, place, 0, keepdims=False)
            for s in range(plane_experts)
        ]
    )
    all_down = lax.all_gather(d_down, "sp")
    result = matmul(hidden, wd_b)
    row_dgate = jnp.sum(result * dy_f, axis=1, keepdims=True)
    weighted = (row_gate * result).astype(BF16)
    d_hidden = contract_cols(d_result, wd_b)
    d_gate_pre = (d_hidden * up_pre * sigma * (1.0 + gate_pre * (1.0 - sigma))).astype(BF16)
    d_up_pre = (d_hidden * act_f).astype(BF16)
    d_in = (contract_cols(d_gate_pre, wg_b) + contract_cols(d_up_pre, wu_b)).astype(BF16)
    dgate_high, dgate_low = two_parts(row_dgate * hot[None, :])
    dgate_lanes = jnp.concatenate(
        [dgate_high, dgate_low, jnp.zeros((n_rows, LANES - 2 * n_experts), BF16)], axis=1
    )

    d_weights = (
        by_shard(contract_rows(hn_in, d_gate_pre), (shard, hidden_size)),
        by_shard(contract_rows(hn_in, d_up_pre), (shard, hidden_size)),
    )
    shard_shapes = [w.shape[2:] for w in d_weights]

    sends = []
    for w in range(2):
        for s in range(plane_experts):
            sends.append(
                Send(
                    lambda i, o, z, f, s=s, w=w: i[w].at[s],
                    lambda i, o, z, f, s=s, w=w: o[w].at[:, s],
                    0,
                    s * parts,
                )
            )
    for w in range(2):
        for p in range(1, parts):
            sends.append(
                Send(
                    lambda i, o, z, f, p=p, w=w: i[2 + w].at[:, flip(lax.rem(f, parts), p)],
                    lambda i, o, z, f, p=p, w=w: o[2 + w].at[p - 1],
                    0,
                    p,
                )
            )
    d_back, dgate_back, *d_others = exchange(
        "rows_from_experts",
        7,
        (
            d_in.reshape(plane_experts, nsp, cap, width),
            dgate_lanes.reshape(plane_experts, nsp, cap, LANES),
        )
        + d_weights,
        [(nsp, plane_experts, cap, width), (nsp, plane_experts, cap, LANES)]
        + [(parts - 1, plane_experts) + tuple(shape) for shape in shard_shapes],
        sends,
        70,
    )

    def combine(returned):
        flat = returned.reshape(nsp, plane_experts * cap, returned.shape[3])
        return jnp.einsum("drt,drc->dtc", pick, flat, preferred_element_type=FLOAT).astype(BF16)

    summed = [
        pair_total(own, [others[p] for p in range(parts - 1)])
        for own, others in zip(d_weights, d_others)
    ]
    sends = [
        Send(lambda i, o, z, f, d=d, w=w: i[w].at[d], lambda i, o, z, f, d=d, w=w: o[w].at[d], d, 0)
        for w in range(2)
        for d in range(nsp)
    ]
    for w in range(2, 4):
        for s in range(plane_experts):
            sends.append(
                Send(
                    lambda i, o, z, f, s=s, w=w: i[w].at[flip(lax.div(f, parts), s)],
                    lambda i, o, z, f, s=s, w=w: o[w].at[lax.div(f, parts)],
                    0,
                    s * parts,
                )
            )
    d_home, dgate_home, *shards = exchange(
        "hidden_grads_home",
        8,
        (combine(d_back), combine(dgate_back), *summed),
        [(nsp, rows, width), (nsp, rows, LANES)]
        + [(plane_experts,) + tuple(shape) for shape in shard_shapes],
        sends,
        58,
    )
    all_gate, all_up = [lax.all_gather(block, "sp", axis=0, tiled=True) for block in shards]
    d_home = jnp.sum(d_home.astype(FLOAT), axis=0)
    tail = jnp.sum(dgate_home.astype(FLOAT), axis=0)
    d_gates = tail[:, :n_experts] + tail[:, n_experts : 2 * n_experts]
    d_logits = gates * (d_gates - jnp.sum(gates * d_gates, axis=1, keepdims=True))
    d_router = jnp.dot(hn_b.astype(FLOAT).T, d_logits, precision=HIGH_PRECISION)
    d_hn = d_home + jnp.dot(d_logits, wr_b.astype(FLOAT).T, precision=HIGH_PRECISION)
    grad_out = cotangent[0].astype(FLOAT)
    unused, ffn_pull = jax.vjp(rms_norm, mid_rows, g_ffn)
    d_mid_norm, d_ffn_gain = ffn_pull(d_hn)
    d_mid = grad_out + d_mid_norm

    d_attn_b = d_mid.astype(BF16)
    d_attn_b, all_down = lax.optimization_barrier((d_attn_b, all_down))
    grad_down = jnp.take(
        all_down,
        jnp.bitwise_xor(jnp.arange(plane_experts, dtype=jnp.int32), place),
        axis=1,
        mode="clip",
    )
    grad_down = grad_down.astype(FLOAT).reshape(n_experts, hid_shard, width)
    sends = [
        Send(lambda i, o, z, f: i[0], lambda i, o, z, f: o[0].at[f], 0, m)
        for m in range(0, nf, 2)
    ]
    for m in range(0, nf, 2):
        if m == 0:
            sends.append(Send(lambda i, o, z, f: i[0], lambda i, o, z, f: o[0].at[f], 0, 1))
        else:
            sends.append(
                Send(
                    lambda i, o, z, f, m=m: o[0].at[flip(f, m)],
                    lambda i, o, z, f, m=m: o[0].at[flip(f, m)],
                    0,
                    1,
                    m // 2,
                )
            )
    (da_all,) = exchange("gather_grads", 9, (d_attn_b,), ((nf, rows, width),), sends, 30)
    da_all = da_all.reshape(seqs * rows, width)
    d_wo = contract_rows(o_mat, da_all)
    d_o = contract_cols(da_all, wo_b).astype(BF16).reshape(seqs, rows, my_heads, head_dim)
    d_o = d_o.transpose(0, 2, 1, 3)
    d_val = jnp.einsum("nhqk,nhqd->nkd", probs, d_o, preferred_element_type=FLOAT)
    d_probs = jnp.einsum("nhqd,nkd->nhqk", d_o, values, preferred_element_type=FLOAT)
    probs_f = probs.astype(FLOAT)
    d_scores = (
        probs_f * (d_probs - jnp.sum(probs_f * d_probs, axis=3, keepdims=True))
    ).astype(BF16)
    dq = (
        jnp.einsum("nhqk,nkd->nqhd", d_scores, keys, preferred_element_type=FLOAT) * score_scale
    ).astype(BF16)
    d_key = (
        jnp.einsum("nhqk,nhqd->nkd", d_scores, q_rows, preferred_element_type=FLOAT) * score_scale
    )
    d_kv = jnp.concatenate([d_key, d_val], axis=2).astype(BF16)
    d_kv = d_kv.reshape(seqs, nsp, rows, 2 * head_dim).transpose(1, 0, 2, 3)
    d_kv = d_kv.reshape(nsp, seqs * rows, 2 * head_dim)
    d_kv = d_kv.reshape(nsp, rep, piece, 2 * head_dim)
    (others,) = exchange(
        "key_grads_group",
        11,
        (d_kv,),
        ((rep - 1, nsp, piece, 2 * head_dim),),
        [
            Send(
                lambda i, o, z, f, p=p: i[0].at[:, flip(lax.rem(f, rep), p)],
                lambda i, o, z, f, p=p: o[0].at[p - 1],
                0,
                p,
            )
            for p in range(1, rep)
        ],
        6,
    )
    d_kv = lax.dynamic_index_in_dim(d_kv, lax.rem(f, rep), 1, keepdims=False)
    d_kv = (d_kv.astype(FLOAT) + jnp.sum(others.astype(FLOAT), axis=0)).astype(BF16)
    sends = [
        Send(lambda i, o, z, f, d=d: i[0].at[d], lambda i, o, z, f, d=d: o[0].at[d - 1], d, 0)
        for d in range(1, nsp)
    ]
    for s in range(plane_experts):
        sends.append(
            Send(
                lambda i, o, z, f, s=s: i[1].at[s],
                lambda i, o, z, f, s=s: o[1].at[:, s],
                0,
                s * parts,
            )
        )
    others, out_back = exchange(
        "key_grads_planes",
        10,
        (d_kv, weighted.reshape(plane_experts, nsp, cap, width)),
        ((nsp - 1, piece, 2 * head_dim), (nsp, plane_experts, cap, width)),
        sends,
        60,
    )
    out_blocks = combine(out_back)
    moe_sum = out_blocks[0].astype(FLOAT)
    for d in range(1, nsp):
        moe_sum = moe_sum + swap_z(out_blocks[d], d).astype(FLOAT)
    mixed = (mid_rows + moe_sum).astype(BF16)[None]
    d_kv = (d_kv[0].astype(FLOAT) + jnp.sum(others.astype(FLOAT), axis=0)).astype(BF16)
    d_kv, all_gate = lax.optimization_barrier((d_kv, all_gate))
    (d_kv,) = exchange(
        "key_grads_share",
        15,
        (d_kv,),
        ((rep, piece, 2 * head_dim),),
        [
            Send(lambda i, o, z, f: i[0], lambda i, o, z, f: o[0].at[lax.rem(f, rep)], 0, p)
            for p in range(rep)
        ],
        6,
    )
    d_kv = d_kv.reshape(seqs * rows, 2 * head_dim).astype(FLOAT)
    unused, q_pull = jax.vjp(prep_heads, q_lin, g_query)
    d_q_lin, d_q_gain = q_pull(dq.astype(FLOAT))
    unused, k_pull = jax.vjp(prep_heads, k_lin, g_key)
    d_k_lin, d_k_gain = k_pull(d_kv[:, :head_dim].reshape(seqs, rows, 1, head_dim))
    dq_b = d_q_lin.astype(BF16).reshape(seqs * rows, q_cols)
    dk_b = d_k_lin.astype(BF16).reshape(seqs * rows, head_dim)
    dv_b = d_kv[:, head_dim:].astype(BF16)
    d_qkv = jnp.concatenate([dq_b, dk_b, dv_b], axis=1)
    share = 1.0 / rep
    d_qkv_shared = jnp.concatenate([dq_b, dk_b * BF16(share), dv_b * BF16(share)], axis=1)
    d_w_qkv = contract_rows(xn_b, d_qkv).astype(BF16).reshape(nf, shard, qkv_cols)
    d_xn = pair_then_plane(contract_cols(d_qkv_shared, w_qkv), "input_sum", 13)
    unused, attn_pull = jax.vjp(rms_norm, x_rows, g_attn)
    d_x_norm, d_attn_gain = attn_pull(d_xn)
    grad_tokens = (d_mid + d_x_norm)[None]

    smalls = jnp.concatenate(
        [
            d_attn_gain.reshape(nf, shard),
            d_ffn_gain.reshape(nf, shard),
            d_q_gain.reshape(nf, head_dim // nf),
            (d_k_gain * share).reshape(nf, head_dim // nf),
            d_router.reshape(nf, shard * n_experts),
        ],
        axis=1,
    ).astype(BF16)
    small_size = smalls.shape[1]
    small_cols = pl.cdiv(small_size, kv_heads * head_dim) * kv_heads * head_dim // small_rows
    small_cols = pl.cdiv(small_cols, LANES) * LANES
    smalls = jnp.pad(smalls, ((0, 0), (0, small_rows * small_cols - small_size)))
    d_w_shard, small_shard = exchange(
        "head_grads_to_shards",
        12,
        (d_w_qkv, smalls.reshape(nf, small_rows, small_cols)),
        ((nf, shard, qkv_cols), (nf, small_rows, small_cols)),
        [
            Send(
                lambda i, o, z, f, m=m, w=w: i[w].at[flip(f, m)],
                lambda i, o, z, f, m=m, w=w: o[w].at[f],
                0,
                m,
            )
            for w in range(2)
            for m in range(nf)
        ],
        36,
    )
    d_wq = d_w_shard[:, :, :q_cols].transpose(1, 0, 2).reshape(shard, n_heads * head_dim)
    d_wkv = d_w_shard[::rep, :, q_cols:].reshape(kv_heads, shard, 2, head_dim)
    d_wkv = d_wkv.transpose(2, 1, 0, 3).reshape(2 * shard, kv_heads * head_dim)
    small_sum = jnp.sum(small_shard.astype(FLOAT), axis=0).astype(BF16)
    sum_out = lax.psum(d_wo.astype(BF16), "sp").astype(FLOAT)
    kv_cols = kv_heads * head_dim
    d_wkv = jnp.concatenate([d_wkv, small_sum.reshape(-1, kv_cols)], axis=0)
    sum_q, sum_kv = lax.psum((d_wq, d_wkv), "sp")
    sum_q = sum_q.astype(FLOAT)
    sum_kv = sum_kv.astype(FLOAT)
    small_sum = sum_kv[2 * shard :].reshape(-1)
    at = 0
    pieces = []
    for size in (shard, shard, head_dim // nf, head_dim // nf, shard * n_experts):
        pieces.append(small_sum[at : at + size])
        at += size
    return (
        mixed,
        grad_tokens,
        pieces[0],
        sum_q,
        sum_kv[:shard],
        sum_kv[shard : 2 * shard],
        pieces[2],
        pieces[3],
        sum_out,
        pieces[1],
        pieces[4].reshape(shard, n_experts),
        all_gate.astype(FLOAT),
        all_up.astype(FLOAT),
        grad_down,
    )


def solution(mesh):
    by_token = P("fsdp", "sp", None)
    by_row = P("fsdp", None)
    by_inner = P(None, "fsdp", None)
    in_specs = (
        by_token,
        by_token,
        P("fsdp"),
        by_row,
        by_row,
        by_row,
        P("fsdp"),
        P("fsdp"),
        by_row,
        P("fsdp"),
        by_row,
        by_inner,
        by_inner,
        by_inner,
        by_token,
    )
    out_specs = (
        by_token,
        by_token,
        P("fsdp"),
        by_row,
        by_row,
        by_row,
        P("fsdp"),
        P("fsdp"),
        by_row,
        P("fsdp"),
        by_row,
        by_inner,
        by_inner,
        by_inner,
    )
    return jax.shard_map(body, mesh=mesh, in_specs=in_specs, out_specs=out_specs, check_vma=False)
```

```python
import math
from typing import Callable, NamedTuple

import jax
import jax.numpy as jnp
from jax import lax
from jax.experimental import pallas as pl
from jax.experimental.pallas import tpu as pltpu
from jax.sharding import PartitionSpec as P

QUERY_HEADS = 32
KEY_VALUE_HEADS = 4
HEAD_SIZE = 128
CAP = 80
LANES = 128

EPS = 1e-06
THETA = 1000000.0
HIGH_PRECISION = lax.Precision.HIGHEST
BF16 = jnp.bfloat16
FLOAT = jnp.float32
MESH = pl.DeviceIdType.MESH


def rms_norm(values_in, gain_vec):
    return (
        values_in
        * lax.rsqrt(jnp.mean(values_in * values_in, axis=-1, keepdims=True) + EPS)
        * gain_vec
    )


def rotate(values_in, cosine, sine_part):
    half_dim = values_in.shape[-1] // 2
    first_half = values_in[..., :half_dim]
    second = values_in[..., half_dim:]
    return jnp.concatenate(
        [first_half * cosine - second * sine_part, second * cosine + first_half * sine_part],
        axis=-1,
    )


def contract_rows(left_mat, right_mat):
    return lax.dot_general(
        left_mat, right_mat, (((0,), (0,)), ((), ())), preferred_element_type=FLOAT
    )


def contract_cols(left_mat, right_mat):
    return lax.dot_general(
        left_mat, right_mat, (((1,), (1,)), ((), ())), preferred_element_type=FLOAT
    )


def matmul(left_mat, right_mat):
    return jnp.dot(left_mat, right_mat, preferred_element_type=FLOAT)


def flip(index, mask):
    bit = 1
    while bit <= mask:
        if mask & bit:
            index = index + bit * (1 - 2 * lax.rem(lax.div(index, bit), 2))
        bit *= 2
    return index


def cols(block, size):
    return pl.ds(pl.multiple_of(block * size, size), size)


class _ShapeOnly:
    def __init__(self, shape):
        self.shape = tuple(shape)

    @property
    def at(self):
        return self

    def __getitem__(self, index):
        index = index if isinstance(index, tuple) else (index,)
        shape = []
        for size, i in zip(self.shape, index):
            if isinstance(i, slice):
                shape.append(len(range(*i.indices(size))))
            elif hasattr(i, "size") and hasattr(i, "start"):
                shape.append(i.size)
        return _ShapeOnly(tuple(shape) + self.shape[len(index) :])


class Send(NamedTuple):
    src: Callable
    dst: Callable
    dz: int
    df: int
    after: int | None = None


def exchange(name, cid, arrays, out_shapes, sends, micros):
    n_in, n_out = len(arrays), len(out_shapes)
    peers = sorted({(s.dz, s.df) for s in sends} - {(0, 0)})
    stays = [k for k, s in enumerate(sends) if (s.dz, s.df) == (0, 0)]
    stay_shapes = []

    def probe(*refs):
        for k in stays:
            view = sends[k].src(refs, None, jnp.int32(0), jnp.int32(0))
            stay_shapes.append(view.shape)

    probe(*[_ShapeOnly(a.shape) for a in arrays])

    def kernel(*refs):
        ins, outs = refs[:n_in], refs[n_in : n_in + n_out]
        send_sems, recv_sems = refs[n_in + n_out : n_in + n_out + 2]
        bounce = dict(zip(stays, refs[n_in + n_out + 2 :]))
        z = lax.axis_index("sp")
        f = lax.axis_index("fsdp")
        barrier = pltpu.get_barrier_semaphore()
        for dz, df in peers:
            pl.semaphore_signal(
                barrier, inc=1, device_id=(flip(z, dz), flip(f, df)), device_id_type=MESH
            )
        pl.semaphore_wait(barrier, len(peers))
        copies = []
        for k, s in enumerate(sends):
            src = s.src(ins, outs, z, f)
            dst = s.dst(ins, outs, z, f)
            if (s.dz, s.df) == (0, 0):
                copies.append(
                    (
                        pltpu.make_async_copy(src, bounce[k], recv_sems.at[k]),
                        pltpu.make_async_copy(bounce[k], dst, send_sems.at[k]),
                    )
                )
            else:
                copies.append(
                    pltpu.make_async_remote_copy(
                        src_ref=src,
                        dst_ref=dst,
                        send_sem=send_sems.at[k],
                        recv_sem=recv_sems.at[k],
                        device_id=(flip(z, s.dz), flip(f, s.df)),
                        device_id_type=MESH,
                    )
                )
        arrived = set()

        def arrive(k):
            if k not in arrived:
                arrived.add(k)
                s = sends[k]
                if (s.dz, s.df) == (0, 0):
                    copies[k][1].wait()
                else:
                    copies[k].wait_recv()

        for k, s in enumerate(sends):
            if k in stays:
                copies[k][0].start()
            elif s.after is None:
                copies[k].start()
        for k in stays:
            copies[k][0].wait()
            copies[k][1].start()
        for k, s in enumerate(sends):
            if s.after is not None:
                arrive(s.after)
                copies[k].start()
        for k, s in enumerate(sends):
            if (s.dz, s.df) != (0, 0):
                copies[k].wait_send()
            arrive(k)

    result = pl.pallas_call(
        kernel,
        out_shape=[jax.ShapeDtypeStruct(shape, BF16) for shape in out_shapes],
        in_specs=[pl.BlockSpec(memory_space=pl.ANY)] * n_in,
        out_specs=[pl.BlockSpec(memory_space=pl.ANY)] * n_out,
        scratch_shapes=[
            pltpu.SemaphoreType.DMA((len(sends),)),
            pltpu.SemaphoreType.DMA((len(sends),)),
        ]
        + [pltpu.VMEM(shape, BF16) for shape in stay_shapes],
        compiler_params=pltpu.CompilerParams(
            collective_id=cid, has_side_effects=True, vmem_limit_bytes=32 * 1024 * 1024
        ),
        cost_estimate=pl.CostEstimate(
            flops=0, bytes_accessed=int(micros * 3.0e6), transcendentals=0
        ),
        name=name,
    )(*arrays)
    return result


def line_sum(cid, arrays, pieces, blocks):
    n = len(arrays)
    chunks = [
        (k, c * (a.shape[0] // p), a.shape[0] // p)
        for k, (a, p) in enumerate(zip(arrays, pieces))
        for c in range(p)
    ]
    far = blocks.shape[0] - 1

    def kernel(*refs):
        ins, blocks_ref = refs[:n], refs[n]
        outs, others_ref = refs[n + 1 : 2 * n + 1], refs[2 * n + 1]
        own, got, swapped = (refs[2 * n + 2 + n * i : 2 * n + 2 + n * (i + 1)] for i in range(3))
        load, store, in_s, in_r, swap_s, swap_r, back_s, back_r, far_s, far_r = refs[5 * n + 2 :]
        z = lax.axis_index("sp")
        f = lax.axis_index("fsdp")
        inner = jnp.logical_or(z == 1, z == 2)
        barrier = pltpu.get_barrier_semaphore()
        for d in range(1, far + 1):
            pl.semaphore_signal(barrier, inc=1, device_id=(flip(z, d), f), device_id_type=MESH)
        pl.semaphore_wait(barrier, far)

        def view(refs, c):
            k, start, size = chunks[c]
            return refs[k].at[pl.ds(start, size)]

        def remote(src, dst, send, recv, c, dz):
            return pltpu.make_async_remote_copy(
                src_ref=view(src, c),
                dst_ref=view(dst, c),
                send_sem=send.at[c],
                recv_sem=recv.at[c],
                device_id=(flip(z, dz), f),
                device_id_type=MESH,
            )

        loads = [
            pltpu.make_async_copy(view(ins, c), view(own, c), load.at[c])
            for c in range(len(chunks))
        ]
        stores = [
            pltpu.make_async_copy(view(got, c), view(outs, c), store.at[c])
            for c in range(len(chunks))
        ]
        far_copies = [
            pltpu.make_async_remote_copy(
                src_ref=blocks_ref.at[d],
                dst_ref=others_ref.at[d - 1],
                send_sem=far_s.at[d - 1],
                recv_sem=far_r.at[d - 1],
                device_id=(flip(z, d), f),
                device_id_type=MESH,
            )
            for d in range(1, far + 1)
        ]
        inwards = [remote(own, got, in_s, in_r, c, 1) for c in range(len(chunks))]
        swaps = [remote(own, swapped, swap_s, swap_r, c, 3) for c in range(len(chunks))]
        backs = [remote(got, got, back_s, back_r, c, 1) for c in range(len(chunks))]
        for copy in loads:
            copy.start()

        def add(left, right, to, c):
            k, start, size = chunks[c]
            step = 16

            def rows(i, carry):
                at = pl.ds(pl.multiple_of(start + i * step, step), step)
                total = left[k][at, :].astype(FLOAT) + right[k][at, :].astype(FLOAT)
                to[k][at, :] = total.astype(BF16)
                return carry

            lax.fori_loop(0, size // step, rows, 0)

        @pl.when(jnp.logical_not(inner))
        def _():
            for c in range(len(chunks)):
                loads[c].wait()
                inwards[c].start()
            for copy in far_copies:
                copy.start()
            for c in range(len(chunks)):
                backs[c].wait_recv()
                stores[c].start()
            for c in range(len(chunks)):
                inwards[c].wait_send()
                stores[c].wait()

        @pl.when(inner)
        def _():
            for copy in far_copies:
                copy.start()
            for c in range(len(chunks) + 1):
                if c < len(chunks):
                    loads[c].wait()
                    inwards[c].wait_recv()
                    add(own, got, own, c)
                    swaps[c].start()
                if c:
                    swaps[c - 1].wait_recv()
                    add(own, swapped, got, c - 1)
                    backs[c - 1].start()
                    stores[c - 1].start()
            for c in range(len(chunks)):
                swaps[c].wait_send()
                backs[c].wait_send()
                stores[c].wait()

        for copy in far_copies:
            copy.wait()

    hbm = pl.BlockSpec(memory_space=pl.ANY)
    buffers = [pltpu.VMEM(a.shape, BF16) for a in arrays]
    count = len(chunks)
    return pl.pallas_call(
        kernel,
        out_shape=[jax.ShapeDtypeStruct(a.shape, BF16) for a in arrays]
        + [jax.ShapeDtypeStruct((far,) + blocks.shape[1:], BF16)],
        in_specs=[hbm] * (n + 1),
        out_specs=[hbm] * (n + 1),
        scratch_shapes=buffers * 3
        + [pltpu.SemaphoreType.DMA((count,))] * 8
        + [pltpu.SemaphoreType.DMA((far,))] * 2,
        compiler_params=pltpu.CompilerParams(
            collective_id=cid, has_side_effects=True, vmem_limit_bytes=40 * 1024 * 1024
        ),
        cost_estimate=pl.CostEstimate(flops=0, bytes_accessed=int(4.0e8), transcendentals=0),
        name="line_sum",
    )(*arrays, blocks)


def body(
    tokens,
    expert_ids,
    attn_gain,
    query_weight,
    key_weight,
    value_weight,
    q_gain,
    k_gain,
    output_weight,
    ffn_gain,
    router_weight,
    w_gate,
    w_up,
    w_down,
    cotangent,
):
    nsp = lax.axis_size("sp")
    nf = lax.axis_size("fsdp")
    z = lax.axis_index("sp")
    f = lax.axis_index("fsdp")
    rows = tokens.shape[1]
    width = tokens.shape[2]
    shard = width // nf
    n_heads, kv_heads, head_dim = QUERY_HEADS, KEY_VALUE_HEADS, HEAD_SIZE
    my_heads = n_heads // nf
    rep = nf // kv_heads
    q_cols = my_heads * head_dim
    qkv_cols = q_cols + 2 * head_dim
    score_scale = 1.0 / math.sqrt(head_dim)
    n_experts = w_gate.shape[0]
    hidden_size = w_gate.shape[2]
    hid_shard = w_down.shape[1]
    plane_experts = n_experts // nsp
    parts = nf // plane_experts
    cap = CAP
    seqs = nf
    part = lax.rem(f, parts)
    place = lax.div(f, parts)
    expert = z * plane_experts + place

    def swap_f(block, mask):
        return lax.ppermute(block, "fsdp", [(i, i ^ mask) for i in range(nf)])

    def swap_z(block, mask):
        return lax.ppermute(block, "sp", [(i, i ^ mask) for i in range(nsp)])

    small = jnp.concatenate(
        [
            attn_gain.astype(BF16),
            ffn_gain.astype(BF16),
            q_gain.astype(BF16),
            k_gain.astype(BF16),
            router_weight.astype(BF16).reshape(-1),
        ]
    )
    small_rows = 16
    small = jnp.pad(small, (0, small_rows * width - small.shape[0])).reshape(small_rows, width)
    x_pay = jnp.concatenate([tokens[0], small], axis=0)
    pay_rows = rows + small_rows
    query_b = query_weight.astype(BF16)
    key_b = key_weight.astype(BF16)
    value_b = value_weight.astype(BF16)
    routes = expert_ids[0]
    expert_iota = jnp.arange(n_experts, dtype=jnp.int32)
    routed = jnp.any(routes[:, :, None] == expert_iota[None, None, :], axis=1)
    dy_pay = jnp.concatenate(
        [
            cotangent[0],
            routed.astype(BF16),
            jnp.zeros((rows, LANES - n_experts), BF16),
        ],
        axis=1,
    )
    wide = width + LANES

    def plane_cast(weight):
        return lax.dynamic_slice_in_dim(weight, z * plane_experts, plane_experts, 0).astype(BF16)

    gate_up_pay = jnp.stack([plane_cast(w_gate), plane_cast(w_up)], axis=1)
    down_pay = plane_cast(w_down)

    sends = []
    for m in range(0, nf, 2):
        sends.append(
            Send(
                lambda i, o, z, f, m=m: i[0],
                lambda i, o, z, f: o[0].at[f],
                0,
                m,
            )
        )
    for m in range(nf):
        sends.append(
            Send(
                lambda i, o, z, f, m=m: i[1].at[:, cols(flip(f, m), q_cols)],
                lambda i, o, z, f: o[1].at[cols(f, shard), pl.ds(0, q_cols)],
                0,
                m,
            )
        )
    for m in range(0, nf, rep):
        for w in range(2):
            sends.append(
                Send(
                    lambda i, o, z, f, m=m, w=w: i[2 + w].at[
                        :, cols(lax.div(flip(f, m), rep), head_dim)
                    ],
                    lambda i, o, z, f, w=w: o[1].at[
                        cols(f, shard), pl.ds(q_cols + w * head_dim, head_dim)
                    ],
                    0,
                    m,
                )
            )
            for p in range(1, rep):
                view = lambda i, o, z, f, m=m, w=w: o[1].at[
                    cols(flip(f, m), shard), pl.ds(q_cols + w * head_dim, head_dim)
                ]
                if m == 0:
                    sends.append(
                        Send(
                            lambda i, o, z, f, w=w: i[2 + w].at[:, cols(lax.div(f, rep), head_dim)],
                            view,
                            0,
                            p,
                        )
                    )
                else:
                    sends.append(Send(view, view, 0, p, len(sends) - p))
    for m in range(nsp):
        sends.append(
            Send(lambda i, o, z, f: i[4], lambda i, o, z, f, m=m: o[2].at[m], m, 0)
        )
    for m in range(0, nf, 2):
        if m == 0:
            sends.append(
                Send(lambda i, o, z, f: i[0], lambda i, o, z, f: o[0].at[f], 0, 1)
            )
        else:
            sends.append(
                Send(
                    lambda i, o, z, f, m=m: o[0].at[flip(f, m)],
                    lambda i, o, z, f, m=m: o[0].at[flip(f, m)],
                    0,
                    1,
                    m // 2,
                )
            )
    x_all, w_qkv, dy_z = exchange(
        "gather_inputs",
        0,
        (x_pay, query_b, key_b, value_b, dy_pay),
        ((nf, pay_rows, width), (width, qkv_cols), (nsp, rows, wide)),
        sends,
        65,
    )

    x_all, gate_up_pay, down_pay = lax.optimization_barrier((x_all, gate_up_pay, down_pay))
    weight_pieces = []
    for pay in (gate_up_pay, down_pay):
        for s in range(plane_experts):
            block = lax.dynamic_index_in_dim(pay, flip(place, s), 0, keepdims=False)
            weight_pieces.append(swap_f(block, s * parts) if s else block)

    small_all = x_all[:, rows:, :].reshape(nf, small_rows * width)
    at = 0
    pieces = []
    for size in (shard, shard, head_dim // nf, head_dim // nf, shard * n_experts):
        pieces.append(small_all[:, at : at + size])
        at += size
    g_attn = pieces[0].reshape(width).astype(FLOAT)
    g_ffn = pieces[1].reshape(width).astype(FLOAT)
    g_query = pieces[2].reshape(head_dim).astype(FLOAT)
    g_key = pieces[3].reshape(head_dim).astype(FLOAT)
    wr_b = pieces[4].reshape(width, n_experts)

    xn_b = (
        rms_norm(x_all[:, :rows, :].astype(FLOAT), g_attn).astype(BF16).reshape(seqs * rows, width)
    )
    qkv_lin = matmul(xn_b, w_qkv)
    q_lin = qkv_lin[:, :q_cols].reshape(seqs, rows, my_heads, head_dim)
    k_lin = qkv_lin[:, q_cols : q_cols + head_dim].reshape(seqs, rows, 1, head_dim)
    v_b = qkv_lin[:, q_cols + head_dim :].astype(BF16)
    half_dim = head_dim // 2
    inverse_freq = THETA ** (-(jnp.arange(half_dim, dtype=FLOAT) * 2.0 / head_dim))
    positions = (z * rows + jnp.arange(rows, dtype=jnp.int32)).astype(FLOAT)
    angles = positions[:, None] * inverse_freq[None, :]
    cosine = jnp.cos(angles)[None, :, None, :]
    sine_part = jnp.sin(angles)[None, :, None, :]

    def prep_heads(linear, gain_vec):
        return rotate(rms_norm(linear, gain_vec), cosine, sine_part)

    q_b = prep_heads(q_lin, g_query).astype(BF16)
    k_b = prep_heads(k_lin, g_key).astype(BF16).reshape(seqs * rows, head_dim)

    kv_pay = jnp.concatenate([k_b, v_b], axis=1)
    piece = seqs * rows // rep
    sends = []
    for d in range(nsp):
        sends.append(
            Send(
                lambda i, o, z, f: i[0].at[pl.ds(lax.rem(f, rep) * piece, piece)],
                lambda i, o, z, f, d=d: o[0].at[d, pl.ds(lax.rem(f, rep) * piece, piece)],
                d,
                0,
            )
        )
    for d in range(nsp):
        for p in range(1, rep):
            sends.append(
                Send(
                    lambda i, o, z, f, d=d: o[0].at[d, pl.ds(lax.rem(f, rep) * piece, piece)],
                    lambda i, o, z, f, d=d: o[0].at[d, pl.ds(lax.rem(f, rep) * piece, piece)],
                    0,
                    p,
                    d,
                )
            )
    (kv_z,) = exchange(
        "gather_keys", 1, (kv_pay,), ((nsp, seqs * rows, 2 * head_dim),), sends, 24
    )
    kv_seq = kv_z.reshape(nsp, seqs, rows, 2 * head_dim).transpose(1, 0, 2, 3)
    kv_seq = kv_seq.reshape(seqs, nsp * rows, 2 * head_dim)
    keys = kv_seq[:, :, :head_dim]
    values = kv_seq[:, :, head_dim:]

    q_rows = q_b.transpose(0, 2, 1, 3)
    plane_of = jnp.bitwise_xor(jnp.arange(nsp, dtype=jnp.int32), z)
    key_pos = (plane_of[:, None] * rows + jnp.arange(rows, dtype=jnp.int32)[None, :]).reshape(-1)
    query_pos = z * rows + jnp.arange(rows, dtype=jnp.int32)
    causal = key_pos[None, :] <= query_pos[:, None]
    scores = (
        jnp.einsum("nhqd,nkd->nhqk", q_rows, keys, preferred_element_type=FLOAT) * score_scale
    )
    scores = jnp.where(causal[None, None], scores, -1e30)
    row_top = jnp.max(scores, axis=3, keepdims=True)
    expo = jnp.exp(scores - row_top)
    probs = (expo / jnp.sum(expo, axis=3, keepdims=True)).astype(BF16)
    o_rows = jnp.einsum("nhqk,nkd->nqhd", probs, values, preferred_element_type=FLOAT)
    o_mat = o_rows.astype(BF16).reshape(seqs * rows, q_cols)
    wo_b = output_weight.astype(BF16)

    def pair_then_plane(partial, name, cid, more=(), more_shapes=(), more_sends=()):
        split = partial.astype(BF16).reshape(nf // 2, 2, rows, width)
        (other,) = exchange(
            name + "_pair",
            cid,
            (split,),
            ((nf // 2, rows, width),),
            [Send(lambda i, o, z, f: i[0].at[:, 1 - lax.rem(f, 2)], lambda i, o, z, f: o[0], 0, 1)],
            8,
        )
        own = lax.dynamic_index_in_dim(split, lax.rem(f, 2), 1, keepdims=False)
        summed = (own.astype(FLOAT) + other.astype(FLOAT)).astype(BF16)
        sends = [
            Send(
                lambda i, o, z, f, j=j: i[0].at[flip(lax.div(f, 2), j)],
                lambda i, o, z, f, j=j: o[0].at[j],
                0,
                2 * j,
            )
            for j in range(nf // 2)
        ]
        blocks, *rest = exchange(
            name + "_plane",
            cid + 1,
            (summed, *more),
            ((nf // 2, rows, width), *more_shapes),
            sends + list(more_sends),
            27,
        )
        return jnp.sum(blocks.astype(FLOAT), axis=0), rest

    sends = []
    for w in range(2):
        for s in range(plane_experts):
            for p in range(parts):
                at = (lambda s=s: lambda f: (slice(None), flip(f, s * parts)))()
                if w:
                    at = (lambda s=s: lambda f: (flip(f, s * parts),))()
                sends.append(
                    Send(
                        lambda i, o, z, f, k=1 + w * plane_experts + s: i[k],
                        lambda i, o, z, f, w=w, at=at: o[1 + w].at[at(f)],
                        0,
                        p,
                    )
                )
    branch, (gate_up_all, down_all) = pair_then_plane(
        matmul(o_mat, wo_b),
        "out_sum",
        3,
        weight_pieces,
        ((2, nf, shard, hidden_size), (nf, hid_shard, width)),
        sends,
    )
    wg_b = gate_up_all[0].reshape(width, hidden_size)
    wu_b = gate_up_all[1].reshape(width, hidden_size)
    wd_b = down_all.reshape(hidden_size, width)
    x_rows = tokens[0].astype(FLOAT)
    mid_rows = x_rows + branch
    hn_b = rms_norm(mid_rows, g_ffn).astype(BF16)
    logits = matmul(hn_b, wr_b)
    logits = jnp.where(routed, logits, -1e30)
    expo = jnp.where(routed, jnp.exp(logits - jnp.max(logits, axis=1, keepdims=True)), 0.0)
    gates = expo / jnp.sum(expo, axis=1, keepdims=True)

    def two_parts(exact):
        high = exact.astype(BF16)
        return high, (exact - high.astype(FLOAT)).astype(BF16)

    own_experts = z * plane_experts + jnp.bitwise_xor(
        place, jnp.arange(plane_experts, dtype=jnp.int32)
    )
    own_hot = (expert_iota[:, None] == own_experts[None, :]).astype(FLOAT)
    routed_z = lax.dot_general(
        own_hot,
        dy_z[:, :, width : width + n_experts].astype(FLOAT),
        (((0,), (2,)), ((), ())),
        preferred_element_type=FLOAT,
    ).transpose(1, 0, 2)
    earlier = jnp.triu(jnp.ones((rows, rows), FLOAT), 1)
    rank = jnp.dot(
        routed_z.reshape(nsp * plane_experts, rows), earlier, preferred_element_type=FLOAT
    ).reshape(nsp, plane_experts, rows)
    rank = rank * routed_z + (routed_z - 1.0)
    pick = (
        rank[:, :, None, :] == jnp.arange(cap, dtype=FLOAT)[None, None, :, None]
    ).astype(BF16)
    pick = pick.reshape(nsp, plane_experts * cap, rows)

    def select(source):
        picked = jnp.einsum("drt,dtc->drc", pick, source, preferred_element_type=FLOAT)
        return picked.astype(BF16).reshape(nsp, plane_experts, cap, source.shape[2])

    def to_experts(which):
        return [
            Send(
                lambda i, o, z, f, s=s: i[which].at[:, s],
                lambda i, o, z, f, s=s: o[which].at[s],
                0,
                s * parts,
            )
            for s in range(plane_experts)
        ]

    gate_high, gate_low = two_parts(gates)
    gate_lanes = jnp.concatenate(
        [gate_high, gate_low, jnp.zeros((rows, LANES - 2 * n_experts), BF16)], axis=1
    )
    hn_z, gate_z, dy_rows = exchange(
        "hidden_planes",
        5,
        (hn_b, gate_lanes, select(dy_z[:, :, :width])),
        ((nsp, rows, width), (nsp, rows, LANES), (plane_experts, nsp, cap, width)),
        [
            Send(lambda i, o, z, f, w=w: i[w], lambda i, o, z, f, d=d, w=w: o[w].at[d], d, 0)
            for w in range(2)
            for d in range(nsp)
        ]
        + to_experts(2),
        58,
    )
    hn_rows, gate_rows = exchange(
        "rows_to_experts",
        6,
        (select(hn_z), select(gate_z)),
        ((plane_experts, nsp, cap, width), (plane_experts, nsp, cap, LANES)),
        to_experts(0) + to_experts(1),
        60,
    )

    n_rows = plane_experts * nsp * cap
    hn_in = hn_rows.reshape(n_rows, width)
    dy_in = dy_rows.reshape(n_rows, width)
    hot = (jnp.arange(n_experts, dtype=jnp.int32) == expert).astype(FLOAT)
    tail = gate_rows.reshape(n_rows, LANES)[:, : 2 * n_experts].astype(FLOAT)
    row_gate = jnp.sum(
        (tail[:, :n_experts] + tail[:, n_experts:]) * hot[None, :], axis=1, keepdims=True
    )
    gate_pre = matmul(hn_in, wg_b)
    up_pre = matmul(hn_in, wu_b)
    sigma = jax.nn.sigmoid(gate_pre)
    act_f = gate_pre * sigma
    hidden = (act_f * up_pre).astype(BF16)
    dy_f = dy_in.astype(FLOAT)
    d_result = (row_gate * dy_f).astype(BF16)

    def by_shard(full, inner):
        return full.astype(BF16).reshape((plane_experts, parts) + inner)

    def pair_total(own, others):
        total = lax.dynamic_index_in_dim(own, part, 1, keepdims=False).astype(FLOAT)
        for other in others:
            total = total + other.astype(FLOAT)
        return total.astype(BF16)

    d_down = by_shard(contract_rows(hidden, d_result), (hid_shard, width))
    d_down = pair_total(
        d_down,
        [
            swap_f(lax.dynamic_index_in_dim(d_down, flip(part, p), 1, keepdims=False), p)
            for p in range(1, parts)
        ],
    )
    d_down = jnp.stack(
        [
            swap_f(
                lax.dynamic_index_in_dim(d_down, flip(place, s), 0, keepdims=False), s * parts
            )
            if s
            else lax.dynamic_index_in_dim(d_down, place, 0, keepdims=False)
            for s in range(plane_experts)
        ]
    )
    in_order = jnp.bitwise_xor(jnp.arange(plane_experts, dtype=jnp.int32), place)
    all_down = lax.all_gather(jnp.take(d_down, in_order, axis=0, mode="clip"), "sp")
    result = matmul(hidden, wd_b)
    row_dgate = jnp.sum(result * dy_f, axis=1, keepdims=True)
    weighted = (row_gate * result).astype(BF16)
    d_hidden = contract_cols(d_result, wd_b)
    d_gate_pre = (d_hidden * up_pre * sigma * (1.0 + gate_pre * (1.0 - sigma))).astype(BF16)
    d_up_pre = (d_hidden * act_f).astype(BF16)
    d_in = (contract_cols(d_gate_pre, wg_b) + contract_cols(d_up_pre, wu_b)).astype(BF16)
    dgate_high, dgate_low = two_parts(row_dgate * hot[None, :])
    dgate_lanes = jnp.concatenate(
        [dgate_high, dgate_low, jnp.zeros((n_rows, LANES - 2 * n_experts), BF16)], axis=1
    )

    d_weights = (
        by_shard(contract_rows(hn_in, d_gate_pre), (shard, hidden_size)),
        by_shard(contract_rows(hn_in, d_up_pre), (shard, hidden_size)),
    )
    shard_shapes = [w.shape[2:] for w in d_weights]

    sends = []
    for w in range(2):
        for s in range(plane_experts):
            sends.append(
                Send(
                    lambda i, o, z, f, s=s, w=w: i[w].at[s],
                    lambda i, o, z, f, s=s, w=w: o[w].at[:, s],
                    0,
                    s * parts,
                )
            )
    for w in range(2):
        for p in range(1, parts):
            sends.append(
                Send(
                    lambda i, o, z, f, p=p, w=w: i[2 + w].at[:, flip(lax.rem(f, parts), p)],
                    lambda i, o, z, f, p=p, w=w: o[2 + w].at[p - 1],
                    0,
                    p,
                )
            )
    d_back, dgate_back, *d_others = exchange(
        "rows_from_experts",
        7,
        (
            d_in.reshape(plane_experts, nsp, cap, width),
            dgate_lanes.reshape(plane_experts, nsp, cap, LANES),
        )
        + d_weights,
        [(nsp, plane_experts, cap, width), (nsp, plane_experts, cap, LANES)]
        + [(parts - 1, plane_experts) + tuple(shape) for shape in shard_shapes],
        sends,
        70,
    )

    def combine(returned):
        flat = returned.reshape(nsp, plane_experts * cap, returned.shape[3])
        return jnp.einsum("drt,drc->dtc", pick, flat, preferred_element_type=FLOAT).astype(BF16)

    summed = [
        pair_total(own, [others[p] for p in range(parts - 1)])
        for own, others in zip(d_weights, d_others)
    ]
    sends = [
        Send(lambda i, o, z, f, d=d, w=w: i[w].at[d], lambda i, o, z, f, d=d, w=w: o[w].at[d], d, 0)
        for w in range(2)
        for d in range(nsp)
    ]
    for w in range(2, 4):
        for s in range(plane_experts):
            sends.append(
                Send(
                    lambda i, o, z, f, s=s, w=w: i[w].at[flip(lax.div(f, parts), s)],
                    lambda i, o, z, f, s=s, w=w: o[2].at[w - 2, lax.div(f, parts)],
                    0,
                    s * parts,
                )
            )
    d_home, dgate_home, shards = exchange(
        "hidden_grads_home",
        8,
        (combine(d_back), combine(dgate_back), *summed),
        ((nsp, rows, width), (nsp, rows, LANES), (2, plane_experts, shard, hidden_size)),
        sends,
        58,
    )
    all_gate_up = lax.all_gather(shards, "sp")
    d_home = jnp.sum(d_home.astype(FLOAT), axis=0)
    tail = jnp.sum(dgate_home.astype(FLOAT), axis=0)
    d_gates = tail[:, :n_experts] + tail[:, n_experts : 2 * n_experts]
    d_logits = gates * (d_gates - jnp.sum(gates * d_gates, axis=1, keepdims=True))
    d_router = jnp.dot(hn_b.astype(FLOAT).T, d_logits, precision=HIGH_PRECISION)
    d_hn = d_home + jnp.dot(d_logits, wr_b.astype(FLOAT).T, precision=HIGH_PRECISION)
    grad_out = cotangent[0].astype(FLOAT)
    unused, ffn_pull = jax.vjp(rms_norm, mid_rows, g_ffn)
    d_mid_norm, d_ffn_gain = ffn_pull(d_hn)
    d_mid = grad_out + d_mid_norm

    d_attn_b = d_mid.astype(BF16)
    d_attn_b, all_down = lax.optimization_barrier((d_attn_b, all_down))
    grad_down = all_down.astype(FLOAT).reshape(n_experts, hid_shard, width)
    sends = [
        Send(lambda i, o, z, f: i[0], lambda i, o, z, f: o[0].at[f], 0, m)
        for m in range(0, nf, 2)
    ]
    for m in range(0, nf, 2):
        if m == 0:
            sends.append(Send(lambda i, o, z, f: i[0], lambda i, o, z, f: o[0].at[f], 0, 1))
        else:
            sends.append(
                Send(
                    lambda i, o, z, f, m=m: o[0].at[flip(f, m)],
                    lambda i, o, z, f, m=m: o[0].at[flip(f, m)],
                    0,
                    1,
                    m // 2,
                )
            )
    (da_all,) = exchange("gather_grads", 9, (d_attn_b,), ((nf, rows, width),), sends, 30)
    da_all = da_all.reshape(seqs * rows, width)
    d_wo = contract_rows(o_mat, da_all)
    d_o = contract_cols(da_all, wo_b).astype(BF16).reshape(seqs, rows, my_heads, head_dim)
    d_o = d_o.transpose(0, 2, 1, 3)
    d_val = jnp.einsum("nhqk,nhqd->nkd", probs, d_o, preferred_element_type=FLOAT)
    d_probs = jnp.einsum("nhqd,nkd->nhqk", d_o, values, preferred_element_type=FLOAT)
    probs_f = probs.astype(FLOAT)
    d_scores = (
        probs_f * (d_probs - jnp.sum(probs_f * d_probs, axis=3, keepdims=True))
    ).astype(BF16)
    dq = (
        jnp.einsum("nhqk,nkd->nqhd", d_scores, keys, preferred_element_type=FLOAT) * score_scale
    ).astype(BF16)
    d_key = (
        jnp.einsum("nhqk,nhqd->nkd", d_scores, q_rows, preferred_element_type=FLOAT) * score_scale
    )
    d_kv = jnp.concatenate([d_key, d_val], axis=2).astype(BF16)
    d_kv = d_kv.reshape(seqs, nsp, rows, 2 * head_dim).transpose(1, 0, 2, 3)
    d_kv = d_kv.reshape(nsp, seqs * rows, 2 * head_dim)
    d_kv = d_kv.reshape(nsp, rep, piece, 2 * head_dim)
    (others,) = exchange(
        "key_grads_group",
        11,
        (d_kv,),
        ((rep - 1, nsp, piece, 2 * head_dim),),
        [
            Send(
                lambda i, o, z, f, p=p: i[0].at[:, flip(lax.rem(f, rep), p)],
                lambda i, o, z, f, p=p: o[0].at[p - 1],
                0,
                p,
            )
            for p in range(1, rep)
        ],
        6,
    )
    d_kv = lax.dynamic_index_in_dim(d_kv, lax.rem(f, rep), 1, keepdims=False)
    d_kv = (d_kv.astype(FLOAT) + jnp.sum(others.astype(FLOAT), axis=0)).astype(BF16)
    sends = [
        Send(lambda i, o, z, f, d=d: i[0].at[d], lambda i, o, z, f, d=d: o[0].at[d - 1], d, 0)
        for d in range(1, nsp)
    ]
    for s in range(plane_experts):
        sends.append(
            Send(
                lambda i, o, z, f, s=s: i[1].at[s],
                lambda i, o, z, f, s=s: o[1].at[:, s],
                0,
                s * parts,
            )
        )
    others, out_back = exchange(
        "key_grads_planes",
        10,
        (d_kv, weighted.reshape(plane_experts, nsp, cap, width)),
        ((nsp - 1, piece, 2 * head_dim), (nsp, plane_experts, cap, width)),
        sends,
        60,
    )
    out_blocks = combine(out_back)
    d_kv = (d_kv[0].astype(FLOAT) + jnp.sum(others.astype(FLOAT), axis=0)).astype(BF16)
    (d_kv,) = exchange(
        "key_grads_share",
        15,
        (d_kv,),
        ((rep, piece, 2 * head_dim),),
        [
            Send(lambda i, o, z, f: i[0], lambda i, o, z, f: o[0].at[lax.rem(f, rep)], 0, p)
            for p in range(rep)
        ],
        6,
    )
    d_kv = d_kv.reshape(seqs * rows, 2 * head_dim).astype(FLOAT)
    unused, q_pull = jax.vjp(prep_heads, q_lin, g_query)
    d_q_lin, d_q_gain = q_pull(dq.astype(FLOAT))
    unused, k_pull = jax.vjp(prep_heads, k_lin, g_key)
    d_k_lin, d_k_gain = k_pull(d_kv[:, :head_dim].reshape(seqs, rows, 1, head_dim))
    dq_b = d_q_lin.astype(BF16).reshape(seqs * rows, q_cols)
    dk_b = d_k_lin.astype(BF16).reshape(seqs * rows, head_dim)
    dv_b = d_kv[:, head_dim:].astype(BF16)
    d_qkv = jnp.concatenate([dq_b, dk_b, dv_b], axis=1)
    share = 1.0 / rep
    d_qkv_shared = jnp.concatenate([dq_b, dk_b * BF16(share), dv_b * BF16(share)], axis=1)
    d_w_qkv = contract_rows(xn_b, d_qkv).astype(BF16)
    d_xn, unused = pair_then_plane(contract_cols(d_qkv_shared, w_qkv), "input_sum", 13)
    unused, attn_pull = jax.vjp(rms_norm, x_rows, g_attn)
    d_x_norm, d_attn_gain = attn_pull(d_xn)
    grad_tokens = (d_mid + d_x_norm)[None]

    smalls = jnp.concatenate(
        [
            d_attn_gain.reshape(nf, shard),
            d_ffn_gain.reshape(nf, shard),
            d_q_gain.reshape(nf, head_dim // nf),
            (d_k_gain * share).reshape(nf, head_dim // nf),
            d_router.reshape(nf, shard * n_experts),
        ],
        axis=1,
    ).astype(BF16)
    small_size = smalls.shape[1]
    small_cols = pl.cdiv(small_size, kv_heads * head_dim) * kv_heads * head_dim // small_rows
    small_cols = pl.cdiv(small_cols, LANES) * LANES
    smalls = jnp.pad(smalls, ((0, 0), (0, small_rows * small_cols - small_size)))
    kv_cols = kv_heads * head_dim
    sends = []
    for m in range(nf):
        sends.append(
            Send(
                lambda i, o, z, f, m=m: i[0].at[cols(flip(f, m), shard), pl.ds(0, q_cols)],
                lambda i, o, z, f: o[0].at[:, cols(f, q_cols)],
                0,
                m,
            )
        )
        sends.append(
            Send(lambda i, o, z, f, m=m: i[1].at[flip(f, m)], lambda i, o, z, f: o[2].at[f], 0, m)
        )
    for m in range(0, nf, rep):
        for w in range(2):
            sends.append(
                Send(
                    lambda i, o, z, f, m=m, w=w: i[0].at[
                        cols(flip(f, m), shard), pl.ds(q_cols + w * head_dim, head_dim)
                    ],
                    lambda i, o, z, f, w=w: o[1].at[
                        pl.ds(w * shard, shard), cols(lax.div(f, rep), head_dim)
                    ],
                    0,
                    m,
                )
            )
    d_wq, d_wkv, small_shard = exchange(
        "head_grads_to_shards",
        12,
        (d_w_qkv, smalls.reshape(nf, small_rows, small_cols)),
        (
            (shard, n_heads * head_dim),
            (2 * shard, kv_cols),
            (nf, small_rows, small_cols),
        ),
        sends,
        36,
    )
    small_sum = jnp.sum(small_shard.astype(FLOAT), axis=0).astype(BF16)
    if nsp == 4:
        sum_q, sum_out, sum_kv, small_sum, out_others = line_sum(
            16, (d_wq, d_wo.astype(BF16), d_wkv, small_sum), (4, 4, 1, 1), out_blocks
        )
        out_others = [out_others[d] for d in range(nsp - 1)]
    else:
        sum_q, sum_out, sum_kv, small_sum = lax.psum(
            (d_wq, d_wo.astype(BF16), d_wkv, small_sum), "sp"
        )
        out_others = [swap_z(out_blocks[d], d) for d in range(1, nsp)]
    moe_sum = out_blocks[0].astype(FLOAT)
    for block in out_others:
        moe_sum = moe_sum + block.astype(FLOAT)
    mixed = (mid_rows + moe_sum).astype(BF16)[None]
    sum_out = sum_out.astype(FLOAT)
    sum_q = sum_q.astype(FLOAT)
    sum_kv = sum_kv.astype(FLOAT)
    small_sum = small_sum.astype(FLOAT).reshape(-1)
    at = 0
    pieces = []
    for size in (shard, shard, head_dim // nf, head_dim // nf, shard * n_experts):
        pieces.append(small_sum[at : at + size])
        at += size
    return (
        mixed,
        grad_tokens,
        pieces[0],
        sum_q,
        sum_kv[:shard],
        sum_kv[shard : 2 * shard],
        pieces[2],
        pieces[3],
        sum_out,
        pieces[1],
        pieces[4].reshape(shard, n_experts),
        all_gate_up[:, 0].astype(FLOAT).reshape(n_experts, shard, hidden_size),
        all_gate_up[:, 1].astype(FLOAT).reshape(n_experts, shard, hidden_size),
        grad_down,
    )


def solution(mesh):
    by_token = P("fsdp", "sp", None)
    by_row = P("fsdp", None)
    by_inner = P(None, "fsdp", None)
    in_specs = (
        by_token,
        by_token,
        P("fsdp"),
        by_row,
        by_row,
        by_row,
        P("fsdp"),
        P("fsdp"),
        by_row,
        P("fsdp"),
        by_row,
        by_inner,
        by_inner,
        by_inner,
        by_token,
    )
    out_specs = (
        by_token,
        by_token,
        P("fsdp"),
        by_row,
        by_row,
        by_row,
        P("fsdp"),
        P("fsdp"),
        by_row,
        P("fsdp"),
        by_row,
        by_inner,
        by_inner,
        by_inner,
    )
    return jax.shard_map(body, mesh=mesh, in_specs=in_specs, out_specs=out_specs, check_vma=False)
```

```python
import math
from typing import Callable, NamedTuple

import jax
import jax.numpy as jnp
from jax import lax
from jax.experimental import pallas as pl
from jax.experimental.pallas import tpu as pltpu
from jax.sharding import PartitionSpec as P

QUERY_HEADS = 32
KEY_VALUE_HEADS = 4
HEAD_SIZE = 128
CAP = 80
LANES = 128

EPS = 1e-06
THETA = 1000000.0
HIGH_PRECISION = lax.Precision.HIGHEST
BF16 = jnp.bfloat16
FLOAT = jnp.float32
MESH = pl.DeviceIdType.MESH


def rms_norm(values_in, gain_vec):
    return (
        values_in
        * lax.rsqrt(jnp.mean(values_in * values_in, axis=-1, keepdims=True) + EPS)
        * gain_vec
    )


def rotate(values_in, cosine, sine_part):
    half_dim = values_in.shape[-1] // 2
    first_half = values_in[..., :half_dim]
    second = values_in[..., half_dim:]
    return jnp.concatenate(
        [first_half * cosine - second * sine_part, second * cosine + first_half * sine_part],
        axis=-1,
    )


def contract_rows(left_mat, right_mat):
    return lax.dot_general(
        left_mat, right_mat, (((0,), (0,)), ((), ())), preferred_element_type=FLOAT
    )


def contract_cols(left_mat, right_mat):
    return lax.dot_general(
        left_mat, right_mat, (((1,), (1,)), ((), ())), preferred_element_type=FLOAT
    )


def matmul(left_mat, right_mat):
    return jnp.dot(left_mat, right_mat, preferred_element_type=FLOAT)


def flip(index, mask):
    bit = 1
    while bit <= mask:
        if mask & bit:
            index = index + bit * (1 - 2 * lax.rem(lax.div(index, bit), 2))
        bit *= 2
    return index


def cols(block, size):
    return pl.ds(pl.multiple_of(block * size, size), size)


class _ShapeOnly:
    def __init__(self, shape):
        self.shape = tuple(shape)

    @property
    def at(self):
        return self

    def __getitem__(self, index):
        index = index if isinstance(index, tuple) else (index,)
        shape = []
        for size, i in zip(self.shape, index):
            if isinstance(i, slice):
                shape.append(len(range(*i.indices(size))))
            elif hasattr(i, "size") and hasattr(i, "start"):
                shape.append(i.size)
        return _ShapeOnly(tuple(shape) + self.shape[len(index) :])


class Send(NamedTuple):
    src: Callable
    dst: Callable
    dz: int
    df: int
    after: int | None = None


def exchange(name, cid, arrays, out_shapes, sends, micros):
    n_in, n_out = len(arrays), len(out_shapes)
    peers = sorted({(s.dz, s.df) for s in sends} - {(0, 0)})
    stays = [k for k, s in enumerate(sends) if (s.dz, s.df) == (0, 0)]
    stay_shapes = []

    def probe(*refs):
        for k in stays:
            view = sends[k].src(refs, None, jnp.int32(0), jnp.int32(0))
            stay_shapes.append(view.shape)

    probe(*[_ShapeOnly(a.shape) for a in arrays])

    def kernel(*refs):
        ins, outs = refs[:n_in], refs[n_in : n_in + n_out]
        send_sems, recv_sems = refs[n_in + n_out : n_in + n_out + 2]
        bounce = dict(zip(stays, refs[n_in + n_out + 2 :]))
        z = lax.axis_index("sp")
        f = lax.axis_index("fsdp")
        barrier = pltpu.get_barrier_semaphore()
        for dz, df in peers:
            pl.semaphore_signal(
                barrier, inc=1, device_id=(flip(z, dz), flip(f, df)), device_id_type=MESH
            )
        pl.semaphore_wait(barrier, len(peers))
        copies = []
        for k, s in enumerate(sends):
            src = s.src(ins, outs, z, f)
            dst = s.dst(ins, outs, z, f)
            if (s.dz, s.df) == (0, 0):
                copies.append(
                    (
                        pltpu.make_async_copy(src, bounce[k], recv_sems.at[k]),
                        pltpu.make_async_copy(bounce[k], dst, send_sems.at[k]),
                    )
                )
            else:
                copies.append(
                    pltpu.make_async_remote_copy(
                        src_ref=src,
                        dst_ref=dst,
                        send_sem=send_sems.at[k],
                        recv_sem=recv_sems.at[k],
                        device_id=(flip(z, s.dz), flip(f, s.df)),
                        device_id_type=MESH,
                    )
                )
        arrived = set()

        def arrive(k):
            if k not in arrived:
                arrived.add(k)
                s = sends[k]
                if (s.dz, s.df) == (0, 0):
                    copies[k][1].wait()
                else:
                    copies[k].wait_recv()

        for k, s in enumerate(sends):
            if k in stays:
                copies[k][0].start()
            elif s.after is None:
                copies[k].start()
        for k in stays:
            copies[k][0].wait()
            copies[k][1].start()
        for k, s in enumerate(sends):
            if s.after is not None:
                arrive(s.after)
                copies[k].start()
        for k, s in enumerate(sends):
            if (s.dz, s.df) != (0, 0):
                copies[k].wait_send()
            arrive(k)

    result = pl.pallas_call(
        kernel,
        out_shape=[jax.ShapeDtypeStruct(shape, BF16) for shape in out_shapes],
        in_specs=[pl.BlockSpec(memory_space=pl.ANY)] * n_in,
        out_specs=[pl.BlockSpec(memory_space=pl.ANY)] * n_out,
        scratch_shapes=[
            pltpu.SemaphoreType.DMA((len(sends),)),
            pltpu.SemaphoreType.DMA((len(sends),)),
        ]
        + [pltpu.VMEM(shape, BF16) for shape in stay_shapes],
        compiler_params=pltpu.CompilerParams(
            collective_id=cid, has_side_effects=True, vmem_limit_bytes=32 * 1024 * 1024
        ),
        cost_estimate=pl.CostEstimate(
            flops=0, bytes_accessed=int(micros * 3.0e6), transcendentals=0
        ),
        name=name,
    )(*arrays)
    return result


def rows_to_experts(cid, tokens, lanes, pick, plane_experts, parts):
    planes, picked, count = pick.shape
    cap = picked // plane_experts
    arrays = (tokens, lanes)
    widths = [a.shape[1] for a in arrays]
    order = [0, 1, 3, 2] if planes == 4 else list(range(planes))
    early = 2 if planes == 4 else planes - 1
    step = 512

    def kernel(tokens_ref, lanes_ref, pick_ref, rows_ref, lane_rows_ref, *scratch):
        here, chosen = scratch[:2], scratch[2:4]
        z_send, z_recv, row_send, row_recv = scratch[4:]
        ins, outs = (tokens_ref, lanes_ref), (rows_ref, lane_rows_ref)
        z = lax.axis_index("sp")
        f = lax.axis_index("fsdp")
        barrier = pltpu.get_barrier_semaphore()
        for d in range(1, planes):
            pl.semaphore_signal(barrier, inc=1, device_id=(flip(z, d), f), device_id_type=MESH)
        for s in range(1, plane_experts):
            pl.semaphore_signal(
                barrier, inc=1, device_id=(z, flip(f, s * parts)), device_id_type=MESH
            )
        pl.semaphore_wait(barrier, planes + plane_experts - 2)

        def across(d, w):
            if d == 0:
                return pltpu.make_async_copy(ins[w], here[w].at[0], z_recv.at[w])
            return pltpu.make_async_remote_copy(
                src_ref=ins[w],
                dst_ref=here[w].at[d],
                send_sem=z_send.at[2 * d + w],
                recv_sem=z_recv.at[2 * d + w],
                device_id=(flip(z, d), f),
                device_id_type=MESH,
            )

        def onward(d, s, w):
            src = chosen[w].at[d, pl.ds(s * cap, cap)]
            dst = outs[w].at[s, d]
            k = (d * plane_experts + s) * 2 + w
            if s == 0:
                return pltpu.make_async_copy(src, dst, row_recv.at[k])
            return pltpu.make_async_remote_copy(
                src_ref=src,
                dst_ref=dst,
                send_sem=row_send.at[k],
                recv_sem=row_recv.at[k],
                device_id=(z, flip(f, s * parts)),
                device_id_type=MESH,
            )

        for d in order[: early + 1]:
            for w in range(2):
                across(d, w).start()
        for turn, d in enumerate(order):
            for w in range(2):
                if d == 0:
                    across(d, w).wait()
                else:
                    across(d, w).wait_recv()
            if turn == 1:
                for later in order[early + 1 :]:
                    for w in range(2):
                        across(later, w).start()

            def columns(i, carry):
                at = pl.ds(pl.multiple_of(i * step, step), step)
                chosen[0][d, :, at] = jnp.dot(
                    pick_ref[d], here[0][d, :, at], preferred_element_type=FLOAT
                ).astype(BF16)
                return carry

            lax.fori_loop(0, widths[0] // step, columns, 0)
            chosen[1][d] = jnp.dot(
                pick_ref[d], here[1][d], preferred_element_type=FLOAT
            ).astype(BF16)
            for s in range(plane_experts):
                for w in range(2):
                    onward(d, s, w).start()
        for d in range(planes):
            for w in range(2):
                if d:
                    across(d, w).wait_send()
                for s in range(plane_experts):
                    onward(d, s, w).wait()

    hbm = pl.BlockSpec(memory_space=pl.ANY)
    sems = planes * plane_experts * 2
    return pl.pallas_call(
        kernel,
        out_shape=[
            jax.ShapeDtypeStruct((plane_experts, planes, cap, width), BF16) for width in widths
        ],
        in_specs=[hbm, hbm, pl.BlockSpec(memory_space=pltpu.VMEM)],
        out_specs=[hbm, hbm],
        scratch_shapes=[pltpu.VMEM((planes, count, width), BF16) for width in widths]
        + [pltpu.VMEM((planes, picked, width), BF16) for width in widths]
        + [pltpu.SemaphoreType.DMA((2 * planes,))] * 2
        + [pltpu.SemaphoreType.DMA((sems,))] * 2,
        compiler_params=pltpu.CompilerParams(
            collective_id=cid, has_side_effects=True, vmem_limit_bytes=40 * 1024 * 1024
        ),
        cost_estimate=pl.CostEstimate(flops=0, bytes_accessed=int(2.1e8), transcendentals=0),
        name="rows_to_experts",
    )(tokens, lanes, pick)


def rows_from_experts(cid, rows_in, lanes_in, pick, weights):
    planes, picked, count = pick.shape
    plane_experts, _, cap, _ = rows_in.shape
    parts = weights[0].shape[1]
    inner_shape = weights[0].shape[2:]
    widths = (rows_in.shape[3], lanes_in.shape[3])
    order = [2, 3, 1, 0] if planes == 4 else list(range(planes - 1, -1, -1))
    step = 512

    def kernel(rows_ref, lanes_ref, pick_ref, first_ref, second_ref, *rest):
        outs, shards_ref = rest[:2], rest[2]
        back, partial, own, others = rest[3:5], rest[5:7], rest[7], rest[8]
        row_send, row_recv, z_send, z_recv, pair_send, pair_recv, load, w_send, w_recv = rest[9:]
        ins, weight_refs = (rows_ref, lanes_ref), (first_ref, second_ref)
        z = lax.axis_index("sp")
        f = lax.axis_index("fsdp")
        part = lax.rem(f, parts)
        place = lax.div(f, parts)
        barrier = pltpu.get_barrier_semaphore()
        for d in range(1, planes):
            pl.semaphore_signal(barrier, inc=1, device_id=(flip(z, d), f), device_id_type=MESH)
        near = list(range(1, parts)) + [s * parts for s in range(1, plane_experts)]
        for m in near:
            pl.semaphore_signal(barrier, inc=1, device_id=(z, flip(f, m)), device_id_type=MESH)
        pl.semaphore_wait(barrier, planes - 1 + len(near))

        def pair(w, p):
            k = w * (parts - 1) + p - 1
            return pltpu.make_async_remote_copy(
                src_ref=weight_refs[w].at[:, flip(part, p)],
                dst_ref=others.at[p - 1, w],
                send_sem=pair_send.at[k],
                recv_sem=pair_recv.at[k],
                device_id=(z, flip(f, p)),
                device_id_type=MESH,
            )

        def load_own(w):
            return pltpu.make_async_copy(weight_refs[w].at[:, part], own.at[w], load.at[w])

        def home(d, s, w):
            src = ins[w].at[s, d]
            dst = back[w].at[d, pl.ds(s * cap, cap)]
            k = (d * plane_experts + s) * 2 + w
            if s == 0:
                return pltpu.make_async_copy(src, dst, row_recv.at[k])
            return pltpu.make_async_remote_copy(
                src_ref=src,
                dst_ref=dst,
                send_sem=row_send.at[k],
                recv_sem=row_recv.at[k],
                device_id=(z, flip(f, s * parts)),
                device_id_type=MESH,
            )

        def across(d, w):
            src, dst = partial[w].at[d], outs[w].at[d]
            if d == 0:
                return pltpu.make_async_copy(src, dst, z_recv.at[w])
            return pltpu.make_async_remote_copy(
                src_ref=src,
                dst_ref=dst,
                send_sem=z_send.at[2 * d + w],
                recv_sem=z_recv.at[2 * d + w],
                device_id=(flip(z, d), f),
                device_id_type=MESH,
            )

        def to_shard(s, w):
            src, dst = own.at[w, flip(place, s)], shards_ref.at[w, place]
            if s == 0:
                return pltpu.make_async_copy(src, dst, w_recv.at[w])
            return pltpu.make_async_remote_copy(
                src_ref=src,
                dst_ref=dst,
                send_sem=w_send.at[2 * s + w],
                recv_sem=w_recv.at[2 * s + w],
                device_id=(z, flip(f, s * parts)),
                device_id_type=MESH,
            )

        for w in range(2):
            load_own(w).start()
            for p in range(1, parts):
                pair(w, p).start()
        for d in order:
            for s in range(plane_experts):
                for w in range(2):
                    home(d, s, w).start()
        for w in range(2):
            load_own(w).wait()
            for p in range(1, parts):
                pair(w, p).wait()

            def add(i, carry):
                e = lax.div(i, inner_shape[0] // 16)
                at = pl.ds(pl.multiple_of(lax.rem(i, inner_shape[0] // 16) * 16, 16), 16)
                total = own[w, e, at, :].astype(FLOAT)
                for p in range(parts - 1):
                    total = total + others[p, w, e, at, :].astype(FLOAT)
                own[w, e, at, :] = total.astype(BF16)
                return carry

            lax.fori_loop(0, plane_experts * (inner_shape[0] // 16), add, 0)
        for turn, d in enumerate(order):
            for s in range(plane_experts):
                for w in range(2):
                    home(d, s, w).wait()
            if turn == planes - 2:
                for s in range(plane_experts):
                    for w in range(2):
                        to_shard(s, w).start()

            def columns(i, carry):
                at = pl.ds(pl.multiple_of(i * step, step), step)
                partial[0][d, :, at] = contract_rows(pick_ref[d], back[0][d, :, at]).astype(BF16)
                return carry

            lax.fori_loop(0, widths[0] // step, columns, 0)
            partial[1][d] = contract_rows(pick_ref[d], back[1][d]).astype(BF16)
            for w in range(2):
                across(d, w).start()
        for d in range(planes):
            for w in range(2):
                across(d, w).wait()
        for s in range(plane_experts):
            for w in range(2):
                to_shard(s, w).wait()

    hbm = pl.BlockSpec(memory_space=pl.ANY)
    dma = pltpu.SemaphoreType.DMA
    row_count = planes * plane_experts * 2
    return pl.pallas_call(
        kernel,
        out_shape=[jax.ShapeDtypeStruct((planes, count, width), BF16) for width in widths]
        + [jax.ShapeDtypeStruct((2, plane_experts) + inner_shape, BF16)],
        in_specs=[hbm, hbm, pl.BlockSpec(memory_space=pltpu.VMEM), hbm, hbm],
        out_specs=[hbm] * 3,
        scratch_shapes=[pltpu.VMEM((planes, picked, width), BF16) for width in widths]
        + [pltpu.VMEM((planes, count, width), BF16) for width in widths]
        + [
            pltpu.VMEM((2, plane_experts) + inner_shape, BF16),
            pltpu.VMEM((parts - 1, 2, plane_experts) + inner_shape, BF16),
        ]
        + [dma((row_count,))] * 2
        + [dma((2 * planes,))] * 2
        + [dma((2 * (parts - 1),))] * 2
        + [dma((2,))]
        + [dma((2 * plane_experts,))] * 2,
        compiler_params=pltpu.CompilerParams(
            collective_id=cid, has_side_effects=True, vmem_limit_bytes=48 * 1024 * 1024
        ),
        cost_estimate=pl.CostEstimate(flops=0, bytes_accessed=int(2.7e8), transcendentals=0),
        name="rows_from_experts",
    )(rows_in, lanes_in, pick, *weights)


def line_sum(cid, arrays, pieces, blocks):
    n = len(arrays)
    chunks = [
        (k, c * (a.shape[0] // p), a.shape[0] // p)
        for k, (a, p) in enumerate(zip(arrays, pieces))
        for c in range(p)
    ]
    far = blocks.shape[0] - 1

    def kernel(*refs):
        ins, blocks_ref = refs[:n], refs[n]
        outs, others_ref = refs[n + 1 : 2 * n + 1], refs[2 * n + 1]
        own, got, swapped = (refs[2 * n + 2 + n * i : 2 * n + 2 + n * (i + 1)] for i in range(3))
        load, store, in_s, in_r, swap_s, swap_r, back_s, back_r, far_s, far_r = refs[5 * n + 2 :]
        z = lax.axis_index("sp")
        f = lax.axis_index("fsdp")
        inner = jnp.logical_or(z == 1, z == 2)
        barrier = pltpu.get_barrier_semaphore()
        for d in range(1, far + 1):
            pl.semaphore_signal(barrier, inc=1, device_id=(flip(z, d), f), device_id_type=MESH)
        pl.semaphore_wait(barrier, far)

        def view(refs, c):
            k, start, size = chunks[c]
            return refs[k].at[pl.ds(start, size)]

        def remote(src, dst, send, recv, c, dz):
            return pltpu.make_async_remote_copy(
                src_ref=view(src, c),
                dst_ref=view(dst, c),
                send_sem=send.at[c],
                recv_sem=recv.at[c],
                device_id=(flip(z, dz), f),
                device_id_type=MESH,
            )

        loads = [
            pltpu.make_async_copy(view(ins, c), view(own, c), load.at[c])
            for c in range(len(chunks))
        ]
        stores = [
            pltpu.make_async_copy(view(got, c), view(outs, c), store.at[c])
            for c in range(len(chunks))
        ]
        far_copies = [
            pltpu.make_async_remote_copy(
                src_ref=blocks_ref.at[d],
                dst_ref=others_ref.at[d - 1],
                send_sem=far_s.at[d - 1],
                recv_sem=far_r.at[d - 1],
                device_id=(flip(z, d), f),
                device_id_type=MESH,
            )
            for d in range(1, far + 1)
        ]
        inwards = [remote(own, got, in_s, in_r, c, 1) for c in range(len(chunks))]
        swaps = [remote(own, swapped, swap_s, swap_r, c, 3) for c in range(len(chunks))]
        backs = [remote(got, got, back_s, back_r, c, 1) for c in range(len(chunks))]
        for copy in loads:
            copy.start()

        def add(left, right, to, c):
            k, start, size = chunks[c]
            step = 16

            def rows(i, carry):
                at = pl.ds(pl.multiple_of(start + i * step, step), step)
                total = left[k][at, :].astype(FLOAT) + right[k][at, :].astype(FLOAT)
                to[k][at, :] = total.astype(BF16)
                return carry

            lax.fori_loop(0, size // step, rows, 0)

        @pl.when(jnp.logical_not(inner))
        def _():
            for c in range(len(chunks)):
                loads[c].wait()
                inwards[c].start()
            for copy in far_copies:
                copy.start()
            for c in range(len(chunks)):
                backs[c].wait_recv()
                stores[c].start()
            for c in range(len(chunks)):
                inwards[c].wait_send()
                stores[c].wait()

        @pl.when(inner)
        def _():
            for copy in far_copies:
                copy.start()
            for c in range(len(chunks) + 1):
                if c < len(chunks):
                    loads[c].wait()
                    inwards[c].wait_recv()
                    add(own, got, own, c)
                    swaps[c].start()
                if c:
                    swaps[c - 1].wait_recv()
                    add(own, swapped, got, c - 1)
                    backs[c - 1].start()
                    stores[c - 1].start()
            for c in range(len(chunks)):
                swaps[c].wait_send()
                backs[c].wait_send()
                stores[c].wait()

        for copy in far_copies:
            copy.wait()

    hbm = pl.BlockSpec(memory_space=pl.ANY)
    buffers = [pltpu.VMEM(a.shape, BF16) for a in arrays]
    count = len(chunks)
    return pl.pallas_call(
        kernel,
        out_shape=[jax.ShapeDtypeStruct(a.shape, BF16) for a in arrays]
        + [jax.ShapeDtypeStruct((far,) + blocks.shape[1:], BF16)],
        in_specs=[hbm] * (n + 1),
        out_specs=[hbm] * (n + 1),
        scratch_shapes=buffers * 3
        + [pltpu.SemaphoreType.DMA((count,))] * 8
        + [pltpu.SemaphoreType.DMA((far,))] * 2,
        compiler_params=pltpu.CompilerParams(
            collective_id=cid, has_side_effects=True, vmem_limit_bytes=40 * 1024 * 1024
        ),
        cost_estimate=pl.CostEstimate(flops=0, bytes_accessed=int(4.0e8), transcendentals=0),
        name="line_sum",
    )(*arrays, blocks)


def body(
    tokens,
    expert_ids,
    attn_gain,
    query_weight,
    key_weight,
    value_weight,
    q_gain,
    k_gain,
    output_weight,
    ffn_gain,
    router_weight,
    w_gate,
    w_up,
    w_down,
    cotangent,
):
    nsp = lax.axis_size("sp")
    nf = lax.axis_size("fsdp")
    z = lax.axis_index("sp")
    f = lax.axis_index("fsdp")
    rows = tokens.shape[1]
    width = tokens.shape[2]
    shard = width // nf
    n_heads, kv_heads, head_dim = QUERY_HEADS, KEY_VALUE_HEADS, HEAD_SIZE
    my_heads = n_heads // nf
    rep = nf // kv_heads
    q_cols = my_heads * head_dim
    qkv_cols = q_cols + 2 * head_dim
    score_scale = 1.0 / math.sqrt(head_dim)
    n_experts = w_gate.shape[0]
    hidden_size = w_gate.shape[2]
    hid_shard = w_down.shape[1]
    plane_experts = n_experts // nsp
    parts = nf // plane_experts
    cap = CAP
    seqs = nf
    part = lax.rem(f, parts)
    place = lax.div(f, parts)
    expert = z * plane_experts + place

    def swap_f(block, mask):
        return lax.ppermute(block, "fsdp", [(i, i ^ mask) for i in range(nf)])

    def swap_z(block, mask):
        return lax.ppermute(block, "sp", [(i, i ^ mask) for i in range(nsp)])

    small = jnp.concatenate(
        [
            attn_gain.astype(BF16),
            ffn_gain.astype(BF16),
            q_gain.astype(BF16),
            k_gain.astype(BF16),
            router_weight.astype(BF16).reshape(-1),
        ]
    )
    small_rows = 16
    small = jnp.pad(small, (0, small_rows * width - small.shape[0])).reshape(small_rows, width)
    x_pay = jnp.concatenate([tokens[0], small], axis=0)
    pay_rows = rows + small_rows
    query_b = query_weight.astype(BF16)
    key_b = key_weight.astype(BF16)
    value_b = value_weight.astype(BF16)
    routes = expert_ids[0]
    expert_iota = jnp.arange(n_experts, dtype=jnp.int32)
    routed = jnp.any(routes[:, :, None] == expert_iota[None, None, :], axis=1)
    dy_pay = jnp.concatenate(
        [
            cotangent[0],
            routed.astype(BF16),
            jnp.zeros((rows, LANES - n_experts), BF16),
        ],
        axis=1,
    )
    wide = width + LANES

    def plane_cast(weight):
        return lax.dynamic_slice_in_dim(weight, z * plane_experts, plane_experts, 0).astype(BF16)

    gate_up_pay = jnp.stack([plane_cast(w_gate), plane_cast(w_up)], axis=1)
    down_pay = plane_cast(w_down)

    sends = []
    for m in range(0, nf, 2):
        sends.append(
            Send(
                lambda i, o, z, f, m=m: i[0],
                lambda i, o, z, f: o[0].at[f],
                0,
                m,
            )
        )
    for m in range(nf):
        sends.append(
            Send(
                lambda i, o, z, f, m=m: i[1].at[:, cols(flip(f, m), q_cols)],
                lambda i, o, z, f: o[1].at[cols(f, shard), pl.ds(0, q_cols)],
                0,
                m,
            )
        )
    for m in range(0, nf, rep):
        for w in range(2):
            sends.append(
                Send(
                    lambda i, o, z, f, m=m, w=w: i[2 + w].at[
                        :, cols(lax.div(flip(f, m), rep), head_dim)
                    ],
                    lambda i, o, z, f, w=w: o[1].at[
                        cols(f, shard), pl.ds(q_cols + w * head_dim, head_dim)
                    ],
                    0,
                    m,
                )
            )
            for p in range(1, rep):
                view = lambda i, o, z, f, m=m, w=w: o[1].at[
                    cols(flip(f, m), shard), pl.ds(q_cols + w * head_dim, head_dim)
                ]
                if m == 0:
                    sends.append(
                        Send(
                            lambda i, o, z, f, w=w: i[2 + w].at[:, cols(lax.div(f, rep), head_dim)],
                            view,
                            0,
                            p,
                        )
                    )
                else:
                    sends.append(Send(view, view, 0, p, len(sends) - p))
    for m in range(nsp):
        sends.append(
            Send(lambda i, o, z, f: i[4], lambda i, o, z, f, m=m: o[2].at[m], m, 0)
        )
    for m in range(0, nf, 2):
        if m == 0:
            sends.append(
                Send(lambda i, o, z, f: i[0], lambda i, o, z, f: o[0].at[f], 0, 1)
            )
        else:
            sends.append(
                Send(
                    lambda i, o, z, f, m=m: o[0].at[flip(f, m)],
                    lambda i, o, z, f, m=m: o[0].at[flip(f, m)],
                    0,
                    1,
                    m // 2,
                )
            )
    x_all, w_qkv, dy_z = exchange(
        "gather_inputs",
        0,
        (x_pay, query_b, key_b, value_b, dy_pay),
        ((nf, pay_rows, width), (width, qkv_cols), (nsp, rows, wide)),
        sends,
        65,
    )

    own_experts = z * plane_experts + jnp.bitwise_xor(
        place, jnp.arange(plane_experts, dtype=jnp.int32)
    )
    own_hot = (expert_iota[:, None] == own_experts[None, :]).astype(FLOAT)
    routed_z = lax.dot_general(
        own_hot,
        dy_z[:, :, width : width + n_experts].astype(FLOAT),
        (((0,), (2,)), ((), ())),
        preferred_element_type=FLOAT,
    ).transpose(1, 0, 2)
    earlier = jnp.triu(jnp.ones((rows, rows), FLOAT), 1)
    rank = jnp.dot(
        routed_z.reshape(nsp * plane_experts, rows), earlier, preferred_element_type=FLOAT
    ).reshape(nsp, plane_experts, rows)
    rank = rank * routed_z + (routed_z - 1.0)
    pick = (
        rank[:, :, None, :] == jnp.arange(cap, dtype=FLOAT)[None, None, :, None]
    ).astype(BF16)
    pick = pick.reshape(nsp, plane_experts * cap, rows)

    def select(source):
        picked = jnp.einsum("drt,dtc->drc", pick, source, preferred_element_type=FLOAT)
        return picked.astype(BF16).reshape(nsp, plane_experts, cap, source.shape[2])

    x_all, gate_up_pay, down_pay = lax.optimization_barrier((x_all, gate_up_pay, down_pay))
    dy_pick = select(dy_z[:, :, :width])
    gate_up_pieces, down_pieces = [], []
    for s in range(plane_experts):
        gate_up_pieces.append(
            lax.dynamic_index_in_dim(gate_up_pay, flip(place, s), 0, keepdims=False)
        )
        down_pieces.append(lax.dynamic_index_in_dim(down_pay, flip(place, s), 0, keepdims=False))
    dy_pieces = [dy_pick[:, 0].reshape(nsp * cap, width)]
    for s in range(1, plane_experts):
        parts_of = [down_pieces[s], dy_pick[:, s].reshape(nsp * cap, width)]
        if s == plane_experts - 1:
            parts_of.append(gate_up_pieces[s].reshape(-1, width))
        else:
            gate_up_pieces[s] = swap_f(gate_up_pieces[s], s * parts)
        down_pieces[s] = swap_f(jnp.concatenate(parts_of, axis=0), s * parts)
        dy_pieces.append(down_pieces[s][hid_shard : hid_shard + nsp * cap])
        if s == plane_experts - 1:
            gate_up_pieces[s] = down_pieces[s][hid_shard + nsp * cap :].reshape(
                2, shard, hidden_size
            )
    dy_in = jnp.concatenate(dy_pieces, axis=0)

    small_all = x_all[:, rows:, :].reshape(nf, small_rows * width)
    at = 0
    pieces = []
    for size in (shard, shard, head_dim // nf, head_dim // nf, shard * n_experts):
        pieces.append(small_all[:, at : at + size])
        at += size
    g_attn = pieces[0].reshape(width).astype(FLOAT)
    g_ffn = pieces[1].reshape(width).astype(FLOAT)
    g_query = pieces[2].reshape(head_dim).astype(FLOAT)
    g_key = pieces[3].reshape(head_dim).astype(FLOAT)
    wr_b = pieces[4].reshape(width, n_experts)

    xn_b = (
        rms_norm(x_all[:, :rows, :].astype(FLOAT), g_attn).astype(BF16).reshape(seqs * rows, width)
    )
    qkv_lin = matmul(xn_b, w_qkv)
    q_lin = qkv_lin[:, :q_cols].reshape(seqs, rows, my_heads, head_dim)
    k_lin = qkv_lin[:, q_cols : q_cols + head_dim].reshape(seqs, rows, 1, head_dim)
    v_b = qkv_lin[:, q_cols + head_dim :].astype(BF16)
    half_dim = head_dim // 2
    inverse_freq = THETA ** (-(jnp.arange(half_dim, dtype=FLOAT) * 2.0 / head_dim))
    positions = (z * rows + jnp.arange(rows, dtype=jnp.int32)).astype(FLOAT)
    angles = positions[:, None] * inverse_freq[None, :]
    cosine = jnp.cos(angles)[None, :, None, :]
    sine_part = jnp.sin(angles)[None, :, None, :]

    def prep_heads(linear, gain_vec):
        return rotate(rms_norm(linear, gain_vec), cosine, sine_part)

    q_b = prep_heads(q_lin, g_query).astype(BF16)
    k_b = prep_heads(k_lin, g_key).astype(BF16).reshape(seqs * rows, head_dim)

    kv_pay = jnp.concatenate([k_b, v_b], axis=1)
    piece = seqs * rows // rep
    sends = []
    for d in range(nsp):
        sends.append(
            Send(
                lambda i, o, z, f: i[0].at[pl.ds(lax.rem(f, rep) * piece, piece)],
                lambda i, o, z, f, d=d: o[0].at[d, pl.ds(lax.rem(f, rep) * piece, piece)],
                d,
                0,
            )
        )
    for d in range(nsp):
        for p in range(1, rep):
            sends.append(
                Send(
                    lambda i, o, z, f, d=d: o[0].at[d, pl.ds(lax.rem(f, rep) * piece, piece)],
                    lambda i, o, z, f, d=d: o[0].at[d, pl.ds(lax.rem(f, rep) * piece, piece)],
                    0,
                    p,
                    d,
                )
            )
    (kv_z,) = exchange(
        "gather_keys", 1, (kv_pay,), ((nsp, seqs * rows, 2 * head_dim),), sends, 24
    )
    kv_seq = kv_z.reshape(nsp, seqs, rows, 2 * head_dim).transpose(1, 0, 2, 3)
    kv_seq = kv_seq.reshape(seqs, nsp * rows, 2 * head_dim)
    keys = kv_seq[:, :, :head_dim]
    values = kv_seq[:, :, head_dim:]

    q_rows = q_b.transpose(0, 2, 1, 3)
    plane_of = jnp.bitwise_xor(jnp.arange(nsp, dtype=jnp.int32), z)
    key_pos = (plane_of[:, None] * rows + jnp.arange(rows, dtype=jnp.int32)[None, :]).reshape(-1)
    query_pos = z * rows + jnp.arange(rows, dtype=jnp.int32)
    causal = key_pos[None, :] <= query_pos[:, None]
    scores = (
        jnp.einsum("nhqd,nkd->nhqk", q_rows, keys, preferred_element_type=FLOAT) * score_scale
    )
    scores = jnp.where(causal[None, None], scores, -1e30)
    row_top = jnp.max(scores, axis=3, keepdims=True)
    expo = jnp.exp(scores - row_top)
    probs = (expo / jnp.sum(expo, axis=3, keepdims=True)).astype(BF16)
    o_rows = jnp.einsum("nhqk,nkd->nqhd", probs, values, preferred_element_type=FLOAT)
    o_mat = o_rows.astype(BF16).reshape(seqs * rows, q_cols)
    wo_b = output_weight.astype(BF16)

    def pair_then_plane(partial, name, cid, more=(), more_shapes=(), more_sends=()):
        split = partial.astype(BF16).reshape(nf // 2, 2, rows, width)
        (other,) = exchange(
            name + "_pair",
            cid,
            (split,),
            ((nf // 2, rows, width),),
            [Send(lambda i, o, z, f: i[0].at[:, 1 - lax.rem(f, 2)], lambda i, o, z, f: o[0], 0, 1)],
            8,
        )
        own = lax.dynamic_index_in_dim(split, lax.rem(f, 2), 1, keepdims=False)
        summed = (own.astype(FLOAT) + other.astype(FLOAT)).astype(BF16)
        sends = [
            Send(
                lambda i, o, z, f, j=j: i[0].at[flip(lax.div(f, 2), j)],
                lambda i, o, z, f, j=j: o[0].at[j],
                0,
                2 * j,
            )
            for j in range(nf // 2)
        ]
        blocks, *rest = exchange(
            name + "_plane",
            cid + 1,
            (summed, *more),
            ((nf // 2, rows, width), *more_shapes),
            sends + list(more_sends),
            27,
        )
        return jnp.sum(blocks.astype(FLOAT), axis=0), rest

    sends = []
    for w in range(2):
        for s in range(plane_experts):
            for p in range(parts):
                at = (lambda s=s: lambda f: (slice(None), flip(f, s * parts)))()
                if w:
                    at = (lambda s=s: lambda f: (flip(f, s * parts),))()
                sends.append(
                    Send(
                        lambda i, o, z, f, w=w, k=1 + w * plane_experts + s: (
                            i[k].at[pl.ds(0, hid_shard)] if w else i[k]
                        ),
                        lambda i, o, z, f, w=w, at=at: o[1 + w].at[at(f)],
                        0,
                        p,
                    )
                )
    branch, (gate_up_all, down_all) = pair_then_plane(
        matmul(o_mat, wo_b),
        "out_sum",
        3,
        gate_up_pieces + down_pieces,
        ((2, nf, shard, hidden_size), (nf, hid_shard, width)),
        sends,
    )
    wg_b = gate_up_all[0].reshape(width, hidden_size)
    wu_b = gate_up_all[1].reshape(width, hidden_size)
    wd_b = down_all.reshape(hidden_size, width)
    x_rows = tokens[0].astype(FLOAT)
    mid_rows = x_rows + branch
    hn_b = rms_norm(mid_rows, g_ffn).astype(BF16)
    logits = matmul(hn_b, wr_b)
    logits = jnp.where(routed, logits, -1e30)
    expo = jnp.where(routed, jnp.exp(logits - jnp.max(logits, axis=1, keepdims=True)), 0.0)
    gates = expo / jnp.sum(expo, axis=1, keepdims=True)

    def two_parts(exact):
        high = exact.astype(BF16)
        return high, (exact - high.astype(FLOAT)).astype(BF16)

    gate_high, gate_low = two_parts(gates)
    gate_lanes = jnp.concatenate(
        [gate_high, gate_low, jnp.zeros((rows, LANES - 2 * n_experts), BF16)], axis=1
    )
    hn_rows, gate_rows = rows_to_experts(5, hn_b, gate_lanes, pick, plane_experts, parts)

    n_rows = plane_experts * nsp * cap
    hn_in = hn_rows.reshape(n_rows, width)
    hot = (jnp.arange(n_experts, dtype=jnp.int32) == expert).astype(FLOAT)
    tail = gate_rows.reshape(n_rows, LANES)[:, : 2 * n_experts].astype(FLOAT)
    row_gate = jnp.sum(
        (tail[:, :n_experts] + tail[:, n_experts:]) * hot[None, :], axis=1, keepdims=True
    )
    gate_pre = matmul(hn_in, wg_b)
    up_pre = matmul(hn_in, wu_b)
    sigma = jax.nn.sigmoid(gate_pre)
    act_f = gate_pre * sigma
    hidden = (act_f * up_pre).astype(BF16)
    dy_f = dy_in.astype(FLOAT)
    d_result = (row_gate * dy_f).astype(BF16)

    def by_shard(full, inner):
        return full.astype(BF16).reshape((plane_experts, parts) + inner)

    def pair_total(own, others):
        total = lax.dynamic_index_in_dim(own, part, 1, keepdims=False).astype(FLOAT)
        for other in others:
            total = total + other.astype(FLOAT)
        return total.astype(BF16)

    d_down = by_shard(contract_rows(hidden, d_result), (hid_shard, width))
    d_down = pair_total(
        d_down,
        [
            swap_f(lax.dynamic_index_in_dim(d_down, flip(part, p), 1, keepdims=False), p)
            for p in range(1, parts)
        ],
    )
    d_down = [
        swap_f(lax.dynamic_index_in_dim(d_down, flip(place, s), 0, keepdims=False), s * parts)
        if s
        else lax.dynamic_index_in_dim(d_down, place, 0, keepdims=False)
        for s in range(plane_experts)
    ]
    result = matmul(hidden, wd_b)
    row_dgate = jnp.sum(result * dy_f, axis=1, keepdims=True)
    weighted = (row_gate * result).astype(BF16)
    d_hidden = contract_cols(d_result, wd_b)
    d_gate_pre = (d_hidden * up_pre * sigma * (1.0 + gate_pre * (1.0 - sigma))).astype(BF16)
    d_up_pre = (d_hidden * act_f).astype(BF16)
    d_down, d_gate_pre, d_up_pre = lax.optimization_barrier((d_down, d_gate_pre, d_up_pre))
    in_order = jnp.bitwise_xor(jnp.arange(plane_experts, dtype=jnp.int32), place)
    d_down = jnp.take(jnp.stack(d_down), in_order, axis=0, mode="clip")
    all_down = lax.all_gather(d_down, "sp")
    d_in = (contract_cols(d_gate_pre, wg_b) + contract_cols(d_up_pre, wu_b)).astype(BF16)
    dgate_high, dgate_low = two_parts(row_dgate * hot[None, :])
    dgate_lanes = jnp.concatenate(
        [dgate_high, dgate_low, jnp.zeros((n_rows, LANES - 2 * n_experts), BF16)], axis=1
    )

    d_weights = (
        by_shard(contract_rows(hn_in, d_gate_pre), (shard, hidden_size)),
        by_shard(contract_rows(hn_in, d_up_pre), (shard, hidden_size)),
    )

    d_home, dgate_home, shards = rows_from_experts(
        7,
        d_in.reshape(plane_experts, nsp, cap, width),
        dgate_lanes.reshape(plane_experts, nsp, cap, LANES),
        pick,
        d_weights,
    )

    def combine(returned):
        flat = returned.reshape(nsp, plane_experts * cap, returned.shape[3])
        return jnp.einsum("drt,drc->dtc", pick, flat, preferred_element_type=FLOAT).astype(BF16)

    all_gate_up = lax.all_gather(shards, "sp")
    d_home = jnp.sum(d_home.astype(FLOAT), axis=0)
    tail = jnp.sum(dgate_home.astype(FLOAT), axis=0)
    d_gates = tail[:, :n_experts] + tail[:, n_experts : 2 * n_experts]
    d_logits = gates * (d_gates - jnp.sum(gates * d_gates, axis=1, keepdims=True))
    d_router = jnp.dot(hn_b.astype(FLOAT).T, d_logits, precision=HIGH_PRECISION)
    d_hn = d_home + jnp.dot(d_logits, wr_b.astype(FLOAT).T, precision=HIGH_PRECISION)
    grad_out = cotangent[0].astype(FLOAT)
    unused, ffn_pull = jax.vjp(rms_norm, mid_rows, g_ffn)
    d_mid_norm, d_ffn_gain = ffn_pull(d_hn)
    d_mid = grad_out + d_mid_norm

    d_attn_b = d_mid.astype(BF16)
    sends = [
        Send(lambda i, o, z, f: i[0], lambda i, o, z, f: o[0].at[f], 0, m)
        for m in range(0, nf, 2)
    ]
    for m in range(0, nf, 2):
        if m == 0:
            sends.append(Send(lambda i, o, z, f: i[0], lambda i, o, z, f: o[0].at[f], 0, 1))
        else:
            sends.append(
                Send(
                    lambda i, o, z, f, m=m: o[0].at[flip(f, m)],
                    lambda i, o, z, f, m=m: o[0].at[flip(f, m)],
                    0,
                    1,
                    m // 2,
                )
            )
    (da_all,) = exchange("gather_grads", 9, (d_attn_b,), ((nf, rows, width),), sends, 30)
    da_all = da_all.reshape(seqs * rows, width)
    d_wo = contract_rows(o_mat, da_all)
    d_o = contract_cols(da_all, wo_b).astype(BF16).reshape(seqs, rows, my_heads, head_dim)
    d_o = d_o.transpose(0, 2, 1, 3)
    d_val = jnp.einsum("nhqk,nhqd->nkd", probs, d_o, preferred_element_type=FLOAT)
    d_probs = jnp.einsum("nhqd,nkd->nhqk", d_o, values, preferred_element_type=FLOAT)
    probs_f = probs.astype(FLOAT)
    d_scores = (
        probs_f * (d_probs - jnp.sum(probs_f * d_probs, axis=3, keepdims=True))
    ).astype(BF16)
    dq = (
        jnp.einsum("nhqk,nkd->nqhd", d_scores, keys, preferred_element_type=FLOAT) * score_scale
    ).astype(BF16)
    d_key = (
        jnp.einsum("nhqk,nhqd->nkd", d_scores, q_rows, preferred_element_type=FLOAT) * score_scale
    )
    d_kv = jnp.concatenate([d_key, d_val], axis=2).astype(BF16)
    d_kv = d_kv.reshape(seqs, nsp, rows, 2 * head_dim).transpose(1, 0, 2, 3)
    d_kv = d_kv.reshape(nsp, seqs * rows, 2 * head_dim)
    d_kv, all_down = lax.optimization_barrier((d_kv, all_down))
    grad_down = all_down.astype(FLOAT).reshape(n_experts, hid_shard, width)
    d_kv = d_kv.reshape(nsp, rep, piece, 2 * head_dim)
    (others,) = exchange(
        "key_grads_group",
        11,
        (d_kv,),
        ((rep - 1, nsp, piece, 2 * head_dim),),
        [
            Send(
                lambda i, o, z, f, p=p: i[0].at[:, flip(lax.rem(f, rep), p)],
                lambda i, o, z, f, p=p: o[0].at[p - 1],
                0,
                p,
            )
            for p in range(1, rep)
        ],
        6,
    )
    d_kv = lax.dynamic_index_in_dim(d_kv, lax.rem(f, rep), 1, keepdims=False)
    d_kv = (d_kv.astype(FLOAT) + jnp.sum(others.astype(FLOAT), axis=0)).astype(BF16)
    sends = [
        Send(lambda i, o, z, f, d=d: i[0].at[d], lambda i, o, z, f, d=d: o[0].at[d - 1], d, 0)
        for d in range(1, nsp)
    ]
    for s in range(plane_experts):
        sends.append(
            Send(
                lambda i, o, z, f, s=s: i[1].at[s],
                lambda i, o, z, f, s=s: o[1].at[:, s],
                0,
                s * parts,
            )
        )
    others, out_back = exchange(
        "key_grads_planes",
        10,
        (d_kv, weighted.reshape(plane_experts, nsp, cap, width)),
        ((nsp - 1, piece, 2 * head_dim), (nsp, plane_experts, cap, width)),
        sends,
        60,
    )
    out_blocks = combine(out_back)
    d_kv = (d_kv[0].astype(FLOAT) + jnp.sum(others.astype(FLOAT), axis=0)).astype(BF16)
    (d_kv,) = exchange(
        "key_grads_share",
        15,
        (d_kv,),
        ((rep, piece, 2 * head_dim),),
        [
            Send(lambda i, o, z, f: i[0], lambda i, o, z, f: o[0].at[lax.rem(f, rep)], 0, p)
            for p in range(rep)
        ],
        6,
    )
    d_kv = d_kv.reshape(seqs * rows, 2 * head_dim).astype(FLOAT)
    dq, grad_down = lax.optimization_barrier((dq, grad_down))
    unused, q_pull = jax.vjp(prep_heads, q_lin, g_query)
    d_q_lin, d_q_gain = q_pull(dq.astype(FLOAT))
    unused, k_pull = jax.vjp(prep_heads, k_lin, g_key)
    d_k_lin, d_k_gain = k_pull(d_kv[:, :head_dim].reshape(seqs, rows, 1, head_dim))
    dq_b = d_q_lin.astype(BF16).reshape(seqs * rows, q_cols)
    dk_b = d_k_lin.astype(BF16).reshape(seqs * rows, head_dim)
    dv_b = d_kv[:, head_dim:].astype(BF16)
    d_qkv = jnp.concatenate([dq_b, dk_b, dv_b], axis=1)
    share = 1.0 / rep
    d_qkv_shared = jnp.concatenate([dq_b, dk_b * BF16(share), dv_b * BF16(share)], axis=1)
    d_w_qkv = contract_rows(xn_b, d_qkv).astype(BF16)
    d_xn, unused = pair_then_plane(contract_cols(d_qkv_shared, w_qkv), "input_sum", 13)
    unused, attn_pull = jax.vjp(rms_norm, x_rows, g_attn)
    d_x_norm, d_attn_gain = attn_pull(d_xn)
    grad_tokens = (d_mid + d_x_norm)[None]

    smalls = jnp.concatenate(
        [
            d_attn_gain.reshape(nf, shard),
            d_ffn_gain.reshape(nf, shard),
            d_q_gain.reshape(nf, head_dim // nf),
            (d_k_gain * share).reshape(nf, head_dim // nf),
            d_router.reshape(nf, shard * n_experts),
        ],
        axis=1,
    ).astype(BF16)
    small_size = smalls.shape[1]
    small_cols = pl.cdiv(small_size, kv_heads * head_dim) * kv_heads * head_dim // small_rows
    small_cols = pl.cdiv(small_cols, LANES) * LANES
    smalls = jnp.pad(smalls, ((0, 0), (0, small_rows * small_cols - small_size)))
    kv_cols = kv_heads * head_dim
    sends = []
    for m in range(nf):
        sends.append(
            Send(
                lambda i, o, z, f, m=m: i[0].at[cols(flip(f, m), shard), pl.ds(0, q_cols)],
                lambda i, o, z, f: o[0].at[:, cols(f, q_cols)],
                0,
                m,
            )
        )
        sends.append(
            Send(lambda i, o, z, f, m=m: i[1].at[flip(f, m)], lambda i, o, z, f: o[2].at[f], 0, m)
        )
    for m in range(0, nf, rep):
        for w in range(2):
            sends.append(
                Send(
                    lambda i, o, z, f, m=m, w=w: i[0].at[
                        cols(flip(f, m), shard), pl.ds(q_cols + w * head_dim, head_dim)
                    ],
                    lambda i, o, z, f, w=w: o[1].at[
                        pl.ds(w * shard, shard), cols(lax.div(f, rep), head_dim)
                    ],
                    0,
                    m,
                )
            )
    d_wq, d_wkv, small_shard = exchange(
        "head_grads_to_shards",
        12,
        (d_w_qkv, smalls.reshape(nf, small_rows, small_cols)),
        (
            (shard, n_heads * head_dim),
            (2 * shard, kv_cols),
            (nf, small_rows, small_cols),
        ),
        sends,
        36,
    )
    small_sum = jnp.sum(small_shard.astype(FLOAT), axis=0).astype(BF16)
    if nsp == 4:
        sum_q, sum_out, sum_kv, small_sum, out_others = line_sum(
            16, (d_wq, d_wo.astype(BF16), d_wkv, small_sum), (4, 4, 1, 1), out_blocks
        )
        out_others = [out_others[d] for d in range(nsp - 1)]
    else:
        sum_q, sum_out, sum_kv, small_sum = lax.psum(
            (d_wq, d_wo.astype(BF16), d_wkv, small_sum), "sp"
        )
        out_others = [swap_z(out_blocks[d], d) for d in range(1, nsp)]
    moe_sum = out_blocks[0].astype(FLOAT)
    for block in out_others:
        moe_sum = moe_sum + block.astype(FLOAT)
    mixed = (mid_rows + moe_sum).astype(BF16)[None]
    sum_out = sum_out.astype(FLOAT)
    sum_q = sum_q.astype(FLOAT)
    sum_kv = sum_kv.astype(FLOAT)
    small_sum = small_sum.astype(FLOAT).reshape(-1)
    at = 0
    pieces = []
    for size in (shard, shard, head_dim // nf, head_dim // nf, shard * n_experts):
        pieces.append(small_sum[at : at + size])
        at += size
    return (
        mixed,
        grad_tokens,
        pieces[0],
        sum_q,
        sum_kv[:shard],
        sum_kv[shard : 2 * shard],
        pieces[2],
        pieces[3],
        sum_out,
        pieces[1],
        pieces[4].reshape(shard, n_experts),
        all_gate_up[:, 0].astype(FLOAT).reshape(n_experts, shard, hidden_size),
        all_gate_up[:, 1].astype(FLOAT).reshape(n_experts, shard, hidden_size),
        grad_down,
    )


def solution(mesh):
    by_token = P("fsdp", "sp", None)
    by_row = P("fsdp", None)
    by_inner = P(None, "fsdp", None)
    in_specs = (
        by_token,
        by_token,
        P("fsdp"),
        by_row,
        by_row,
        by_row,
        P("fsdp"),
        P("fsdp"),
        by_row,
        P("fsdp"),
        by_row,
        by_inner,
        by_inner,
        by_inner,
        by_token,
    )
    out_specs = (
        by_token,
        by_token,
        P("fsdp"),
        by_row,
        by_row,
        by_row,
        P("fsdp"),
        P("fsdp"),
        by_row,
        P("fsdp"),
        by_row,
        by_inner,
        by_inner,
        by_inner,
    )
    return jax.shard_map(body, mesh=mesh, in_specs=in_specs, out_specs=out_specs, check_vma=False)
```

```python
import math
from typing import Callable, NamedTuple

import jax
import jax.numpy as jnp
from jax import lax
from jax.experimental import pallas as pl
from jax.experimental.pallas import tpu as pltpu
from jax.sharding import PartitionSpec as P

QUERY_HEADS = 32
KEY_VALUE_HEADS = 4
HEAD_SIZE = 128
CAP = 80
LANES = 128

EPS = 1e-06
THETA = 1000000.0
HIGH_PRECISION = lax.Precision.HIGHEST
BF16 = jnp.bfloat16
FLOAT = jnp.float32
MESH = pl.DeviceIdType.MESH


def rms_norm(values_in, gain_vec):
    return (
        values_in
        * lax.rsqrt(jnp.mean(values_in * values_in, axis=-1, keepdims=True) + EPS)
        * gain_vec
    )


def rotate(values_in, cosine, sine_part):
    half_dim = values_in.shape[-1] // 2
    first_half = values_in[..., :half_dim]
    second = values_in[..., half_dim:]
    return jnp.concatenate(
        [first_half * cosine - second * sine_part, second * cosine + first_half * sine_part],
        axis=-1,
    )


def contract_rows(left_mat, right_mat):
    return lax.dot_general(
        left_mat, right_mat, (((0,), (0,)), ((), ())), preferred_element_type=FLOAT
    )


def contract_cols(left_mat, right_mat):
    return lax.dot_general(
        left_mat, right_mat, (((1,), (1,)), ((), ())), preferred_element_type=FLOAT
    )


def matmul(left_mat, right_mat):
    return jnp.dot(left_mat, right_mat, preferred_element_type=FLOAT)


def flip(index, mask):
    bit = 1
    while bit <= mask:
        if mask & bit:
            index = index + bit * (1 - 2 * lax.rem(lax.div(index, bit), 2))
        bit *= 2
    return index


def cols(block, size):
    return pl.ds(pl.multiple_of(block * size, size), size)


class _ShapeOnly:
    def __init__(self, shape):
        self.shape = tuple(shape)

    @property
    def at(self):
        return self

    def __getitem__(self, index):
        index = index if isinstance(index, tuple) else (index,)
        shape = []
        for size, i in zip(self.shape, index):
            if isinstance(i, slice):
                shape.append(len(range(*i.indices(size))))
            elif hasattr(i, "size") and hasattr(i, "start"):
                shape.append(i.size)
        return _ShapeOnly(tuple(shape) + self.shape[len(index) :])


class Send(NamedTuple):
    src: Callable
    dst: Callable
    dz: int
    df: int
    after: int | None = None


def exchange(name, cid, arrays, out_shapes, sends, micros):
    n_in, n_out = len(arrays), len(out_shapes)
    peers = sorted({(s.dz, s.df) for s in sends} - {(0, 0)})
    stays = [k for k, s in enumerate(sends) if (s.dz, s.df) == (0, 0)]
    stay_shapes = []

    def probe(*refs):
        for k in stays:
            view = sends[k].src(refs, None, jnp.int32(0), jnp.int32(0))
            stay_shapes.append(view.shape)

    probe(*[_ShapeOnly(a.shape) for a in arrays])

    def kernel(*refs):
        ins, outs = refs[:n_in], refs[n_in : n_in + n_out]
        send_sems, recv_sems = refs[n_in + n_out : n_in + n_out + 2]
        bounce = dict(zip(stays, refs[n_in + n_out + 2 :]))
        z = lax.axis_index("sp")
        f = lax.axis_index("fsdp")
        barrier = pltpu.get_barrier_semaphore()
        for dz, df in peers:
            pl.semaphore_signal(
                barrier, inc=1, device_id=(flip(z, dz), flip(f, df)), device_id_type=MESH
            )
        pl.semaphore_wait(barrier, len(peers))
        copies = []
        for k, s in enumerate(sends):
            src = s.src(ins, outs, z, f)
            dst = s.dst(ins, outs, z, f)
            if (s.dz, s.df) == (0, 0):
                copies.append(
                    (
                        pltpu.make_async_copy(src, bounce[k], recv_sems.at[k]),
                        pltpu.make_async_copy(bounce[k], dst, send_sems.at[k]),
                    )
                )
            else:
                copies.append(
                    pltpu.make_async_remote_copy(
                        src_ref=src,
                        dst_ref=dst,
                        send_sem=send_sems.at[k],
                        recv_sem=recv_sems.at[k],
                        device_id=(flip(z, s.dz), flip(f, s.df)),
                        device_id_type=MESH,
                    )
                )
        arrived = set()

        def arrive(k):
            if k not in arrived:
                arrived.add(k)
                s = sends[k]
                if (s.dz, s.df) == (0, 0):
                    copies[k][1].wait()
                else:
                    copies[k].wait_recv()

        for k, s in enumerate(sends):
            if k in stays:
                copies[k][0].start()
            elif s.after is None:
                copies[k].start()
        for k in stays:
            copies[k][0].wait()
            copies[k][1].start()
        for k, s in enumerate(sends):
            if s.after is not None:
                arrive(s.after)
                copies[k].start()
        for k, s in enumerate(sends):
            if (s.dz, s.df) != (0, 0):
                copies[k].wait_send()
            arrive(k)

    result = pl.pallas_call(
        kernel,
        out_shape=[jax.ShapeDtypeStruct(shape, BF16) for shape in out_shapes],
        in_specs=[pl.BlockSpec(memory_space=pl.ANY)] * n_in,
        out_specs=[pl.BlockSpec(memory_space=pl.ANY)] * n_out,
        scratch_shapes=[
            pltpu.SemaphoreType.DMA((len(sends),)),
            pltpu.SemaphoreType.DMA((len(sends),)),
        ]
        + [pltpu.VMEM(shape, BF16) for shape in stay_shapes],
        compiler_params=pltpu.CompilerParams(
            collective_id=cid, has_side_effects=True, vmem_limit_bytes=32 * 1024 * 1024
        ),
        cost_estimate=pl.CostEstimate(
            flops=0, bytes_accessed=int(micros * 3.0e6), transcendentals=0
        ),
        name=name,
    )(*arrays)
    return result


def rows_to_experts(cid, tokens, lanes, pick, plane_experts, parts):
    planes, picked, count = pick.shape
    cap = picked // plane_experts
    arrays = (tokens, lanes)
    widths = [a.shape[1] for a in arrays]
    order = [0, 1, 3, 2] if planes == 4 else list(range(planes))
    early = 2 if planes == 4 else planes - 1
    step = 512

    def kernel(tokens_ref, lanes_ref, pick_ref, rows_ref, lane_rows_ref, *scratch):
        here, chosen = scratch[:2], scratch[2:4]
        z_send, z_recv, row_send, row_recv = scratch[4:]
        ins, outs = (tokens_ref, lanes_ref), (rows_ref, lane_rows_ref)
        z = lax.axis_index("sp")
        f = lax.axis_index("fsdp")
        barrier = pltpu.get_barrier_semaphore()
        for d in range(1, planes):
            pl.semaphore_signal(barrier, inc=1, device_id=(flip(z, d), f), device_id_type=MESH)
        for s in range(1, plane_experts):
            pl.semaphore_signal(
                barrier, inc=1, device_id=(z, flip(f, s * parts)), device_id_type=MESH
            )
        pl.semaphore_wait(barrier, planes + plane_experts - 2)

        def across(d, w):
            if d == 0:
                return pltpu.make_async_copy(ins[w], here[w].at[0], z_recv.at[w])
            return pltpu.make_async_remote_copy(
                src_ref=ins[w],
                dst_ref=here[w].at[d],
                send_sem=z_send.at[2 * d + w],
                recv_sem=z_recv.at[2 * d + w],
                device_id=(flip(z, d), f),
                device_id_type=MESH,
            )

        def onward(d, s, w):
            src = chosen[w].at[d, pl.ds(s * cap, cap)]
            dst = outs[w].at[s, d]
            k = (d * plane_experts + s) * 2 + w
            if s == 0:
                return pltpu.make_async_copy(src, dst, row_recv.at[k])
            return pltpu.make_async_remote_copy(
                src_ref=src,
                dst_ref=dst,
                send_sem=row_send.at[k],
                recv_sem=row_recv.at[k],
                device_id=(z, flip(f, s * parts)),
                device_id_type=MESH,
            )

        for d in order[: early + 1]:
            for w in range(2):
                across(d, w).start()
        for turn, d in enumerate(order):
            for w in range(2):
                if d == 0:
                    across(d, w).wait()
                else:
                    across(d, w).wait_recv()
            if turn == 1:
                for later in order[early + 1 :]:
                    for w in range(2):
                        across(later, w).start()

            def columns(i, carry):
                at = pl.ds(pl.multiple_of(i * step, step), step)
                chosen[0][d, :, at] = jnp.dot(
                    pick_ref[d], here[0][d, :, at], preferred_element_type=FLOAT
                ).astype(BF16)
                return carry

            lax.fori_loop(0, widths[0] // step, columns, 0)
            chosen[1][d] = jnp.dot(
                pick_ref[d], here[1][d], preferred_element_type=FLOAT
            ).astype(BF16)
            for s in range(plane_experts):
                for w in range(2):
                    onward(d, s, w).start()
        for d in range(planes):
            for w in range(2):
                if d:
                    across(d, w).wait_send()
                for s in range(plane_experts):
                    onward(d, s, w).wait()

    hbm = pl.BlockSpec(memory_space=pl.ANY)
    sems = planes * plane_experts * 2
    return pl.pallas_call(
        kernel,
        out_shape=[
            jax.ShapeDtypeStruct((plane_experts, planes, cap, width), BF16) for width in widths
        ],
        in_specs=[hbm, hbm, pl.BlockSpec(memory_space=pltpu.VMEM)],
        out_specs=[hbm, hbm],
        scratch_shapes=[pltpu.VMEM((planes, count, width), BF16) for width in widths]
        + [pltpu.VMEM((planes, picked, width), BF16) for width in widths]
        + [pltpu.SemaphoreType.DMA((2 * planes,))] * 2
        + [pltpu.SemaphoreType.DMA((sems,))] * 2,
        compiler_params=pltpu.CompilerParams(
            collective_id=cid, has_side_effects=True, vmem_limit_bytes=40 * 1024 * 1024
        ),
        cost_estimate=pl.CostEstimate(flops=0, bytes_accessed=int(2.1e8), transcendentals=0),
        name="rows_to_experts",
    )(tokens, lanes, pick)


def rows_from_experts(cid, rows_in, lanes_in, pick, weights):
    planes, picked, count = pick.shape
    plane_experts, _, cap, _ = rows_in.shape
    parts = weights[0].shape[1]
    inner_shape = weights[0].shape[2:]
    widths = (rows_in.shape[3], lanes_in.shape[3])
    order = [2, 3, 1, 0] if planes == 4 else list(range(planes - 1, -1, -1))
    step = 512

    def kernel(rows_ref, lanes_ref, pick_ref, first_ref, second_ref, *rest):
        outs, shards_ref = rest[:2], rest[2]
        back, partial, own, others = rest[3:5], rest[5:7], rest[7], rest[8]
        row_send, row_recv, z_send, z_recv, pair_send, pair_recv, load, w_send, w_recv = rest[9:]
        ins, weight_refs = (rows_ref, lanes_ref), (first_ref, second_ref)
        z = lax.axis_index("sp")
        f = lax.axis_index("fsdp")
        part = lax.rem(f, parts)
        place = lax.div(f, parts)
        barrier = pltpu.get_barrier_semaphore()
        for d in range(1, planes):
            pl.semaphore_signal(barrier, inc=1, device_id=(flip(z, d), f), device_id_type=MESH)
        near = list(range(1, parts)) + [s * parts for s in range(1, plane_experts)]
        for m in near:
            pl.semaphore_signal(barrier, inc=1, device_id=(z, flip(f, m)), device_id_type=MESH)
        pl.semaphore_wait(barrier, planes - 1 + len(near))

        def pair(w, p):
            k = w * (parts - 1) + p - 1
            return pltpu.make_async_remote_copy(
                src_ref=weight_refs[w].at[:, flip(part, p)],
                dst_ref=others.at[p - 1, w],
                send_sem=pair_send.at[k],
                recv_sem=pair_recv.at[k],
                device_id=(z, flip(f, p)),
                device_id_type=MESH,
            )

        def load_own(w):
            return pltpu.make_async_copy(weight_refs[w].at[:, part], own.at[w], load.at[w])

        def home(d, s, w):
            src = ins[w].at[s, d]
            dst = back[w].at[d, pl.ds(s * cap, cap)]
            k = (d * plane_experts + s) * 2 + w
            if s == 0:
                return pltpu.make_async_copy(src, dst, row_recv.at[k])
            return pltpu.make_async_remote_copy(
                src_ref=src,
                dst_ref=dst,
                send_sem=row_send.at[k],
                recv_sem=row_recv.at[k],
                device_id=(z, flip(f, s * parts)),
                device_id_type=MESH,
            )

        def across(d, w):
            src, dst = partial[w].at[d], outs[w].at[d]
            if d == 0:
                return pltpu.make_async_copy(src, dst, z_recv.at[w])
            return pltpu.make_async_remote_copy(
                src_ref=src,
                dst_ref=dst,
                send_sem=z_send.at[2 * d + w],
                recv_sem=z_recv.at[2 * d + w],
                device_id=(flip(z, d), f),
                device_id_type=MESH,
            )

        def to_shard(s, w):
            src, dst = own.at[w, flip(place, s)], shards_ref.at[w, place]
            if s == 0:
                return pltpu.make_async_copy(src, dst, w_recv.at[w])
            return pltpu.make_async_remote_copy(
                src_ref=src,
                dst_ref=dst,
                send_sem=w_send.at[2 * s + w],
                recv_sem=w_recv.at[2 * s + w],
                device_id=(z, flip(f, s * parts)),
                device_id_type=MESH,
            )

        for w in range(2):
            load_own(w).start()
            for p in range(1, parts):
                pair(w, p).start()
        for d in order:
            for s in range(plane_experts):
                for w in range(2):
                    home(d, s, w).start()
        for w in range(2):
            load_own(w).wait()
            for p in range(1, parts):
                pair(w, p).wait()

            def add(i, carry):
                e = lax.div(i, inner_shape[0] // 16)
                at = pl.ds(pl.multiple_of(lax.rem(i, inner_shape[0] // 16) * 16, 16), 16)
                total = own[w, e, at, :].astype(FLOAT)
                for p in range(parts - 1):
                    total = total + others[p, w, e, at, :].astype(FLOAT)
                own[w, e, at, :] = total.astype(BF16)
                return carry

            lax.fori_loop(0, plane_experts * (inner_shape[0] // 16), add, 0)
        for turn, d in enumerate(order):
            for s in range(plane_experts):
                for w in range(2):
                    home(d, s, w).wait()
            if turn == planes - 2:
                for s in range(plane_experts):
                    for w in range(2):
                        to_shard(s, w).start()

            def columns(i, carry):
                at = pl.ds(pl.multiple_of(i * step, step), step)
                partial[0][d, :, at] = contract_rows(pick_ref[d], back[0][d, :, at]).astype(BF16)
                return carry

            lax.fori_loop(0, widths[0] // step, columns, 0)
            partial[1][d] = contract_rows(pick_ref[d], back[1][d]).astype(BF16)
            for w in range(2):
                across(d, w).start()
        for d in range(planes):
            for w in range(2):
                across(d, w).wait()
        for s in range(plane_experts):
            for w in range(2):
                to_shard(s, w).wait()

    hbm = pl.BlockSpec(memory_space=pl.ANY)
    dma = pltpu.SemaphoreType.DMA
    row_count = planes * plane_experts * 2
    return pl.pallas_call(
        kernel,
        out_shape=[jax.ShapeDtypeStruct((planes, count, width), BF16) for width in widths]
        + [jax.ShapeDtypeStruct((2, plane_experts) + inner_shape, BF16)],
        in_specs=[hbm, hbm, pl.BlockSpec(memory_space=pltpu.VMEM), hbm, hbm],
        out_specs=[hbm] * 3,
        scratch_shapes=[pltpu.VMEM((planes, picked, width), BF16) for width in widths]
        + [pltpu.VMEM((planes, count, width), BF16) for width in widths]
        + [
            pltpu.VMEM((2, plane_experts) + inner_shape, BF16),
            pltpu.VMEM((parts - 1, 2, plane_experts) + inner_shape, BF16),
        ]
        + [dma((row_count,))] * 2
        + [dma((2 * planes,))] * 2
        + [dma((2 * (parts - 1),))] * 2
        + [dma((2,))]
        + [dma((2 * plane_experts,))] * 2,
        compiler_params=pltpu.CompilerParams(
            collective_id=cid, has_side_effects=True, vmem_limit_bytes=48 * 1024 * 1024
        ),
        cost_estimate=pl.CostEstimate(flops=0, bytes_accessed=int(2.7e8), transcendentals=0),
        name="rows_from_experts",
    )(rows_in, lanes_in, pick, *weights)


def line_sum(cid, arrays, pieces, blocks):
    n = len(arrays)
    chunks = [
        (k, c * (a.shape[0] // p), a.shape[0] // p)
        for k, (a, p) in enumerate(zip(arrays, pieces))
        for c in range(p)
    ]
    far = blocks.shape[0] - 1

    def kernel(*refs):
        ins, blocks_ref = refs[:n], refs[n]
        outs, others_ref = refs[n + 1 : 2 * n + 1], refs[2 * n + 1]
        own, got, swapped = (refs[2 * n + 2 + n * i : 2 * n + 2 + n * (i + 1)] for i in range(3))
        load, store, in_s, in_r, swap_s, swap_r, back_s, back_r, far_s, far_r = refs[5 * n + 2 :]
        z = lax.axis_index("sp")
        f = lax.axis_index("fsdp")
        inner = jnp.logical_or(z == 1, z == 2)
        barrier = pltpu.get_barrier_semaphore()
        for d in range(1, far + 1):
            pl.semaphore_signal(barrier, inc=1, device_id=(flip(z, d), f), device_id_type=MESH)
        pl.semaphore_wait(barrier, far)

        def view(refs, c):
            k, start, size = chunks[c]
            return refs[k].at[pl.ds(start, size)]

        def remote(src, dst, send, recv, c, dz):
            return pltpu.make_async_remote_copy(
                src_ref=view(src, c),
                dst_ref=view(dst, c),
                send_sem=send.at[c],
                recv_sem=recv.at[c],
                device_id=(flip(z, dz), f),
                device_id_type=MESH,
            )

        loads = [
            pltpu.make_async_copy(view(ins, c), view(own, c), load.at[c])
            for c in range(len(chunks))
        ]
        stores = [
            pltpu.make_async_copy(view(got, c), view(outs, c), store.at[c])
            for c in range(len(chunks))
        ]
        far_copies = [
            pltpu.make_async_remote_copy(
                src_ref=blocks_ref.at[d],
                dst_ref=others_ref.at[d - 1],
                send_sem=far_s.at[d - 1],
                recv_sem=far_r.at[d - 1],
                device_id=(flip(z, d), f),
                device_id_type=MESH,
            )
            for d in range(1, far + 1)
        ]
        inwards = [remote(own, got, in_s, in_r, c, 1) for c in range(len(chunks))]
        swaps = [remote(own, swapped, swap_s, swap_r, c, 3) for c in range(len(chunks))]
        backs = [remote(got, got, back_s, back_r, c, 1) for c in range(len(chunks))]
        for copy in loads:
            copy.start()

        def add(left, right, to, c):
            k, start, size = chunks[c]
            step = 16

            def rows(i, carry):
                at = pl.ds(pl.multiple_of(start + i * step, step), step)
                total = left[k][at, :].astype(FLOAT) + right[k][at, :].astype(FLOAT)
                to[k][at, :] = total.astype(BF16)
                return carry

            lax.fori_loop(0, size // step, rows, 0)

        @pl.when(jnp.logical_not(inner))
        def _():
            for c in range(len(chunks)):
                loads[c].wait()
                inwards[c].start()
            for copy in far_copies:
                copy.start()
            for c in range(len(chunks)):
                backs[c].wait_recv()
                stores[c].start()
            for c in range(len(chunks)):
                inwards[c].wait_send()
                stores[c].wait()

        @pl.when(inner)
        def _():
            for copy in far_copies:
                copy.start()
            for c in range(len(chunks) + 1):
                if c < len(chunks):
                    loads[c].wait()
                    inwards[c].wait_recv()
                    add(own, got, own, c)
                    swaps[c].start()
                if c:
                    swaps[c - 1].wait_recv()
                    add(own, swapped, got, c - 1)
                    backs[c - 1].start()
                    stores[c - 1].start()
            for c in range(len(chunks)):
                swaps[c].wait_send()
                backs[c].wait_send()
                stores[c].wait()

        for copy in far_copies:
            copy.wait()

    hbm = pl.BlockSpec(memory_space=pl.ANY)
    buffers = [pltpu.VMEM(a.shape, BF16) for a in arrays]
    count = len(chunks)
    return pl.pallas_call(
        kernel,
        out_shape=[jax.ShapeDtypeStruct(a.shape, BF16) for a in arrays]
        + [jax.ShapeDtypeStruct((far,) + blocks.shape[1:], BF16)],
        in_specs=[hbm] * (n + 1),
        out_specs=[hbm] * (n + 1),
        scratch_shapes=buffers * 3
        + [pltpu.SemaphoreType.DMA((count,))] * 8
        + [pltpu.SemaphoreType.DMA((far,))] * 2,
        compiler_params=pltpu.CompilerParams(
            collective_id=cid, has_side_effects=True, vmem_limit_bytes=40 * 1024 * 1024
        ),
        cost_estimate=pl.CostEstimate(flops=0, bytes_accessed=int(4.0e8), transcendentals=0),
        name="line_sum",
    )(*arrays, blocks)


def body(
    tokens,
    expert_ids,
    attn_gain,
    query_weight,
    key_weight,
    value_weight,
    q_gain,
    k_gain,
    output_weight,
    ffn_gain,
    router_weight,
    w_gate,
    w_up,
    w_down,
    cotangent,
):
    nsp = lax.axis_size("sp")
    nf = lax.axis_size("fsdp")
    z = lax.axis_index("sp")
    f = lax.axis_index("fsdp")
    rows = tokens.shape[1]
    width = tokens.shape[2]
    shard = width // nf
    n_heads, kv_heads, head_dim = QUERY_HEADS, KEY_VALUE_HEADS, HEAD_SIZE
    my_heads = n_heads // nf
    rep = nf // kv_heads
    q_cols = my_heads * head_dim
    qkv_cols = q_cols + 2 * head_dim
    score_scale = 1.0 / math.sqrt(head_dim)
    n_experts = w_gate.shape[0]
    hidden_size = w_gate.shape[2]
    hid_shard = w_down.shape[1]
    plane_experts = n_experts // nsp
    parts = nf // plane_experts
    cap = CAP
    seqs = nf
    part = lax.rem(f, parts)
    place = lax.div(f, parts)
    expert = z * plane_experts + place

    def swap_f(block, mask):
        return lax.ppermute(block, "fsdp", [(i, i ^ mask) for i in range(nf)])

    def swap_z(block, mask):
        return lax.ppermute(block, "sp", [(i, i ^ mask) for i in range(nsp)])

    small = jnp.concatenate(
        [
            attn_gain.astype(BF16),
            ffn_gain.astype(BF16),
            q_gain.astype(BF16),
            k_gain.astype(BF16),
            router_weight.astype(BF16).reshape(-1),
        ]
    )
    small_rows = 16
    small = jnp.pad(small, (0, small_rows * width - small.shape[0])).reshape(small_rows, width)
    x_pay = jnp.concatenate([tokens[0], small], axis=0)
    pay_rows = rows + small_rows
    query_b = query_weight.astype(BF16)
    key_b = key_weight.astype(BF16)
    value_b = value_weight.astype(BF16)
    routes = expert_ids[0]
    expert_iota = jnp.arange(n_experts, dtype=jnp.int32)
    routed = jnp.any(routes[:, :, None] == expert_iota[None, None, :], axis=1)
    dy_pay = jnp.concatenate(
        [
            cotangent[0],
            routed.astype(BF16),
            jnp.zeros((rows, LANES - n_experts), BF16),
        ],
        axis=1,
    )
    wide = width + LANES

    def plane_cast(weight):
        return lax.dynamic_slice_in_dim(weight, z * plane_experts, plane_experts, 0).astype(BF16)

    gate_up_pay = jnp.stack([plane_cast(w_gate), plane_cast(w_up)], axis=1)
    down_pay = plane_cast(w_down)

    sends = []
    for m in range(0, nf, 2):
        sends.append(
            Send(
                lambda i, o, z, f, m=m: i[0],
                lambda i, o, z, f: o[0].at[f],
                0,
                m,
            )
        )
    for m in range(0, nf, 2):
        if m == 0:
            sends.append(
                Send(lambda i, o, z, f: i[0], lambda i, o, z, f: o[0].at[f], 0, 1)
            )
        else:
            sends.append(
                Send(
                    lambda i, o, z, f, m=m: o[0].at[flip(f, m)],
                    lambda i, o, z, f, m=m: o[0].at[flip(f, m)],
                    0,
                    1,
                    m // 2,
                )
            )
    for m in range(0, nf, rep):
        for w in range(2):
            sends.append(
                Send(
                    lambda i, o, z, f, m=m, w=w: i[2 + w].at[
                        :, cols(lax.div(flip(f, m), rep), head_dim)
                    ],
                    lambda i, o, z, f, w=w: o[1].at[
                        cols(f, shard), pl.ds(q_cols + w * head_dim, head_dim)
                    ],
                    0,
                    m,
                )
            )
            for p in range(1, rep):
                view = lambda i, o, z, f, m=m, w=w: o[1].at[
                    cols(flip(f, m), shard), pl.ds(q_cols + w * head_dim, head_dim)
                ]
                if m == 0:
                    sends.append(
                        Send(
                            lambda i, o, z, f, w=w: i[2 + w].at[:, cols(lax.div(f, rep), head_dim)],
                            view,
                            0,
                            p,
                        )
                    )
                else:
                    sends.append(Send(view, view, 0, p, len(sends) - p))
    for m in range(nf):
        sends.append(
            Send(
                lambda i, o, z, f, m=m: i[1].at[:, cols(flip(f, m), q_cols)],
                lambda i, o, z, f: o[1].at[cols(f, shard), pl.ds(0, q_cols)],
                0,
                m,
            )
        )
    for m in range(nsp):
        sends.append(
            Send(lambda i, o, z, f: i[4], lambda i, o, z, f, m=m: o[2].at[m], m, 0)
        )
    x_all, w_qkv, dy_z = exchange(
        "gather_inputs",
        0,
        (x_pay, query_b, key_b, value_b, dy_pay),
        ((nf, pay_rows, width), (width, qkv_cols), (nsp, rows, wide)),
        sends,
        65,
    )

    own_experts = z * plane_experts + jnp.bitwise_xor(
        place, jnp.arange(plane_experts, dtype=jnp.int32)
    )
    own_hot = (expert_iota[:, None] == own_experts[None, :]).astype(FLOAT)
    routed_z = lax.dot_general(
        own_hot,
        dy_z[:, :, width : width + n_experts].astype(FLOAT),
        (((0,), (2,)), ((), ())),
        preferred_element_type=FLOAT,
    ).transpose(1, 0, 2)
    earlier = jnp.triu(jnp.ones((rows, rows), FLOAT), 1)
    rank = jnp.dot(
        routed_z.reshape(nsp * plane_experts, rows), earlier, preferred_element_type=FLOAT
    ).reshape(nsp, plane_experts, rows)
    rank = rank * routed_z + (routed_z - 1.0)
    pick = (
        rank[:, :, None, :] == jnp.arange(cap, dtype=FLOAT)[None, None, :, None]
    ).astype(BF16)
    pick = pick.reshape(nsp, plane_experts * cap, rows)

    x_all, gate_up_pay = lax.optimization_barrier((x_all, gate_up_pay))
    by_expert = pick.reshape(nsp, plane_experts, cap, rows)
    gate_up_pieces, dy_pieces = [], []
    for s in range(plane_experts):
        weights = lax.dynamic_index_in_dim(gate_up_pay, flip(place, s), 0, keepdims=False)
        dy_rows = jnp.einsum(
            "drt,dtc->drc", by_expert[:, s], dy_z[:, :, :width], preferred_element_type=FLOAT
        )
        dy_rows = dy_rows.astype(BF16).reshape(nsp * cap, width)
        if s and s == plane_experts - 1:
            both = jnp.concatenate([dy_rows, weights.reshape(-1, width)], axis=0)
            both = swap_f(both, s * parts)
            dy_rows = both[: nsp * cap]
            weights = both[nsp * cap :].reshape(2, shard, hidden_size)
        elif s:
            weights = swap_f(weights, s * parts)
            dy_rows = swap_f(dy_rows, s * parts)
        gate_up_pieces.append(weights)
        dy_pieces.append(dy_rows)
    dy_in = jnp.concatenate(dy_pieces, axis=0)

    small_all = x_all[:, rows:, :].reshape(nf, small_rows * width)
    at = 0
    pieces = []
    for size in (shard, shard, head_dim // nf, head_dim // nf, shard * n_experts):
        pieces.append(small_all[:, at : at + size])
        at += size
    g_attn = pieces[0].reshape(width).astype(FLOAT)
    g_ffn = pieces[1].reshape(width).astype(FLOAT)
    g_query = pieces[2].reshape(head_dim).astype(FLOAT)
    g_key = pieces[3].reshape(head_dim).astype(FLOAT)
    wr_b = pieces[4].reshape(width, n_experts)

    xn_b = (
        rms_norm(x_all[:, :rows, :].astype(FLOAT), g_attn).astype(BF16).reshape(seqs * rows, width)
    )
    qkv_lin = matmul(xn_b, w_qkv)
    q_lin = qkv_lin[:, :q_cols].reshape(seqs, rows, my_heads, head_dim)
    k_lin = qkv_lin[:, q_cols : q_cols + head_dim].reshape(seqs, rows, 1, head_dim)
    v_b = qkv_lin[:, q_cols + head_dim :].astype(BF16)
    half_dim = head_dim // 2
    inverse_freq = THETA ** (-(jnp.arange(half_dim, dtype=FLOAT) * 2.0 / head_dim))
    positions = (z * rows + jnp.arange(rows, dtype=jnp.int32)).astype(FLOAT)
    angles = positions[:, None] * inverse_freq[None, :]
    cosine = jnp.cos(angles)[None, :, None, :]
    sine_part = jnp.sin(angles)[None, :, None, :]

    def prep_heads(linear, gain_vec):
        return rotate(rms_norm(linear, gain_vec), cosine, sine_part)

    q_b = prep_heads(q_lin, g_query).astype(BF16)
    k_b = prep_heads(k_lin, g_key).astype(BF16).reshape(seqs * rows, head_dim)

    kv_pay = jnp.concatenate([k_b, v_b], axis=1)
    piece = seqs * rows // rep
    sends = []
    for d in range(nsp):
        sends.append(
            Send(
                lambda i, o, z, f: i[0].at[pl.ds(lax.rem(f, rep) * piece, piece)],
                lambda i, o, z, f, d=d: o[0].at[d, pl.ds(lax.rem(f, rep) * piece, piece)],
                d,
                0,
            )
        )
    for d in range(nsp):
        for p in range(1, rep):
            sends.append(
                Send(
                    lambda i, o, z, f, d=d: o[0].at[d, pl.ds(lax.rem(f, rep) * piece, piece)],
                    lambda i, o, z, f, d=d: o[0].at[d, pl.ds(lax.rem(f, rep) * piece, piece)],
                    0,
                    p,
                    d,
                )
            )
    (kv_z,) = exchange(
        "gather_keys", 1, (kv_pay,), ((nsp, seqs * rows, 2 * head_dim),), sends, 24
    )
    kv_seq = kv_z.reshape(nsp, seqs, rows, 2 * head_dim).transpose(1, 0, 2, 3)
    kv_seq = kv_seq.reshape(seqs, nsp * rows, 2 * head_dim)
    keys = kv_seq[:, :, :head_dim]
    values = kv_seq[:, :, head_dim:]

    q_rows = q_b.transpose(0, 2, 1, 3)
    plane_of = jnp.bitwise_xor(jnp.arange(nsp, dtype=jnp.int32), z)
    key_pos = (plane_of[:, None] * rows + jnp.arange(rows, dtype=jnp.int32)[None, :]).reshape(-1)
    query_pos = z * rows + jnp.arange(rows, dtype=jnp.int32)
    causal = key_pos[None, :] <= query_pos[:, None]
    scores = (
        jnp.einsum("nhqd,nkd->nhqk", q_rows, keys, preferred_element_type=FLOAT) * score_scale
    )
    scores = jnp.where(causal[None, None], scores, -1e30)
    row_top = jnp.max(scores, axis=3, keepdims=True)
    expo = jnp.exp(scores - row_top)
    probs = (expo / jnp.sum(expo, axis=3, keepdims=True)).astype(BF16)
    o_rows = jnp.einsum("nhqk,nkd->nqhd", probs, values, preferred_element_type=FLOAT)
    o_mat = o_rows.astype(BF16).reshape(seqs * rows, q_cols)
    wo_b = output_weight.astype(BF16)

    def pair_then_plane(partial, name, cid, more=(), more_shapes=(), more_sends=()):
        split = partial.astype(BF16).reshape(nf // 2, 2, rows, width)
        (other,) = exchange(
            name + "_pair",
            cid,
            (split,),
            ((nf // 2, rows, width),),
            [Send(lambda i, o, z, f: i[0].at[:, 1 - lax.rem(f, 2)], lambda i, o, z, f: o[0], 0, 1)],
            8,
        )
        own = lax.dynamic_index_in_dim(split, lax.rem(f, 2), 1, keepdims=False)
        summed = (own.astype(FLOAT) + other.astype(FLOAT)).astype(BF16)
        sends = [
            Send(
                lambda i, o, z, f, j=j: i[0].at[flip(lax.div(f, 2), j)],
                lambda i, o, z, f, j=j: o[0].at[j],
                0,
                2 * j,
            )
            for j in range(nf // 2)
        ]
        blocks, *rest = exchange(
            name + "_plane",
            cid + 1,
            (summed, *more),
            ((nf // 2, rows, width), *more_shapes),
            sends + list(more_sends),
            27,
        )
        return jnp.sum(blocks.astype(FLOAT), axis=0), rest

    sends = []
    for s in range(plane_experts):
        for p in range(parts):
            sends.append(
                Send(
                    lambda i, o, z, f, s=s: i[1 + s],
                    lambda i, o, z, f, s=s: o[1].at[:, flip(f, s * parts)],
                    0,
                    p,
                )
            )
    branch, (gate_up_all,) = pair_then_plane(
        matmul(o_mat, wo_b), "out_sum", 3, gate_up_pieces, ((2, nf, shard, hidden_size),), sends
    )
    wg_b = gate_up_all[0].reshape(width, hidden_size)
    wu_b = gate_up_all[1].reshape(width, hidden_size)
    x_rows = tokens[0].astype(FLOAT)
    mid_rows = x_rows + branch
    hn_b = rms_norm(mid_rows, g_ffn).astype(BF16)
    logits = matmul(hn_b, wr_b)
    logits = jnp.where(routed, logits, -1e30)
    expo = jnp.where(routed, jnp.exp(logits - jnp.max(logits, axis=1, keepdims=True)), 0.0)
    gates = expo / jnp.sum(expo, axis=1, keepdims=True)

    def two_parts(exact):
        high = exact.astype(BF16)
        return high, (exact - high.astype(FLOAT)).astype(BF16)

    gate_high, gate_low = two_parts(gates)
    gate_lanes = jnp.concatenate(
        [gate_high, gate_low, jnp.zeros((rows, LANES - 2 * n_experts), BF16)], axis=1
    )
    hn_rows, gate_rows = rows_to_experts(5, hn_b, gate_lanes, pick, plane_experts, parts)
    hn_rows, down_pay = lax.optimization_barrier((hn_rows, down_pay))
    down_pieces = []
    for s in range(plane_experts):
        block = lax.dynamic_index_in_dim(down_pay, flip(place, s), 0, keepdims=False)
        down_pieces.append(swap_f(block, s * parts) if s else block)

    n_rows = plane_experts * nsp * cap
    hn_in = hn_rows.reshape(n_rows, width)
    hot = (jnp.arange(n_experts, dtype=jnp.int32) == expert).astype(FLOAT)
    tail = gate_rows.reshape(n_rows, LANES)[:, : 2 * n_experts].astype(FLOAT)
    row_gate = jnp.sum(
        (tail[:, :n_experts] + tail[:, n_experts:]) * hot[None, :], axis=1, keepdims=True
    )
    gate_pre = matmul(hn_in, wg_b)
    up_pre = matmul(hn_in, wu_b)
    sigma = jax.nn.sigmoid(gate_pre)
    act_f = gate_pre * sigma
    hidden = (act_f * up_pre).astype(BF16)
    dy_f = dy_in.astype(FLOAT)
    d_result = (row_gate * dy_f).astype(BF16)

    def by_shard(full, inner):
        return full.astype(BF16).reshape((plane_experts, parts) + inner)

    def pair_total(own, others):
        total = lax.dynamic_index_in_dim(own, part, 1, keepdims=False).astype(FLOAT)
        for other in others:
            total = total + other.astype(FLOAT)
        return total.astype(BF16)

    d_down = by_shard(contract_rows(hidden, d_result), (hid_shard, width))
    d_down, down_pieces = lax.optimization_barrier((d_down, down_pieces))
    d_down = pair_total(
        d_down,
        [
            swap_f(lax.dynamic_index_in_dim(d_down, flip(part, p), 1, keepdims=False), p)
            for p in range(1, parts)
        ],
    )
    d_down = [
        swap_f(lax.dynamic_index_in_dim(d_down, flip(place, s), 0, keepdims=False), s * parts)
        if s
        else lax.dynamic_index_in_dim(d_down, place, 0, keepdims=False)
        for s in range(plane_experts)
    ]
    down_pieces = jnp.stack(down_pieces)
    down_pieces = jnp.stack(
        [swap_f(down_pieces, p) if p else down_pieces for p in range(parts)], axis=1
    ).reshape(nf, hid_shard, width)
    wd_b = jnp.take(
        down_pieces, jnp.bitwise_xor(jnp.arange(nf, dtype=jnp.int32), f), axis=0, mode="clip"
    ).reshape(hidden_size, width)
    result = matmul(hidden, wd_b)
    row_dgate = jnp.sum(result * dy_f, axis=1, keepdims=True)
    weighted = (row_gate * result).astype(BF16)
    d_hidden = contract_cols(d_result, wd_b)
    d_gate_pre = (d_hidden * up_pre * sigma * (1.0 + gate_pre * (1.0 - sigma))).astype(BF16)
    d_up_pre = (d_hidden * act_f).astype(BF16)
    d_down, d_gate_pre, d_up_pre = lax.optimization_barrier((d_down, d_gate_pre, d_up_pre))
    in_order = jnp.bitwise_xor(jnp.arange(plane_experts, dtype=jnp.int32), place)
    d_down = jnp.take(jnp.stack(d_down), in_order, axis=0, mode="clip")
    all_down = lax.all_gather(d_down, "sp")
    d_in = (contract_cols(d_gate_pre, wg_b) + contract_cols(d_up_pre, wu_b)).astype(BF16)
    dgate_high, dgate_low = two_parts(row_dgate * hot[None, :])
    dgate_lanes = jnp.concatenate(
        [dgate_high, dgate_low, jnp.zeros((n_rows, LANES - 2 * n_experts), BF16)], axis=1
    )

    d_weights = (
        by_shard(contract_rows(hn_in, d_gate_pre), (shard, hidden_size)),
        by_shard(contract_rows(hn_in, d_up_pre), (shard, hidden_size)),
    )

    d_home, dgate_home, shards = rows_from_experts(
        7,
        d_in.reshape(plane_experts, nsp, cap, width),
        dgate_lanes.reshape(plane_experts, nsp, cap, LANES),
        pick,
        d_weights,
    )

    def combine(returned):
        flat = returned.reshape(nsp, plane_experts * cap, returned.shape[3])
        return jnp.einsum("drt,drc->dtc", pick, flat, preferred_element_type=FLOAT).astype(BF16)

    all_gate_up = lax.all_gather(shards, "sp")
    d_home = jnp.sum(d_home.astype(FLOAT), axis=0)
    tail = jnp.sum(dgate_home.astype(FLOAT), axis=0)
    d_gates = tail[:, :n_experts] + tail[:, n_experts : 2 * n_experts]
    d_logits = gates * (d_gates - jnp.sum(gates * d_gates, axis=1, keepdims=True))
    d_router = jnp.dot(hn_b.astype(FLOAT).T, d_logits, precision=HIGH_PRECISION)
    d_hn = d_home + jnp.dot(d_logits, wr_b.astype(FLOAT).T, precision=HIGH_PRECISION)
    grad_out = cotangent[0].astype(FLOAT)
    unused, ffn_pull = jax.vjp(rms_norm, mid_rows, g_ffn)
    d_mid_norm, d_ffn_gain = ffn_pull(d_hn)
    d_mid = grad_out + d_mid_norm

    d_attn_b = d_mid.astype(BF16)
    sends = [
        Send(lambda i, o, z, f: i[0], lambda i, o, z, f: o[0].at[f], 0, m)
        for m in range(0, nf, 2)
    ]
    for m in range(0, nf, 2):
        if m == 0:
            sends.append(Send(lambda i, o, z, f: i[0], lambda i, o, z, f: o[0].at[f], 0, 1))
        else:
            sends.append(
                Send(
                    lambda i, o, z, f, m=m: o[0].at[flip(f, m)],
                    lambda i, o, z, f, m=m: o[0].at[flip(f, m)],
                    0,
                    1,
                    m // 2,
                )
            )
    (da_all,) = exchange("gather_grads", 9, (d_attn_b,), ((nf, rows, width),), sends, 30)
    da_all = da_all.reshape(seqs * rows, width)
    d_wo = contract_rows(o_mat, da_all)
    d_o = contract_cols(da_all, wo_b).astype(BF16).reshape(seqs, rows, my_heads, head_dim)
    d_o = d_o.transpose(0, 2, 1, 3)
    d_val = jnp.einsum("nhqk,nhqd->nkd", probs, d_o, preferred_element_type=FLOAT)
    d_probs = jnp.einsum("nhqd,nkd->nhqk", d_o, values, preferred_element_type=FLOAT)
    probs_f = probs.astype(FLOAT)
    d_scores = (
        probs_f * (d_probs - jnp.sum(probs_f * d_probs, axis=3, keepdims=True))
    ).astype(BF16)
    dq = (
        jnp.einsum("nhqk,nkd->nqhd", d_scores, keys, preferred_element_type=FLOAT) * score_scale
    ).astype(BF16)
    d_key = (
        jnp.einsum("nhqk,nhqd->nkd", d_scores, q_rows, preferred_element_type=FLOAT) * score_scale
    )
    d_kv = jnp.concatenate([d_key, d_val], axis=2).astype(BF16)
    d_kv = d_kv.reshape(seqs, nsp, rows, 2 * head_dim).transpose(1, 0, 2, 3)
    d_kv = d_kv.reshape(nsp, seqs * rows, 2 * head_dim)
    d_kv, all_down = lax.optimization_barrier((d_kv, all_down))
    grad_down = all_down.astype(FLOAT).reshape(n_experts, hid_shard, width)
    d_kv = d_kv.reshape(nsp, rep, piece, 2 * head_dim)
    (others,) = exchange(
        "key_grads_group",
        11,
        (d_kv,),
        ((rep - 1, nsp, piece, 2 * head_dim),),
        [
            Send(
                lambda i, o, z, f, p=p: i[0].at[:, flip(lax.rem(f, rep), p)],
                lambda i, o, z, f, p=p: o[0].at[p - 1],
                0,
                p,
            )
            for p in range(1, rep)
        ],
        6,
    )
    d_kv = lax.dynamic_index_in_dim(d_kv, lax.rem(f, rep), 1, keepdims=False)
    d_kv = (d_kv.astype(FLOAT) + jnp.sum(others.astype(FLOAT), axis=0)).astype(BF16)
    sends = [
        Send(lambda i, o, z, f, d=d: i[0].at[d], lambda i, o, z, f, d=d: o[0].at[d - 1], d, 0)
        for d in range(1, nsp)
    ]
    for s in range(plane_experts):
        sends.append(
            Send(
                lambda i, o, z, f, s=s: i[1].at[s],
                lambda i, o, z, f, s=s: o[1].at[:, s],
                0,
                s * parts,
            )
        )
    others, out_back = exchange(
        "key_grads_planes",
        10,
        (d_kv, weighted.reshape(plane_experts, nsp, cap, width)),
        ((nsp - 1, piece, 2 * head_dim), (nsp, plane_experts, cap, width)),
        sends,
        60,
    )
    out_blocks = combine(out_back)
    d_kv = (d_kv[0].astype(FLOAT) + jnp.sum(others.astype(FLOAT), axis=0)).astype(BF16)
    (d_kv,) = exchange(
        "key_grads_share",
        15,
        (d_kv,),
        ((rep, piece, 2 * head_dim),),
        [
            Send(lambda i, o, z, f: i[0], lambda i, o, z, f: o[0].at[lax.rem(f, rep)], 0, p)
            for p in range(rep)
        ],
        6,
    )
    d_kv = d_kv.reshape(seqs * rows, 2 * head_dim).astype(FLOAT)
    dq, grad_down = lax.optimization_barrier((dq, grad_down))
    unused, q_pull = jax.vjp(prep_heads, q_lin, g_query)
    d_q_lin, d_q_gain = q_pull(dq.astype(FLOAT))
    unused, k_pull = jax.vjp(prep_heads, k_lin, g_key)
    d_k_lin, d_k_gain = k_pull(d_kv[:, :head_dim].reshape(seqs, rows, 1, head_dim))
    dq_b = d_q_lin.astype(BF16).reshape(seqs * rows, q_cols)
    dk_b = d_k_lin.astype(BF16).reshape(seqs * rows, head_dim)
    dv_b = d_kv[:, head_dim:].astype(BF16)
    d_qkv = jnp.concatenate([dq_b, dk_b, dv_b], axis=1)
    share = 1.0 / rep
    d_qkv_shared = jnp.concatenate([dq_b, dk_b * BF16(share), dv_b * BF16(share)], axis=1)
    d_w_qkv = contract_rows(xn_b, d_qkv).astype(BF16)
    d_xn, unused = pair_then_plane(contract_cols(d_qkv_shared, w_qkv), "input_sum", 13)
    unused, attn_pull = jax.vjp(rms_norm, x_rows, g_attn)
    d_x_norm, d_attn_gain = attn_pull(d_xn)
    grad_tokens = (d_mid + d_x_norm)[None]

    smalls = jnp.concatenate(
        [
            d_attn_gain.reshape(nf, shard),
            d_ffn_gain.reshape(nf, shard),
            d_q_gain.reshape(nf, head_dim // nf),
            (d_k_gain * share).reshape(nf, head_dim // nf),
            d_router.reshape(nf, shard * n_experts),
        ],
        axis=1,
    ).astype(BF16)
    small_size = smalls.shape[1]
    small_cols = pl.cdiv(small_size, kv_heads * head_dim) * kv_heads * head_dim // small_rows
    small_cols = pl.cdiv(small_cols, LANES) * LANES
    smalls = jnp.pad(smalls, ((0, 0), (0, small_rows * small_cols - small_size)))
    kv_cols = kv_heads * head_dim
    sends = []
    for m in range(nf):
        sends.append(
            Send(
                lambda i, o, z, f, m=m: i[0].at[cols(flip(f, m), shard), pl.ds(0, q_cols)],
                lambda i, o, z, f: o[0].at[:, cols(f, q_cols)],
                0,
                m,
            )
        )
        sends.append(
            Send(lambda i, o, z, f, m=m: i[1].at[flip(f, m)], lambda i, o, z, f: o[2].at[f], 0, m)
        )
    for m in range(0, nf, rep):
        for w in range(2):
            sends.append(
                Send(
                    lambda i, o, z, f, m=m, w=w: i[0].at[
                        cols(flip(f, m), shard), pl.ds(q_cols + w * head_dim, head_dim)
                    ],
                    lambda i, o, z, f, w=w: o[1].at[
                        pl.ds(w * shard, shard), cols(lax.div(f, rep), head_dim)
                    ],
                    0,
                    m,
                )
            )
    d_wq, d_wkv, small_shard = exchange(
        "head_grads_to_shards",
        12,
        (d_w_qkv, smalls.reshape(nf, small_rows, small_cols)),
        (
            (shard, n_heads * head_dim),
            (2 * shard, kv_cols),
            (nf, small_rows, small_cols),
        ),
        sends,
        36,
    )
    small_sum = jnp.sum(small_shard.astype(FLOAT), axis=0).astype(BF16)
    if nsp == 4:
        sum_q, sum_out, sum_kv, small_sum, out_others = line_sum(
            16, (d_wq, d_wo.astype(BF16), d_wkv, small_sum), (4, 4, 1, 1), out_blocks
        )
        out_others = [out_others[d] for d in range(nsp - 1)]
    else:
        sum_q, sum_out, sum_kv, small_sum = lax.psum(
            (d_wq, d_wo.astype(BF16), d_wkv, small_sum), "sp"
        )
        out_others = [swap_z(out_blocks[d], d) for d in range(1, nsp)]
    moe_sum = out_blocks[0].astype(FLOAT)
    for block in out_others:
        moe_sum = moe_sum + block.astype(FLOAT)
    mixed = (mid_rows + moe_sum).astype(BF16)[None]
    sum_out = sum_out.astype(FLOAT)
    sum_q = sum_q.astype(FLOAT)
    sum_kv = sum_kv.astype(FLOAT)
    small_sum = small_sum.astype(FLOAT).reshape(-1)
    at = 0
    pieces = []
    for size in (shard, shard, head_dim // nf, head_dim // nf, shard * n_experts):
        pieces.append(small_sum[at : at + size])
        at += size
    return (
        mixed,
        grad_tokens,
        pieces[0],
        sum_q,
        sum_kv[:shard],
        sum_kv[shard : 2 * shard],
        pieces[2],
        pieces[3],
        sum_out,
        pieces[1],
        pieces[4].reshape(shard, n_experts),
        all_gate_up[:, 0].astype(FLOAT).reshape(n_experts, shard, hidden_size),
        all_gate_up[:, 1].astype(FLOAT).reshape(n_experts, shard, hidden_size),
        grad_down,
    )


def solution(mesh):
    by_token = P("fsdp", "sp", None)
    by_row = P("fsdp", None)
    by_inner = P(None, "fsdp", None)
    in_specs = (
        by_token,
        by_token,
        P("fsdp"),
        by_row,
        by_row,
        by_row,
        P("fsdp"),
        P("fsdp"),
        by_row,
        P("fsdp"),
        by_row,
        by_inner,
        by_inner,
        by_inner,
        by_token,
    )
    out_specs = (
        by_token,
        by_token,
        P("fsdp"),
        by_row,
        by_row,
        by_row,
        P("fsdp"),
        P("fsdp"),
        by_row,
        P("fsdp"),
        by_row,
        by_inner,
        by_inner,
        by_inner,
    )
    return jax.shard_map(body, mesh=mesh, in_specs=in_specs, out_specs=out_specs, check_vma=False)
```

```python
import math
from typing import Callable, NamedTuple

import jax
import jax.numpy as jnp
from jax import lax
from jax.experimental import pallas as pl
from jax.experimental.pallas import tpu as pltpu
from jax.sharding import PartitionSpec as P

QUERY_HEADS = 32
KEY_VALUE_HEADS = 4
HEAD_SIZE = 128
CAP = 80
LANES = 128

EPS = 1e-06
THETA = 1000000.0
HIGH_PRECISION = lax.Precision.HIGHEST
BF16 = jnp.bfloat16
FLOAT = jnp.float32
MESH = pl.DeviceIdType.MESH


def rms_norm(values_in, gain_vec):
    return (
        values_in
        * lax.rsqrt(jnp.mean(values_in * values_in, axis=-1, keepdims=True) + EPS)
        * gain_vec
    )


def rotate(values_in, cosine, sine_part):
    half_dim = values_in.shape[-1] // 2
    first_half = values_in[..., :half_dim]
    second = values_in[..., half_dim:]
    return jnp.concatenate(
        [first_half * cosine - second * sine_part, second * cosine + first_half * sine_part],
        axis=-1,
    )


def contract_rows(left_mat, right_mat):
    return lax.dot_general(
        left_mat, right_mat, (((0,), (0,)), ((), ())), preferred_element_type=FLOAT
    )


def contract_cols(left_mat, right_mat):
    return lax.dot_general(
        left_mat, right_mat, (((1,), (1,)), ((), ())), preferred_element_type=FLOAT
    )


def matmul(left_mat, right_mat):
    return jnp.dot(left_mat, right_mat, preferred_element_type=FLOAT)


def flip(index, mask):
    bit = 1
    while bit <= mask:
        if mask & bit:
            index = index + bit * (1 - 2 * lax.rem(lax.div(index, bit), 2))
        bit *= 2
    return index


def cols(block, size):
    return pl.ds(pl.multiple_of(block * size, size), size)


class _ShapeOnly:
    def __init__(self, shape):
        self.shape = tuple(shape)

    @property
    def at(self):
        return self

    def __getitem__(self, index):
        index = index if isinstance(index, tuple) else (index,)
        shape = []
        for size, i in zip(self.shape, index):
            if isinstance(i, slice):
                shape.append(len(range(*i.indices(size))))
            elif hasattr(i, "size") and hasattr(i, "start"):
                shape.append(i.size)
        return _ShapeOnly(tuple(shape) + self.shape[len(index) :])


class Send(NamedTuple):
    src: Callable
    dst: Callable
    dz: int
    df: int
    after: int | None = None
    planes: tuple | None = None


def only_on(planes, z, do):
    if planes is None:
        do()
        return
    here = z == planes[0]
    for plane in planes[1:]:
        here = jnp.logical_or(here, z == plane)
    pl.when(here)(do)


def exchange(name, cid, arrays, out_shapes, sends, micros):
    n_in, n_out = len(arrays), len(out_shapes)
    peers = sorted({(s.dz, s.df) for s in sends} - {(0, 0)})
    stays = [k for k, s in enumerate(sends) if (s.dz, s.df) == (0, 0)]
    stay_shapes = []

    def probe(*refs):
        for k in stays:
            view = sends[k].src(refs, None, jnp.int32(0), jnp.int32(0))
            stay_shapes.append(view.shape)

    probe(*[_ShapeOnly(a.shape) for a in arrays])

    def kernel(*refs):
        ins, outs = refs[:n_in], refs[n_in : n_in + n_out]
        send_sems, recv_sems = refs[n_in + n_out : n_in + n_out + 2]
        bounce = dict(zip(stays, refs[n_in + n_out + 2 :]))
        z = lax.axis_index("sp")
        f = lax.axis_index("fsdp")
        barrier = pltpu.get_barrier_semaphore()
        for dz, df in peers:
            pl.semaphore_signal(
                barrier, inc=1, device_id=(flip(z, dz), flip(f, df)), device_id_type=MESH
            )
        pl.semaphore_wait(barrier, len(peers))
        copies = []
        for k, s in enumerate(sends):
            src = s.src(ins, outs, z, f)
            dst = s.dst(ins, outs, z, f)
            if (s.dz, s.df) == (0, 0):
                copies.append(
                    (
                        pltpu.make_async_copy(src, bounce[k], recv_sems.at[k]),
                        pltpu.make_async_copy(bounce[k], dst, send_sems.at[k]),
                    )
                )
            else:
                copies.append(
                    pltpu.make_async_remote_copy(
                        src_ref=src,
                        dst_ref=dst,
                        send_sem=send_sems.at[k],
                        recv_sem=recv_sems.at[k],
                        device_id=(flip(z, s.dz), flip(f, s.df)),
                        device_id_type=MESH,
                    )
                )
        arrived = set()

        def arrive(k):
            if k not in arrived:
                arrived.add(k)
                s = sends[k]
                if (s.dz, s.df) == (0, 0):
                    copies[k][1].wait()
                else:
                    only_on(s.planes, flip(z, s.dz), copies[k].wait_recv)

        for k, s in enumerate(sends):
            if k in stays:
                copies[k][0].start()
            elif s.after is None:
                only_on(s.planes, z, copies[k].start)
        for k in stays:
            copies[k][0].wait()
            copies[k][1].start()
        for k, s in enumerate(sends):
            if s.after is not None:
                arrive(s.after)
                copies[k].start()
        for k, s in enumerate(sends):
            if (s.dz, s.df) != (0, 0):
                only_on(s.planes, z, copies[k].wait_send)
            arrive(k)

    result = pl.pallas_call(
        kernel,
        out_shape=[jax.ShapeDtypeStruct(shape, BF16) for shape in out_shapes],
        in_specs=[pl.BlockSpec(memory_space=pl.ANY)] * n_in,
        out_specs=[pl.BlockSpec(memory_space=pl.ANY)] * n_out,
        scratch_shapes=[
            pltpu.SemaphoreType.DMA((len(sends),)),
            pltpu.SemaphoreType.DMA((len(sends),)),
        ]
        + [pltpu.VMEM(shape, BF16) for shape in stay_shapes],
        compiler_params=pltpu.CompilerParams(
            collective_id=cid, has_side_effects=True, vmem_limit_bytes=32 * 1024 * 1024
        ),
        cost_estimate=pl.CostEstimate(
            flops=0, bytes_accessed=int(micros * 3.0e6), transcendentals=0
        ),
        name=name,
    )(*arrays)
    return result


def rows_to_experts(cid, tokens, lanes, pick, plane_experts, parts):
    planes, picked, count = pick.shape
    cap = picked // plane_experts
    arrays = (tokens, lanes)
    widths = [a.shape[1] for a in arrays]
    order = [0, 1, 3, 2] if planes == 4 else list(range(planes))
    early = 2 if planes == 4 else planes - 1
    step = 512

    def kernel(tokens_ref, lanes_ref, pick_ref, rows_ref, lane_rows_ref, *scratch):
        here, chosen = scratch[:2], scratch[2:4]
        z_send, z_recv, row_send, row_recv = scratch[4:]
        ins, outs = (tokens_ref, lanes_ref), (rows_ref, lane_rows_ref)
        z = lax.axis_index("sp")
        f = lax.axis_index("fsdp")
        barrier = pltpu.get_barrier_semaphore()
        for d in range(1, planes):
            pl.semaphore_signal(barrier, inc=1, device_id=(flip(z, d), f), device_id_type=MESH)
        for s in range(1, plane_experts):
            pl.semaphore_signal(
                barrier, inc=1, device_id=(z, flip(f, s * parts)), device_id_type=MESH
            )
        pl.semaphore_wait(barrier, planes + plane_experts - 2)

        def across(d, w):
            if d == 0:
                return pltpu.make_async_copy(ins[w], here[w].at[0], z_recv.at[w])
            return pltpu.make_async_remote_copy(
                src_ref=ins[w],
                dst_ref=here[w].at[d],
                send_sem=z_send.at[2 * d + w],
                recv_sem=z_recv.at[2 * d + w],
                device_id=(flip(z, d), f),
                device_id_type=MESH,
            )

        def onward(d, s, w):
            src = chosen[w].at[d, pl.ds(s * cap, cap)]
            dst = outs[w].at[s, d]
            k = (d * plane_experts + s) * 2 + w
            if s == 0:
                return pltpu.make_async_copy(src, dst, row_recv.at[k])
            return pltpu.make_async_remote_copy(
                src_ref=src,
                dst_ref=dst,
                send_sem=row_send.at[k],
                recv_sem=row_recv.at[k],
                device_id=(z, flip(f, s * parts)),
                device_id_type=MESH,
            )

        for d in order[: early + 1]:
            for w in range(2):
                across(d, w).start()
        for turn, d in enumerate(order):
            for w in range(2):
                if d == 0:
                    across(d, w).wait()
                else:
                    across(d, w).wait_recv()
            if turn == 1:
                for later in order[early + 1 :]:
                    for w in range(2):
                        across(later, w).start()

            def columns(i, carry):
                at = pl.ds(pl.multiple_of(i * step, step), step)
                chosen[0][d, :, at] = jnp.dot(
                    pick_ref[d], here[0][d, :, at], preferred_element_type=FLOAT
                ).astype(BF16)
                return carry

            lax.fori_loop(0, widths[0] // step, columns, 0)
            chosen[1][d] = jnp.dot(
                pick_ref[d], here[1][d], preferred_element_type=FLOAT
            ).astype(BF16)
            for s in range(plane_experts):
                for w in range(2):
                    onward(d, s, w).start()
        for d in range(planes):
            for w in range(2):
                if d:
                    across(d, w).wait_send()
                for s in range(plane_experts):
                    onward(d, s, w).wait()

    hbm = pl.BlockSpec(memory_space=pl.ANY)
    sems = planes * plane_experts * 2
    return pl.pallas_call(
        kernel,
        out_shape=[
            jax.ShapeDtypeStruct((plane_experts, planes, cap, width), BF16) for width in widths
        ],
        in_specs=[hbm, hbm, pl.BlockSpec(memory_space=pltpu.VMEM)],
        out_specs=[hbm, hbm],
        scratch_shapes=[pltpu.VMEM((planes, count, width), BF16) for width in widths]
        + [pltpu.VMEM((planes, picked, width), BF16) for width in widths]
        + [pltpu.SemaphoreType.DMA((2 * planes,))] * 2
        + [pltpu.SemaphoreType.DMA((sems,))] * 2,
        compiler_params=pltpu.CompilerParams(
            collective_id=cid, has_side_effects=True, vmem_limit_bytes=40 * 1024 * 1024
        ),
        cost_estimate=pl.CostEstimate(flops=0, bytes_accessed=int(2.1e8), transcendentals=0),
        name="rows_to_experts",
    )(tokens, lanes, pick)


def rows_from_experts(cid, rows_in, lanes_in, pick, weights):
    planes, picked, count = pick.shape
    plane_experts, _, cap, _ = rows_in.shape
    parts = weights[0].shape[1]
    inner_shape = weights[0].shape[2:]
    widths = (rows_in.shape[3], lanes_in.shape[3])
    order = [2, 3, 1, 0] if planes == 4 else list(range(planes - 1, -1, -1))
    step = 512

    def kernel(rows_ref, lanes_ref, pick_ref, first_ref, second_ref, *rest):
        outs, shards_ref = rest[:2], rest[2]
        back, partial, own, others = rest[3:5], rest[5:7], rest[7], rest[8]
        row_send, row_recv, z_send, z_recv, pair_send, pair_recv, load, w_send, w_recv = rest[9:]
        ins, weight_refs = (rows_ref, lanes_ref), (first_ref, second_ref)
        z = lax.axis_index("sp")
        f = lax.axis_index("fsdp")
        part = lax.rem(f, parts)
        place = lax.div(f, parts)
        barrier = pltpu.get_barrier_semaphore()
        for d in range(1, planes):
            pl.semaphore_signal(barrier, inc=1, device_id=(flip(z, d), f), device_id_type=MESH)
        near = list(range(1, parts)) + [s * parts for s in range(1, plane_experts)]
        for m in near:
            pl.semaphore_signal(barrier, inc=1, device_id=(z, flip(f, m)), device_id_type=MESH)
        pl.semaphore_wait(barrier, planes - 1 + len(near))

        def pair(w, p):
            k = w * (parts - 1) + p - 1
            return pltpu.make_async_remote_copy(
                src_ref=weight_refs[w].at[:, flip(part, p)],
                dst_ref=others.at[p - 1, w],
                send_sem=pair_send.at[k],
                recv_sem=pair_recv.at[k],
                device_id=(z, flip(f, p)),
                device_id_type=MESH,
            )

        def load_own(w):
            return pltpu.make_async_copy(weight_refs[w].at[:, part], own.at[w], load.at[w])

        def home(d, s, w):
            src = ins[w].at[s, d]
            dst = back[w].at[d, pl.ds(s * cap, cap)]
            k = (d * plane_experts + s) * 2 + w
            if s == 0:
                return pltpu.make_async_copy(src, dst, row_recv.at[k])
            return pltpu.make_async_remote_copy(
                src_ref=src,
                dst_ref=dst,
                send_sem=row_send.at[k],
                recv_sem=row_recv.at[k],
                device_id=(z, flip(f, s * parts)),
                device_id_type=MESH,
            )

        def across(d, w):
            src, dst = partial[w].at[d], outs[w].at[d]
            if d == 0:
                return pltpu.make_async_copy(src, dst, z_recv.at[w])
            return pltpu.make_async_remote_copy(
                src_ref=src,
                dst_ref=dst,
                send_sem=z_send.at[2 * d + w],
                recv_sem=z_recv.at[2 * d + w],
                device_id=(flip(z, d), f),
                device_id_type=MESH,
            )

        def to_shard(s, w):
            src, dst = own.at[w, flip(place, s)], shards_ref.at[w, place]
            if s == 0:
                return pltpu.make_async_copy(src, dst, w_recv.at[w])
            return pltpu.make_async_remote_copy(
                src_ref=src,
                dst_ref=dst,
                send_sem=w_send.at[2 * s + w],
                recv_sem=w_recv.at[2 * s + w],
                device_id=(z, flip(f, s * parts)),
                device_id_type=MESH,
            )

        for w in range(2):
            load_own(w).start()
            for p in range(1, parts):
                pair(w, p).start()
        for d in order:
            for s in range(plane_experts):
                for w in range(2):
                    home(d, s, w).start()
        for w in range(2):
            load_own(w).wait()
            for p in range(1, parts):
                pair(w, p).wait()

            def add(i, carry):
                e = lax.div(i, inner_shape[0] // 16)
                at = pl.ds(pl.multiple_of(lax.rem(i, inner_shape[0] // 16) * 16, 16), 16)
                total = own[w, e, at, :].astype(FLOAT)
                for p in range(parts - 1):
                    total = total + others[p, w, e, at, :].astype(FLOAT)
                own[w, e, at, :] = total.astype(BF16)
                return carry

            lax.fori_loop(0, plane_experts * (inner_shape[0] // 16), add, 0)
        for turn, d in enumerate(order):
            for s in range(plane_experts):
                for w in range(2):
                    home(d, s, w).wait()
            if turn == planes - 2:
                for s in range(plane_experts):
                    for w in range(2):
                        to_shard(s, w).start()

            def columns(i, carry):
                at = pl.ds(pl.multiple_of(i * step, step), step)
                partial[0][d, :, at] = contract_rows(pick_ref[d], back[0][d, :, at]).astype(BF16)
                return carry

            lax.fori_loop(0, widths[0] // step, columns, 0)
            partial[1][d] = contract_rows(pick_ref[d], back[1][d]).astype(BF16)
            for w in range(2):
                across(d, w).start()
        for d in range(planes):
            for w in range(2):
                across(d, w).wait()
        for s in range(plane_experts):
            for w in range(2):
                to_shard(s, w).wait()

    hbm = pl.BlockSpec(memory_space=pl.ANY)
    dma = pltpu.SemaphoreType.DMA
    row_count = planes * plane_experts * 2
    return pl.pallas_call(
        kernel,
        out_shape=[jax.ShapeDtypeStruct((planes, count, width), BF16) for width in widths]
        + [jax.ShapeDtypeStruct((2, plane_experts) + inner_shape, BF16)],
        in_specs=[hbm, hbm, pl.BlockSpec(memory_space=pltpu.VMEM), hbm, hbm],
        out_specs=[hbm] * 3,
        scratch_shapes=[pltpu.VMEM((planes, picked, width), BF16) for width in widths]
        + [pltpu.VMEM((planes, count, width), BF16) for width in widths]
        + [
            pltpu.VMEM((2, plane_experts) + inner_shape, BF16),
            pltpu.VMEM((parts - 1, 2, plane_experts) + inner_shape, BF16),
        ]
        + [dma((row_count,))] * 2
        + [dma((2 * planes,))] * 2
        + [dma((2 * (parts - 1),))] * 2
        + [dma((2,))]
        + [dma((2 * plane_experts,))] * 2,
        compiler_params=pltpu.CompilerParams(
            collective_id=cid, has_side_effects=True, vmem_limit_bytes=48 * 1024 * 1024
        ),
        cost_estimate=pl.CostEstimate(flops=0, bytes_accessed=int(2.7e8), transcendentals=0),
        name="rows_from_experts",
    )(rows_in, lanes_in, pick, *weights)


def line_sum(cid, arrays, pieces, blocks, handed):
    n = len(arrays)
    chunks = [
        (k, c * (a.shape[0] // p), a.shape[0] // p)
        for k, (a, p) in enumerate(zip(arrays, pieces))
        for c in range(p)
    ]
    far = blocks.shape[0] - 1
    assert far == 3

    def kernel(*refs):
        ins, blocks_ref, handed_ref = refs[:n], refs[n], refs[n + 1]
        outs, others_ref = refs[n + 2 : 2 * n + 2], refs[2 * n + 2]
        own, got, swapped = (refs[2 * n + 3 + n * i : 2 * n + 3 + n * (i + 1)] for i in range(3))
        mine, theirs = refs[5 * n + 3 : 5 * n + 5]
        load, store, in_s, in_r, swap_s, swap_r, back_s, back_r, far_s, far_r = refs[5 * n + 5 :]
        z = lax.axis_index("sp")
        f = lax.axis_index("fsdp")
        inner = jnp.logical_or(z == 1, z == 2)
        barrier = pltpu.get_barrier_semaphore()
        for d in range(1, far + 1):
            pl.semaphore_signal(barrier, inc=1, device_id=(flip(z, d), f), device_id_type=MESH)
        pl.semaphore_wait(barrier, far)

        def view(refs, c):
            k, start, size = chunks[c]
            return refs[k].at[pl.ds(start, size)]

        def remote(src, dst, send, recv, c, dz):
            return pltpu.make_async_remote_copy(
                src_ref=view(src, c),
                dst_ref=view(dst, c),
                send_sem=send.at[c],
                recv_sem=recv.at[c],
                device_id=(flip(z, dz), f),
                device_id_type=MESH,
            )

        loads = [
            pltpu.make_async_copy(view(ins, c), view(own, c), load.at[c])
            for c in range(len(chunks))
        ]
        stores = [
            pltpu.make_async_copy(view(got, c), view(outs, c), store.at[c])
            for c in range(len(chunks))
        ]

        def block_copy(src, dst, send, recv, d):
            return pltpu.make_async_remote_copy(
                src_ref=src,
                dst_ref=dst,
                send_sem=far_s.at[send],
                recv_sem=far_r.at[recv],
                device_id=(flip(z, d), f),
                device_id_type=MESH,
            )

        near = block_copy(blocks_ref.at[1], others_ref.at[0], 0, 0, 1)
        block_loads = [
            pltpu.make_async_copy(blocks_ref.at[2 + k], mine.at[k], far_r.at[2 + k])
            for k in range(2)
        ] + [
            pltpu.make_async_copy(handed_ref.at[k], theirs.at[k], far_r.at[4 + k])
            for k in range(2)
        ]
        beyond = [block_copy(mine.at[k], others_ref.at[1], 1 + k, 1, 2 + k) for k in range(2)]
        inwards = [remote(own, got, in_s, in_r, c, 1) for c in range(len(chunks))]
        swaps = [remote(own, swapped, swap_s, swap_r, c, 3) for c in range(len(chunks))]
        backs = [remote(got, got, back_s, back_r, c, 1) for c in range(len(chunks))]
        for copy in loads:
            copy.start()

        def add(left, right, to, c):
            k, start, size = chunks[c]
            step = 16

            def rows(i, carry):
                at = pl.ds(pl.multiple_of(start + i * step, step), step)
                total = left[k][at, :].astype(FLOAT) + right[k][at, :].astype(FLOAT)
                to[k][at, :] = total.astype(BF16)
                return carry

            lax.fori_loop(0, size // step, rows, 0)

        def pass_on(k):
            def rows(i, carry):
                at = pl.ds(pl.multiple_of(i * 16, 16), 16)
                total = mine[k, at, :].astype(FLOAT) + theirs[1 - k, at, :].astype(FLOAT)
                mine[k, at, :] = total.astype(BF16)
                return carry

            lax.fori_loop(0, blocks.shape[1] // 16, rows, 0)
            beyond[k].start()

        near.start()

        @pl.when(jnp.logical_not(inner))
        def _():
            for c in range(len(chunks)):
                loads[c].wait()
                inwards[c].start()
            for c in range(len(chunks)):
                backs[c].wait_recv()
                stores[c].start()
            for c in range(len(chunks)):
                inwards[c].wait_send()
                stores[c].wait()

        @pl.when(inner)
        def _():
            for copy in block_loads:
                copy.start()
            for copy in block_loads:
                copy.wait()
            for k in range(2):
                pass_on(k)
            for c in range(len(chunks) + 1):
                if c < len(chunks):
                    loads[c].wait()
                    inwards[c].wait_recv()
                    add(own, got, own, c)
                    swaps[c].start()
                if c:
                    swaps[c - 1].wait_recv()
                    add(own, swapped, got, c - 1)
                    backs[c - 1].start()
                    stores[c - 1].start()
            for c in range(len(chunks)):
                swaps[c].wait_send()
                backs[c].wait_send()
                stores[c].wait()

            for copy in beyond:
                copy.wait_send()

        near.wait()
        beyond[0].wait_recv()

    hbm = pl.BlockSpec(memory_space=pl.ANY)
    buffers = [pltpu.VMEM(a.shape, BF16) for a in arrays]
    count = len(chunks)
    return pl.pallas_call(
        kernel,
        out_shape=[jax.ShapeDtypeStruct(a.shape, BF16) for a in arrays]
        + [jax.ShapeDtypeStruct((2,) + blocks.shape[1:], BF16)],
        in_specs=[hbm] * (n + 2),
        out_specs=[hbm] * (n + 1),
        scratch_shapes=buffers * 3
        + [pltpu.VMEM((2,) + blocks.shape[1:], BF16)] * 2
        + [pltpu.SemaphoreType.DMA((count,))] * 8
        + [pltpu.SemaphoreType.DMA((6,))] * 2,
        compiler_params=pltpu.CompilerParams(
            collective_id=cid, has_side_effects=True, vmem_limit_bytes=40 * 1024 * 1024
        ),
        cost_estimate=pl.CostEstimate(flops=0, bytes_accessed=int(4.0e8), transcendentals=0),
        name="line_sum",
    )(*arrays, blocks, handed)


def body(
    tokens,
    expert_ids,
    attn_gain,
    query_weight,
    key_weight,
    value_weight,
    q_gain,
    k_gain,
    output_weight,
    ffn_gain,
    router_weight,
    w_gate,
    w_up,
    w_down,
    cotangent,
):
    nsp = lax.axis_size("sp")
    nf = lax.axis_size("fsdp")
    z = lax.axis_index("sp")
    f = lax.axis_index("fsdp")
    rows = tokens.shape[1]
    width = tokens.shape[2]
    shard = width // nf
    n_heads, kv_heads, head_dim = QUERY_HEADS, KEY_VALUE_HEADS, HEAD_SIZE
    my_heads = n_heads // nf
    rep = nf // kv_heads
    q_cols = my_heads * head_dim
    qkv_cols = q_cols + 2 * head_dim
    score_scale = 1.0 / math.sqrt(head_dim)
    n_experts = w_gate.shape[0]
    hidden_size = w_gate.shape[2]
    hid_shard = w_down.shape[1]
    plane_experts = n_experts // nsp
    parts = nf // plane_experts
    cap = CAP
    seqs = nf
    part = lax.rem(f, parts)
    place = lax.div(f, parts)
    expert = z * plane_experts + place

    def swap_f(block, mask):
        return lax.ppermute(block, "fsdp", [(i, i ^ mask) for i in range(nf)])

    def swap_z(block, mask):
        return lax.ppermute(block, "sp", [(i, i ^ mask) for i in range(nsp)])

    small = jnp.concatenate(
        [
            attn_gain.astype(BF16),
            ffn_gain.astype(BF16),
            q_gain.astype(BF16),
            k_gain.astype(BF16),
            router_weight.astype(BF16).reshape(-1),
        ]
    )
    small_rows = 16
    small = jnp.pad(small, (0, small_rows * width - small.shape[0])).reshape(small_rows, width)
    x_pay = jnp.concatenate([tokens[0], small], axis=0)
    pay_rows = rows + small_rows
    query_b = query_weight.astype(BF16)
    key_b = key_weight.astype(BF16)
    value_b = value_weight.astype(BF16)
    routes = expert_ids[0]
    expert_iota = jnp.arange(n_experts, dtype=jnp.int32)
    routed = jnp.any(routes[:, :, None] == expert_iota[None, None, :], axis=1)
    dy_pay = jnp.concatenate(
        [
            cotangent[0],
            routed.astype(BF16),
            jnp.zeros((rows, LANES - n_experts), BF16),
        ],
        axis=1,
    )
    wide = width + LANES

    def plane_cast(weight):
        return lax.dynamic_slice_in_dim(weight, z * plane_experts, plane_experts, 0).astype(BF16)

    gate_up_pay = jnp.stack([plane_cast(w_gate), plane_cast(w_up)], axis=1)
    down_pay = plane_cast(w_down)

    sends = []
    for m in range(0, nf, 2):
        sends.append(
            Send(
                lambda i, o, z, f, m=m: i[0],
                lambda i, o, z, f: o[0].at[f],
                0,
                m,
            )
        )
    for m in range(0, nf, 2):
        if m == 0:
            sends.append(
                Send(lambda i, o, z, f: i[0], lambda i, o, z, f: o[0].at[f], 0, 1)
            )
        else:
            sends.append(
                Send(
                    lambda i, o, z, f, m=m: o[0].at[flip(f, m)],
                    lambda i, o, z, f, m=m: o[0].at[flip(f, m)],
                    0,
                    1,
                    m // 2,
                )
            )
    for m in range(0, nf, rep):
        for w in range(2):
            sends.append(
                Send(
                    lambda i, o, z, f, m=m, w=w: i[2 + w].at[
                        :, cols(lax.div(flip(f, m), rep), head_dim)
                    ],
                    lambda i, o, z, f, w=w: o[1].at[
                        cols(f, shard), pl.ds(q_cols + w * head_dim, head_dim)
                    ],
                    0,
                    m,
                )
            )
            for p in range(1, rep):
                view = lambda i, o, z, f, m=m, w=w: o[1].at[
                    cols(flip(f, m), shard), pl.ds(q_cols + w * head_dim, head_dim)
                ]
                if m == 0:
                    sends.append(
                        Send(
                            lambda i, o, z, f, w=w: i[2 + w].at[:, cols(lax.div(f, rep), head_dim)],
                            view,
                            0,
                            p,
                        )
                    )
                else:
                    sends.append(Send(view, view, 0, p, len(sends) - p))
    for m in range(nf):
        sends.append(
            Send(
                lambda i, o, z, f, m=m: i[1].at[:, cols(flip(f, m), q_cols)],
                lambda i, o, z, f: o[1].at[cols(f, shard), pl.ds(0, q_cols)],
                0,
                m,
            )
        )
    for m in range(nsp):
        sends.append(
            Send(lambda i, o, z, f: i[4], lambda i, o, z, f, m=m: o[2].at[m], m, 0)
        )
    x_all, w_qkv, dy_z = exchange(
        "gather_inputs",
        0,
        (x_pay, query_b, key_b, value_b, dy_pay),
        ((nf, pay_rows, width), (width, qkv_cols), (nsp, rows, wide)),
        sends,
        65,
    )

    own_experts = z * plane_experts + jnp.bitwise_xor(
        place, jnp.arange(plane_experts, dtype=jnp.int32)
    )
    own_hot = (expert_iota[:, None] == own_experts[None, :]).astype(FLOAT)
    routed_z = lax.dot_general(
        own_hot,
        dy_z[:, :, width : width + n_experts].astype(FLOAT),
        (((0,), (2,)), ((), ())),
        preferred_element_type=FLOAT,
    ).transpose(1, 0, 2)
    earlier = jnp.triu(jnp.ones((rows, rows), FLOAT), 1)
    rank = jnp.dot(
        routed_z.reshape(nsp * plane_experts, rows), earlier, preferred_element_type=FLOAT
    ).reshape(nsp, plane_experts, rows)
    rank = rank * routed_z + (routed_z - 1.0)
    pick = (
        rank[:, :, None, :] == jnp.arange(cap, dtype=FLOAT)[None, None, :, None]
    ).astype(BF16)
    pick = pick.reshape(nsp, plane_experts * cap, rows)

    x_all, gate_up_pay = lax.optimization_barrier((x_all, gate_up_pay))
    by_expert = pick.reshape(nsp, plane_experts, cap, rows)
    gate_up_pieces, dy_pieces = [], []
    for s in range(plane_experts):
        weights = lax.dynamic_index_in_dim(gate_up_pay, flip(place, s), 0, keepdims=False)
        dy_rows = jnp.einsum(
            "drt,dtc->drc", by_expert[:, s], dy_z[:, :, :width], preferred_element_type=FLOAT
        )
        dy_rows = dy_rows.astype(BF16).reshape(nsp * cap, width)
        if s and s == plane_experts - 1:
            both = jnp.concatenate([dy_rows, weights.reshape(-1, width)], axis=0)
            both = swap_f(both, s * parts)
            dy_rows = both[: nsp * cap]
            weights = both[nsp * cap :].reshape(2, shard, hidden_size)
        elif s:
            weights = swap_f(weights, s * parts)
            dy_rows = swap_f(dy_rows, s * parts)
        gate_up_pieces.append(weights)
        dy_pieces.append(dy_rows)
    dy_in = jnp.concatenate(dy_pieces, axis=0)

    small_all = x_all[:, rows:, :].reshape(nf, small_rows * width)
    at = 0
    pieces = []
    for size in (shard, shard, head_dim // nf, head_dim // nf, shard * n_experts):
        pieces.append(small_all[:, at : at + size])
        at += size
    g_attn = pieces[0].reshape(width).astype(FLOAT)
    g_ffn = pieces[1].reshape(width).astype(FLOAT)
    g_query = pieces[2].reshape(head_dim).astype(FLOAT)
    g_key = pieces[3].reshape(head_dim).astype(FLOAT)
    wr_b = pieces[4].reshape(width, n_experts)

    xn_b = (
        rms_norm(x_all[:, :rows, :].astype(FLOAT), g_attn).astype(BF16).reshape(seqs * rows, width)
    )
    qkv_lin = matmul(xn_b, w_qkv)

    def split_heads(flat):
        flat = flat.reshape(seqs, rows, -1)
        return jnp.stack(
            [
                flat[:, :, h * head_dim : (h + 1) * head_dim]
                for h in range(flat.shape[2] // head_dim)
            ],
            axis=1,
        )

    def join_heads(split):
        joined = jnp.concatenate([split[:, h] for h in range(split.shape[1])], axis=2)
        return joined.reshape(seqs * rows, -1)

    q_lin = split_heads(qkv_lin[:, :q_cols])
    k_lin = split_heads(qkv_lin[:, q_cols : q_cols + head_dim])
    v_b = qkv_lin[:, q_cols + head_dim :].astype(BF16)
    half_dim = head_dim // 2
    inverse_freq = THETA ** (-(jnp.arange(half_dim, dtype=FLOAT) * 2.0 / head_dim))
    positions = (z * rows + jnp.arange(rows, dtype=jnp.int32)).astype(FLOAT)
    angles = positions[:, None] * inverse_freq[None, :]
    cosine = jnp.cos(angles)[None, None]
    sine_part = jnp.sin(angles)[None, None]

    def prep_heads(linear, gain_vec):
        return rotate(rms_norm(linear, gain_vec), cosine, sine_part)

    q_rows = prep_heads(q_lin, g_query).astype(BF16)
    k_b = join_heads(prep_heads(k_lin, g_key).astype(BF16))

    kv_pay = jnp.concatenate([k_b, v_b], axis=1)
    piece = seqs * rows // rep
    sends = []
    for d in range(nsp):
        sends.append(
            Send(
                lambda i, o, z, f: i[0].at[pl.ds(lax.rem(f, rep) * piece, piece)],
                lambda i, o, z, f, d=d: o[0].at[d, pl.ds(lax.rem(f, rep) * piece, piece)],
                d,
                0,
            )
        )
    for d in range(nsp):
        for p in range(1, rep):
            sends.append(
                Send(
                    lambda i, o, z, f, d=d: o[0].at[d, pl.ds(lax.rem(f, rep) * piece, piece)],
                    lambda i, o, z, f, d=d: o[0].at[d, pl.ds(lax.rem(f, rep) * piece, piece)],
                    0,
                    p,
                    d,
                )
            )
    (kv_z,) = exchange(
        "gather_keys", 1, (kv_pay,), ((nsp, seqs * rows, 2 * head_dim),), sends, 24
    )
    kv_seq = kv_z.reshape(nsp, seqs, rows, 2 * head_dim).transpose(1, 0, 2, 3)
    kv_seq = kv_seq.reshape(seqs, nsp * rows, 2 * head_dim)
    keys = kv_seq[:, :, :head_dim]
    values = kv_seq[:, :, head_dim:]

    plane_of = jnp.bitwise_xor(jnp.arange(nsp, dtype=jnp.int32), z)
    key_pos = (plane_of[:, None] * rows + jnp.arange(rows, dtype=jnp.int32)[None, :]).reshape(-1)
    query_pos = z * rows + jnp.arange(rows, dtype=jnp.int32)
    causal = key_pos[None, :] <= query_pos[:, None]
    scores = (
        jnp.einsum("nhqd,nkd->nhqk", q_rows, keys, preferred_element_type=FLOAT) * score_scale
    )
    expo = jnp.where(causal[None, None], jnp.exp(scores), 0.0)
    probs = (expo / jnp.sum(expo, axis=3, keepdims=True)).astype(BF16)
    o_rows = jnp.einsum("nhqk,nkd->nhqd", probs, values, preferred_element_type=FLOAT)
    o_mat = join_heads(o_rows.astype(BF16))
    wo_b = output_weight.astype(BF16)

    def pair_then_plane(partial, name, cid, more=(), more_shapes=(), more_sends=()):
        split = partial.astype(BF16).reshape(nf // 2, 2, rows, width)
        (other,) = exchange(
            name + "_pair",
            cid,
            (split,),
            ((nf // 2, rows, width),),
            [Send(lambda i, o, z, f: i[0].at[:, 1 - lax.rem(f, 2)], lambda i, o, z, f: o[0], 0, 1)],
            8,
        )
        own = lax.dynamic_index_in_dim(split, lax.rem(f, 2), 1, keepdims=False)
        summed = (own.astype(FLOAT) + other.astype(FLOAT)).astype(BF16)
        sends = [
            Send(
                lambda i, o, z, f, j=j: i[0].at[flip(lax.div(f, 2), j)],
                lambda i, o, z, f, j=j: o[0].at[j],
                0,
                2 * j,
            )
            for j in range(nf // 2)
        ]
        blocks, *rest = exchange(
            name + "_plane",
            cid + 1,
            (summed, *more),
            ((nf // 2, rows, width), *more_shapes),
            sends + list(more_sends),
            27,
        )
        return jnp.sum(blocks.astype(FLOAT), axis=0), rest

    sends = []
    for s in range(plane_experts):
        for p in range(parts):
            sends.append(
                Send(
                    lambda i, o, z, f, s=s: i[1 + s],
                    lambda i, o, z, f, s=s: o[1].at[:, flip(f, s * parts)],
                    0,
                    p,
                )
            )
    branch, (gate_up_all,) = pair_then_plane(
        matmul(o_mat, wo_b), "out_sum", 3, gate_up_pieces, ((2, nf, shard, hidden_size),), sends
    )
    wg_b = gate_up_all[0].reshape(width, hidden_size)
    wu_b = gate_up_all[1].reshape(width, hidden_size)
    x_rows = tokens[0].astype(FLOAT)
    mid_rows = x_rows + branch
    hn_b = rms_norm(mid_rows, g_ffn).astype(BF16)
    logits = matmul(hn_b, wr_b)
    logits = jnp.where(routed, logits, -1e30)
    expo = jnp.where(routed, jnp.exp(logits - jnp.max(logits, axis=1, keepdims=True)), 0.0)
    gates = expo / jnp.sum(expo, axis=1, keepdims=True)

    def two_parts(exact):
        high = exact.astype(BF16)
        return high, (exact - high.astype(FLOAT)).astype(BF16)

    gate_high, gate_low = two_parts(gates)
    gate_lanes = jnp.concatenate(
        [gate_high, gate_low, jnp.zeros((rows, LANES - 2 * n_experts), BF16)], axis=1
    )
    hn_rows, gate_rows = rows_to_experts(5, hn_b, gate_lanes, pick, plane_experts, parts)
    hn_rows, down_pay = lax.optimization_barrier((hn_rows, down_pay))
    down_pieces = []
    for s in range(plane_experts):
        block = lax.dynamic_index_in_dim(down_pay, flip(place, s), 0, keepdims=False)
        down_pieces.append(swap_f(block, s * parts) if s else block)

    n_rows = plane_experts * nsp * cap
    hn_in = hn_rows.reshape(n_rows, width)
    hot = (jnp.arange(n_experts, dtype=jnp.int32) == expert).astype(FLOAT)
    tail = gate_rows.reshape(n_rows, LANES)[:, : 2 * n_experts].astype(FLOAT)
    row_gate = jnp.sum(
        (tail[:, :n_experts] + tail[:, n_experts:]) * hot[None, :], axis=1, keepdims=True
    )
    gate_pre = matmul(hn_in, wg_b)
    up_pre = matmul(hn_in, wu_b)
    sigma = jax.nn.sigmoid(gate_pre)
    act_f = gate_pre * sigma
    hidden = (act_f * up_pre).astype(BF16)
    dy_f = dy_in.astype(FLOAT)
    d_result = (row_gate * dy_f).astype(BF16)

    def by_shard(full, inner):
        return full.astype(BF16).reshape((plane_experts, parts) + inner)

    def pair_total(own, others):
        total = lax.dynamic_index_in_dim(own, part, 1, keepdims=False).astype(FLOAT)
        for other in others:
            total = total + other.astype(FLOAT)
        return total.astype(BF16)

    d_down = by_shard(contract_rows(hidden, d_result), (hid_shard, width))
    d_down, down_pieces = lax.optimization_barrier((d_down, down_pieces))
    d_down = pair_total(
        d_down,
        [
            swap_f(lax.dynamic_index_in_dim(d_down, flip(part, p), 1, keepdims=False), p)
            for p in range(1, parts)
        ],
    )
    d_down = [
        swap_f(lax.dynamic_index_in_dim(d_down, flip(place, s), 0, keepdims=False), s * parts)
        if s
        else lax.dynamic_index_in_dim(d_down, place, 0, keepdims=False)
        for s in range(plane_experts)
    ]
    down_pieces = jnp.stack(down_pieces)
    down_pieces = jnp.stack(
        [swap_f(down_pieces, p) if p else down_pieces for p in range(parts)], axis=1
    ).reshape(nf, hid_shard, width)
    wd_b = jnp.take(
        down_pieces, jnp.bitwise_xor(jnp.arange(nf, dtype=jnp.int32), f), axis=0, mode="clip"
    ).reshape(hidden_size, width)
    result = matmul(hidden, wd_b)
    row_dgate = jnp.sum(result * dy_f, axis=1, keepdims=True)
    weighted = (row_gate * result).astype(BF16)
    d_hidden = contract_cols(d_result, wd_b)
    d_gate_pre = (d_hidden * up_pre * sigma * (1.0 + gate_pre * (1.0 - sigma))).astype(BF16)
    d_up_pre = (d_hidden * act_f).astype(BF16)
    d_down, d_gate_pre, d_up_pre = lax.optimization_barrier((d_down, d_gate_pre, d_up_pre))
    in_order = jnp.bitwise_xor(jnp.arange(plane_experts, dtype=jnp.int32), place)
    d_down = jnp.take(jnp.stack(d_down), in_order, axis=0, mode="clip")
    all_down = lax.all_gather(d_down, "sp")
    d_in = (contract_cols(d_gate_pre, wg_b) + contract_cols(d_up_pre, wu_b)).astype(BF16)
    dgate_high, dgate_low = two_parts(row_dgate * hot[None, :])
    dgate_lanes = jnp.concatenate(
        [dgate_high, dgate_low, jnp.zeros((n_rows, LANES - 2 * n_experts), BF16)], axis=1
    )

    d_weights = (
        by_shard(contract_rows(hn_in, d_gate_pre), (shard, hidden_size)),
        by_shard(contract_rows(hn_in, d_up_pre), (shard, hidden_size)),
    )

    d_home, dgate_home, shards = rows_from_experts(
        7,
        d_in.reshape(plane_experts, nsp, cap, width),
        dgate_lanes.reshape(plane_experts, nsp, cap, LANES),
        pick,
        d_weights,
    )

    def combine(returned):
        flat = returned.reshape(nsp, plane_experts * cap, returned.shape[3])
        return jnp.einsum("drt,drc->dtc", pick, flat, preferred_element_type=FLOAT).astype(BF16)

    all_gate_up = lax.all_gather(shards, "sp")
    d_home = jnp.sum(d_home.astype(FLOAT), axis=0)
    tail = jnp.sum(dgate_home.astype(FLOAT), axis=0)
    d_gates = tail[:, :n_experts] + tail[:, n_experts : 2 * n_experts]
    d_logits = gates * (d_gates - jnp.sum(gates * d_gates, axis=1, keepdims=True))
    d_router = jnp.dot(hn_b.astype(FLOAT).T, d_logits, precision=HIGH_PRECISION)
    d_hn = d_home + jnp.dot(d_logits, wr_b.astype(FLOAT).T, precision=HIGH_PRECISION)
    grad_out = cotangent[0].astype(FLOAT)
    unused, ffn_pull = jax.vjp(rms_norm, mid_rows, g_ffn)
    d_mid_norm, d_ffn_gain = ffn_pull(d_hn)
    d_mid = grad_out + d_mid_norm

    d_attn_b = d_mid.astype(BF16)
    sends = [
        Send(lambda i, o, z, f: i[0], lambda i, o, z, f: o[0].at[f], 0, m)
        for m in range(0, nf, 2)
    ]
    for m in range(0, nf, 2):
        if m == 0:
            sends.append(Send(lambda i, o, z, f: i[0], lambda i, o, z, f: o[0].at[f], 0, 1))
        else:
            sends.append(
                Send(
                    lambda i, o, z, f, m=m: o[0].at[flip(f, m)],
                    lambda i, o, z, f, m=m: o[0].at[flip(f, m)],
                    0,
                    1,
                    m // 2,
                )
            )
    (da_all,) = exchange("gather_grads", 9, (d_attn_b,), ((nf, rows, width),), sends, 30)
    da_all = da_all.reshape(seqs * rows, width)
    d_wo = contract_rows(o_mat, da_all)
    d_o = split_heads(contract_cols(da_all, wo_b).astype(BF16))
    d_val = jnp.einsum("nhqk,nhqd->nkd", probs, d_o, preferred_element_type=FLOAT)
    d_probs = jnp.einsum("nhqd,nkd->nhqk", d_o, values, preferred_element_type=FLOAT)
    probs_f = probs.astype(FLOAT)
    d_scores = (
        probs_f * (d_probs - jnp.sum(probs_f * d_probs, axis=3, keepdims=True))
    ).astype(BF16)
    dq = (
        jnp.einsum("nhqk,nkd->nhqd", d_scores, keys, preferred_element_type=FLOAT) * score_scale
    ).astype(BF16)
    d_key = (
        jnp.einsum("nhqk,nhqd->nkd", d_scores, q_rows, preferred_element_type=FLOAT) * score_scale
    )
    d_kv = jnp.concatenate([d_key, d_val], axis=2).astype(BF16)
    d_kv = d_kv.reshape(seqs, nsp, rows, 2 * head_dim).transpose(1, 0, 2, 3)
    d_kv = d_kv.reshape(nsp, seqs * rows, 2 * head_dim)
    d_kv, all_down = lax.optimization_barrier((d_kv, all_down))
    grad_down = all_down.astype(FLOAT).reshape(n_experts, hid_shard, width)
    d_kv = d_kv.reshape(nsp, rep, piece, 2 * head_dim)
    (others,) = exchange(
        "key_grads_group",
        11,
        (d_kv,),
        ((rep - 1, nsp, piece, 2 * head_dim),),
        [
            Send(
                lambda i, o, z, f, p=p: i[0].at[:, flip(lax.rem(f, rep), p)],
                lambda i, o, z, f, p=p: o[0].at[p - 1],
                0,
                p,
            )
            for p in range(1, rep)
        ],
        6,
    )
    d_kv = lax.dynamic_index_in_dim(d_kv, lax.rem(f, rep), 1, keepdims=False)
    d_kv = (d_kv.astype(FLOAT) + jnp.sum(others.astype(FLOAT), axis=0)).astype(BF16)
    sends = [
        Send(lambda i, o, z, f, d=d: i[0].at[d], lambda i, o, z, f, d=d: o[0].at[d - 1], d, 0)
        for d in range(1, nsp)
    ]
    for s in range(plane_experts):
        sends.append(
            Send(
                lambda i, o, z, f, s=s: i[1].at[s],
                lambda i, o, z, f, s=s: o[1].at[:, s],
                0,
                s * parts,
            )
        )
    others, out_back = exchange(
        "key_grads_planes",
        10,
        (d_kv, weighted.reshape(plane_experts, nsp, cap, width)),
        ((nsp - 1, piece, 2 * head_dim), (nsp, plane_experts, cap, width)),
        sends,
        60,
    )
    out_blocks = combine(out_back)
    d_kv = (d_kv[0].astype(FLOAT) + jnp.sum(others.astype(FLOAT), axis=0)).astype(BF16)
    (d_kv,) = exchange(
        "key_grads_share",
        15,
        (d_kv,),
        ((rep, piece, 2 * head_dim),),
        [
            Send(lambda i, o, z, f: i[0], lambda i, o, z, f: o[0].at[lax.rem(f, rep)], 0, p)
            for p in range(rep)
        ],
        6,
    )
    d_kv = d_kv.reshape(seqs * rows, 2 * head_dim).astype(FLOAT)
    dq, grad_down = lax.optimization_barrier((dq, grad_down))
    unused, q_pull = jax.vjp(prep_heads, q_lin, g_query)
    d_q_lin, d_q_gain = q_pull(dq.astype(FLOAT))
    unused, k_pull = jax.vjp(prep_heads, k_lin, g_key)
    d_k_lin, d_k_gain = k_pull(d_kv[:, :head_dim].reshape(seqs, 1, rows, head_dim))
    dq_b = join_heads(d_q_lin.astype(BF16))
    dk_b = join_heads(d_k_lin.astype(BF16))
    dv_b = d_kv[:, head_dim:].astype(BF16)
    d_qkv = jnp.concatenate([dq_b, dk_b, dv_b], axis=1)
    share = 1.0 / rep
    d_qkv_shared = jnp.concatenate([dq_b, dk_b * BF16(share), dv_b * BF16(share)], axis=1)
    d_w_qkv = contract_rows(xn_b, d_qkv).astype(BF16)
    d_xn, unused = pair_then_plane(contract_cols(d_qkv_shared, w_qkv), "input_sum", 13)
    unused, attn_pull = jax.vjp(rms_norm, x_rows, g_attn)
    d_x_norm, d_attn_gain = attn_pull(d_xn)
    grad_tokens = (d_mid + d_x_norm)[None]

    smalls = jnp.concatenate(
        [
            d_attn_gain.reshape(nf, shard),
            d_ffn_gain.reshape(nf, shard),
            d_q_gain.reshape(nf, head_dim // nf),
            (d_k_gain * share).reshape(nf, head_dim // nf),
            d_router.reshape(nf, shard * n_experts),
        ],
        axis=1,
    ).astype(BF16)
    small_size = smalls.shape[1]
    small_cols = pl.cdiv(small_size, kv_heads * head_dim) * kv_heads * head_dim // small_rows
    small_cols = pl.cdiv(small_cols, LANES) * LANES
    smalls = jnp.pad(smalls, ((0, 0), (0, small_rows * small_cols - small_size)))
    kv_cols = kv_heads * head_dim
    sends = []
    for m in range(nf):
        sends.append(
            Send(
                lambda i, o, z, f, m=m: i[0].at[cols(flip(f, m), shard), pl.ds(0, q_cols)],
                lambda i, o, z, f: o[0].at[:, cols(f, q_cols)],
                0,
                m,
            )
        )
        sends.append(
            Send(lambda i, o, z, f, m=m: i[1].at[flip(f, m)], lambda i, o, z, f: o[2].at[f], 0, m)
        )
    for m in range(0, nf, rep):
        for w in range(2):
            sends.append(
                Send(
                    lambda i, o, z, f, m=m, w=w: i[0].at[
                        cols(flip(f, m), shard), pl.ds(q_cols + w * head_dim, head_dim)
                    ],
                    lambda i, o, z, f, w=w: o[1].at[
                        pl.ds(w * shard, shard), cols(lax.div(f, rep), head_dim)
                    ],
                    0,
                    m,
                )
            )
    if nsp == 4:
        sends.append(
            Send(
                lambda i, o, z, f: i[2].at[pl.ds(2, 2)],
                lambda i, o, z, f: o[3],
                1,
                0,
                None,
                (0, 3),
            )
        )
    d_wq, d_wkv, small_shard, handed = exchange(
        "head_grads_to_shards",
        12,
        (d_w_qkv, smalls.reshape(nf, small_rows, small_cols), out_blocks),
        (
            (shard, n_heads * head_dim),
            (2 * shard, kv_cols),
            (nf, small_rows, small_cols),
            (2, rows, width),
        ),
        sends,
        36,
    )
    small_sum = jnp.sum(small_shard.astype(FLOAT), axis=0).astype(BF16)
    if nsp == 4:
        sum_q, sum_out, sum_kv, small_sum, out_others = line_sum(
            16, (d_wq, d_wo.astype(BF16), d_wkv, small_sum), (4, 4, 1, 1), out_blocks, handed
        )
        out_others = [out_others[d] for d in range(2)]
    else:
        sum_q, sum_out, sum_kv, small_sum = lax.psum(
            (d_wq, d_wo.astype(BF16), d_wkv, small_sum), "sp"
        )
        out_others = [swap_z(out_blocks[d], d) for d in range(1, nsp)]
    moe_sum = out_blocks[0].astype(FLOAT)
    for block in out_others:
        moe_sum = moe_sum + block.astype(FLOAT)
    mixed = (mid_rows + moe_sum).astype(BF16)[None]
    sum_out = sum_out.astype(FLOAT)
    sum_q = sum_q.astype(FLOAT)
    sum_kv = sum_kv.astype(FLOAT)
    small_sum = small_sum.astype(FLOAT).reshape(-1)
    at = 0
    pieces = []
    for size in (shard, shard, head_dim // nf, head_dim // nf, shard * n_experts):
        pieces.append(small_sum[at : at + size])
        at += size
    grad_gate = all_gate_up[:, 0].astype(FLOAT).reshape(n_experts, shard, hidden_size)
    all_gate_up, grad_gate = lax.optimization_barrier((all_gate_up, grad_gate))
    grad_up = all_gate_up[:, 1].astype(FLOAT).reshape(n_experts, shard, hidden_size)
    return (
        mixed,
        grad_tokens,
        pieces[0],
        sum_q,
        sum_kv[:shard],
        sum_kv[shard : 2 * shard],
        pieces[2],
        pieces[3],
        sum_out,
        pieces[1],
        pieces[4].reshape(shard, n_experts),
        grad_gate,
        grad_up,
        grad_down,
    )


def solution(mesh):
    by_token = P("fsdp", "sp", None)
    by_row = P("fsdp", None)
    by_inner = P(None, "fsdp", None)
    in_specs = (
        by_token,
        by_token,
        P("fsdp"),
        by_row,
        by_row,
        by_row,
        P("fsdp"),
        P("fsdp"),
        by_row,
        P("fsdp"),
        by_row,
        by_inner,
        by_inner,
        by_inner,
        by_token,
    )
    out_specs = (
        by_token,
        by_token,
        P("fsdp"),
        by_row,
        by_row,
        by_row,
        P("fsdp"),
        P("fsdp"),
        by_row,
        P("fsdp"),
        by_row,
        by_inner,
        by_inner,
        by_inner,
    )
    return jax.shard_map(body, mesh=mesh, in_specs=in_specs, out_specs=out_specs, check_vma=False)
```

```python
import math
from typing import Callable, NamedTuple

import jax
import jax.numpy as jnp
from jax import lax
from jax.experimental import pallas as pl
from jax.experimental.pallas import tpu as pltpu
from jax.sharding import PartitionSpec as P

QUERY_HEADS = 32
KEY_VALUE_HEADS = 4
HEAD_SIZE = 128
CAP = 80
LANES = 128

EPS = 1e-06
THETA = 1000000.0
HIGH_PRECISION = lax.Precision.HIGHEST
BF16 = jnp.bfloat16
FLOAT = jnp.float32
MESH = pl.DeviceIdType.MESH


def rms_norm(values_in, gain_vec):
    return (
        values_in
        * lax.rsqrt(jnp.mean(values_in * values_in, axis=-1, keepdims=True) + EPS)
        * gain_vec
    )


def rotate(values_in, cosine, sine_part):
    half_dim = values_in.shape[-1] // 2
    first_half = values_in[..., :half_dim]
    second = values_in[..., half_dim:]
    return jnp.concatenate(
        [first_half * cosine - second * sine_part, second * cosine + first_half * sine_part],
        axis=-1,
    )


def contract_rows(left_mat, right_mat):
    return lax.dot_general(
        left_mat, right_mat, (((0,), (0,)), ((), ())), preferred_element_type=FLOAT
    )


def contract_cols(left_mat, right_mat):
    return lax.dot_general(
        left_mat, right_mat, (((1,), (1,)), ((), ())), preferred_element_type=FLOAT
    )


def matmul(left_mat, right_mat):
    return jnp.dot(left_mat, right_mat, preferred_element_type=FLOAT)


def flip(index, mask):
    bit = 1
    while bit <= mask:
        if mask & bit:
            index = index + bit * (1 - 2 * lax.rem(lax.div(index, bit), 2))
        bit *= 2
    return index


def cols(block, size):
    return pl.ds(pl.multiple_of(block * size, size), size)


class _ShapeOnly:
    def __init__(self, shape):
        self.shape = tuple(shape)

    @property
    def at(self):
        return self

    def __getitem__(self, index):
        index = index if isinstance(index, tuple) else (index,)
        shape = []
        for size, i in zip(self.shape, index):
            if isinstance(i, slice):
                shape.append(len(range(*i.indices(size))))
            elif hasattr(i, "size") and hasattr(i, "start"):
                shape.append(i.size)
        return _ShapeOnly(tuple(shape) + self.shape[len(index) :])


class Send(NamedTuple):
    src: Callable
    dst: Callable
    dz: int
    df: int
    after: int | None = None
    planes: tuple | None = None


def only_on(planes, z, do):
    if planes is None:
        do()
        return
    here = z == planes[0]
    for plane in planes[1:]:
        here = jnp.logical_or(here, z == plane)
    pl.when(here)(do)


def exchange(name, cid, arrays, out_shapes, sends, micros):
    n_in, n_out = len(arrays), len(out_shapes)
    peers = sorted({(s.dz, s.df) for s in sends} - {(0, 0)})
    stays = [k for k, s in enumerate(sends) if (s.dz, s.df) == (0, 0)]
    stay_shapes = []

    def probe(*refs):
        for k in stays:
            view = sends[k].src(refs, None, jnp.int32(0), jnp.int32(0))
            stay_shapes.append(view.shape)

    probe(*[_ShapeOnly(a.shape) for a in arrays])

    def kernel(*refs):
        ins, outs = refs[:n_in], refs[n_in : n_in + n_out]
        send_sems, recv_sems = refs[n_in + n_out : n_in + n_out + 2]
        bounce = dict(zip(stays, refs[n_in + n_out + 2 :]))
        z = lax.axis_index("sp")
        f = lax.axis_index("fsdp")
        barrier = pltpu.get_barrier_semaphore()
        for dz, df in peers:
            pl.semaphore_signal(
                barrier, inc=1, device_id=(flip(z, dz), flip(f, df)), device_id_type=MESH
            )
        pl.semaphore_wait(barrier, len(peers))
        copies = []
        for k, s in enumerate(sends):
            src = s.src(ins, outs, z, f)
            dst = s.dst(ins, outs, z, f)
            if (s.dz, s.df) == (0, 0):
                copies.append(
                    (
                        pltpu.make_async_copy(src, bounce[k], recv_sems.at[k]),
                        pltpu.make_async_copy(bounce[k], dst, send_sems.at[k]),
                    )
                )
            else:
                copies.append(
                    pltpu.make_async_remote_copy(
                        src_ref=src,
                        dst_ref=dst,
                        send_sem=send_sems.at[k],
                        recv_sem=recv_sems.at[k],
                        device_id=(flip(z, s.dz), flip(f, s.df)),
                        device_id_type=MESH,
                    )
                )
        arrived = set()

        def arrive(k):
            if k not in arrived:
                arrived.add(k)
                s = sends[k]
                if (s.dz, s.df) == (0, 0):
                    copies[k][1].wait()
                else:
                    only_on(s.planes, flip(z, s.dz), copies[k].wait_recv)

        for k, s in enumerate(sends):
            if k in stays:
                copies[k][0].start()
            elif s.after is None:
                only_on(s.planes, z, copies[k].start)
        for k in stays:
            copies[k][0].wait()
            copies[k][1].start()
        for k, s in enumerate(sends):
            if s.after is not None:
                arrive(s.after)
                copies[k].start()
        for k, s in enumerate(sends):
            if (s.dz, s.df) != (0, 0):
                only_on(s.planes, z, copies[k].wait_send)
            arrive(k)

    result = pl.pallas_call(
        kernel,
        out_shape=[jax.ShapeDtypeStruct(shape, BF16) for shape in out_shapes],
        in_specs=[pl.BlockSpec(memory_space=pl.ANY)] * n_in,
        out_specs=[pl.BlockSpec(memory_space=pl.ANY)] * n_out,
        scratch_shapes=[
            pltpu.SemaphoreType.DMA((len(sends),)),
            pltpu.SemaphoreType.DMA((len(sends),)),
        ]
        + [pltpu.VMEM(shape, BF16) for shape in stay_shapes],
        compiler_params=pltpu.CompilerParams(
            collective_id=cid, has_side_effects=True, vmem_limit_bytes=32 * 1024 * 1024
        ),
        cost_estimate=pl.CostEstimate(
            flops=0, bytes_accessed=int(micros * 3.0e6), transcendentals=0
        ),
        name=name,
    )(*arrays)
    return result


def rows_to_experts(cid, tokens, lanes, pick, plane_experts, parts):
    planes, picked, count = pick.shape
    cap = picked // plane_experts
    arrays = (tokens, lanes)
    widths = [a.shape[1] for a in arrays]
    order = [0, 1, 3, 2] if planes == 4 else list(range(planes))
    early = 2 if planes == 4 else planes - 1
    step = 512

    def kernel(tokens_ref, lanes_ref, pick_ref, rows_ref, lane_rows_ref, *scratch):
        here, chosen = scratch[:2], scratch[2:4]
        z_send, z_recv, row_send, row_recv = scratch[4:]
        ins, outs = (tokens_ref, lanes_ref), (rows_ref, lane_rows_ref)
        z = lax.axis_index("sp")
        f = lax.axis_index("fsdp")
        barrier = pltpu.get_barrier_semaphore()
        for d in range(1, planes):
            pl.semaphore_signal(barrier, inc=1, device_id=(flip(z, d), f), device_id_type=MESH)
        for s in range(1, plane_experts):
            pl.semaphore_signal(
                barrier, inc=1, device_id=(z, flip(f, s * parts)), device_id_type=MESH
            )
        pl.semaphore_wait(barrier, planes + plane_experts - 2)

        def across(d, w):
            if d == 0:
                return pltpu.make_async_copy(ins[w], here[w].at[0], z_recv.at[w])
            return pltpu.make_async_remote_copy(
                src_ref=ins[w],
                dst_ref=here[w].at[d],
                send_sem=z_send.at[2 * d + w],
                recv_sem=z_recv.at[2 * d + w],
                device_id=(flip(z, d), f),
                device_id_type=MESH,
            )

        def onward(d, s, w):
            src = chosen[w].at[d, pl.ds(s * cap, cap)]
            dst = outs[w].at[s, d]
            k = (d * plane_experts + s) * 2 + w
            if s == 0:
                return pltpu.make_async_copy(src, dst, row_recv.at[k])
            return pltpu.make_async_remote_copy(
                src_ref=src,
                dst_ref=dst,
                send_sem=row_send.at[k],
                recv_sem=row_recv.at[k],
                device_id=(z, flip(f, s * parts)),
                device_id_type=MESH,
            )

        for d in order[: early + 1]:
            for w in range(2):
                across(d, w).start()
        for turn, d in enumerate(order):
            for w in range(2):
                if d == 0:
                    across(d, w).wait()
                else:
                    across(d, w).wait_recv()
            if turn == 1:
                for later in order[early + 1 :]:
                    for w in range(2):
                        across(later, w).start()

            def columns(i, carry):
                at = pl.ds(pl.multiple_of(i * step, step), step)
                chosen[0][d, :, at] = jnp.dot(
                    pick_ref[d], here[0][d, :, at], preferred_element_type=FLOAT
                ).astype(BF16)
                return carry

            lax.fori_loop(0, widths[0] // step, columns, 0)
            chosen[1][d] = jnp.dot(
                pick_ref[d], here[1][d], preferred_element_type=FLOAT
            ).astype(BF16)
            for s in range(plane_experts):
                for w in range(2):
                    onward(d, s, w).start()
        for d in range(planes):
            for w in range(2):
                if d:
                    across(d, w).wait_send()
                for s in range(plane_experts):
                    onward(d, s, w).wait()

    hbm = pl.BlockSpec(memory_space=pl.ANY)
    sems = planes * plane_experts * 2
    return pl.pallas_call(
        kernel,
        out_shape=[
            jax.ShapeDtypeStruct((plane_experts, planes, cap, width), BF16) for width in widths
        ],
        in_specs=[hbm, hbm, pl.BlockSpec(memory_space=pltpu.VMEM)],
        out_specs=[hbm, hbm],
        scratch_shapes=[pltpu.VMEM((planes, count, width), BF16) for width in widths]
        + [pltpu.VMEM((planes, picked, width), BF16) for width in widths]
        + [pltpu.SemaphoreType.DMA((2 * planes,))] * 2
        + [pltpu.SemaphoreType.DMA((sems,))] * 2,
        compiler_params=pltpu.CompilerParams(
            collective_id=cid, has_side_effects=True, vmem_limit_bytes=40 * 1024 * 1024
        ),
        cost_estimate=pl.CostEstimate(flops=0, bytes_accessed=int(2.1e8), transcendentals=0),
        name="rows_to_experts",
    )(tokens, lanes, pick)


def rows_from_experts(cid, rows_in, lanes_in, pick, weights):
    planes, picked, count = pick.shape
    plane_experts, _, cap, _ = rows_in.shape
    parts = weights[0].shape[1]
    inner_shape = weights[0].shape[2:]
    widths = (rows_in.shape[3], lanes_in.shape[3])
    order = [2, 3, 1, 0] if planes == 4 else list(range(planes - 1, -1, -1))
    step = 512

    def kernel(rows_ref, lanes_ref, pick_ref, first_ref, second_ref, *rest):
        outs, shards_ref = rest[:2], rest[2]
        back, partial, own, others = rest[3:5], rest[5:7], rest[7], rest[8]
        row_send, row_recv, z_send, z_recv, pair_send, pair_recv, load, w_send, w_recv = rest[9:]
        ins, weight_refs = (rows_ref, lanes_ref), (first_ref, second_ref)
        z = lax.axis_index("sp")
        f = lax.axis_index("fsdp")
        part = lax.rem(f, parts)
        place = lax.div(f, parts)
        barrier = pltpu.get_barrier_semaphore()
        for d in range(1, planes):
            pl.semaphore_signal(barrier, inc=1, device_id=(flip(z, d), f), device_id_type=MESH)
        near = list(range(1, parts)) + [s * parts for s in range(1, plane_experts)]
        for m in near:
            pl.semaphore_signal(barrier, inc=1, device_id=(z, flip(f, m)), device_id_type=MESH)
        pl.semaphore_wait(barrier, planes - 1 + len(near))

        def pair(w, p):
            k = w * (parts - 1) + p - 1
            return pltpu.make_async_remote_copy(
                src_ref=weight_refs[w].at[:, flip(part, p)],
                dst_ref=others.at[p - 1, w],
                send_sem=pair_send.at[k],
                recv_sem=pair_recv.at[k],
                device_id=(z, flip(f, p)),
                device_id_type=MESH,
            )

        def load_own(w):
            return pltpu.make_async_copy(weight_refs[w].at[:, part], own.at[w], load.at[w])

        def home(d, s, w):
            src = ins[w].at[s, d]
            dst = back[w].at[d, pl.ds(s * cap, cap)]
            k = (d * plane_experts + s) * 2 + w
            if s == 0:
                return pltpu.make_async_copy(src, dst, row_recv.at[k])
            return pltpu.make_async_remote_copy(
                src_ref=src,
                dst_ref=dst,
                send_sem=row_send.at[k],
                recv_sem=row_recv.at[k],
                device_id=(z, flip(f, s * parts)),
                device_id_type=MESH,
            )

        def across(d, w):
            src, dst = partial[w].at[d], outs[w].at[d]
            if d == 0:
                return pltpu.make_async_copy(src, dst, z_recv.at[w])
            return pltpu.make_async_remote_copy(
                src_ref=src,
                dst_ref=dst,
                send_sem=z_send.at[2 * d + w],
                recv_sem=z_recv.at[2 * d + w],
                device_id=(flip(z, d), f),
                device_id_type=MESH,
            )

        def to_shard(s, w):
            src, dst = own.at[w, flip(place, s)], shards_ref.at[w, place]
            if s == 0:
                return pltpu.make_async_copy(src, dst, w_recv.at[w])
            return pltpu.make_async_remote_copy(
                src_ref=src,
                dst_ref=dst,
                send_sem=w_send.at[2 * s + w],
                recv_sem=w_recv.at[2 * s + w],
                device_id=(z, flip(f, s * parts)),
                device_id_type=MESH,
            )

        for w in range(2):
            load_own(w).start()
            for p in range(1, parts):
                pair(w, p).start()
        for d in order:
            for s in range(plane_experts):
                for w in range(2):
                    home(d, s, w).start()
        for w in range(2):
            load_own(w).wait()
            for p in range(1, parts):
                pair(w, p).wait()

            def add(i, carry):
                e = lax.div(i, inner_shape[0] // 16)
                at = pl.ds(pl.multiple_of(lax.rem(i, inner_shape[0] // 16) * 16, 16), 16)
                total = own[w, e, at, :].astype(FLOAT)
                for p in range(parts - 1):
                    total = total + others[p, w, e, at, :].astype(FLOAT)
                own[w, e, at, :] = total.astype(BF16)
                return carry

            lax.fori_loop(0, plane_experts * (inner_shape[0] // 16), add, 0)
        for turn, d in enumerate(order):
            for s in range(plane_experts):
                for w in range(2):
                    home(d, s, w).wait()
            if turn == planes - 2:
                for s in range(plane_experts):
                    for w in range(2):
                        to_shard(s, w).start()

            def columns(i, carry):
                at = pl.ds(pl.multiple_of(i * step, step), step)
                partial[0][d, :, at] = contract_rows(pick_ref[d], back[0][d, :, at]).astype(BF16)
                return carry

            lax.fori_loop(0, widths[0] // step, columns, 0)
            partial[1][d] = contract_rows(pick_ref[d], back[1][d]).astype(BF16)
            for w in range(2):
                across(d, w).start()
        for d in range(planes):
            for w in range(2):
                across(d, w).wait()
        for s in range(plane_experts):
            for w in range(2):
                to_shard(s, w).wait()

    hbm = pl.BlockSpec(memory_space=pl.ANY)
    dma = pltpu.SemaphoreType.DMA
    row_count = planes * plane_experts * 2
    return pl.pallas_call(
        kernel,
        out_shape=[jax.ShapeDtypeStruct((planes, count, width), BF16) for width in widths]
        + [jax.ShapeDtypeStruct((2, plane_experts) + inner_shape, BF16)],
        in_specs=[hbm, hbm, pl.BlockSpec(memory_space=pltpu.VMEM), hbm, hbm],
        out_specs=[hbm] * 3,
        scratch_shapes=[pltpu.VMEM((planes, picked, width), BF16) for width in widths]
        + [pltpu.VMEM((planes, count, width), BF16) for width in widths]
        + [
            pltpu.VMEM((2, plane_experts) + inner_shape, BF16),
            pltpu.VMEM((parts - 1, 2, plane_experts) + inner_shape, BF16),
        ]
        + [dma((row_count,))] * 2
        + [dma((2 * planes,))] * 2
        + [dma((2 * (parts - 1),))] * 2
        + [dma((2,))]
        + [dma((2 * plane_experts,))] * 2,
        compiler_params=pltpu.CompilerParams(
            collective_id=cid, has_side_effects=True, vmem_limit_bytes=48 * 1024 * 1024
        ),
        cost_estimate=pl.CostEstimate(flops=0, bytes_accessed=int(2.7e8), transcendentals=0),
        name="rows_from_experts",
    )(rows_in, lanes_in, pick, *weights)


def line_sum(cid, arrays, pieces, blocks, handed):
    n = len(arrays)
    chunks = [
        (k, c * (a.shape[0] // p), a.shape[0] // p)
        for k, (a, p) in enumerate(zip(arrays, pieces))
        for c in range(p)
    ]
    far = blocks.shape[0] - 1
    assert far == 3

    def kernel(*refs):
        ins, blocks_ref, handed_refs = refs[:n], refs[n], refs[n + 1 : n + 3]
        outs, others_ref = refs[n + 3 : 2 * n + 3], refs[2 * n + 3]
        own, got, swapped = (refs[2 * n + 4 + n * i : 2 * n + 4 + n * (i + 1)] for i in range(3))
        mine, theirs = refs[5 * n + 4 : 5 * n + 6]
        load, store, in_s, in_r, swap_s, swap_r, back_s, back_r, far_s, far_r = refs[5 * n + 6 :]
        z = lax.axis_index("sp")
        f = lax.axis_index("fsdp")
        inner = jnp.logical_or(z == 1, z == 2)
        barrier = pltpu.get_barrier_semaphore()
        for d in range(1, far + 1):
            pl.semaphore_signal(barrier, inc=1, device_id=(flip(z, d), f), device_id_type=MESH)
        pl.semaphore_wait(barrier, far)

        def view(refs, c):
            k, start, size = chunks[c]
            return refs[k].at[pl.ds(start, size)]

        def remote(src, dst, send, recv, c, dz):
            return pltpu.make_async_remote_copy(
                src_ref=view(src, c),
                dst_ref=view(dst, c),
                send_sem=send.at[c],
                recv_sem=recv.at[c],
                device_id=(flip(z, dz), f),
                device_id_type=MESH,
            )

        loads = [
            pltpu.make_async_copy(view(ins, c), view(own, c), load.at[c])
            for c in range(len(chunks))
        ]
        stores = [
            pltpu.make_async_copy(view(got, c), view(outs, c), store.at[c])
            for c in range(len(chunks))
        ]

        def block_copy(src, dst, send, recv, d):
            return pltpu.make_async_remote_copy(
                src_ref=src,
                dst_ref=dst,
                send_sem=far_s.at[send],
                recv_sem=far_r.at[recv],
                device_id=(flip(z, d), f),
                device_id_type=MESH,
            )

        near = block_copy(blocks_ref.at[1], others_ref.at[0], 0, 0, 1)
        block_loads = [
            pltpu.make_async_copy(blocks_ref.at[2 + k], mine.at[k], far_r.at[2 + k])
            for k in range(2)
        ] + [
            pltpu.make_async_copy(handed_refs[k], theirs.at[k], far_r.at[4 + k])
            for k in range(2)
        ]
        beyond = [block_copy(mine.at[k], others_ref.at[1], 1 + k, 1, 2 + k) for k in range(2)]
        inwards = [remote(own, got, in_s, in_r, c, 1) for c in range(len(chunks))]
        swaps = [remote(own, swapped, swap_s, swap_r, c, 3) for c in range(len(chunks))]
        backs = [remote(got, got, back_s, back_r, c, 1) for c in range(len(chunks))]
        for copy in loads:
            copy.start()

        def add(left, right, to, c):
            k, start, size = chunks[c]
            step = 16

            def rows(i, carry):
                at = pl.ds(pl.multiple_of(start + i * step, step), step)
                total = left[k][at, :].astype(FLOAT) + right[k][at, :].astype(FLOAT)
                to[k][at, :] = total.astype(BF16)
                return carry

            lax.fori_loop(0, size // step, rows, 0)

        def pass_on(k):
            def rows(i, carry):
                at = pl.ds(pl.multiple_of(i * 16, 16), 16)
                total = mine[k, at, :].astype(FLOAT) + theirs[1 - k, at, :].astype(FLOAT)
                mine[k, at, :] = total.astype(BF16)
                return carry

            lax.fori_loop(0, blocks.shape[1] // 16, rows, 0)
            beyond[k].start()

        @pl.when(jnp.logical_not(inner))
        def _():
            for c in range(len(chunks)):
                loads[c].wait()
                inwards[c].start()
            near.start()
            for c in range(len(chunks)):
                backs[c].wait_recv()
                stores[c].start()
            for c in range(len(chunks)):
                inwards[c].wait_send()
                stores[c].wait()

        @pl.when(inner)
        def _():
            near.start()
            for copy in block_loads:
                copy.start()
            for copy in block_loads:
                copy.wait()
            for k in range(2):
                pass_on(k)
            for c in range(len(chunks) + 1):
                if c < len(chunks):
                    loads[c].wait()
                    inwards[c].wait_recv()
                    add(own, got, own, c)
                    swaps[c].start()
                if c:
                    swaps[c - 1].wait_recv()
                    add(own, swapped, got, c - 1)
                    backs[c - 1].start()
                    stores[c - 1].start()
            for c in range(len(chunks)):
                swaps[c].wait_send()
                backs[c].wait_send()
                stores[c].wait()

            for copy in beyond:
                copy.wait_send()

        near.wait()
        beyond[0].wait_recv()

    hbm = pl.BlockSpec(memory_space=pl.ANY)
    buffers = [pltpu.VMEM(a.shape, BF16) for a in arrays]
    count = len(chunks)
    return pl.pallas_call(
        kernel,
        out_shape=[jax.ShapeDtypeStruct(a.shape, BF16) for a in arrays]
        + [jax.ShapeDtypeStruct((2,) + blocks.shape[1:], BF16)],
        in_specs=[hbm] * (n + 3),
        out_specs=[hbm] * (n + 1),
        scratch_shapes=buffers * 3
        + [pltpu.VMEM((2,) + blocks.shape[1:], BF16)] * 2
        + [pltpu.SemaphoreType.DMA((count,))] * 8
        + [pltpu.SemaphoreType.DMA((6,))] * 2,
        compiler_params=pltpu.CompilerParams(
            collective_id=cid, has_side_effects=True, vmem_limit_bytes=40 * 1024 * 1024
        ),
        cost_estimate=pl.CostEstimate(flops=0, bytes_accessed=int(4.0e8), transcendentals=0),
        name="line_sum",
    )(*arrays, blocks, *handed)


def body(
    tokens,
    expert_ids,
    attn_gain,
    query_weight,
    key_weight,
    value_weight,
    q_gain,
    k_gain,
    output_weight,
    ffn_gain,
    router_weight,
    w_gate,
    w_up,
    w_down,
    cotangent,
):
    nsp = lax.axis_size("sp")
    nf = lax.axis_size("fsdp")
    z = lax.axis_index("sp")
    f = lax.axis_index("fsdp")
    rows = tokens.shape[1]
    width = tokens.shape[2]
    shard = width // nf
    n_heads, kv_heads, head_dim = QUERY_HEADS, KEY_VALUE_HEADS, HEAD_SIZE
    my_heads = n_heads // nf
    rep = nf // kv_heads
    q_cols = my_heads * head_dim
    qkv_cols = q_cols + 2 * head_dim
    score_scale = 1.0 / math.sqrt(head_dim)
    n_experts = w_gate.shape[0]
    hidden_size = w_gate.shape[2]
    hid_shard = w_down.shape[1]
    plane_experts = n_experts // nsp
    parts = nf // plane_experts
    cap = CAP
    seqs = nf
    part = lax.rem(f, parts)
    place = lax.div(f, parts)
    expert = z * plane_experts + place

    def swap_f(block, mask):
        return lax.ppermute(block, "fsdp", [(i, i ^ mask) for i in range(nf)])

    def swap_z(block, mask):
        return lax.ppermute(block, "sp", [(i, i ^ mask) for i in range(nsp)])

    small = jnp.concatenate(
        [
            attn_gain.astype(BF16),
            ffn_gain.astype(BF16),
            q_gain.astype(BF16),
            k_gain.astype(BF16),
            router_weight.astype(BF16).reshape(-1),
        ]
    )
    small_rows = 16
    small = jnp.pad(small, (0, small_rows * width - small.shape[0])).reshape(small_rows, width)
    x_pay = jnp.concatenate([tokens[0], small], axis=0)
    pay_rows = rows + small_rows
    query_b = query_weight.astype(BF16)
    key_b = key_weight.astype(BF16)
    value_b = value_weight.astype(BF16)
    routes = expert_ids[0]
    expert_iota = jnp.arange(n_experts, dtype=jnp.int32)
    routed = jnp.any(routes[:, :, None] == expert_iota[None, None, :], axis=1)
    dy_pay = jnp.concatenate(
        [
            cotangent[0],
            routed.astype(BF16),
            jnp.zeros((rows, LANES - n_experts), BF16),
        ],
        axis=1,
    )
    wide = width + LANES

    def plane_cast(weight):
        return lax.dynamic_slice_in_dim(weight, z * plane_experts, plane_experts, 0).astype(BF16)

    gate_up_pay = jnp.stack([plane_cast(w_gate), plane_cast(w_up)], axis=1)
    down_pay = plane_cast(w_down)

    sends = []
    for m in range(0, nf, 2):
        sends.append(
            Send(
                lambda i, o, z, f, m=m: i[0],
                lambda i, o, z, f: o[0].at[f],
                0,
                m,
            )
        )
    for m in range(0, nf, 2):
        if m == 0:
            sends.append(
                Send(lambda i, o, z, f: i[0], lambda i, o, z, f: o[0].at[f], 0, 1)
            )
        else:
            sends.append(
                Send(
                    lambda i, o, z, f, m=m: o[0].at[flip(f, m)],
                    lambda i, o, z, f, m=m: o[0].at[flip(f, m)],
                    0,
                    1,
                    m // 2,
                )
            )
    for m in range(0, nf, rep):
        for w in range(2):
            sends.append(
                Send(
                    lambda i, o, z, f, m=m, w=w: i[2 + w].at[
                        :, cols(lax.div(flip(f, m), rep), head_dim)
                    ],
                    lambda i, o, z, f, w=w: o[1].at[
                        cols(f, shard), pl.ds(q_cols + w * head_dim, head_dim)
                    ],
                    0,
                    m,
                )
            )
            for p in range(1, rep):
                view = lambda i, o, z, f, m=m, w=w: o[1].at[
                    cols(flip(f, m), shard), pl.ds(q_cols + w * head_dim, head_dim)
                ]
                if m == 0:
                    sends.append(
                        Send(
                            lambda i, o, z, f, w=w: i[2 + w].at[:, cols(lax.div(f, rep), head_dim)],
                            view,
                            0,
                            p,
                        )
                    )
                else:
                    sends.append(Send(view, view, 0, p, len(sends) - p))
    for m in range(nf):
        sends.append(
            Send(
                lambda i, o, z, f, m=m: i[1].at[:, cols(flip(f, m), q_cols)],
                lambda i, o, z, f: o[1].at[cols(f, shard), pl.ds(0, q_cols)],
                0,
                m,
            )
        )
    for m in range(nsp):
        sends.append(
            Send(lambda i, o, z, f: i[4], lambda i, o, z, f, m=m: o[2].at[m], m, 0)
        )
    x_all, w_qkv, dy_z = exchange(
        "gather_inputs",
        0,
        (x_pay, query_b, key_b, value_b, dy_pay),
        ((nf, pay_rows, width), (width, qkv_cols), (nsp, rows, wide)),
        sends,
        65,
    )

    own_experts = z * plane_experts + jnp.bitwise_xor(
        place, jnp.arange(plane_experts, dtype=jnp.int32)
    )
    own_hot = (expert_iota[:, None] == own_experts[None, :]).astype(FLOAT)
    routed_z = lax.dot_general(
        own_hot,
        dy_z[:, :, width : width + n_experts].astype(FLOAT),
        (((0,), (2,)), ((), ())),
        preferred_element_type=FLOAT,
    ).transpose(1, 0, 2)
    earlier = jnp.triu(jnp.ones((rows, rows), FLOAT), 1)
    rank = jnp.dot(
        routed_z.reshape(nsp * plane_experts, rows), earlier, preferred_element_type=FLOAT
    ).reshape(nsp, plane_experts, rows)
    rank = rank * routed_z + (routed_z - 1.0)
    pick = (
        rank[:, :, None, :] == jnp.arange(cap, dtype=FLOAT)[None, None, :, None]
    ).astype(BF16)
    pick = pick.reshape(nsp, plane_experts * cap, rows)

    x_all, gate_up_pay = lax.optimization_barrier((x_all, gate_up_pay))
    by_expert = pick.reshape(nsp, plane_experts, cap, rows)
    gate_up_pieces, dy_pieces = [], []
    for s in range(plane_experts):
        weights = lax.dynamic_index_in_dim(gate_up_pay, flip(place, s), 0, keepdims=False)
        dy_rows = jnp.einsum(
            "drt,dtc->drc", by_expert[:, s], dy_z[:, :, :width], preferred_element_type=FLOAT
        )
        dy_rows = dy_rows.astype(BF16).reshape(nsp * cap, width)
        if s and s == plane_experts - 1:
            both = jnp.concatenate([dy_rows, weights.reshape(-1, width)], axis=0)
            both = swap_f(both, s * parts)
            dy_rows = both[: nsp * cap]
            weights = both[nsp * cap :].reshape(2, shard, hidden_size)
        elif s:
            weights = swap_f(weights, s * parts)
            dy_rows = swap_f(dy_rows, s * parts)
        gate_up_pieces.append(weights)
        dy_pieces.append(dy_rows)
    dy_in = jnp.concatenate(dy_pieces, axis=0)

    small_all = x_all[:, rows:, :].reshape(nf, small_rows * width)
    at = 0
    pieces = []
    for size in (shard, shard, head_dim // nf, head_dim // nf, shard * n_experts):
        pieces.append(small_all[:, at : at + size])
        at += size
    g_attn = pieces[0].reshape(width).astype(FLOAT)
    g_ffn = pieces[1].reshape(width).astype(FLOAT)
    g_query = pieces[2].reshape(head_dim).astype(FLOAT)
    g_key = pieces[3].reshape(head_dim).astype(FLOAT)
    wr_b = pieces[4].reshape(width, n_experts)

    xn_b = (
        rms_norm(x_all[:, :rows, :].astype(FLOAT), g_attn).astype(BF16).reshape(seqs * rows, width)
    )
    qkv_lin = matmul(xn_b, w_qkv)

    def split_heads(flat):
        flat = flat.reshape(seqs, rows, -1)
        return jnp.stack(
            [
                flat[:, :, h * head_dim : (h + 1) * head_dim]
                for h in range(flat.shape[2] // head_dim)
            ],
            axis=1,
        )

    def join_heads(split):
        joined = jnp.concatenate([split[:, h] for h in range(split.shape[1])], axis=2)
        return joined.reshape(seqs * rows, -1)

    q_lin = split_heads(qkv_lin[:, :q_cols])
    k_lin = split_heads(qkv_lin[:, q_cols : q_cols + head_dim])
    v_b = qkv_lin[:, q_cols + head_dim :].astype(BF16)
    half_dim = head_dim // 2
    inverse_freq = THETA ** (-(jnp.arange(half_dim, dtype=FLOAT) * 2.0 / head_dim))
    positions = (z * rows + jnp.arange(rows, dtype=jnp.int32)).astype(FLOAT)
    angles = positions[:, None] * inverse_freq[None, :]
    cosine = jnp.cos(angles)[None, None]
    sine_part = jnp.sin(angles)[None, None]

    def prep_heads(linear, gain_vec):
        return rotate(rms_norm(linear, gain_vec), cosine, sine_part)

    q_rows = prep_heads(q_lin, g_query).astype(BF16)
    k_b = join_heads(prep_heads(k_lin, g_key).astype(BF16))

    kv_pay = jnp.concatenate([k_b, v_b], axis=1)
    piece = seqs * rows // rep
    sends = []
    for d in range(nsp):
        sends.append(
            Send(
                lambda i, o, z, f: i[0].at[pl.ds(lax.rem(f, rep) * piece, piece)],
                lambda i, o, z, f, d=d: o[0].at[d, pl.ds(lax.rem(f, rep) * piece, piece)],
                d,
                0,
            )
        )
    for d in range(nsp):
        for p in range(1, rep):
            sends.append(
                Send(
                    lambda i, o, z, f, d=d: o[0].at[d, pl.ds(lax.rem(f, rep) * piece, piece)],
                    lambda i, o, z, f, d=d: o[0].at[d, pl.ds(lax.rem(f, rep) * piece, piece)],
                    0,
                    p,
                    d,
                )
            )
    (kv_z,) = exchange(
        "gather_keys", 1, (kv_pay,), ((nsp, seqs * rows, 2 * head_dim),), sends, 24
    )
    kv_seq = kv_z.reshape(nsp, seqs, rows, 2 * head_dim).transpose(1, 0, 2, 3)
    kv_seq = kv_seq.reshape(seqs, nsp * rows, 2 * head_dim)
    keys = kv_seq[:, :, :head_dim]
    values = kv_seq[:, :, head_dim:]

    plane_of = jnp.bitwise_xor(jnp.arange(nsp, dtype=jnp.int32), z)
    key_pos = (plane_of[:, None] * rows + jnp.arange(rows, dtype=jnp.int32)[None, :]).reshape(-1)
    query_pos = z * rows + jnp.arange(rows, dtype=jnp.int32)
    causal = key_pos[None, :] <= query_pos[:, None]
    scores = (
        jnp.einsum("nhqd,nkd->nhqk", q_rows, keys, preferred_element_type=FLOAT) * score_scale
    )
    expo = jnp.where(causal[None, None], jnp.exp(scores), 0.0)
    probs = (expo / jnp.sum(expo, axis=3, keepdims=True)).astype(BF16)
    o_rows = jnp.einsum("nhqk,nkd->nhqd", probs, values, preferred_element_type=FLOAT)
    o_mat = join_heads(o_rows.astype(BF16))
    wo_b = output_weight.astype(BF16)

    def pair_then_plane(partial, name, cid, more=(), more_shapes=(), more_sends=()):
        split = partial.astype(BF16).reshape(nf // 2, 2, rows, width)
        (other,) = exchange(
            name + "_pair",
            cid,
            (split,),
            ((nf // 2, rows, width),),
            [Send(lambda i, o, z, f: i[0].at[:, 1 - lax.rem(f, 2)], lambda i, o, z, f: o[0], 0, 1)],
            8,
        )
        own = lax.dynamic_index_in_dim(split, lax.rem(f, 2), 1, keepdims=False)
        summed = (own.astype(FLOAT) + other.astype(FLOAT)).astype(BF16)
        sends = [
            Send(
                lambda i, o, z, f, j=j: i[0].at[flip(lax.div(f, 2), j)],
                lambda i, o, z, f, j=j: o[0].at[j],
                0,
                2 * j,
            )
            for j in range(nf // 2)
        ]
        blocks, *rest = exchange(
            name + "_plane",
            cid + 1,
            (summed, *more),
            ((nf // 2, rows, width), *more_shapes),
            sends + list(more_sends),
            27,
        )
        return jnp.sum(blocks.astype(FLOAT), axis=0), rest

    sends = []
    for s in range(plane_experts):
        for p in range(parts):
            sends.append(
                Send(
                    lambda i, o, z, f, s=s: i[1 + s],
                    lambda i, o, z, f, s=s: o[1].at[:, flip(f, s * parts)],
                    0,
                    p,
                )
            )
    branch, (gate_up_all,) = pair_then_plane(
        matmul(o_mat, wo_b), "out_sum", 3, gate_up_pieces, ((2, nf, shard, hidden_size),), sends
    )
    wg_b = gate_up_all[0].reshape(width, hidden_size)
    wu_b = gate_up_all[1].reshape(width, hidden_size)
    x_rows = tokens[0].astype(FLOAT)
    mid_rows = x_rows + branch
    hn_b = rms_norm(mid_rows, g_ffn).astype(BF16)
    logits = matmul(hn_b, wr_b)
    logits = jnp.where(routed, logits, -1e30)
    expo = jnp.where(routed, jnp.exp(logits - jnp.max(logits, axis=1, keepdims=True)), 0.0)
    gates = expo / jnp.sum(expo, axis=1, keepdims=True)

    def two_parts(exact):
        high = exact.astype(BF16)
        return high, (exact - high.astype(FLOAT)).astype(BF16)

    gate_high, gate_low = two_parts(gates)
    gate_lanes = jnp.concatenate(
        [gate_high, gate_low, jnp.zeros((rows, LANES - 2 * n_experts), BF16)], axis=1
    )
    hn_rows, gate_rows = rows_to_experts(5, hn_b, gate_lanes, pick, plane_experts, parts)
    hn_rows, down_pay = lax.optimization_barrier((hn_rows, down_pay))
    down_pieces = []
    for s in range(plane_experts):
        block = lax.dynamic_index_in_dim(down_pay, flip(place, s), 0, keepdims=False)
        down_pieces.append(swap_f(block, s * parts) if s else block)

    n_rows = plane_experts * nsp * cap
    hn_in = hn_rows.reshape(n_rows, width)
    hot = (jnp.arange(n_experts, dtype=jnp.int32) == expert).astype(FLOAT)
    tail = gate_rows.reshape(n_rows, LANES)[:, : 2 * n_experts].astype(FLOAT)
    row_gate = jnp.sum(
        (tail[:, :n_experts] + tail[:, n_experts:]) * hot[None, :], axis=1, keepdims=True
    )
    gate_pre = matmul(hn_in, wg_b)
    up_pre = matmul(hn_in, wu_b)
    sigma = jax.nn.sigmoid(gate_pre)
    act_f = gate_pre * sigma
    hidden = (act_f * up_pre).astype(BF16)
    dy_f = dy_in.astype(FLOAT)
    d_result = (row_gate * dy_f).astype(BF16)

    def by_shard(full, inner):
        return full.astype(BF16).reshape((plane_experts, parts) + inner)

    def pair_total(own, others):
        total = lax.dynamic_index_in_dim(own, part, 1, keepdims=False).astype(FLOAT)
        for other in others:
            total = total + other.astype(FLOAT)
        return total.astype(BF16)

    d_down = by_shard(contract_rows(hidden, d_result), (hid_shard, width))
    d_down, down_pieces = lax.optimization_barrier((d_down, down_pieces))
    d_down = pair_total(
        d_down,
        [
            swap_f(lax.dynamic_index_in_dim(d_down, flip(part, p), 1, keepdims=False), p)
            for p in range(1, parts)
        ],
    )
    d_down = [
        swap_f(lax.dynamic_index_in_dim(d_down, flip(place, s), 0, keepdims=False), s * parts)
        if s
        else lax.dynamic_index_in_dim(d_down, place, 0, keepdims=False)
        for s in range(plane_experts)
    ]
    down_pieces = jnp.stack(down_pieces)
    down_pieces = jnp.stack(
        [swap_f(down_pieces, p) if p else down_pieces for p in range(parts)], axis=1
    ).reshape(nf, hid_shard, width)
    wd_b = jnp.take(
        down_pieces, jnp.bitwise_xor(jnp.arange(nf, dtype=jnp.int32), f), axis=0, mode="clip"
    ).reshape(hidden_size, width)
    result = matmul(hidden, wd_b)
    row_dgate = jnp.sum(result * dy_f, axis=1, keepdims=True)
    weighted = (row_gate * result).astype(BF16)
    d_hidden = contract_cols(d_result, wd_b)
    d_gate_pre = (d_hidden * up_pre * sigma * (1.0 + gate_pre * (1.0 - sigma))).astype(BF16)
    d_up_pre = (d_hidden * act_f).astype(BF16)
    d_down, d_gate_pre, d_up_pre = lax.optimization_barrier((d_down, d_gate_pre, d_up_pre))
    in_order = jnp.bitwise_xor(jnp.arange(plane_experts, dtype=jnp.int32), place)
    d_down = jnp.take(jnp.stack(d_down), in_order, axis=0, mode="clip")
    all_down = lax.all_gather(d_down, "sp")
    d_in = (contract_cols(d_gate_pre, wg_b) + contract_cols(d_up_pre, wu_b)).astype(BF16)
    dgate_high, dgate_low = two_parts(row_dgate * hot[None, :])
    dgate_lanes = jnp.concatenate(
        [dgate_high, dgate_low, jnp.zeros((n_rows, LANES - 2 * n_experts), BF16)], axis=1
    )

    d_weights = (
        by_shard(contract_rows(hn_in, d_gate_pre), (shard, hidden_size)),
        by_shard(contract_rows(hn_in, d_up_pre), (shard, hidden_size)),
    )

    d_home, dgate_home, shards = rows_from_experts(
        7,
        d_in.reshape(plane_experts, nsp, cap, width),
        dgate_lanes.reshape(plane_experts, nsp, cap, LANES),
        pick,
        d_weights,
    )

    def combine(returned):
        flat = returned.reshape(nsp, plane_experts * cap, returned.shape[3])
        return jnp.einsum("drt,drc->dtc", pick, flat, preferred_element_type=FLOAT).astype(BF16)

    all_gate_up = lax.all_gather(shards, "sp")
    d_home = jnp.sum(d_home.astype(FLOAT), axis=0)
    tail = jnp.sum(dgate_home.astype(FLOAT), axis=0)
    d_gates = tail[:, :n_experts] + tail[:, n_experts : 2 * n_experts]
    d_logits = gates * (d_gates - jnp.sum(gates * d_gates, axis=1, keepdims=True))
    d_router = jnp.dot(hn_b.astype(FLOAT).T, d_logits, precision=HIGH_PRECISION)
    d_hn = d_home + jnp.dot(d_logits, wr_b.astype(FLOAT).T, precision=HIGH_PRECISION)
    grad_out = cotangent[0].astype(FLOAT)
    unused, ffn_pull = jax.vjp(rms_norm, mid_rows, g_ffn)
    d_mid_norm, d_ffn_gain = ffn_pull(d_hn)
    d_mid = grad_out + d_mid_norm

    d_attn_b = d_mid.astype(BF16)
    sends = [
        Send(lambda i, o, z, f: i[0], lambda i, o, z, f: o[0].at[f], 0, m)
        for m in range(0, nf, 2)
    ]
    for m in range(0, nf, 2):
        if m == 0:
            sends.append(Send(lambda i, o, z, f: i[0], lambda i, o, z, f: o[0].at[f], 0, 1))
        else:
            sends.append(
                Send(
                    lambda i, o, z, f, m=m: o[0].at[flip(f, m)],
                    lambda i, o, z, f, m=m: o[0].at[flip(f, m)],
                    0,
                    1,
                    m // 2,
                )
            )
    (da_all,) = exchange("gather_grads", 9, (d_attn_b,), ((nf, rows, width),), sends, 30)
    da_all = da_all.reshape(seqs * rows, width)
    d_wo = contract_rows(o_mat, da_all)
    d_o = split_heads(contract_cols(da_all, wo_b).astype(BF16))
    d_val = jnp.einsum("nhqk,nhqd->nkd", probs, d_o, preferred_element_type=FLOAT)
    d_probs = jnp.einsum("nhqd,nkd->nhqk", d_o, values, preferred_element_type=FLOAT)
    probs_f = probs.astype(FLOAT)
    d_scores = (
        probs_f * (d_probs - jnp.sum(probs_f * d_probs, axis=3, keepdims=True))
    ).astype(BF16)
    dq = (
        jnp.einsum("nhqk,nkd->nhqd", d_scores, keys, preferred_element_type=FLOAT) * score_scale
    ).astype(BF16)
    d_key = (
        jnp.einsum("nhqk,nhqd->nkd", d_scores, q_rows, preferred_element_type=FLOAT) * score_scale
    )
    d_kv = jnp.concatenate([d_key, d_val], axis=2).astype(BF16)
    d_kv = d_kv.reshape(seqs, nsp, rows, 2 * head_dim).transpose(1, 0, 2, 3)
    d_kv = d_kv.reshape(nsp, seqs * rows, 2 * head_dim)
    d_kv, all_down = lax.optimization_barrier((d_kv, all_down))
    grad_down = all_down.astype(FLOAT).reshape(n_experts, hid_shard, width)
    d_kv = d_kv.reshape(nsp, rep, piece, 2 * head_dim)
    (others,) = exchange(
        "key_grads_group",
        11,
        (d_kv,),
        ((rep - 1, nsp, piece, 2 * head_dim),),
        [
            Send(
                lambda i, o, z, f, p=p: i[0].at[:, flip(lax.rem(f, rep), p)],
                lambda i, o, z, f, p=p: o[0].at[p - 1],
                0,
                p,
            )
            for p in range(1, rep)
        ],
        6,
    )
    d_kv = lax.dynamic_index_in_dim(d_kv, lax.rem(f, rep), 1, keepdims=False)
    d_kv = (d_kv.astype(FLOAT) + jnp.sum(others.astype(FLOAT), axis=0)).astype(BF16)
    sends = [
        Send(lambda i, o, z, f, d=d: i[0].at[d], lambda i, o, z, f, d=d: o[0].at[d - 1], d, 0)
        for d in range(1, nsp)
    ]
    for s in range(plane_experts):
        sends.append(
            Send(
                lambda i, o, z, f, s=s: i[1].at[s],
                lambda i, o, z, f, s=s: o[1].at[:, s],
                0,
                s * parts,
            )
        )
    others, out_back = exchange(
        "key_grads_planes",
        10,
        (d_kv, weighted.reshape(plane_experts, nsp, cap, width)),
        ((nsp - 1, piece, 2 * head_dim), (nsp, plane_experts, cap, width)),
        sends,
        60,
    )
    out_blocks = combine(out_back)
    d_kv = (d_kv[0].astype(FLOAT) + jnp.sum(others.astype(FLOAT), axis=0)).astype(BF16)
    (d_kv,) = exchange(
        "key_grads_share",
        15,
        (d_kv,),
        ((rep, piece, 2 * head_dim),),
        [
            Send(lambda i, o, z, f: i[0], lambda i, o, z, f: o[0].at[lax.rem(f, rep)], 0, p)
            for p in range(rep)
        ],
        6,
    )
    d_kv = d_kv.reshape(seqs * rows, 2 * head_dim).astype(FLOAT)
    dq, grad_down = lax.optimization_barrier((dq, grad_down))
    unused, q_pull = jax.vjp(prep_heads, q_lin, g_query)
    d_q_lin, d_q_gain = q_pull(dq.astype(FLOAT))
    unused, k_pull = jax.vjp(prep_heads, k_lin, g_key)
    d_k_lin, d_k_gain = k_pull(d_kv[:, :head_dim].reshape(seqs, 1, rows, head_dim))
    dq_b = join_heads(d_q_lin.astype(BF16))
    dk_b = join_heads(d_k_lin.astype(BF16))
    dv_b = d_kv[:, head_dim:].astype(BF16)
    d_qkv = jnp.concatenate([dq_b, dk_b, dv_b], axis=1)
    share = 1.0 / rep
    d_qkv_shared = jnp.concatenate([dq_b, dk_b * BF16(share), dv_b * BF16(share)], axis=1)
    d_w_qkv = contract_rows(xn_b, d_qkv).astype(BF16)

    def hand_over(which, i_at, o_at):
        return Send(
            lambda i, o, z, f: i[i_at].at[which], lambda i, o, z, f: o[o_at], 1, 0, None, (0, 3)
        )

    more = ((), (), ())
    if nsp == 4:
        more = ((out_blocks,), ((rows, width),), (hand_over(2, 1, 1),))
    d_xn, handed = pair_then_plane(contract_cols(d_qkv_shared, w_qkv), "input_sum", 13, *more)
    unused, attn_pull = jax.vjp(rms_norm, x_rows, g_attn)
    d_x_norm, d_attn_gain = attn_pull(d_xn)
    grad_tokens = (d_mid + d_x_norm)[None]

    smalls = jnp.concatenate(
        [
            d_attn_gain.reshape(nf, shard),
            d_ffn_gain.reshape(nf, shard),
            d_q_gain.reshape(nf, head_dim // nf),
            (d_k_gain * share).reshape(nf, head_dim // nf),
            d_router.reshape(nf, shard * n_experts),
        ],
        axis=1,
    ).astype(BF16)
    small_size = smalls.shape[1]
    small_cols = pl.cdiv(small_size, kv_heads * head_dim) * kv_heads * head_dim // small_rows
    small_cols = pl.cdiv(small_cols, LANES) * LANES
    smalls = jnp.pad(smalls, ((0, 0), (0, small_rows * small_cols - small_size)))
    kv_cols = kv_heads * head_dim
    sends = []
    for m in range(nf):
        sends.append(
            Send(
                lambda i, o, z, f, m=m: i[0].at[cols(flip(f, m), shard), pl.ds(0, q_cols)],
                lambda i, o, z, f: o[0].at[:, cols(f, q_cols)],
                0,
                m,
            )
        )
        sends.append(
            Send(lambda i, o, z, f, m=m: i[1].at[flip(f, m)], lambda i, o, z, f: o[2].at[f], 0, m)
        )
    for m in range(0, nf, rep):
        for w in range(2):
            sends.append(
                Send(
                    lambda i, o, z, f, m=m, w=w: i[0].at[
                        cols(flip(f, m), shard), pl.ds(q_cols + w * head_dim, head_dim)
                    ],
                    lambda i, o, z, f, w=w: o[1].at[
                        pl.ds(w * shard, shard), cols(lax.div(f, rep), head_dim)
                    ],
                    0,
                    m,
                )
            )
    if nsp == 4:
        sends.append(hand_over(3, 2, 3))
    d_wq, d_wkv, small_shard, handed_last = exchange(
        "head_grads_to_shards",
        12,
        (d_w_qkv, smalls.reshape(nf, small_rows, small_cols), out_blocks),
        (
            (shard, n_heads * head_dim),
            (2 * shard, kv_cols),
            (nf, small_rows, small_cols),
            (rows, width),
        ),
        sends,
        36,
    )
    small_sum = jnp.sum(small_shard.astype(FLOAT), axis=0).astype(BF16)
    if nsp == 4:
        sum_q, sum_out, sum_kv, small_sum, out_others = line_sum(
            16, (d_wq, d_wo.astype(BF16), d_wkv, small_sum), (8, 8, 2, 1), out_blocks, (handed[0], handed_last)
        )
        out_others = [out_others[d] for d in range(2)]
    else:
        sum_q, sum_out, sum_kv, small_sum = lax.psum(
            (d_wq, d_wo.astype(BF16), d_wkv, small_sum), "sp"
        )
        out_others = [swap_z(out_blocks[d], d) for d in range(1, nsp)]
    moe_sum = out_blocks[0].astype(FLOAT)
    for block in out_others:
        moe_sum = moe_sum + block.astype(FLOAT)
    mixed = (mid_rows + moe_sum).astype(BF16)[None]
    sum_out = sum_out.astype(FLOAT)
    sum_q = sum_q.astype(FLOAT)
    sum_kv = sum_kv.astype(FLOAT)
    small_sum = small_sum.astype(FLOAT).reshape(-1)
    at = 0
    pieces = []
    for size in (shard, shard, head_dim // nf, head_dim // nf, shard * n_experts):
        pieces.append(small_sum[at : at + size])
        at += size
    grad_gate = all_gate_up[:, 0].astype(FLOAT).reshape(n_experts, shard, hidden_size)
    all_gate_up, grad_gate = lax.optimization_barrier((all_gate_up, grad_gate))
    grad_up = all_gate_up[:, 1].astype(FLOAT).reshape(n_experts, shard, hidden_size)
    return (
        mixed,
        grad_tokens,
        pieces[0],
        sum_q,
        sum_kv[:shard],
        sum_kv[shard : 2 * shard],
        pieces[2],
        pieces[3],
        sum_out,
        pieces[1],
        pieces[4].reshape(shard, n_experts),
        grad_gate,
        grad_up,
        grad_down,
    )


def solution(mesh):
    by_token = P("fsdp", "sp", None)
    by_row = P("fsdp", None)
    by_inner = P(None, "fsdp", None)
    in_specs = (
        by_token,
        by_token,
        P("fsdp"),
        by_row,
        by_row,
        by_row,
        P("fsdp"),
        P("fsdp"),
        by_row,
        P("fsdp"),
        by_row,
        by_inner,
        by_inner,
        by_inner,
        by_token,
    )
    out_specs = (
        by_token,
        by_token,
        P("fsdp"),
        by_row,
        by_row,
        by_row,
        P("fsdp"),
        P("fsdp"),
        by_row,
        P("fsdp"),
        by_row,
        by_inner,
        by_inner,
        by_inner,
    )
    return jax.shard_map(body, mesh=mesh, in_specs=in_specs, out_specs=out_specs, check_vma=False)
```

```python
import math
from typing import Callable, NamedTuple

import jax
import jax.numpy as jnp
from jax import lax
from jax.experimental import pallas as pl
from jax.experimental.pallas import tpu as pltpu
from jax.sharding import PartitionSpec as P

QUERY_HEADS = 32
KEY_VALUE_HEADS = 4
HEAD_SIZE = 128
CAP = 80
LANES = 128

EPS = 1e-06
THETA = 1000000.0
HIGH_PRECISION = lax.Precision.HIGHEST
BF16 = jnp.bfloat16
FLOAT = jnp.float32
MESH = pl.DeviceIdType.MESH


def rms_norm(values_in, gain_vec):
    return (
        values_in
        * lax.rsqrt(jnp.mean(values_in * values_in, axis=-1, keepdims=True) + EPS)
        * gain_vec
    )


def rotate(values_in, cosine, sine_part):
    half_dim = values_in.shape[-1] // 2
    first_half = values_in[..., :half_dim]
    second = values_in[..., half_dim:]
    return jnp.concatenate(
        [first_half * cosine - second * sine_part, second * cosine + first_half * sine_part],
        axis=-1,
    )


def contract_rows(left_mat, right_mat):
    return lax.dot_general(
        left_mat, right_mat, (((0,), (0,)), ((), ())), preferred_element_type=FLOAT
    )


def contract_cols(left_mat, right_mat):
    return lax.dot_general(
        left_mat, right_mat, (((1,), (1,)), ((), ())), preferred_element_type=FLOAT
    )


def matmul(left_mat, right_mat):
    return jnp.dot(left_mat, right_mat, preferred_element_type=FLOAT)


def flip(index, mask):
    bit = 1
    while bit <= mask:
        if mask & bit:
            index = index + bit * (1 - 2 * lax.rem(lax.div(index, bit), 2))
        bit *= 2
    return index


def cols(block, size):
    return pl.ds(pl.multiple_of(block * size, size), size)


class _ShapeOnly:
    def __init__(self, shape):
        self.shape = tuple(shape)

    @property
    def at(self):
        return self

    def __getitem__(self, index):
        index = index if isinstance(index, tuple) else (index,)
        shape = []
        for size, i in zip(self.shape, index):
            if isinstance(i, slice):
                shape.append(len(range(*i.indices(size))))
            elif hasattr(i, "size") and hasattr(i, "start"):
                shape.append(i.size)
        return _ShapeOnly(tuple(shape) + self.shape[len(index) :])


class Send(NamedTuple):
    src: Callable
    dst: Callable
    dz: int
    df: int
    after: int | None = None
    planes: tuple | None = None


def only_on(planes, z, do):
    if planes is None:
        do()
        return
    here = z == planes[0]
    for plane in planes[1:]:
        here = jnp.logical_or(here, z == plane)
    pl.when(here)(do)


def exchange(name, cid, arrays, out_shapes, sends, micros):
    n_in, n_out = len(arrays), len(out_shapes)
    peers = sorted({(s.dz, s.df) for s in sends} - {(0, 0)})
    stays = [k for k, s in enumerate(sends) if (s.dz, s.df) == (0, 0)]
    stay_shapes = []

    def probe(*refs):
        for k in stays:
            view = sends[k].src(refs, None, jnp.int32(0), jnp.int32(0))
            stay_shapes.append(view.shape)

    probe(*[_ShapeOnly(a.shape) for a in arrays])

    def kernel(*refs):
        ins, outs = refs[:n_in], refs[n_in : n_in + n_out]
        send_sems, recv_sems = refs[n_in + n_out : n_in + n_out + 2]
        bounce = dict(zip(stays, refs[n_in + n_out + 2 :]))
        z = lax.axis_index("sp")
        f = lax.axis_index("fsdp")
        barrier = pltpu.get_barrier_semaphore()
        for dz, df in peers:
            pl.semaphore_signal(
                barrier, inc=1, device_id=(flip(z, dz), flip(f, df)), device_id_type=MESH
            )
        pl.semaphore_wait(barrier, len(peers))
        copies = []
        for k, s in enumerate(sends):
            src = s.src(ins, outs, z, f)
            dst = s.dst(ins, outs, z, f)
            if (s.dz, s.df) == (0, 0):
                copies.append(
                    (
                        pltpu.make_async_copy(src, bounce[k], recv_sems.at[k]),
                        pltpu.make_async_copy(bounce[k], dst, send_sems.at[k]),
                    )
                )
            else:
                copies.append(
                    pltpu.make_async_remote_copy(
                        src_ref=src,
                        dst_ref=dst,
                        send_sem=send_sems.at[k],
                        recv_sem=recv_sems.at[k],
                        device_id=(flip(z, s.dz), flip(f, s.df)),
                        device_id_type=MESH,
                    )
                )
        arrived = set()

        def arrive(k):
            if k not in arrived:
                arrived.add(k)
                s = sends[k]
                if (s.dz, s.df) == (0, 0):
                    copies[k][1].wait()
                else:
                    only_on(s.planes, flip(z, s.dz), copies[k].wait_recv)

        for k, s in enumerate(sends):
            if k in stays:
                copies[k][0].start()
            elif s.after is None:
                only_on(s.planes, z, copies[k].start)
        for k in stays:
            copies[k][0].wait()
            copies[k][1].start()
        for k, s in enumerate(sends):
            if s.after is not None:
                arrive(s.after)
                copies[k].start()
        for k, s in enumerate(sends):
            if (s.dz, s.df) != (0, 0):
                only_on(s.planes, z, copies[k].wait_send)
            arrive(k)

    result = pl.pallas_call(
        kernel,
        out_shape=[jax.ShapeDtypeStruct(shape, BF16) for shape in out_shapes],
        in_specs=[pl.BlockSpec(memory_space=pl.ANY)] * n_in,
        out_specs=[pl.BlockSpec(memory_space=pl.ANY)] * n_out,
        scratch_shapes=[
            pltpu.SemaphoreType.DMA((len(sends),)),
            pltpu.SemaphoreType.DMA((len(sends),)),
        ]
        + [pltpu.VMEM(shape, BF16) for shape in stay_shapes],
        compiler_params=pltpu.CompilerParams(
            collective_id=cid, has_side_effects=True, vmem_limit_bytes=32 * 1024 * 1024
        ),
        cost_estimate=pl.CostEstimate(
            flops=0, bytes_accessed=int(micros * 3.0e6), transcendentals=0
        ),
        name=name,
    )(*arrays)
    return result


def rows_to_experts(cid, tokens, lanes, pick, plane_experts, parts):
    planes, picked, count = pick.shape
    cap = picked // plane_experts
    arrays = (tokens, lanes)
    widths = [a.shape[1] for a in arrays]
    order = [0, 1, 3, 2] if planes == 4 else list(range(planes))
    early = 2 if planes == 4 else planes - 1
    step = 512

    def kernel(tokens_ref, lanes_ref, pick_ref, rows_ref, lane_rows_ref, *scratch):
        here, chosen = scratch[:2], scratch[2:4]
        z_send, z_recv, row_send, row_recv = scratch[4:]
        ins, outs = (tokens_ref, lanes_ref), (rows_ref, lane_rows_ref)
        z = lax.axis_index("sp")
        f = lax.axis_index("fsdp")
        barrier = pltpu.get_barrier_semaphore()
        for d in range(1, planes):
            pl.semaphore_signal(barrier, inc=1, device_id=(flip(z, d), f), device_id_type=MESH)
        for s in range(1, plane_experts):
            pl.semaphore_signal(
                barrier, inc=1, device_id=(z, flip(f, s * parts)), device_id_type=MESH
            )
        pl.semaphore_wait(barrier, planes + plane_experts - 2)

        def across(d, w):
            if d == 0:
                return pltpu.make_async_copy(ins[w], here[w].at[0], z_recv.at[w])
            return pltpu.make_async_remote_copy(
                src_ref=ins[w],
                dst_ref=here[w].at[d],
                send_sem=z_send.at[2 * d + w],
                recv_sem=z_recv.at[2 * d + w],
                device_id=(flip(z, d), f),
                device_id_type=MESH,
            )

        def onward(d, s, w):
            src = chosen[w].at[d, pl.ds(s * cap, cap)]
            dst = outs[w].at[s, d]
            k = (d * plane_experts + s) * 2 + w
            if s == 0:
                return pltpu.make_async_copy(src, dst, row_recv.at[k])
            return pltpu.make_async_remote_copy(
                src_ref=src,
                dst_ref=dst,
                send_sem=row_send.at[k],
                recv_sem=row_recv.at[k],
                device_id=(z, flip(f, s * parts)),
                device_id_type=MESH,
            )

        for d in order[: early + 1]:
            for w in range(2):
                across(d, w).start()
        for turn, d in enumerate(order):
            for w in range(2):
                if d == 0:
                    across(d, w).wait()
                else:
                    across(d, w).wait_recv()
            if turn == 1:
                for later in order[early + 1 :]:
                    for w in range(2):
                        across(later, w).start()

            def columns(i, carry):
                at = pl.ds(pl.multiple_of(i * step, step), step)
                chosen[0][d, :, at] = jnp.dot(
                    pick_ref[d], here[0][d, :, at], preferred_element_type=FLOAT
                ).astype(BF16)
                return carry

            lax.fori_loop(0, widths[0] // step, columns, 0)
            chosen[1][d] = jnp.dot(
                pick_ref[d], here[1][d], preferred_element_type=FLOAT
            ).astype(BF16)
            for s in range(plane_experts):
                for w in range(2):
                    onward(d, s, w).start()
        for d in range(planes):
            for w in range(2):
                if d:
                    across(d, w).wait_send()
                for s in range(plane_experts):
                    onward(d, s, w).wait()

    hbm = pl.BlockSpec(memory_space=pl.ANY)
    sems = planes * plane_experts * 2
    return pl.pallas_call(
        kernel,
        out_shape=[
            jax.ShapeDtypeStruct((plane_experts, planes, cap, width), BF16) for width in widths
        ],
        in_specs=[hbm, hbm, pl.BlockSpec(memory_space=pltpu.VMEM)],
        out_specs=[hbm, hbm],
        scratch_shapes=[pltpu.VMEM((planes, count, width), BF16) for width in widths]
        + [pltpu.VMEM((planes, picked, width), BF16) for width in widths]
        + [pltpu.SemaphoreType.DMA((2 * planes,))] * 2
        + [pltpu.SemaphoreType.DMA((sems,))] * 2,
        compiler_params=pltpu.CompilerParams(
            collective_id=cid, has_side_effects=True, vmem_limit_bytes=40 * 1024 * 1024
        ),
        cost_estimate=pl.CostEstimate(flops=0, bytes_accessed=int(2.1e8), transcendentals=0),
        name="rows_to_experts",
    )(tokens, lanes, pick)


def rows_from_experts(cid, rows_in, lanes_in, pick, weights):
    planes, picked, count = pick.shape
    plane_experts, _, cap, _ = rows_in.shape
    parts = weights[0].shape[1]
    inner_shape = weights[0].shape[2:]
    widths = (rows_in.shape[3], lanes_in.shape[3])
    order = [2, 3, 1, 0] if planes == 4 else list(range(planes - 1, -1, -1))
    step = 512

    def kernel(rows_ref, lanes_ref, pick_ref, first_ref, second_ref, *rest):
        outs, shards_ref = rest[:2], rest[2]
        back, partial, own, others = rest[3:5], rest[5:7], rest[7], rest[8]
        row_send, row_recv, z_send, z_recv, pair_send, pair_recv, load, w_send, w_recv = rest[9:]
        ins, weight_refs = (rows_ref, lanes_ref), (first_ref, second_ref)
        z = lax.axis_index("sp")
        f = lax.axis_index("fsdp")
        part = lax.rem(f, parts)
        place = lax.div(f, parts)
        barrier = pltpu.get_barrier_semaphore()
        for d in range(1, planes):
            pl.semaphore_signal(barrier, inc=1, device_id=(flip(z, d), f), device_id_type=MESH)
        near = list(range(1, parts)) + [s * parts for s in range(1, plane_experts)]
        for m in near:
            pl.semaphore_signal(barrier, inc=1, device_id=(z, flip(f, m)), device_id_type=MESH)
        pl.semaphore_wait(barrier, planes - 1 + len(near))

        def pair(w, p):
            k = w * (parts - 1) + p - 1
            return pltpu.make_async_remote_copy(
                src_ref=weight_refs[w].at[:, flip(part, p)],
                dst_ref=others.at[p - 1, w],
                send_sem=pair_send.at[k],
                recv_sem=pair_recv.at[k],
                device_id=(z, flip(f, p)),
                device_id_type=MESH,
            )

        def load_own(w):
            return pltpu.make_async_copy(weight_refs[w].at[:, part], own.at[w], load.at[w])

        def home(d, s, w):
            src = ins[w].at[s, d]
            dst = back[w].at[d, pl.ds(s * cap, cap)]
            k = (d * plane_experts + s) * 2 + w
            if s == 0:
                return pltpu.make_async_copy(src, dst, row_recv.at[k])
            return pltpu.make_async_remote_copy(
                src_ref=src,
                dst_ref=dst,
                send_sem=row_send.at[k],
                recv_sem=row_recv.at[k],
                device_id=(z, flip(f, s * parts)),
                device_id_type=MESH,
            )

        def across(d, w):
            src, dst = partial[w].at[d], outs[w].at[d]
            if d == 0:
                return pltpu.make_async_copy(src, dst, z_recv.at[w])
            return pltpu.make_async_remote_copy(
                src_ref=src,
                dst_ref=dst,
                send_sem=z_send.at[2 * d + w],
                recv_sem=z_recv.at[2 * d + w],
                device_id=(flip(z, d), f),
                device_id_type=MESH,
            )

        def to_shard(s, w):
            src, dst = own.at[w, flip(place, s)], shards_ref.at[w, place]
            if s == 0:
                return pltpu.make_async_copy(src, dst, w_recv.at[w])
            return pltpu.make_async_remote_copy(
                src_ref=src,
                dst_ref=dst,
                send_sem=w_send.at[2 * s + w],
                recv_sem=w_recv.at[2 * s + w],
                device_id=(z, flip(f, s * parts)),
                device_id_type=MESH,
            )

        for w in range(2):
            load_own(w).start()
            for p in range(1, parts):
                pair(w, p).start()
        for d in order:
            for s in range(plane_experts):
                for w in range(2):
                    home(d, s, w).start()
        for w in range(2):
            load_own(w).wait()
            for p in range(1, parts):
                pair(w, p).wait()

            def add(i, carry):
                e = lax.div(i, inner_shape[0] // 16)
                at = pl.ds(pl.multiple_of(lax.rem(i, inner_shape[0] // 16) * 16, 16), 16)
                total = own[w, e, at, :].astype(FLOAT)
                for p in range(parts - 1):
                    total = total + others[p, w, e, at, :].astype(FLOAT)
                own[w, e, at, :] = total.astype(BF16)
                return carry

            lax.fori_loop(0, plane_experts * (inner_shape[0] // 16), add, 0)
        for turn, d in enumerate(order):
            for s in range(plane_experts):
                for w in range(2):
                    home(d, s, w).wait()
            if turn == planes - 2:
                for s in range(plane_experts):
                    for w in range(2):
                        to_shard(s, w).start()

            def columns(i, carry):
                at = pl.ds(pl.multiple_of(i * step, step), step)
                partial[0][d, :, at] = contract_rows(pick_ref[d], back[0][d, :, at]).astype(BF16)
                return carry

            lax.fori_loop(0, widths[0] // step, columns, 0)
            partial[1][d] = contract_rows(pick_ref[d], back[1][d]).astype(BF16)
            for w in range(2):
                across(d, w).start()
        for d in range(planes):
            for w in range(2):
                across(d, w).wait()
        for s in range(plane_experts):
            for w in range(2):
                to_shard(s, w).wait()

    hbm = pl.BlockSpec(memory_space=pl.ANY)
    dma = pltpu.SemaphoreType.DMA
    row_count = planes * plane_experts * 2
    return pl.pallas_call(
        kernel,
        out_shape=[jax.ShapeDtypeStruct((planes, count, width), BF16) for width in widths]
        + [jax.ShapeDtypeStruct((2, plane_experts) + inner_shape, BF16)],
        in_specs=[hbm, hbm, pl.BlockSpec(memory_space=pltpu.VMEM), hbm, hbm],
        out_specs=[hbm] * 3,
        scratch_shapes=[pltpu.VMEM((planes, picked, width), BF16) for width in widths]
        + [pltpu.VMEM((planes, count, width), BF16) for width in widths]
        + [
            pltpu.VMEM((2, plane_experts) + inner_shape, BF16),
            pltpu.VMEM((parts - 1, 2, plane_experts) + inner_shape, BF16),
        ]
        + [dma((row_count,))] * 2
        + [dma((2 * planes,))] * 2
        + [dma((2 * (parts - 1),))] * 2
        + [dma((2,))]
        + [dma((2 * plane_experts,))] * 2,
        compiler_params=pltpu.CompilerParams(
            collective_id=cid, has_side_effects=True, vmem_limit_bytes=48 * 1024 * 1024
        ),
        cost_estimate=pl.CostEstimate(flops=0, bytes_accessed=int(2.7e8), transcendentals=0),
        name="rows_from_experts",
    )(rows_in, lanes_in, pick, *weights)


def line_sum(cid, arrays, pieces, blocks, handed):
    n = len(arrays)
    chunks = [
        (k, c * (a.shape[0] // p), a.shape[0] // p)
        for k, (a, p) in enumerate(zip(arrays, pieces))
        for c in range(p)
    ]
    far = blocks.shape[0] - 1
    assert far == 3

    def kernel(*refs):
        ins, blocks_ref, handed_refs = refs[:n], refs[n], refs[n + 1 : n + 3]
        outs, others_ref = refs[n + 3 : 2 * n + 3], refs[2 * n + 3]
        own, got, swapped = (refs[2 * n + 4 + n * i : 2 * n + 4 + n * (i + 1)] for i in range(3))
        mine, theirs = refs[5 * n + 4 : 5 * n + 6]
        load, store, in_s, in_r, swap_s, swap_r, back_s, back_r, far_s, far_r = refs[5 * n + 6 :]
        z = lax.axis_index("sp")
        f = lax.axis_index("fsdp")
        inner = jnp.logical_or(z == 1, z == 2)
        barrier = pltpu.get_barrier_semaphore()
        for d in range(1, far + 1):
            pl.semaphore_signal(barrier, inc=1, device_id=(flip(z, d), f), device_id_type=MESH)
        pl.semaphore_wait(barrier, far)

        def view(refs, c):
            k, start, size = chunks[c]
            return refs[k].at[pl.ds(start, size)]

        def remote(src, dst, send, recv, c, dz):
            return pltpu.make_async_remote_copy(
                src_ref=view(src, c),
                dst_ref=view(dst, c),
                send_sem=send.at[c],
                recv_sem=recv.at[c],
                device_id=(flip(z, dz), f),
                device_id_type=MESH,
            )

        loads = [
            pltpu.make_async_copy(view(ins, c), view(own, c), load.at[c])
            for c in range(len(chunks))
        ]
        stores = [
            pltpu.make_async_copy(view(got, c), view(outs, c), store.at[c])
            for c in range(len(chunks))
        ]

        def block_copy(src, dst, send, recv, d):
            return pltpu.make_async_remote_copy(
                src_ref=src,
                dst_ref=dst,
                send_sem=far_s.at[send],
                recv_sem=far_r.at[recv],
                device_id=(flip(z, d), f),
                device_id_type=MESH,
            )

        near = block_copy(blocks_ref.at[1], others_ref.at[0], 0, 0, 1)
        block_loads = [
            pltpu.make_async_copy(blocks_ref.at[2 + k], mine.at[k], far_r.at[2 + k])
            for k in range(2)
        ] + [
            pltpu.make_async_copy(handed_refs[k], theirs.at[k], far_r.at[4 + k])
            for k in range(2)
        ]
        beyond = [block_copy(mine.at[k], others_ref.at[1], 1 + k, 1, 2 + k) for k in range(2)]
        inwards = [remote(own, got, in_s, in_r, c, 1) for c in range(len(chunks))]
        swaps = [remote(own, swapped, swap_s, swap_r, c, 3) for c in range(len(chunks))]
        backs = [remote(got, got, back_s, back_r, c, 1) for c in range(len(chunks))]
        for copy in loads:
            copy.start()

        def add(left, right, to, c):
            k, start, size = chunks[c]
            step = 16

            def rows(i, carry):
                at = pl.ds(pl.multiple_of(start + i * step, step), step)
                total = left[k][at, :].astype(FLOAT) + right[k][at, :].astype(FLOAT)
                to[k][at, :] = total.astype(BF16)
                return carry

            lax.fori_loop(0, size // step, rows, 0)

        def pass_on(k):
            def rows(i, carry):
                at = pl.ds(pl.multiple_of(i * 16, 16), 16)
                total = mine[k, at, :].astype(FLOAT) + theirs[1 - k, at, :].astype(FLOAT)
                mine[k, at, :] = total.astype(BF16)
                return carry

            lax.fori_loop(0, blocks.shape[1] // 16, rows, 0)
            beyond[k].start()

        @pl.when(jnp.logical_not(inner))
        def _():
            for c in range(len(chunks)):
                loads[c].wait()
                inwards[c].start()
            near.start()
            for c in range(len(chunks)):
                backs[c].wait_recv()
                stores[c].start()
            for c in range(len(chunks)):
                inwards[c].wait_send()
                stores[c].wait()

        @pl.when(inner)
        def _():
            near.start()
            for copy in block_loads:
                copy.start()
            for copy in block_loads:
                copy.wait()
            for k in range(2):
                pass_on(k)
            for c in range(len(chunks) + 1):
                if c < len(chunks):
                    loads[c].wait()
                    inwards[c].wait_recv()
                    add(own, got, own, c)
                    swaps[c].start()
                if c:
                    swaps[c - 1].wait_recv()
                    add(own, swapped, got, c - 1)
                    backs[c - 1].start()
                    stores[c - 1].start()
            for c in range(len(chunks)):
                swaps[c].wait_send()
                backs[c].wait_send()
                stores[c].wait()

            for copy in beyond:
                copy.wait_send()

        near.wait()
        beyond[0].wait_recv()

    hbm = pl.BlockSpec(memory_space=pl.ANY)
    buffers = [pltpu.VMEM(a.shape, BF16) for a in arrays]
    count = len(chunks)
    return pl.pallas_call(
        kernel,
        out_shape=[jax.ShapeDtypeStruct(a.shape, BF16) for a in arrays]
        + [jax.ShapeDtypeStruct((2,) + blocks.shape[1:], BF16)],
        in_specs=[hbm] * (n + 3),
        out_specs=[hbm] * (n + 1),
        scratch_shapes=buffers * 3
        + [pltpu.VMEM((2,) + blocks.shape[1:], BF16)] * 2
        + [pltpu.SemaphoreType.DMA((count,))] * 8
        + [pltpu.SemaphoreType.DMA((6,))] * 2,
        compiler_params=pltpu.CompilerParams(
            collective_id=cid, has_side_effects=True, vmem_limit_bytes=40 * 1024 * 1024
        ),
        cost_estimate=pl.CostEstimate(flops=0, bytes_accessed=int(4.0e8), transcendentals=0),
        name="line_sum",
    )(*arrays, blocks, *handed)


def body(
    tokens,
    expert_ids,
    attn_gain,
    query_weight,
    key_weight,
    value_weight,
    q_gain,
    k_gain,
    output_weight,
    ffn_gain,
    router_weight,
    w_gate,
    w_up,
    w_down,
    cotangent,
):
    nsp = lax.axis_size("sp")
    nf = lax.axis_size("fsdp")
    z = lax.axis_index("sp")
    f = lax.axis_index("fsdp")
    rows = tokens.shape[1]
    width = tokens.shape[2]
    shard = width // nf
    n_heads, kv_heads, head_dim = QUERY_HEADS, KEY_VALUE_HEADS, HEAD_SIZE
    my_heads = n_heads // nf
    rep = nf // kv_heads
    q_cols = my_heads * head_dim
    qkv_cols = q_cols + 2 * head_dim
    score_scale = 1.0 / math.sqrt(head_dim)
    n_experts = w_gate.shape[0]
    hidden_size = w_gate.shape[2]
    hid_shard = w_down.shape[1]
    plane_experts = n_experts // nsp
    parts = nf // plane_experts
    cap = CAP
    seqs = nf
    part = lax.rem(f, parts)
    place = lax.div(f, parts)
    expert = z * plane_experts + place

    def swap_f(block, mask):
        return lax.ppermute(block, "fsdp", [(i, i ^ mask) for i in range(nf)])

    def swap_z(block, mask):
        return lax.ppermute(block, "sp", [(i, i ^ mask) for i in range(nsp)])

    small = jnp.concatenate(
        [
            attn_gain.astype(BF16),
            ffn_gain.astype(BF16),
            q_gain.astype(BF16),
            k_gain.astype(BF16),
            router_weight.astype(BF16).reshape(-1),
        ]
    )
    small_rows = 16
    small = jnp.pad(small, (0, small_rows * width - small.shape[0])).reshape(small_rows, width)
    x_pay = jnp.concatenate([tokens[0], small], axis=0)
    pay_rows = rows + small_rows
    query_b = query_weight.astype(BF16)
    key_b = key_weight.astype(BF16)
    value_b = value_weight.astype(BF16)
    routes = expert_ids[0]
    expert_iota = jnp.arange(n_experts, dtype=jnp.int32)
    routed = jnp.any(routes[:, :, None] == expert_iota[None, None, :], axis=1)
    dy_pay = jnp.concatenate(
        [
            cotangent[0],
            routed.astype(BF16),
            jnp.zeros((rows, LANES - n_experts), BF16),
        ],
        axis=1,
    )
    wide = width + LANES

    def plane_cast(weight):
        return lax.dynamic_slice_in_dim(weight, z * plane_experts, plane_experts, 0).astype(BF16)

    gate_up_pay = jnp.stack([plane_cast(w_gate), plane_cast(w_up)], axis=1)
    down_pay = plane_cast(w_down)

    sends = []
    for m in range(0, nf, 2):
        sends.append(
            Send(
                lambda i, o, z, f, m=m: i[0],
                lambda i, o, z, f: o[0].at[f],
                0,
                m,
            )
        )
    for m in range(0, nf, 2):
        if m == 0:
            sends.append(
                Send(lambda i, o, z, f: i[0], lambda i, o, z, f: o[0].at[f], 0, 1)
            )
        else:
            sends.append(
                Send(
                    lambda i, o, z, f, m=m: o[0].at[flip(f, m)],
                    lambda i, o, z, f, m=m: o[0].at[flip(f, m)],
                    0,
                    1,
                    m // 2,
                )
            )
    for m in range(0, nf, rep):
        for w in range(2):
            sends.append(
                Send(
                    lambda i, o, z, f, m=m, w=w: i[2 + w].at[
                        :, cols(lax.div(flip(f, m), rep), head_dim)
                    ],
                    lambda i, o, z, f, w=w: o[1].at[
                        cols(f, shard), pl.ds(q_cols + w * head_dim, head_dim)
                    ],
                    0,
                    m,
                )
            )
            for p in range(1, rep):
                view = lambda i, o, z, f, m=m, w=w: o[1].at[
                    cols(flip(f, m), shard), pl.ds(q_cols + w * head_dim, head_dim)
                ]
                if m == 0:
                    sends.append(
                        Send(
                            lambda i, o, z, f, w=w: i[2 + w].at[:, cols(lax.div(f, rep), head_dim)],
                            view,
                            0,
                            p,
                        )
                    )
                else:
                    sends.append(Send(view, view, 0, p, len(sends) - p))
    for m in range(nf):
        sends.append(
            Send(
                lambda i, o, z, f, m=m: i[1].at[:, cols(flip(f, m), q_cols)],
                lambda i, o, z, f: o[1].at[cols(f, shard), pl.ds(0, q_cols)],
                0,
                m,
            )
        )
    for m in range(nsp):
        sends.append(
            Send(lambda i, o, z, f: i[4], lambda i, o, z, f, m=m: o[2].at[m], m, 0)
        )
    x_all, w_qkv, dy_z = exchange(
        "gather_inputs",
        0,
        (x_pay, query_b, key_b, value_b, dy_pay),
        ((nf, pay_rows, width), (width, qkv_cols), (nsp, rows, wide)),
        sends,
        65,
    )

    own_experts = z * plane_experts + jnp.bitwise_xor(
        place, jnp.arange(plane_experts, dtype=jnp.int32)
    )
    own_hot = (expert_iota[:, None] == own_experts[None, :]).astype(FLOAT)
    routed_z = lax.dot_general(
        own_hot,
        dy_z[:, :, width : width + n_experts].astype(FLOAT),
        (((0,), (2,)), ((), ())),
        preferred_element_type=FLOAT,
    ).transpose(1, 0, 2)
    earlier = jnp.triu(jnp.ones((rows, rows), FLOAT), 1)
    rank = jnp.dot(
        routed_z.reshape(nsp * plane_experts, rows), earlier, preferred_element_type=FLOAT
    ).reshape(nsp, plane_experts, rows)
    rank = rank * routed_z + (routed_z - 1.0)
    pick = (
        rank[:, :, None, :] == jnp.arange(cap, dtype=FLOAT)[None, None, :, None]
    ).astype(BF16)
    pick = pick.reshape(nsp, plane_experts * cap, rows)

    x_all, gate_up_pay = lax.optimization_barrier((x_all, gate_up_pay))
    by_expert = pick.reshape(nsp, plane_experts, cap, rows)
    gate_up_pieces, dy_pieces = [], []
    for s in range(plane_experts):
        weights = lax.dynamic_index_in_dim(gate_up_pay, flip(place, s), 0, keepdims=False)
        dy_rows = jnp.einsum(
            "drt,dtc->drc", by_expert[:, s], dy_z[:, :, :width], preferred_element_type=FLOAT
        )
        dy_rows = dy_rows.astype(BF16).reshape(nsp * cap, width)
        if s and s == plane_experts - 1:
            both = jnp.concatenate([dy_rows, weights.reshape(-1, width)], axis=0)
            both = swap_f(both, s * parts)
            dy_rows = both[: nsp * cap]
            weights = both[nsp * cap :].reshape(2, shard, hidden_size)
        elif s:
            weights = swap_f(weights, s * parts)
            dy_rows = swap_f(dy_rows, s * parts)
        gate_up_pieces.append(weights)
        dy_pieces.append(dy_rows)
    dy_in = jnp.concatenate(dy_pieces, axis=0)

    small_all = x_all[:, rows:, :].reshape(nf, small_rows * width)
    at = 0
    pieces = []
    for size in (shard, shard, head_dim // nf, head_dim // nf, shard * n_experts):
        pieces.append(small_all[:, at : at + size])
        at += size
    g_attn = pieces[0].reshape(width).astype(FLOAT)
    g_ffn = pieces[1].reshape(width).astype(FLOAT)
    g_query = pieces[2].reshape(head_dim).astype(FLOAT)
    g_key = pieces[3].reshape(head_dim).astype(FLOAT)
    wr_b = pieces[4].reshape(width, n_experts)

    xn_b = (
        rms_norm(x_all[:, :rows, :].astype(FLOAT), g_attn).astype(BF16).reshape(seqs * rows, width)
    )
    qkv_lin = matmul(xn_b, w_qkv)

    def split_heads(flat):
        flat = flat.reshape(seqs, rows, -1)
        return jnp.stack(
            [
                flat[:, :, h * head_dim : (h + 1) * head_dim]
                for h in range(flat.shape[2] // head_dim)
            ],
            axis=1,
        )

    def join_heads(split):
        joined = jnp.concatenate([split[:, h] for h in range(split.shape[1])], axis=2)
        return joined.reshape(seqs * rows, -1)

    q_lin = split_heads(qkv_lin[:, :q_cols])
    k_lin = split_heads(qkv_lin[:, q_cols : q_cols + head_dim])
    v_b = qkv_lin[:, q_cols + head_dim :].astype(BF16)
    half_dim = head_dim // 2
    inverse_freq = THETA ** (-(jnp.arange(half_dim, dtype=FLOAT) * 2.0 / head_dim))
    positions = (z * rows + jnp.arange(rows, dtype=jnp.int32)).astype(FLOAT)
    angles = positions[:, None] * inverse_freq[None, :]
    cosine = jnp.cos(angles)[None, None]
    sine_part = jnp.sin(angles)[None, None]

    def prep_heads(linear, gain_vec):
        return rotate(rms_norm(linear, gain_vec), cosine, sine_part)

    q_rows = prep_heads(q_lin, g_query).astype(BF16)
    k_b = join_heads(prep_heads(k_lin, g_key).astype(BF16))

    kv_pay = jnp.concatenate([k_b, v_b], axis=1)
    piece = seqs * rows // rep
    sends = []
    for d in range(nsp):
        sends.append(
            Send(
                lambda i, o, z, f: i[0].at[pl.ds(lax.rem(f, rep) * piece, piece)],
                lambda i, o, z, f, d=d: o[0].at[d, pl.ds(lax.rem(f, rep) * piece, piece)],
                d,
                0,
            )
        )
    for d in range(nsp):
        for p in range(1, rep):
            sends.append(
                Send(
                    lambda i, o, z, f, d=d: o[0].at[d, pl.ds(lax.rem(f, rep) * piece, piece)],
                    lambda i, o, z, f, d=d: o[0].at[d, pl.ds(lax.rem(f, rep) * piece, piece)],
                    0,
                    p,
                    d,
                )
            )
    (kv_z,) = exchange(
        "gather_keys", 1, (kv_pay,), ((nsp, seqs * rows, 2 * head_dim),), sends, 24
    )
    kv_seq = kv_z.reshape(nsp, seqs, rows, 2 * head_dim).transpose(1, 0, 2, 3)
    kv_seq = kv_seq.reshape(seqs, nsp * rows, 2 * head_dim)
    keys = kv_seq[:, :, :head_dim]
    values = kv_seq[:, :, head_dim:]

    plane_of = jnp.bitwise_xor(jnp.arange(nsp, dtype=jnp.int32), z)
    key_pos = (plane_of[:, None] * rows + jnp.arange(rows, dtype=jnp.int32)[None, :]).reshape(-1)
    query_pos = z * rows + jnp.arange(rows, dtype=jnp.int32)
    causal = key_pos[None, :] <= query_pos[:, None]
    scores = (
        jnp.einsum("nhqd,nkd->nhqk", q_rows, keys, preferred_element_type=FLOAT) * score_scale
    )
    expo = jnp.where(causal[None, None], jnp.exp(scores), 0.0)
    probs = (expo / jnp.sum(expo, axis=3, keepdims=True)).astype(BF16)
    o_rows = jnp.einsum("nhqk,nkd->nhqd", probs, values, preferred_element_type=FLOAT)
    o_mat = join_heads(o_rows.astype(BF16))
    wo_b = output_weight.astype(BF16)

    def pair_then_plane(partial, name, cid, more=(), more_shapes=(), more_sends=()):
        split = partial.astype(BF16).reshape(nf // 2, 2, rows, width)
        (other,) = exchange(
            name + "_pair",
            cid,
            (split,),
            ((nf // 2, rows, width),),
            [Send(lambda i, o, z, f: i[0].at[:, 1 - lax.rem(f, 2)], lambda i, o, z, f: o[0], 0, 1)],
            8,
        )
        own = lax.dynamic_index_in_dim(split, lax.rem(f, 2), 1, keepdims=False)
        summed = (own.astype(FLOAT) + other.astype(FLOAT)).astype(BF16)
        sends = [
            Send(
                lambda i, o, z, f, j=j: i[0].at[flip(lax.div(f, 2), j)],
                lambda i, o, z, f, j=j: o[0].at[j],
                0,
                2 * j,
            )
            for j in range(nf // 2)
        ]
        blocks, *rest = exchange(
            name + "_plane",
            cid + 1,
            (summed, *more),
            ((nf // 2, rows, width), *more_shapes),
            sends + list(more_sends),
            27,
        )
        return jnp.sum(blocks.astype(FLOAT), axis=0), rest

    sends = []
    for s in range(plane_experts):
        for p in range(parts):
            sends.append(
                Send(
                    lambda i, o, z, f, s=s: i[1 + s],
                    lambda i, o, z, f, s=s: o[1].at[:, flip(f, s * parts)],
                    0,
                    p,
                )
            )
    branch, (gate_up_all,) = pair_then_plane(
        matmul(o_mat, wo_b), "out_sum", 3, gate_up_pieces, ((2, nf, shard, hidden_size),), sends
    )
    wg_b = gate_up_all[0].reshape(width, hidden_size)
    wu_b = gate_up_all[1].reshape(width, hidden_size)
    x_rows = tokens[0].astype(FLOAT)
    mid_rows = x_rows + branch
    hn_b = rms_norm(mid_rows, g_ffn).astype(BF16)
    logits = matmul(hn_b, wr_b)
    logits = jnp.where(routed, logits, -1e30)
    expo = jnp.where(routed, jnp.exp(logits - jnp.max(logits, axis=1, keepdims=True)), 0.0)
    gates = expo / jnp.sum(expo, axis=1, keepdims=True)

    def two_parts(exact):
        high = exact.astype(BF16)
        return high, (exact - high.astype(FLOAT)).astype(BF16)

    gate_high, gate_low = two_parts(gates)
    gate_lanes = jnp.concatenate(
        [gate_high, gate_low, jnp.zeros((rows, LANES - 2 * n_experts), BF16)], axis=1
    )
    hn_rows, gate_rows = rows_to_experts(5, hn_b, gate_lanes, pick, plane_experts, parts)
    hn_rows, down_pay = lax.optimization_barrier((hn_rows, down_pay))
    down_pieces = []
    for s in range(plane_experts):
        block = lax.dynamic_index_in_dim(down_pay, flip(place, s), 0, keepdims=False)
        down_pieces.append(swap_f(block, s * parts) if s else block)

    n_rows = plane_experts * nsp * cap
    hn_in = hn_rows.reshape(n_rows, width)
    hot = (jnp.arange(n_experts, dtype=jnp.int32) == expert).astype(FLOAT)
    tail = gate_rows.reshape(n_rows, LANES)[:, : 2 * n_experts].astype(FLOAT)
    row_gate = jnp.sum(
        (tail[:, :n_experts] + tail[:, n_experts:]) * hot[None, :], axis=1, keepdims=True
    )
    gate_pre = matmul(hn_in, wg_b)
    up_pre = matmul(hn_in, wu_b)
    sigma = jax.nn.sigmoid(gate_pre)
    act_f = gate_pre * sigma
    hidden = (act_f * up_pre).astype(BF16)
    dy_f = dy_in.astype(FLOAT)
    d_result = (row_gate * dy_f).astype(BF16)

    def by_shard(full, inner):
        return full.astype(BF16).reshape((plane_experts, parts) + inner)

    def pair_total(own, others):
        total = lax.dynamic_index_in_dim(own, part, 1, keepdims=False).astype(FLOAT)
        for other in others:
            total = total + other.astype(FLOAT)
        return total.astype(BF16)

    d_down = by_shard(contract_rows(hidden, d_result), (hid_shard, width))
    d_down, down_pieces = lax.optimization_barrier((d_down, down_pieces))
    d_down = pair_total(
        d_down,
        [
            swap_f(lax.dynamic_index_in_dim(d_down, flip(part, p), 1, keepdims=False), p)
            for p in range(1, parts)
        ],
    )
    d_down = [
        swap_f(lax.dynamic_index_in_dim(d_down, flip(place, s), 0, keepdims=False), s * parts)
        if s
        else lax.dynamic_index_in_dim(d_down, place, 0, keepdims=False)
        for s in range(plane_experts)
    ]
    down_pieces = jnp.stack(down_pieces)
    down_pieces = jnp.stack(
        [swap_f(down_pieces, p) if p else down_pieces for p in range(parts)], axis=1
    ).reshape(nf, hid_shard, width)
    wd_b = jnp.take(
        down_pieces, jnp.bitwise_xor(jnp.arange(nf, dtype=jnp.int32), f), axis=0, mode="clip"
    ).reshape(hidden_size, width)
    result = matmul(hidden, wd_b)
    row_dgate = jnp.sum(result * dy_f, axis=1, keepdims=True)
    weighted = (row_gate * result).astype(BF16)
    d_hidden = contract_cols(d_result, wd_b)
    d_gate_pre = (d_hidden * up_pre * sigma * (1.0 + gate_pre * (1.0 - sigma))).astype(BF16)
    d_up_pre = (d_hidden * act_f).astype(BF16)
    d_down, d_gate_pre, d_up_pre = lax.optimization_barrier((d_down, d_gate_pre, d_up_pre))
    in_order = jnp.bitwise_xor(jnp.arange(plane_experts, dtype=jnp.int32), place)
    d_down = jnp.take(jnp.stack(d_down), in_order, axis=0, mode="clip")
    all_down = lax.all_gather(d_down, "sp")
    d_in = (contract_cols(d_gate_pre, wg_b) + contract_cols(d_up_pre, wu_b)).astype(BF16)
    dgate_high, dgate_low = two_parts(row_dgate * hot[None, :])
    dgate_lanes = jnp.concatenate(
        [dgate_high, dgate_low, jnp.zeros((n_rows, LANES - 2 * n_experts), BF16)], axis=1
    )

    d_weights = (
        by_shard(contract_rows(hn_in, d_gate_pre), (shard, hidden_size)),
        by_shard(contract_rows(hn_in, d_up_pre), (shard, hidden_size)),
    )

    d_home, dgate_home, shards = rows_from_experts(
        7,
        d_in.reshape(plane_experts, nsp, cap, width),
        dgate_lanes.reshape(plane_experts, nsp, cap, LANES),
        pick,
        d_weights,
    )

    def combine(returned):
        flat = returned.reshape(nsp, plane_experts * cap, returned.shape[3])
        return jnp.einsum("drt,drc->dtc", pick, flat, preferred_element_type=FLOAT).astype(BF16)

    all_gate_up = lax.all_gather(shards, "sp")
    d_home = jnp.sum(d_home.astype(FLOAT), axis=0)
    tail = jnp.sum(dgate_home.astype(FLOAT), axis=0)
    d_gates = tail[:, :n_experts] + tail[:, n_experts : 2 * n_experts]
    d_logits = gates * (d_gates - jnp.sum(gates * d_gates, axis=1, keepdims=True))
    d_router = jnp.dot(hn_b.astype(FLOAT).T, d_logits, precision=HIGH_PRECISION)
    d_hn = d_home + jnp.dot(d_logits, wr_b.astype(FLOAT).T, precision=HIGH_PRECISION)
    grad_out = cotangent[0].astype(FLOAT)
    unused, ffn_pull = jax.vjp(rms_norm, mid_rows, g_ffn)
    d_mid_norm, d_ffn_gain = ffn_pull(d_hn)
    d_mid = grad_out + d_mid_norm

    d_attn_b = d_mid.astype(BF16)
    sends = [
        Send(lambda i, o, z, f: i[0], lambda i, o, z, f: o[0].at[f], 0, m)
        for m in range(0, nf, 2)
    ]
    for m in range(0, nf, 2):
        if m == 0:
            sends.append(Send(lambda i, o, z, f: i[0], lambda i, o, z, f: o[0].at[f], 0, 1))
        else:
            sends.append(
                Send(
                    lambda i, o, z, f, m=m: o[0].at[flip(f, m)],
                    lambda i, o, z, f, m=m: o[0].at[flip(f, m)],
                    0,
                    1,
                    m // 2,
                )
            )
    (da_all,) = exchange("gather_grads", 9, (d_attn_b,), ((nf, rows, width),), sends, 30)
    da_all = da_all.reshape(seqs * rows, width)
    d_wo = contract_rows(o_mat, da_all)
    d_o = split_heads(contract_cols(da_all, wo_b).astype(BF16))
    d_val = jnp.einsum("nhqk,nhqd->nkd", probs, d_o, preferred_element_type=FLOAT)
    d_probs = jnp.einsum("nhqd,nkd->nhqk", d_o, values, preferred_element_type=FLOAT)
    probs_f = probs.astype(FLOAT)
    d_scores = (
        probs_f * (d_probs - jnp.sum(probs_f * d_probs, axis=3, keepdims=True))
    ).astype(BF16)
    dq = (
        jnp.einsum("nhqk,nkd->nhqd", d_scores, keys, preferred_element_type=FLOAT) * score_scale
    ).astype(BF16)
    d_key = (
        jnp.einsum("nhqk,nhqd->nkd", d_scores, q_rows, preferred_element_type=FLOAT) * score_scale
    )
    d_kv = jnp.concatenate([d_key, d_val], axis=2).astype(BF16)
    d_kv = d_kv.reshape(seqs, nsp, rows, 2 * head_dim).transpose(1, 0, 2, 3)
    d_kv = d_kv.reshape(nsp, seqs * rows, 2 * head_dim)
    d_kv, all_down = lax.optimization_barrier((d_kv, all_down))
    grad_down = all_down.astype(FLOAT).reshape(n_experts, hid_shard, width)
    d_kv = d_kv.reshape(nsp, rep, piece, 2 * head_dim)
    (others,) = exchange(
        "key_grads_group",
        11,
        (d_kv,),
        ((rep - 1, nsp, piece, 2 * head_dim),),
        [
            Send(
                lambda i, o, z, f, p=p: i[0].at[:, flip(lax.rem(f, rep), p)],
                lambda i, o, z, f, p=p: o[0].at[p - 1],
                0,
                p,
            )
            for p in range(1, rep)
        ],
        6,
    )
    d_kv = lax.dynamic_index_in_dim(d_kv, lax.rem(f, rep), 1, keepdims=False)
    d_kv = (d_kv.astype(FLOAT) + jnp.sum(others.astype(FLOAT), axis=0)).astype(BF16)
    sends = [
        Send(lambda i, o, z, f, d=d: i[0].at[d], lambda i, o, z, f, d=d: o[0].at[d - 1], d, 0)
        for d in range(1, nsp)
    ]
    for s in range(plane_experts):
        sends.append(
            Send(
                lambda i, o, z, f, s=s: i[1].at[s],
                lambda i, o, z, f, s=s: o[1].at[:, s],
                0,
                s * parts,
            )
        )
    others, out_back = exchange(
        "key_grads_planes",
        10,
        (d_kv, weighted.reshape(plane_experts, nsp, cap, width)),
        ((nsp - 1, piece, 2 * head_dim), (nsp, plane_experts, cap, width)),
        sends,
        60,
    )
    out_blocks = combine(out_back)
    d_kv = (d_kv[0].astype(FLOAT) + jnp.sum(others.astype(FLOAT), axis=0)).astype(BF16)
    (d_kv,) = exchange(
        "key_grads_share",
        15,
        (d_kv,),
        ((rep, piece, 2 * head_dim),),
        [
            Send(lambda i, o, z, f: i[0], lambda i, o, z, f: o[0].at[lax.rem(f, rep)], 0, p)
            for p in range(rep)
        ],
        6,
    )
    d_kv = d_kv.reshape(seqs * rows, 2 * head_dim).astype(FLOAT)
    dq, grad_down = lax.optimization_barrier((dq, grad_down))
    unused, q_pull = jax.vjp(prep_heads, q_lin, g_query)
    d_q_lin, d_q_gain = q_pull(dq.astype(FLOAT))
    unused, k_pull = jax.vjp(prep_heads, k_lin, g_key)
    d_k_lin, d_k_gain = k_pull(d_kv[:, :head_dim].reshape(seqs, 1, rows, head_dim))
    dq_b = join_heads(d_q_lin.astype(BF16))
    dk_b = join_heads(d_k_lin.astype(BF16))
    dv_b = d_kv[:, head_dim:].astype(BF16)
    d_qkv = jnp.concatenate([dq_b, dk_b, dv_b], axis=1)
    share = 1.0 / rep
    d_qkv_shared = jnp.concatenate([dq_b, dk_b * BF16(share), dv_b * BF16(share)], axis=1)
    d_w_qkv = contract_rows(xn_b, d_qkv).astype(BF16)

    def hand_over(which, i_at, o_at):
        return Send(
            lambda i, o, z, f: i[i_at].at[which], lambda i, o, z, f: o[o_at], 1, 0, None, (0, 3)
        )

    more = ((), (), ())
    if nsp == 4:
        more = ((out_blocks,), ((rows, width),), (hand_over(2, 1, 1),))
    d_xn, handed = pair_then_plane(contract_cols(d_qkv_shared, w_qkv), "input_sum", 13, *more)
    unused, attn_pull = jax.vjp(rms_norm, x_rows, g_attn)
    d_x_norm, d_attn_gain = attn_pull(d_xn)
    grad_tokens = (d_mid + d_x_norm)[None]

    smalls = jnp.concatenate(
        [
            d_attn_gain.reshape(nf, shard),
            d_ffn_gain.reshape(nf, shard),
            d_q_gain.reshape(nf, head_dim // nf),
            (d_k_gain * share).reshape(nf, head_dim // nf),
            d_router.reshape(nf, shard * n_experts),
        ],
        axis=1,
    ).astype(BF16)
    small_size = smalls.shape[1]
    small_cols = pl.cdiv(small_size, kv_heads * head_dim) * kv_heads * head_dim // small_rows
    small_cols = pl.cdiv(small_cols, LANES) * LANES
    smalls = jnp.pad(smalls, ((0, 0), (0, small_rows * small_cols - small_size)))
    kv_cols = kv_heads * head_dim
    sends = []
    for m in range(nf):
        sends.append(
            Send(
                lambda i, o, z, f, m=m: i[0].at[cols(flip(f, m), shard), pl.ds(0, q_cols)],
                lambda i, o, z, f: o[0].at[:, cols(f, q_cols)],
                0,
                m,
            )
        )
        sends.append(
            Send(lambda i, o, z, f, m=m: i[1].at[flip(f, m)], lambda i, o, z, f: o[2].at[f], 0, m)
        )
    for m in range(0, nf, rep):
        for w in range(2):
            sends.append(
                Send(
                    lambda i, o, z, f, m=m, w=w: i[0].at[
                        cols(flip(f, m), shard), pl.ds(q_cols + w * head_dim, head_dim)
                    ],
                    lambda i, o, z, f, w=w: o[1].at[
                        pl.ds(w * shard, shard), cols(lax.div(f, rep), head_dim)
                    ],
                    0,
                    m,
                )
            )
    if nsp == 4:
        sends.append(hand_over(3, 2, 3))
    d_wq, d_wkv, small_shard, handed_last = exchange(
        "head_grads_to_shards",
        12,
        (d_w_qkv, smalls.reshape(nf, small_rows, small_cols), out_blocks),
        (
            (shard, n_heads * head_dim),
            (2 * shard, kv_cols),
            (nf, small_rows, small_cols),
            (rows, width),
        ),
        sends,
        36,
    )
    small_sum = jnp.sum(small_shard.astype(FLOAT), axis=0).astype(BF16)
    if nsp == 4:
        sum_q, sum_out, sum_kv, small_sum, out_others = line_sum(
            16, (d_wq, d_wo.astype(BF16), d_wkv, small_sum), (16, 16, 4, 1), out_blocks, (handed[0], handed_last)
        )
        out_others = [out_others[d] for d in range(2)]
    else:
        sum_q, sum_out, sum_kv, small_sum = lax.psum(
            (d_wq, d_wo.astype(BF16), d_wkv, small_sum), "sp"
        )
        out_others = [swap_z(out_blocks[d], d) for d in range(1, nsp)]
    moe_sum = out_blocks[0].astype(FLOAT)
    for block in out_others:
        moe_sum = moe_sum + block.astype(FLOAT)
    mixed = (mid_rows + moe_sum).astype(BF16)[None]
    sum_out = sum_out.astype(FLOAT)
    sum_q = sum_q.astype(FLOAT)
    sum_kv = sum_kv.astype(FLOAT)
    small_sum = small_sum.astype(FLOAT).reshape(-1)
    at = 0
    pieces = []
    for size in (shard, shard, head_dim // nf, head_dim // nf, shard * n_experts):
        pieces.append(small_sum[at : at + size])
        at += size
    grad_gate = all_gate_up[:, 0].astype(FLOAT).reshape(n_experts, shard, hidden_size)
    all_gate_up, grad_gate = lax.optimization_barrier((all_gate_up, grad_gate))
    grad_up = all_gate_up[:, 1].astype(FLOAT).reshape(n_experts, shard, hidden_size)
    return (
        mixed,
        grad_tokens,
        pieces[0],
        sum_q,
        sum_kv[:shard],
        sum_kv[shard : 2 * shard],
        pieces[2],
        pieces[3],
        sum_out,
        pieces[1],
        pieces[4].reshape(shard, n_experts),
        grad_gate,
        grad_up,
        grad_down,
    )


def solution(mesh):
    by_token = P("fsdp", "sp", None)
    by_row = P("fsdp", None)
    by_inner = P(None, "fsdp", None)
    in_specs = (
        by_token,
        by_token,
        P("fsdp"),
        by_row,
        by_row,
        by_row,
        P("fsdp"),
        P("fsdp"),
        by_row,
        P("fsdp"),
        by_row,
        by_inner,
        by_inner,
        by_inner,
        by_token,
    )
    out_specs = (
        by_token,
        by_token,
        P("fsdp"),
        by_row,
        by_row,
        by_row,
        P("fsdp"),
        P("fsdp"),
        by_row,
        P("fsdp"),
        by_row,
        by_inner,
        by_inner,
        by_inner,
    )
    return jax.shard_map(body, mesh=mesh, in_specs=in_specs, out_specs=out_specs, check_vma=False)
```
